32 devices in a mesh: section: 4 (over z), tensor: 2 (over y), dp: 4 (over x, core).
Axes of the slice: x: 2, y: 2, z: 4, core: 2. Of those that a mesh axis runs over, the one named last changes fastest.
Arguments:
- tokens: bfloat16 [8, 1024, 1024], P('dp', 'tensor'), may hold values from -6 to 6
- timesteps: int32 [8], P('dp'), may hold values from 0 to 4999
- seg_starts: int32 [8, 4], P('dp'), may hold values from 0 to 768, as said below
- time_params: bfloat16 [2, 1024], replicated, may hold values from -5 to 5
- qkv_weight: bfloat16 [4, 1024, 3, 1024], P('section', None, None, 'tensor'), may hold values from -0.1875 to 0.1875
- qv_bias: bfloat16 [4, 2, 1024], P('section', None, 'tensor'), may hold values from -3 to 3
- out_weight: bfloat16 [4, 1024, 1024], P('section', 'tensor'), may hold values from -0.75 to 0.75
- ffn_in: bfloat16 [4, 1024, 4096], P('section', None, 'tensor'), may hold values from -0.1875 to 0.1875
- ffn_bias: bfloat16 [4, 4096], P('section', 'tensor'), may hold values from -3 to 3
- ffn_out: bfloat16 [4, 4096, 1024], P('section', 'tensor'), may hold values from -0.09375 to 0.09375
- ln_gains: bfloat16 [4, 2, 1024], P('section'), may hold values from 0.5 to 1.5
- row_biases: bfloat16 [4, 4, 1024], P('section'), may hold values from -2 to 2
- cotangent: bfloat16 [8, 1024, 1024], P('dp', 'tensor'), may hold values from -6 to 6
Outputs:
- layer_outs: bfloat16 [4, 8, 1024, 1024], P('section', 'dp', 'tensor')
- input_grads: bfloat16 [4, 8, 1024, 1024], P('section', 'dp', 'tensor')
- grad_qkv: float32 [4, 1024, 3, 1024], P('section', 'dp', None, 'tensor')
- grad_qv_bias: float32 [4, 2, 1024], P('section', None, ('tensor', 'dp'))
- grad_out_weight: float32 [4, 1024, 1024], P('section', ('tensor', 'dp'))
- grad_ffn_in: float32 [4, 1024, 4096], P('section', 'dp', 'tensor')
- grad_ffn_bias: float32 [4, 4096], P('section', ('tensor', 'dp'))
- grad_ffn_out: float32 [4, 4096, 1024], P('section', ('tensor', 'dp'))
- grad_gains: float32 [4, 2, 1024], P('section', None, ('tensor', 'dp'))
- grad_row_biases: float32 [4, 4, 1024], P('section', None, ('tensor', 'dp'))
- grad_time: float32 [2, 1024], replicated
The draws below stay inside these ranges and needn't reach their ends.
Inputs may be any that keep to these rules, and one draw needn't show every extreme that they name: `seg_starts`: in every row the first start is 0 and the starts rise strictly, by at most 256 from one to the next; position i belongs to the document of the last start at or before it.
All inputs are finite; a program needn't handle non-finite values.
Results may differ from the reference program's by a relative error of at most 0.025.
Values may be sent and summed in bfloat16 or wider, within the bound.
A program may use at most 256 MiB of HBM per device.

```python
import jax
import jax.numpy as jnp
from jax import lax

D = 1024
HEADS = 16
HEAD = 64
FF = 4096
SEQ = 1024
NSEG = 4
LAYERS = 4
ROWS = 8


def draw_seg_starts(key, part):
    key = jax.random.fold_in(key, 11)
    gap_key = jax.random.fold_in(key, 1)
    row_key = jax.random.fold_in(key, 2)
    widest = SEQ // NSEG
    gaps = jax.random.randint(gap_key, (ROWS, NSEG - 1), 1, widest + 1)
    chosen = jax.random.randint(row_key, (), 0, ROWS)
    row_index = jnp.arange(ROWS, dtype=jnp.int32)[:, None]
    gaps = jnp.where(row_index == chosen, widest, gaps).astype(jnp.int32)
    starts = jnp.cumsum(gaps, axis=1).astype(jnp.int32)
    return jnp.concatenate([jnp.zeros((ROWS, 1), jnp.int32), starts], axis=1)


def set_ends(result, own_key, smallest, largest):
    longest = result.shape.index(max(result.shape))
    spots = []
    for shift in (0, 1):
        where = [jax.random.randint(jax.random.fold_in(own_key, axis), (), 0, length) for axis, length in enumerate(result.shape)]
        where[longest] = (where[longest] + shift) % result.shape[longest]
        spots.append(tuple(where))
    return result.at[spots[0]].set(smallest).at[spots[1]].set(largest)


def shard_levels(rng, extent, pieces, least, high):
    factor_of, own = 1.0, jax.random.fold_in(rng, 6)
    for position, parts in pieces:
        steps = jnp.exp(jax.random.uniform(jax.random.fold_in(own, position), (parts,), jnp.float32, least / len(pieces), high / len(pieces)))
        factor_of = factor_of * jnp.repeat(steps, extent[position] // parts).reshape([-1 if axis == position else 1 for axis in range(len(extent))])
    return factor_of


def bell_draw(own_key, dims, scale, limit, split=(), kind=jnp.bfloat16):
    entries = scale * jax.random.normal(own_key, dims, jnp.float32)
    if split:
        entries = entries * shard_levels(own_key, dims, split, -0.22, 0.18)
    return jnp.clip(entries, -limit, limit).astype(kind)


def setup_inputs(seed: int = 0) -> dict:
    splits = jax.random.split(jax.random.key(seed), 14)
    tokens = bell_draw(splits[0], (ROWS, SEQ, D), 1.0, 6.0, ((0, 4), (1, 2)))
    timesteps = set_ends(jax.random.randint(splits[1], (ROWS,), 0, 5000), jax.random.fold_in(splits[1], 1), 0, 4999).astype(jnp.int32)
    seg_starts = draw_seg_starts(jax.random.fold_in(splits[13], 71), 0)
    time_params = bell_draw(splits[3], (2, D), 1.0, 5.0)
    qkv_weight = bell_draw(splits[4], (LAYERS, D, 3, D), D ** -0.5, 0.1875, ((0, 4), (3, 2)))
    qv_bias = bell_draw(splits[5], (LAYERS, 2, D), 0.5, 3.0, ((0, 4), (2, 2)))
    out_weight = bell_draw(splits[6], (LAYERS, D, D), (D // 16) ** -0.5, 0.75, ((0, 4), (1, 2)))
    ffn_in = bell_draw(splits[7], (LAYERS, D, FF), D ** -0.5, 0.1875, ((0, 4), (2, 2)))
    ffn_bias = bell_draw(splits[8], (LAYERS, FF), 0.5, 3.0, ((0, 4), (1, 2)))
    ffn_out = bell_draw(splits[9], (LAYERS, FF, D), FF ** -0.5, 0.09375, ((0, 4), (1, 2)))
    ln_gains = jnp.clip(1.0 + 0.1 * jax.random.normal(splits[10], (LAYERS, 2, D), jnp.float32), 0.5, 1.5).astype(jnp.bfloat16)
    row_biases = bell_draw(splits[11], (LAYERS, 4, D), 0.3, 2.0, ((0, 4),))
    cotangent = bell_draw(splits[12], (ROWS, SEQ, D), 1.0, 6.0, ((0, 4), (1, 2)))
    return dict(tokens=tokens, timesteps=timesteps, seg_starts=seg_starts, time_params=time_params, qkv_weight=qkv_weight, qv_bias=qv_bias, out_weight=out_weight, ffn_in=ffn_in, ffn_bias=ffn_bias, ffn_out=ffn_out, ln_gains=ln_gains, row_biases=row_biases, cotangent=cotangent)


@jax.custom_vjp
def low(v):
    return lax.optimization_barrier(v.astype(jnp.bfloat16)).astype(jnp.float32)

@jax.custom_vjp
def low_back(v):
    return v

def low_keep(v):
    return (low(v), None)

def low_pass(kept, grad):
    return (grad,)

def back_keep(v):
    return (v, None)

def back_low(kept, grad):
    return (low(grad),)
low.defvjp(low_keep, low_pass)
low_back.defvjp(back_keep, back_low)
highest = lax.Precision.HIGHEST
eps_norm = 1e-05

def doc_ids(starts, length):
    places = lax.broadcasted_iota(jnp.int32, (length, starts.shape[0]), 0)
    return lax.optimization_barrier(jnp.sum((starts[None, :] <= places).astype(jnp.int32), axis=1))

def layer_norm(value, gain_row, offset_row):
    average = lax.optimization_barrier(jnp.mean(value, axis=-1, keepdims=True))
    centered = value - average
    spread = lax.optimization_barrier(jnp.mean(centered * centered, axis=-1, keepdims=True))
    return centered * lax.rsqrt(spread + eps_norm) * gain_row + offset_row

def run_layer(inputs, segments, weights):
    qkv_w, qv_b, out_w, in_w, in_b, down_w, gains, biases = weights
    projected = jnp.einsum('td,dcf->tcf', inputs, qkv_w, precision=highest)
    queries = low(low_back(projected[:, 0] + qv_b[0])).reshape(SEQ, HEADS, HEAD)
    keys_all = low(low_back(projected[:, 1])).reshape(SEQ, HEADS, HEAD)
    values_all = low(low_back(projected[:, 2] + qv_b[1])).reshape(SEQ, HEADS, HEAD)
    scores = jnp.einsum('qhe,khe->hqk', queries, keys_all, precision=highest) * HEAD ** (-0.5)
    same_doc = segments[:, None] == segments[None, :]
    scores = low_back(jnp.where(same_doc[None], scores, -1e+30))
    probs = low(jax.nn.softmax(scores, axis=-1))
    mixed = jnp.einsum('hqk,khe->qhe', probs, values_all, precision=highest).reshape(SEQ, D)
    mixed = low(low_back(mixed))
    branch = low_back(jnp.dot(mixed, out_w, precision=highest))
    normed_a = layer_norm(branch + biases[0] + inputs, gains[0], biases[1])
    pre = low_back(jnp.dot(low(normed_a), in_w, precision=highest) + in_b)
    hidden = low(jax.nn.gelu(pre, approximate=False))
    branch_two = low_back(jnp.dot(hidden, down_w, precision=highest))
    return layer_norm(branch_two + biases[2] + normed_a, gains[1], biases[3])

def reference(tokens, timesteps, seg_starts, time_params, qkv_weight, qv_bias, out_weight, ffn_in, ffn_bias, ffn_out, ln_gains, row_biases, cotangent):
    floats = tuple((array.astype(jnp.float32) for array in (qkv_weight, qv_bias, out_weight, ffn_in, ffn_bias, ffn_out, ln_gains, row_biases)))
    fractions = timesteps.astype(jnp.float32) / 5000.0
    zero_pad = jnp.zeros((ROWS, LAYERS, SEQ, D), jnp.float32)

    def forward(token_values, time_values, weight_values, pads):

        def one_row(items):
            row_tokens, fraction, starts, row_pads = items
            segments = doc_ids(starts, SEQ)
            rounded = low(row_tokens + fraction * time_values[0] + time_values[1])
            results = []
            for layer_index in range(LAYERS):
                layer_input = low_back(rounded + row_pads[layer_index])
                weights = tuple((array[layer_index] for array in weight_values))
                rounded = low(run_layer(layer_input, segments, weights))
                results.append(rounded)
            return jnp.stack(results, 0)
        return lax.map(jax.checkpoint(one_row), (token_values, fractions, seg_starts, pads))
    outputs, pullback = jax.vjp(forward, tokens.astype(jnp.float32), time_params.astype(jnp.float32), floats, zero_pad)
    seed_grad = zero_pad.at[:, LAYERS - 1].set(cotangent.astype(jnp.float32))
    grad_tokens, grad_time, grad_weights, grad_pads = pullback(seed_grad)
    layer_outs = jnp.transpose(outputs, (1, 0, 2, 3)).astype(jnp.bfloat16)
    input_grads = jnp.transpose(grad_pads, (1, 0, 2, 3)).astype(jnp.bfloat16)
    return (layer_outs, input_grads, grad_weights[0], grad_weights[1], grad_weights[2], grad_weights[3], grad_weights[4], grad_weights[5], grad_weights[6], grad_weights[7], grad_time)
```

```python
import functools

import jax
import jax.numpy as jnp
from jax import lax
from jax.experimental import pallas as pl
from jax.experimental.pallas import tpu as pltpu
from jax.sharding import PartitionSpec as P

HEAD = 64
LANES = 128
MASKED = -1e30
eps_norm = 1e-05
AXES = ("section", "tensor", "dp")
low_type = jnp.bfloat16


class Layout:
    def __init__(self):
        self.sections = lax.axis_size("section")
        self.tensor = lax.axis_size("tensor")
        self.dp = lax.axis_size("dp")
        self.halves = self.tensor // 2
        self.chips = self.dp // 2
        self.size = self.tensor
        self.section = lax.axis_index("section")
        tensor, dp = lax.axis_index("tensor"), lax.axis_index("dp")
        self.group, self.part = tensor // self.halves, tensor % self.halves
        self.chip, self.core = dp // 2, dp % 2
        self.rank = self.core * self.halves + self.part
        self.home = self.group == self.core

    def move(self, value, target):
        pairs = []
        for s in range(self.sections):
            for t in range(self.tensor):
                for d in range(self.dp):
                    goal = target(s, t // self.halves, t % self.halves, d // 2, d % 2)
                    if goal is None:
                        continue
                    s2, g2, u2, x2, c2 = goal
                    here = (s * self.tensor + t) * self.dp + d
                    there = (s2 * self.tensor + g2 * self.halves + u2) * self.dp + x2 * 2 + c2
                    if here != there:
                        pairs.append((here, there))
        return lax.ppermute(value, AXES, pairs)

    def turn(self, value, step):
        def target(s, g, u, x, c):
            rank = (c * self.halves + u + step) % self.size
            return (s, g, rank % self.halves, x, rank // self.halves)

        return self.move(value, target)

    def group_sum(self, value):
        total = value.astype(jnp.float32)
        for step in range(1, self.size):
            total = total + self.turn(value, step).astype(jnp.float32)
        return total

    def group_gather(self, value):
        if self.size == 2:
            other = self.turn(value, 1)
            first = self.rank == 0
            return jnp.stack([jnp.where(first, value, other), jnp.where(first, other, value)])
        whole = jnp.zeros((self.size,) + value.shape, value.dtype)
        for step in range(self.size):
            piece = value if step == 0 else self.turn(value, step)
            whole = lax.dynamic_update_index_in_dim(
                whole, piece, (self.rank - step) % self.size, 0
            )
        return whole


def dot_rows(a, b):
    return lax.dot_general(a, b, (((1,), (1,)), ((), ())), preferred_element_type=jnp.float32)


def dot_plain(a, b):
    return lax.dot_general(a, b, (((1,), (0,)), ((), ())), preferred_element_type=jnp.float32)


def dot_first(a, b):
    return lax.dot_general(a, b, (((0,), (0,)), ((), ())), preferred_element_type=jnp.float32)


def tile_docs(starts_ref, length, count):
    place = lax.broadcasted_iota(jnp.int32, (length, LANES), 0)
    doc = jnp.zeros((length, LANES), jnp.int32)
    for j in range(count):
        doc = doc + (starts_ref[j] <= place).astype(jnp.int32)
    lane = lax.broadcasted_iota(jnp.int32, (length, LANES), 1)
    rel = lane % HEAD
    return lane < HEAD, rel, rel + 1 == doc


def three_parts(value):
    high = value.astype(low_type)
    rest = value - high.astype(jnp.float32)
    middle = rest.astype(low_type)
    return high, middle, (rest - middle.astype(jnp.float32)).astype(low_type)


def lanes(rel, count, value, base):
    high, middle, small = three_parts(value)
    return jnp.where(
        rel == count,
        high,
        jnp.where(rel == count + 1, middle, jnp.where(rel == count + 2, small, base)),
    )


def attend_kernel(starts_ref, q_ref, k_ref, v_ref, o_ref, l_ref, *, count, rows):
    length = q_ref.shape[0]
    first, rel, own = tile_docs(starts_ref, length, count)
    extra_k = jnp.where(own, 1.0, 0.0).astype(low_type)
    extra_q = jnp.where(
        jnp.logical_and(rel < count, jnp.logical_not(own)), MASKED, 0.0
    ).astype(low_type)
    q = q_ref[...] * low_type(HEAD**-0.5)
    k = k_ref[...]
    v = v_ref[...]
    ones = jnp.ones_like(v)
    heads = (
        (jnp.where(first, q, extra_q), jnp.where(first, k, extra_k), jnp.where(first, v, ones)),
        (jnp.where(first, extra_q, q), jnp.where(first, extra_k, k), jnp.where(first, ones, v)),
    )
    side = first[:rows]
    for start in range(0, length, rows):
        peaks, sums = [], []
        for q_head, k_head, v_head in heads:
            scores = dot_rows(q_head[start : start + rows], k_head)
            peak = jnp.max(scores, axis=-1, keepdims=True)
            powers = jnp.exp(scores - peak).astype(low_type)
            peaks.append(peak)
            sums.append(dot_plain(powers, v_head))
        mixed = jnp.where(side, sums[0], sums[1])
        totals = jnp.where(side, sums[1], sums[0])
        log_sums = jnp.where(side, peaks[1], peaks[0]) + jnp.log(totals)
        l_ref[start : start + rows] = lanes(
            rel[:rows], count, -log_sums, extra_q[start : start + rows]
        )
        o_ref[start : start + rows] = (mixed / pltpu.roll(totals, HEAD, 1)).astype(low_type)


def attend(qkv, starts):
    length, columns = qkv.shape[0], qkv.shape[1] // 3
    pairs = columns // LANES
    rows = min(512, length)

    def block(offset):
        return pl.BlockSpec((length, LANES), lambda j: (0, offset + j))

    return pl.pallas_call(
        functools.partial(attend_kernel, count=starts.shape[0], rows=rows),
        grid=(pairs,),
        in_specs=[
            pl.BlockSpec(memory_space=pltpu.SMEM),
            block(0),
            block(pairs),
            block(2 * pairs),
        ],
        out_specs=[block(0), block(0)],
        out_shape=[
            jax.ShapeDtypeStruct((length, columns), low_type),
            jax.ShapeDtypeStruct((length, columns), low_type),
        ],
        compiler_params=pltpu.CompilerParams(vmem_limit_bytes=48 * 1024 * 1024),
        cost_estimate=pl.CostEstimate(
            flops=16 * length * length * columns // 4,
            bytes_accessed=12 * length * columns,
            transcendentals=length * length * columns // HEAD,
        ),
        name="attend",
    )(starts, qkv, qkv, qkv)


def attend_back_kernel(
    starts_ref, q_ref, k_ref, v_ref, o_ref, l_ref, g_ref, dq_ref, dk_ref, dv_ref, *, count, rows
):
    length = q_ref.shape[0]
    first, rel, own = tile_docs(starts_ref, length, count)
    stat = jnp.logical_and(rel >= count, rel < count + 3)
    extra_k = jnp.where(jnp.logical_or(own, stat), 1.0, 0.0).astype(low_type)
    extra_v = jnp.where(stat, 1.0, 0.0).astype(low_type)
    extra_q = l_ref[...]
    g = g_ref[...]
    product = g.astype(jnp.float32) * o_ref[...].astype(jnp.float32)
    dots = [
        jnp.sum(jnp.where(first, product, 0.0), axis=-1, keepdims=True),
        jnp.sum(jnp.where(first, 0.0, product), axis=-1, keepdims=True),
    ]
    extra_g = lanes(rel, count, -jnp.where(first, dots[1], dots[0]), jnp.zeros_like(extra_q))
    q = q_ref[...] * low_type(HEAD**-0.5)
    k = k_ref[...]
    v = v_ref[...]
    heads = (
        tuple(
            jnp.where(first, a, b)
            for a, b in ((q, extra_q), (k, extra_k), (v, extra_v), (g, extra_g))
        ),
        tuple(
            jnp.where(first, b, a)
            for a, b in ((q, extra_q), (k, extra_k), (v, extra_v), (g, extra_g))
        ),
    )
    grad_k = [jnp.zeros((length, LANES), jnp.float32)] * 2
    grad_v = [jnp.zeros((length, LANES), jnp.float32)] * 2
    for start in range(0, length, rows):
        part = slice(start, start + rows)
        grad_q = []
        for i, (q_head, k_head, v_head, g_head) in enumerate(heads):
            probs = jnp.exp(dot_rows(k_head, q_head[part]))
            slopes = (probs * dot_rows(v_head, g_head[part])).astype(low_type)
            grad_v[i] = grad_v[i] + dot_plain(probs.astype(low_type), g[part])
            grad_k[i] = grad_k[i] + dot_plain(slopes, q[part])
            grad_q.append(dot_first(slopes, k))
        dq_ref[part] = (
            jnp.where(first[:rows], grad_q[0], grad_q[1]) * (HEAD**-0.5)
        ).astype(low_type)
    dk_ref[...] = jnp.where(first, grad_k[0], grad_k[1]).astype(low_type)
    dv_ref[...] = jnp.where(first, grad_v[0], grad_v[1]).astype(low_type)


def attend_back(qkv, starts, mixed, log_sums, grad_mixed):
    length, columns = mixed.shape
    pairs = columns // LANES
    rows = min(256, length)

    def block(offset):
        return pl.BlockSpec((length, LANES), lambda j: (0, offset + j))

    return pl.pallas_call(
        functools.partial(attend_back_kernel, count=starts.shape[0], rows=rows),
        grid=(pairs,),
        in_specs=[
            pl.BlockSpec(memory_space=pltpu.SMEM),
            block(0),
            block(pairs),
            block(2 * pairs),
            block(0),
            block(0),
            block(0),
        ],
        out_specs=[block(0)] * 3,
        out_shape=[jax.ShapeDtypeStruct((length, columns), low_type)] * 3,
        compiler_params=pltpu.CompilerParams(vmem_limit_bytes=48 * 1024 * 1024),
        cost_estimate=pl.CostEstimate(
            flops=40 * length * length * columns // 4,
            bytes_accessed=20 * length * columns,
            transcendentals=length * length * columns // HEAD,
        ),
        name="attend_back",
    )(starts, qkv, qkv, qkv, mixed, log_sums, grad_mixed)


def unit_norm(value):
    average = jnp.mean(value, axis=-1, keepdims=True)
    centered = value - average
    inv_scale = lax.rsqrt(jnp.mean(centered * centered, axis=-1, keepdims=True) + eps_norm)
    return centered * inv_scale, inv_scale


def norm_back(gradient, normed, inv_scale, gain_row):
    weighted = gradient * gain_row
    adjusted = (
        weighted
        - jnp.mean(weighted, axis=-1, keepdims=True)
        - normed * jnp.mean(weighted * normed, axis=-1, keepdims=True)
    )
    return inv_scale * adjusted


def gelu_pair(pre):
    normal = 0.5 * (1.0 + lax.erf(pre * 0.7071067811865476))
    density = jnp.exp(-0.5 * pre * pre) * 0.3989422804014327
    return pre * normal, normal + pre * density


def forward_layer(at, inputs, starts, params):
    qkv_w, qkv_b, out_w, in_w, in_b, down_w, gains, biases = params
    qkv = (dot_plain(inputs, qkv_w) + qkv_b).astype(low_type)
    mixed, log_sums = attend(qkv, starts)
    branch = at.group_sum(dot_plain(mixed, out_w).astype(low_type))
    unit_a, scale_a = unit_norm(branch + biases[0] + inputs.astype(jnp.float32))
    middle = unit_a * gains[0] + biases[1]
    low_middle = middle.astype(low_type)
    hidden, slope = gelu_pair(dot_plain(low_middle, in_w) + in_b)
    hidden = hidden.astype(low_type)
    branch_two = at.group_sum(dot_plain(hidden, down_w).astype(low_type))
    unit_z, scale_z = unit_norm(branch_two + biases[2] + middle)
    result = (unit_z * gains[1] + biases[3]).astype(low_type)
    saved = dict(
        inputs=inputs,
        qkv=qkv,
        mixed=mixed,
        log_sums=log_sums,
        scale_a=scale_a[:, 0],
        middle=low_middle,
        hidden=hidden,
        slope=slope.astype(low_type),
        scale_z=scale_z[:, 0],
    )
    return result, saved


def backward_layer(at, saved, incoming, starts, params):
    qkv_w, qkv_b, out_w, in_w, in_b, down_w, gains, biases = params
    gradient = incoming.astype(jnp.float32)
    unit_z = (saved["result"].astype(jnp.float32) - biases[3]) / gains[1]
    grad_z = norm_back(gradient, unit_z, saved["scale_z"][:, None], gains[1])
    low_gz = grad_z.astype(low_type)
    grad_pre = (dot_rows(low_gz, down_w) * saved["slope"].astype(jnp.float32)).astype(low_type)
    grad_mid = at.group_sum(dot_rows(grad_pre, in_w).astype(low_type)) + grad_z
    unit_a = (saved["middle"].astype(jnp.float32) - biases[1]) / gains[0]
    grad_a = norm_back(grad_mid, unit_a, saved["scale_a"][:, None], gains[0])
    low_ga = grad_a.astype(low_type)
    grad_mixed = dot_rows(low_ga, out_w).astype(low_type)
    grad_qkv = jnp.concatenate(
        attend_back(saved["qkv"], starts, saved["mixed"], saved["log_sums"], grad_mixed), 1
    )
    grad_x = at.group_sum(dot_rows(grad_qkv, qkv_w).astype(low_type)) + grad_a
    sums = jnp.stack(
        [
            jnp.sum(grad_mid * unit_a, axis=0),
            jnp.sum(gradient * unit_z, axis=0),
            jnp.sum(grad_a, axis=0),
            jnp.sum(grad_mid, axis=0),
            jnp.sum(grad_z, axis=0),
            jnp.sum(gradient, axis=0),
        ]
    )
    kept = dict(grad_z=low_gz, slope=grad_pre, grad_a=low_ga, qkv=grad_qkv)
    return grad_x.astype(low_type), kept, sums


def store(buffers, values, slot):
    return jax.tree.map(
        lambda buffer, value: lax.dynamic_update_index_in_dim(buffer, value, slot, 0),
        buffers,
        values,
    )


def pick(buffers, slot):
    return jax.tree.map(
        lambda buffer: lax.dynamic_index_in_dim(buffer, slot, 0, keepdims=False), buffers
    )


def group_weight(at, weight):
    parts = weight.reshape((at.chips, -1) + weight.shape[1:])

    def across(s, g, u, x, c):
        return (s, c, u, x, g) if g != c else None

    def along(step):
        return lambda s, g, u, x, c: (s, g, u, (x + step) % at.chips, c) if g != c else None

    piece = at.move(lax.dynamic_index_in_dim(parts, at.chip, 0, keepdims=False), across)
    pieces = [piece]
    for step in range(1, at.chips):
        pieces.append(at.move(piece, along(step)))
    whole = parts
    for step, piece in enumerate(pieces):
        spot = (at.chip - step) % at.chips
        own = lax.dynamic_index_in_dim(parts, spot, 0, keepdims=False)
        whole = lax.dynamic_update_index_in_dim(whole, jnp.where(at.home, own, piece), spot, 0)
    return whole.reshape(weight.shape)


def group_rows(at, tokens, section):
    def across(s, g, u, x, c):
        return (s, 1 - g, u, x, c) if s == section else None

    own = lax.dynamic_index_in_dim(tokens, at.group, 0, keepdims=False)
    other = at.move(lax.dynamic_index_in_dim(tokens, 1 - at.group, 0, keepdims=False), across)
    lower = at.group == 0
    pair = jnp.stack([jnp.where(lower, own, other), jnp.where(lower, other, own)])
    whole = at.group_gather(pair)
    whole = whole.reshape((2, at.halves) + pair.shape)
    whole = jnp.swapaxes(whole, 1, 2)
    return whole.reshape(2, -1, tokens.shape[-1])


def spread_rows(at, rows, length):
    def across(s, g, u, x, c):
        return (s, 1 - g, u, x, c)

    row = lax.dynamic_index_in_dim(rows, at.core, 0, keepdims=False)
    tile = length // at.tensor

    def piece(group):
        return lax.dynamic_slice_in_dim(row, (group * at.halves + at.part) * tile, tile, 0)

    own = piece(at.group)
    other = at.move(piece(1 - at.group), across)
    lower = at.group == 0
    return jnp.stack([jnp.where(lower, own, other), jnp.where(lower, other, own)])


def sum_weight(at, gradient, across_first):
    parts = gradient.reshape((at.chips, -1) + gradient.shape[1:])

    def across(s, g, u, x, c):
        return (s, c, u, x, c) if g != c else None

    def along(step):
        def target(s, g, u, x, c):
            if across_first and g != c:
                return None
            return (s, g, u, (x + step) % at.chips, c)

        return target

    def fold_chips(parts):
        total = lax.dynamic_index_in_dim(parts, at.chip, 0, keepdims=False).astype(jnp.float32)
        for step in range(1, at.chips):
            piece = lax.dynamic_index_in_dim(
                parts, (at.chip + step) % at.chips, 0, keepdims=False
            )
            total = total + at.move(piece, along(step)).astype(jnp.float32)
        return total.astype(low_type)

    if across_first:
        total = fold_chips(
            (parts.astype(jnp.float32) + at.move(parts, across).astype(jnp.float32)).astype(
                low_type
            )
        )
    else:
        part = fold_chips(parts)
        total = (part.astype(jnp.float32) + at.move(part, across).astype(jnp.float32)).astype(
            low_type
        )
    halves = total.reshape((2, -1) + total.shape[1:])

    def over(s, g, u, x, c):
        return (s, g, u, x, 1 - c) if g == c else None

    own = lax.dynamic_index_in_dim(halves, at.core, 0, keepdims=False)
    other = at.move(lax.dynamic_index_in_dim(halves, 1 - at.core, 0, keepdims=False), over)
    return jnp.where(at.home, own, other).astype(jnp.float32)


def shards(
    tokens,
    timesteps,
    seg_starts,
    time_params,
    qkv_weight,
    qv_bias,
    out_weight,
    ffn_in,
    ffn_bias,
    ffn_out,
    ln_gains,
    row_biases,
    cotangent,
):
    at = Layout()
    width = tokens.shape[-1]
    length = tokens.shape[1] * at.tensor
    micro_count = 2
    tick_count = micro_count + at.sections - 1
    slots = micro_count + 1
    columns = qkv_weight.shape[3]

    def both_cores(value):
        def over(s, g, u, x, c):
            return (s, g, u, x, 1 - c)

        other = at.move(value, over)
        first = at.core == 0
        mine = jnp.stack([jnp.where(first, value, other), jnp.where(first, other, value)])
        return lax.dynamic_index_in_dim(mine, at.group, 1, keepdims=False)

    starts = both_cores(seg_starts)
    fractions_own = timesteps.astype(jnp.float32) / 5000.0
    fractions = both_cores(fractions_own)
    time_values = time_params.astype(jnp.float32)
    embedded = (
        tokens.astype(jnp.float32) + fractions_own[:, None, None] * time_values[0] + time_values[1]
    ).astype(low_type)
    rows_in = group_rows(at, embedded, 0)
    qv_low = group_weight(at, qv_bias[0].T).T.astype(jnp.float32)
    qkv_w = group_weight(at, qkv_weight[0].reshape(width, 3 * columns))
    out_w = group_weight(at, out_weight[0])
    in_w = group_weight(at, ffn_in[0])
    in_b = group_weight(at, ffn_bias[0])
    down_w = group_weight(at, ffn_out[0])
    rows_back = group_rows(at, cotangent, at.sections - 1)
    qkv_b = jnp.concatenate([qv_low[0], jnp.zeros((columns,), jnp.float32), qv_low[1]])
    params = (
        qkv_w,
        qkv_b,
        out_w,
        in_w,
        in_b.astype(jnp.float32),
        down_w,
        ln_gains[0].astype(jnp.float32),
        row_biases[0].astype(jnp.float32),
    )

    def hop(result, distance):
        def target(s, g, u, x, c):
            return (s + distance, g, u, x, c) if 0 <= s + distance < at.sections else None

        tile = length // at.size
        piece = at.move(lax.dynamic_slice_in_dim(result, at.rank * tile, tile, 0), target)
        return at.group_gather(piece).reshape(length, width)

    def place_of(tick_value, stage):
        place = tick_value - stage
        usable = jnp.logical_and(place >= 0, place < micro_count)
        return usable, jnp.clip(place, 0, micro_count - 1), jnp.where(usable, place, micro_count)

    def empty(values):
        return jax.tree.map(
            lambda value: jnp.zeros((slots,) + value.shape, value.dtype), values
        )

    def forward_tick(tick_value, arrived, stash, outputs):
        usable, position, slot = place_of(tick_value, at.section)
        inputs = jnp.where(at.section == 0, rows_in[position], arrived)
        result, saved = forward_layer(at, inputs, starts[position], params)
        if stash is None:
            return result, saved
        return result, store(stash, saved, slot), store(outputs, result, slot)

    blank = jnp.zeros((length, width), low_type)
    shapes = jax.eval_shape(lambda: forward_tick(0, blank, None, None))
    stash, outputs = empty(shapes[1]), empty(shapes[0])

    def forward_loop(tick_value, carry):
        result, stash, outputs = forward_tick(tick_value, *carry)
        return hop(result, 1), stash, outputs

    carry = lax.fori_loop(0, tick_count - 1, forward_loop, (blank, stash, outputs))
    _, stash, outputs = forward_tick(tick_count - 1, *carry)
    layer_outs = spread_rows(at, outputs, length)

    def backward_tick(tick_value, arrived, stash, grads, totals):
        usable, position, slot = place_of(tick_value, at.sections - 1 - at.section)
        incoming = jnp.where(at.section == at.sections - 1, rows_back[position], arrived)
        grad_x, kept_now, sums = backward_layer(
            at, pick(dict(stash, result=outputs), slot), incoming, starts[position], params
        )
        totals = totals + jnp.where(usable, sums, 0.0)
        kept = store({name: stash[name] for name in kept_now}, kept_now, slot)
        return grad_x, dict(stash, **kept), store(grads, grad_x, slot), totals

    for name in ("grad_z", "grad_a"):
        stash[name] = empty(blank)
    totals = jnp.zeros((6, width), jnp.float32)

    def backward_loop(tick_value, carry):
        grad_x, stash, grads, totals = backward_tick(tick_value, *carry)
        return hop(grad_x, -1), stash, grads, totals

    carry = lax.fori_loop(
        0, tick_count - 1, backward_loop, (blank, stash, empty(blank), totals)
    )
    _, stash, grads, totals = backward_tick(tick_count - 1, *carry)
    input_grads = spread_rows(at, grads, length)

    def both(buffer):
        return buffer[:micro_count].reshape((micro_count * length,) + buffer.shape[2:])

    low_gz, grad_pre, low_ga, grad_qkv = (
        both(stash[name]) for name in ("grad_z", "slope", "grad_a", "qkv")
    )
    down_g = sum_weight(at, dot_first(both(stash["hidden"]), low_gz).astype(low_type), True)
    in_g = sum_weight(at, dot_first(both(stash["middle"]), grad_pre).astype(low_type), False)
    out_g = sum_weight(at, dot_first(both(stash["mixed"]), low_ga).astype(low_type), True)
    qkv_g = sum_weight(at, dot_first(both(stash["inputs"]), grad_qkv).astype(low_type), False)

    in_bias_g = jnp.sum(grad_pre, axis=0, dtype=jnp.float32)
    qkv_bias_g = jnp.sum(grad_qkv, axis=0, dtype=jnp.float32).reshape(3, columns)
    sliced = jnp.concatenate([qkv_bias_g[0], qkv_bias_g[2], in_bias_g])
    every = jnp.zeros((at.size,) + sliced.shape, jnp.float32)
    every = lax.dynamic_update_index_in_dim(every, sliced, at.rank, 0)
    row_terms = jnp.where(at.rank == 0, totals, 0.0)
    small = lax.psum(
        jnp.concatenate([row_terms.reshape(-1), every.reshape(-1)]), ("tensor", "dp")
    )
    row_sums = small[: row_terms.size].reshape(row_terms.shape)
    tensor = lax.axis_index("tensor")
    dp = lax.axis_index("dp")
    mine = lax.dynamic_index_in_dim(
        small[row_terms.size :].reshape(every.shape), tensor, 0, keepdims=False
    )

    def share(value, count, index):
        size = value.shape[-1] // count
        return lax.dynamic_slice_in_dim(value, index * size, size, value.ndim - 1)

    qv_g = share(mine[: 2 * columns].reshape(2, columns), at.dp, dp)
    in_bias_g = share(mine[2 * columns :], at.dp, dp)
    row_share = share(row_sums, at.tensor * at.dp, tensor * at.dp + dp)

    grad_rows = grads[:micro_count].astype(jnp.float32)
    row_grads = jnp.sum(grad_rows, axis=1)
    time_terms = jnp.stack([jnp.sum(fractions[:, None] * row_grads, 0), jnp.sum(row_grads, 0)])
    time_terms = jnp.where(jnp.logical_and(at.section == 0, at.rank == 0), time_terms, 0.0)
    grad_time = lax.psum(time_terms, AXES)
    return (
        layer_outs[None],
        input_grads[None],
        qkv_g.reshape(-1, 3, columns)[None],
        qv_g[None],
        out_g[None],
        in_g[None],
        in_bias_g[None],
        down_g[None],
        row_share[None, :2],
        row_share[None, 2:],
        grad_time,
    )


def solution(mesh):
    return jax.shard_map(
        shards,
        mesh=mesh,
        in_specs=(
            P("dp", "tensor", None),
            P("dp"),
            P("dp", None),
            P(),
            P("section", None, None, "tensor"),
            P("section", None, "tensor"),
            P("section", "tensor", None),
            P("section", None, "tensor"),
            P("section", "tensor"),
            P("section", "tensor", None),
            P("section", None, None),
            P("section", None, None),
            P("dp", "tensor", None),
        ),
        out_specs=(
            P("section", "dp", "tensor", None),
            P("section", "dp", "tensor", None),
            P("section", "dp", None, "tensor"),
            P("section", None, ("tensor", "dp")),
            P("section", ("tensor", "dp"), None),
            P("section", "dp", "tensor"),
            P("section", ("tensor", "dp")),
            P("section", ("tensor", "dp"), None),
            P("section", None, ("tensor", "dp")),
            P("section", None, ("tensor", "dp")),
            P(),
        ),
        check_vma=False,
    )
```

```python
import functools

import jax
import jax.numpy as jnp
from jax import lax
from jax.experimental import pallas as pl
from jax.experimental.pallas import tpu as pltpu
from jax.sharding import PartitionSpec as P

HEAD = 64
LANES = 128
MASKED = -1e30
eps_norm = 1e-05
AXES = ("section", "tensor", "dp")
low_type = jnp.bfloat16


class Layout:
    def __init__(self):
        self.sections = lax.axis_size("section")
        self.tensor = lax.axis_size("tensor")
        self.dp = lax.axis_size("dp")
        self.halves = self.tensor // 2
        self.chips = self.dp // 2
        self.size = self.tensor
        self.section = lax.axis_index("section")
        tensor, dp = lax.axis_index("tensor"), lax.axis_index("dp")
        self.group, self.part = tensor // self.halves, tensor % self.halves
        self.chip, self.core = dp // 2, dp % 2
        self.rank = self.core * self.halves + self.part
        self.home = self.group == self.core

    def move(self, value, target):
        pairs = []
        for s in range(self.sections):
            for t in range(self.tensor):
                for d in range(self.dp):
                    goal = target(s, t // self.halves, t % self.halves, d // 2, d % 2)
                    if goal is None:
                        continue
                    s2, g2, u2, x2, c2 = goal
                    here = (s * self.tensor + t) * self.dp + d
                    there = (s2 * self.tensor + g2 * self.halves + u2) * self.dp + x2 * 2 + c2
                    if here != there:
                        pairs.append((here, there))
        return lax.ppermute(value, AXES, pairs)

    def turn(self, value, step):
        def target(s, g, u, x, c):
            rank = (c * self.halves + u + step) % self.size
            return (s, g, rank % self.halves, x, rank // self.halves)

        return self.move(value, target)

    def group_sum(self, value):
        total = value.astype(jnp.float32)
        for step in range(1, self.size):
            total = total + self.turn(value, step).astype(jnp.float32)
        return total

    def group_gather(self, value):
        if self.size == 2:
            other = self.turn(value, 1)
            first = self.rank == 0
            return jnp.stack([jnp.where(first, value, other), jnp.where(first, other, value)])
        whole = jnp.zeros((self.size,) + value.shape, value.dtype)
        for step in range(self.size):
            piece = value if step == 0 else self.turn(value, step)
            whole = lax.dynamic_update_index_in_dim(
                whole, piece, (self.rank - step) % self.size, 0
            )
        return whole


def dot_rows(a, b):
    return lax.dot_general(a, b, (((1,), (1,)), ((), ())), preferred_element_type=jnp.float32)


def dot_plain(a, b):
    return lax.dot_general(a, b, (((1,), (0,)), ((), ())), preferred_element_type=jnp.float32)


def dot_first(a, b):
    return lax.dot_general(a, b, (((0,), (0,)), ((), ())), preferred_element_type=jnp.float32)


def tile_docs(starts_ref, length, count):
    place = lax.broadcasted_iota(jnp.int32, (length, LANES), 0)
    doc = jnp.zeros((length, LANES), jnp.int32)
    for j in range(count):
        doc = doc + (starts_ref[j] <= place).astype(jnp.int32)
    lane = lax.broadcasted_iota(jnp.int32, (length, LANES), 1)
    rel = lane % HEAD
    return lane < HEAD, rel, rel + 1 == doc


def three_parts(value):
    high = value.astype(low_type)
    rest = value - high.astype(jnp.float32)
    middle = rest.astype(low_type)
    return high, middle, (rest - middle.astype(jnp.float32)).astype(low_type)


def lanes(rel, count, value, base):
    high, middle, small = three_parts(value)
    return jnp.where(
        rel == count,
        high,
        jnp.where(rel == count + 1, middle, jnp.where(rel == count + 2, small, base)),
    )


def attend_kernel(starts_ref, q_ref, k_ref, v_ref, o_ref, l_ref, *, count, rows):
    length = q_ref.shape[0]
    first, rel, own = tile_docs(starts_ref, length, count)
    extra_k = jnp.where(own, 1.0, 0.0).astype(low_type)
    extra_q = jnp.where(
        jnp.logical_and(rel < count, jnp.logical_not(own)), MASKED, 0.0
    ).astype(low_type)
    q = q_ref[...] * low_type(HEAD**-0.5)
    k = k_ref[...]
    v = v_ref[...]
    ones = jnp.ones_like(v)
    heads = (
        (jnp.where(first, q, extra_q), jnp.where(first, k, extra_k), jnp.where(first, v, ones)),
        (jnp.where(first, extra_q, q), jnp.where(first, extra_k, k), jnp.where(first, ones, v)),
    )
    side = first[:rows]
    for start in range(0, length, rows):
        peaks, sums = [], []
        for q_head, k_head, v_head in heads:
            scores = dot_rows(q_head[start : start + rows], k_head)
            peak = jnp.max(scores, axis=-1, keepdims=True)
            powers = jnp.exp(scores - peak).astype(low_type)
            peaks.append(peak)
            sums.append(dot_plain(powers, v_head))
        mixed = jnp.where(side, sums[0], sums[1])
        totals = jnp.where(side, sums[1], sums[0])
        log_sums = jnp.where(side, peaks[1], peaks[0]) + jnp.log(totals)
        l_ref[start : start + rows] = lanes(
            rel[:rows], count, -log_sums, extra_q[start : start + rows]
        )
        o_ref[start : start + rows] = (mixed / pltpu.roll(totals, HEAD, 1)).astype(low_type)


def attend(qkv, starts):
    length, columns = qkv.shape[0], qkv.shape[1] // 3
    pairs = columns // LANES
    rows = min(512, length)

    def block(offset):
        return pl.BlockSpec((length, LANES), lambda j: (0, offset + j))

    return pl.pallas_call(
        functools.partial(attend_kernel, count=starts.shape[0], rows=rows),
        grid=(pairs,),
        in_specs=[
            pl.BlockSpec(memory_space=pltpu.SMEM),
            block(0),
            block(pairs),
            block(2 * pairs),
        ],
        out_specs=[block(0), block(0)],
        out_shape=[
            jax.ShapeDtypeStruct((length, columns), low_type),
            jax.ShapeDtypeStruct((length, columns), low_type),
        ],
        compiler_params=pltpu.CompilerParams(vmem_limit_bytes=48 * 1024 * 1024),
        cost_estimate=pl.CostEstimate(
            flops=16 * length * length * columns // 4,
            bytes_accessed=12 * length * columns,
            transcendentals=length * length * columns // HEAD,
        ),
        name="attend",
    )(starts, qkv, qkv, qkv)


def attend_back_kernel(
    starts_ref, q_ref, k_ref, v_ref, o_ref, l_ref, g_ref, dq_ref, dk_ref, dv_ref, *, count, rows
):
    length = q_ref.shape[0]
    first, rel, own = tile_docs(starts_ref, length, count)
    stat = jnp.logical_and(rel >= count, rel < count + 3)
    extra_k = jnp.where(jnp.logical_or(own, stat), 1.0, 0.0).astype(low_type)
    extra_v = jnp.where(stat, 1.0, 0.0).astype(low_type)
    extra_q = l_ref[...]
    g = g_ref[...]
    product = g.astype(jnp.float32) * o_ref[...].astype(jnp.float32)
    dots = [
        jnp.sum(jnp.where(first, product, 0.0), axis=-1, keepdims=True),
        jnp.sum(jnp.where(first, 0.0, product), axis=-1, keepdims=True),
    ]
    extra_g = lanes(rel, count, -jnp.where(first, dots[1], dots[0]), jnp.zeros_like(extra_q))
    q = q_ref[...] * low_type(HEAD**-0.5)
    k = k_ref[...]
    v = v_ref[...]
    heads = (
        tuple(
            jnp.where(first, a, b)
            for a, b in ((q, extra_q), (k, extra_k), (v, extra_v), (g, extra_g))
        ),
        tuple(
            jnp.where(first, b, a)
            for a, b in ((q, extra_q), (k, extra_k), (v, extra_v), (g, extra_g))
        ),
    )
    grad_k = [jnp.zeros((length, LANES), jnp.float32)] * 2
    grad_v = [jnp.zeros((length, LANES), jnp.float32)] * 2
    for start in range(0, length, rows):
        part = slice(start, start + rows)
        grad_q = []
        for i, (q_head, k_head, v_head, g_head) in enumerate(heads):
            probs = jnp.exp(dot_rows(k_head, q_head[part]))
            slopes = (probs * dot_rows(v_head, g_head[part])).astype(low_type)
            grad_v[i] = grad_v[i] + dot_plain(probs.astype(low_type), g[part])
            grad_k[i] = grad_k[i] + dot_plain(slopes, q[part])
            grad_q.append(dot_first(slopes, k))
        dq_ref[part] = (
            jnp.where(first[:rows], grad_q[0], grad_q[1]) * (HEAD**-0.5)
        ).astype(low_type)
    dk_ref[...] = jnp.where(first, grad_k[0], grad_k[1]).astype(low_type)
    dv_ref[...] = jnp.where(first, grad_v[0], grad_v[1]).astype(low_type)


def attend_back(qkv, starts, mixed, log_sums, grad_mixed):
    length, columns = mixed.shape
    pairs = columns // LANES
    rows = min(256, length)

    def block(offset):
        return pl.BlockSpec((length, LANES), lambda j: (0, offset + j))

    return pl.pallas_call(
        functools.partial(attend_back_kernel, count=starts.shape[0], rows=rows),
        grid=(pairs,),
        in_specs=[
            pl.BlockSpec(memory_space=pltpu.SMEM),
            block(0),
            block(pairs),
            block(2 * pairs),
            block(0),
            block(0),
            block(0),
        ],
        out_specs=[block(0)] * 3,
        out_shape=[jax.ShapeDtypeStruct((length, columns), low_type)] * 3,
        compiler_params=pltpu.CompilerParams(vmem_limit_bytes=48 * 1024 * 1024),
        cost_estimate=pl.CostEstimate(
            flops=40 * length * length * columns // 4,
            bytes_accessed=20 * length * columns,
            transcendentals=length * length * columns // HEAD,
        ),
        name="attend_back",
    )(starts, qkv, qkv, qkv, mixed, log_sums, grad_mixed)


MESH = pl.DeviceIdType.MESH


def rows_of(index, size):
    return pl.ds(pl.multiple_of(index * size, size), size)


def erf_pair(pre):
    bell = jnp.exp(-0.5 * pre * pre)
    size = jnp.abs(pre)
    t = 1.0 / (1.0 + 0.2316418882663604 * size)
    tail = bell * t * (
        0.127414796
        + t * (-0.142248368 + t * (0.7107068705 + t * (-0.7265760135 + t * 0.5307027145)))
    )
    return jnp.where(pre < 0.0, tail, 1.0 - tail), bell * 0.3989422804014327


def norm_rows(value):
    average = jnp.mean(value, axis=-1, keepdims=True)
    centered = value - average
    inv_scale = lax.rsqrt(jnp.mean(centered * centered, axis=-1, keepdims=True) + eps_norm)
    return centered * inv_scale, inv_scale


def doc_lanes(starts_ref, row, first_row, shape, count):
    place = lax.broadcasted_iota(jnp.int32, shape, 0) + first_row
    doc = jnp.zeros(shape, jnp.int32)
    for j in range(count):
        doc = doc + (starts_ref[row, j] <= place).astype(jnp.int32)
    lane = lax.broadcasted_iota(jnp.int32, shape, 1)
    rel = lane % HEAD
    return lane < HEAD, rel, rel + 1 == doc


def forward_kernel(
    sections,
    chunk,
    starts_ref,
    qkv_b,
    in_b,
    gains,
    biases,
    rows_in,
    qkv_w,
    out_w,
    in_w,
    down_w,
    qkv_out,
    stat_out,
    mixed_out,
    middle_out,
    hidden_out,
    slope_out,
    inputs_out,
    result_out,
    scale_out,
    wq,
    wo,
    wi,
    wd,
    hbuf,
    qkv,
    keys,
    values,
    mixed,
    stat,
    send_a,
    send_b,
    got_a,
    got_b,
    high_mid,
    low_mid,
    hidden,
    slope,
    result,
    scale_a,
    scale_z,
    w_sem,
    load_sem,
    hop_send,
    hop_got,
    pass_send,
    pass_got,
    keep_sem,
    qkv_sem,
    a_send,
    a_got,
    b_send,
    b_got,
    first_sem,
    second_sem,
    third_sem,
):
    section = lax.axis_index("section")
    dp = lax.axis_index("dp")
    core = lax.rem(dp, 2)
    peer = {"dp": dp + 1 - 2 * core}
    length = hbuf.shape[1]
    count = starts_ref.shape[1]
    width = hbuf.shape[2]
    columns = mixed.shape[1]
    pairs = columns // LANES
    chunks = length // chunk
    half = chunk // 2
    micro = hbuf.shape[0]

    weights = [
        pltpu.make_async_copy(source, target, w_sem.at[i])
        for i, (source, target) in enumerate(
            ((qkv_w, wq), (out_w, wo), (in_w, wi), (down_w, wd))
        )
    ]
    for copy in weights:
        copy.start()

    barrier = pltpu.get_barrier_semaphore()
    pl.semaphore_signal(barrier, inc=1, device_id=peer, device_id_type=MESH)

    @pl.when(section > 0)
    def _():
        pl.semaphore_signal(
            barrier, inc=1, device_id={"section": section - 1}, device_id_type=MESH
        )

    @pl.when(section < sections - 1)
    def _():
        pl.semaphore_signal(
            barrier, inc=1, device_id={"section": section + 1}, device_id_type=MESH
        )

    inner = jnp.logical_and(section > 0, section < sections - 1)

    @pl.when(inner)
    def _():
        pl.semaphore_wait(barrier, 3)

    @pl.when(jnp.logical_not(inner))
    def _():
        pl.semaphore_wait(barrier, 2)

    def load(m, j):
        rows = rows_of(j, chunk)
        return pltpu.make_async_copy(
            rows_in.at[m, rows], hbuf.at[m, rows], load_sem.at[m, j]
        )

    def hop(m, j):
        rows = pl.ds(pl.multiple_of(core * half, half), half)
        target = pl.ds(pl.multiple_of(j * chunk + core * half, half), half)
        return pltpu.make_async_remote_copy(
            src_ref=result.at[rows],
            dst_ref=hbuf.at[m, target],
            send_sem=hop_send,
            recv_sem=hop_got.at[m, j],
            device_id={"section": section + 1},
            device_id_type=MESH,
        )

    def hand_over(m, j):
        rows = pl.ds(pl.multiple_of(j * chunk + core * half, half), half)
        return pltpu.make_async_remote_copy(
            src_ref=hbuf.at[m, rows],
            dst_ref=hbuf.at[m, rows],
            send_sem=pass_send.at[m, j],
            recv_sem=pass_got.at[m, j],
            device_id=peer,
            device_id_type=MESH,
        )

    def exchange_a(m, j):
        slot = lax.rem(j, 2)
        return pltpu.make_async_remote_copy(
            src_ref=send_a.at[slot],
            dst_ref=got_a.at[m, j],
            send_sem=a_send.at[slot],
            recv_sem=a_got.at[m, j],
            device_id=peer,
            device_id_type=MESH,
        )

    def exchange_b(m, j):
        slot = lax.rem(j, 2)
        return pltpu.make_async_remote_copy(
            src_ref=send_b.at[slot],
            dst_ref=got_b.at[m, j],
            send_sem=b_send.at[slot],
            recv_sem=b_got.at[m, j],
            device_id=peer,
            device_id_type=MESH,
        )

    def keep(m, j):
        rows = rows_of(j, chunk)
        return pltpu.make_async_copy(
            hbuf.at[m, rows], inputs_out.at[m, rows], keep_sem.at[m, j]
        )

    def keep_qkv(m, j):
        rows = rows_of(j, chunk)
        return pltpu.make_async_copy(qkv.at[rows], qkv_out.at[m, rows], qkv_sem.at[j])

    def keep_first(m, j):
        rows = rows_of(j, chunk)
        return [
            pltpu.make_async_copy(mixed, mixed_out.at[m, rows], first_sem.at[0]),
            pltpu.make_async_copy(stat, stat_out.at[m, rows], first_sem.at[1]),
        ]

    def keep_second(m, j):
        rows = rows_of(j, chunk)
        return [
            pltpu.make_async_copy(low_mid, middle_out.at[m, rows], second_sem.at[0]),
            pltpu.make_async_copy(hidden, hidden_out.at[m, rows], second_sem.at[1]),
            pltpu.make_async_copy(slope, slope_out.at[m, rows], second_sem.at[2]),
            pltpu.make_async_copy(scale_a, scale_out.at[m, 0, rows], second_sem.at[3]),
        ]

    def keep_third(m, j):
        rows = rows_of(j, chunk)
        return [
            pltpu.make_async_copy(result, result_out.at[m, rows], third_sem.at[0]),
            pltpu.make_async_copy(scale_z, scale_out.at[m, 1, rows], third_sem.at[1]),
        ]

    @pl.when(section == 0)
    def _():
        for m in range(micro):
            for j in range(chunks):
                load(m, j).start()

    weights[0].wait()
    shape = (chunk, LANES)

    def project(m, j):
        rows = rows_of(j, chunk)

        @pl.when(section == 0)
        def _():
            load(m, j).wait()

        @pl.when(section > 0)
        def _():
            hop(m, j).wait_recv()
            hand_over(m, j).start()
            hand_over(m, j).wait_recv()

        keep(m, j).start()

        @pl.when(m > 0)
        def _():
            keep_qkv(m - 1, j).wait()

        qkv[rows] = (dot_plain(hbuf[m, rows], wq[...]) + qkv_b[...]).astype(low_type)
        keep_qkv(m, j).start()
        first, rel, own = doc_lanes(starts_ref, m, j * chunk, shape, count)
        extra = jnp.where(own, 1.0, 0.0).astype(low_type)
        ones = jnp.ones(shape, low_type)
        for p in range(pairs):
            k = qkv[rows, columns + p * LANES : columns + (p + 1) * LANES]
            v = qkv[rows, 2 * columns + p * LANES : 2 * columns + (p + 1) * LANES]
            keys[2 * p, rows] = jnp.where(first, k, extra)
            keys[2 * p + 1, rows] = jnp.where(first, extra, k)
            values[2 * p, rows] = jnp.where(first, v, ones)
            values[2 * p + 1, rows] = jnp.where(first, ones, v)

    def mix(m, j):
        rows = rows_of(j, chunk)
        first, rel, own = doc_lanes(starts_ref, m, j * chunk, shape, count)
        extra = jnp.where(
            jnp.logical_and(rel < count, jnp.logical_not(own)), MASKED, 0.0
        ).astype(low_type)

        def scores(index):
            p = index // 2
            q = qkv[rows, p * LANES : (p + 1) * LANES] * low_type(HEAD**-0.5)
            q = jnp.where(first, q, extra) if index % 2 == 0 else jnp.where(first, extra, q)
            return dot_rows(q, keys[index])

        current = scores(0)
        peaks, sums = [], []
        for index in range(2 * pairs):
            later = scores(index + 1) if index + 1 < 2 * pairs else None
            peak = jnp.max(current, axis=-1, keepdims=True)
            powers = jnp.exp(current - peak).astype(low_type)
            peaks.append(peak)
            sums.append(dot_plain(powers, values[index]))
            current = later
            if index % 2 == 1:
                lane = slice((index // 2) * LANES, (index // 2 + 1) * LANES)
                total = jnp.where(first, sums[index], sums[index - 1])
                log_sum = jnp.where(first, peaks[index], peaks[index - 1]) + jnp.log(total)
                stat[:, lane] = lanes(rel, count, -log_sum, extra)
                mixed[:, lane] = (
                    jnp.where(first, sums[index - 1], sums[index]) / pltpu.roll(total, HEAD, 1)
                ).astype(low_type)
        for copy in keep_first(m, j):
            copy.start()
        send_a[lax.rem(j, 2)] = dot_plain(mixed[...], wo[...]).astype(low_type)
        exchange_a(m, j).start()

    def feed(m, j):
        rows = rows_of(j, chunk)
        slot = lax.rem(j, 2)
        exchange_a(m, j).wait()
        total = (
            send_a[slot].astype(jnp.float32)
            + got_a[m, j].astype(jnp.float32)
            + biases[0:1]
            + hbuf[m, rows].astype(jnp.float32)
        )
        unit, inv_scale = norm_rows(total)
        scale_a[...] = jnp.broadcast_to(inv_scale, shape)
        middle = unit * gains[0:1] + biases[1:2]
        high_mid[slot] = middle
        low_mid[...] = middle.astype(low_type)
        hidden_size = wi.shape[1]
        step = min(512, hidden_size)

        def before(start):
            part = slice(start, start + step)
            return dot_plain(low_mid[...], wi[:, part]) + in_b[:, part]

        pre = before(0)
        branch = jnp.zeros((chunk, width), jnp.float32)
        for start in range(0, hidden_size, step):
            part = slice(start, start + step)
            later = before(start + step) if start + step < hidden_size else None
            normal, density = erf_pair(pre)
            hidden[:, part] = (pre * normal).astype(low_type)
            slope[:, part] = (normal + pre * density).astype(low_type)
            branch = branch + dot_plain(hidden[:, part], wd[part])
            pre = later
        send_b[slot] = branch.astype(low_type)
        exchange_b(m, j).start()
        for copy in keep_second(m, j):
            copy.start()

    def finish(m, j):
        slot = lax.rem(j, 2)
        exchange_b(m, j).wait()
        total = (
            send_b[slot].astype(jnp.float32)
            + got_b[m, j].astype(jnp.float32)
            + biases[2:3]
            + high_mid[slot]
        )
        unit, inv_scale = norm_rows(total)
        scale_z[...] = jnp.broadcast_to(inv_scale, shape)
        result[...] = (unit * gains[1:2] + biases[3:4]).astype(low_type)

        @pl.when(section < sections - 1)
        def _():
            hop(m, j).start()

        for copy in keep_third(m, j):
            copy.start()

    def finish_wait(m, j):
        for copy in keep_third(m, j):
            copy.wait()

        @pl.when(section < sections - 1)
        def _():
            hop(m, j).wait_send()

    def one_row(m, carry):
        def first_step(j, carry):
            project(m, j)
            return carry

        lax.fori_loop(0, chunks, first_step, 0)

        @pl.when(m == 0)
        def _():
            for copy in weights[1:]:
                copy.wait()

        def step(i, carry):
            @pl.when(jnp.logical_and(i >= 1, i <= chunks))
            def _():
                for copy in keep_first(m, i - 1):
                    copy.wait()

            @pl.when(i < chunks)
            def _():
                mix(m, i)

            @pl.when(jnp.logical_and(i >= 2, i <= chunks + 1))
            def _():
                for copy in keep_second(m, i - 2):
                    copy.wait()

            @pl.when(jnp.logical_and(i >= 1, i <= chunks))
            def _():
                feed(m, i - 1)

            @pl.when(i >= 3)
            def _():
                finish_wait(m, i - 3)

            @pl.when(i >= 2)
            def _():
                finish(m, i - 2)

            return carry

        lax.fori_loop(0, chunks + 2, step, 0)
        finish_wait(m, chunks - 1)
        return carry

    lax.fori_loop(0, micro, one_row, 0)
    for j in range(chunks):
        keep_qkv(micro - 1, j).wait()
    for m in range(micro):
        for j in range(chunks):
            keep(m, j).wait()

    @pl.when(section > 0)
    def _():
        for m in range(micro):
            for j in range(chunks):
                hand_over(m, j).wait_send()


def forward_pass(sections, starts, qkv_b, in_b, gains, biases, rows_in, qkv_w, out_w, in_w, down_w):
    micro, length, width = rows_in.shape
    columns, hidden = out_w.shape[0], in_w.shape[1]
    chunk = min(256, length)
    chunks = length // chunk
    low, high = low_type, jnp.float32

    def out(*shape, dtype=low):
        return jax.ShapeDtypeStruct(shape, dtype)

    outs = dict(
        qkv=out(micro, length, 3 * columns),
        log_sums=out(micro, length, columns),
        mixed=out(micro, length, columns),
        middle=out(micro, length, width),
        hidden=out(micro, length, hidden),
        slope=out(micro, length, hidden),
        inputs=out(micro, length, width),
        result=out(micro, length, width),
        scales=out(micro, 2, length, LANES, dtype=high),
    )
    vmem = pl.BlockSpec(memory_space=pltpu.VMEM)
    anywhere = pl.BlockSpec(memory_space=pl.ANY)
    dma = pltpu.SemaphoreType.DMA
    results = pl.pallas_call(
        functools.partial(forward_kernel, sections, chunk),
        in_specs=[pl.BlockSpec(memory_space=pltpu.SMEM)] + [vmem] * 4 + [anywhere] * 5,
        out_specs=[anywhere] * len(outs),
        out_shape=list(outs.values()),
        scratch_shapes=[
            pltpu.VMEM(qkv_w.shape, low),
            pltpu.VMEM(out_w.shape, low),
            pltpu.VMEM(in_w.shape, low),
            pltpu.VMEM(down_w.shape, low),
            pltpu.VMEM((micro, length, width), low),
            pltpu.VMEM((length, 3 * columns), low),
            pltpu.VMEM((columns // HEAD, length, LANES), low),
            pltpu.VMEM((columns // HEAD, length, LANES), low),
            pltpu.VMEM((chunk, columns), low),
            pltpu.VMEM((chunk, columns), low),
            pltpu.VMEM((2, chunk, width), low),
            pltpu.VMEM((2, chunk, width), low),
            pltpu.VMEM((micro, chunks, chunk, width), low),
            pltpu.VMEM((micro, chunks, chunk, width), low),
            pltpu.VMEM((2, chunk, width), high),
            pltpu.VMEM((chunk, width), low),
            pltpu.VMEM((chunk, hidden), low),
            pltpu.VMEM((chunk, hidden), low),
            pltpu.VMEM((chunk, width), low),
            pltpu.VMEM((chunk, LANES), high),
            pltpu.VMEM((chunk, LANES), high),
            dma((4,)),
            dma((micro, chunks)),
            dma,
            dma((micro, chunks)),
            dma((micro, chunks)),
            dma((micro, chunks)),
            dma((micro, chunks)),
            dma((chunks,)),
            dma((2,)),
            dma((micro, chunks)),
            dma((2,)),
            dma((micro, chunks)),
            dma((2,)),
            dma((4,)),
            dma((2,)),
        ],
        compiler_params=pltpu.CompilerParams(
            collective_id=0, has_side_effects=True, vmem_limit_bytes=62 * 1024 * 1024
        ),
        name="forward_pass",
    )(starts, qkv_b, in_b, gains, biases, rows_in, qkv_w, out_w, in_w, down_w)
    return dict(zip(outs, results))


def unit_norm(value):
    average = jnp.mean(value, axis=-1, keepdims=True)
    centered = value - average
    inv_scale = lax.rsqrt(jnp.mean(centered * centered, axis=-1, keepdims=True) + eps_norm)
    return centered * inv_scale, inv_scale


def norm_back(gradient, normed, inv_scale, gain_row):
    weighted = gradient * gain_row
    adjusted = (
        weighted
        - jnp.mean(weighted, axis=-1, keepdims=True)
        - normed * jnp.mean(weighted * normed, axis=-1, keepdims=True)
    )
    return inv_scale * adjusted


def gelu_pair(pre):
    normal = 0.5 * (1.0 + lax.erf(pre * 0.7071067811865476))
    density = jnp.exp(-0.5 * pre * pre) * 0.3989422804014327
    return pre * normal, normal + pre * density


def forward_layer(at, inputs, starts, params):
    qkv_w, qkv_b, out_w, in_w, in_b, down_w, gains, biases = params
    qkv = (dot_plain(inputs, qkv_w) + qkv_b).astype(low_type)
    mixed, log_sums = attend(qkv, starts)
    branch = at.group_sum(dot_plain(mixed, out_w).astype(low_type))
    unit_a, scale_a = unit_norm(branch + biases[0] + inputs.astype(jnp.float32))
    middle = unit_a * gains[0] + biases[1]
    low_middle = middle.astype(low_type)
    hidden, slope = gelu_pair(dot_plain(low_middle, in_w) + in_b)
    hidden = hidden.astype(low_type)
    branch_two = at.group_sum(dot_plain(hidden, down_w).astype(low_type))
    unit_z, scale_z = unit_norm(branch_two + biases[2] + middle)
    result = (unit_z * gains[1] + biases[3]).astype(low_type)
    saved = dict(
        inputs=inputs,
        qkv=qkv,
        mixed=mixed,
        log_sums=log_sums,
        scale_a=scale_a[:, 0],
        middle=low_middle,
        hidden=hidden,
        slope=slope.astype(low_type),
        scale_z=scale_z[:, 0],
    )
    return result, saved


def backward_layer(at, saved, incoming, starts, params):
    qkv_w, qkv_b, out_w, in_w, in_b, down_w, gains, biases = params
    gradient = incoming.astype(jnp.float32)
    unit_z = (saved["result"].astype(jnp.float32) - biases[3]) / gains[1]
    grad_z = norm_back(gradient, unit_z, saved["scale_z"][:, None], gains[1])
    low_gz = grad_z.astype(low_type)
    grad_pre = (dot_rows(low_gz, down_w) * saved["slope"].astype(jnp.float32)).astype(low_type)
    grad_mid = at.group_sum(dot_rows(grad_pre, in_w).astype(low_type)) + grad_z
    unit_a = (saved["middle"].astype(jnp.float32) - biases[1]) / gains[0]
    grad_a = norm_back(grad_mid, unit_a, saved["scale_a"][:, None], gains[0])
    low_ga = grad_a.astype(low_type)
    grad_mixed = dot_rows(low_ga, out_w).astype(low_type)
    grad_qkv = jnp.concatenate(
        attend_back(saved["qkv"], starts, saved["mixed"], saved["log_sums"], grad_mixed), 1
    )
    grad_x = at.group_sum(dot_rows(grad_qkv, qkv_w).astype(low_type)) + grad_a
    sums = jnp.stack(
        [
            jnp.sum(grad_mid * unit_a, axis=0),
            jnp.sum(gradient * unit_z, axis=0),
            jnp.sum(grad_a, axis=0),
            jnp.sum(grad_mid, axis=0),
            jnp.sum(grad_z, axis=0),
            jnp.sum(gradient, axis=0),
        ]
    )
    kept = dict(grad_z=low_gz, slope=grad_pre, grad_a=low_ga, qkv=grad_qkv)
    return grad_x.astype(low_type), kept, sums


def store(buffers, values, slot):
    return jax.tree.map(
        lambda buffer, value: lax.dynamic_update_index_in_dim(buffer, value, slot, 0),
        buffers,
        values,
    )


def pick(buffers, slot):
    return jax.tree.map(
        lambda buffer: lax.dynamic_index_in_dim(buffer, slot, 0, keepdims=False), buffers
    )


def group_weight(at, weight):
    parts = weight.reshape((at.chips, -1) + weight.shape[1:])

    def across(s, g, u, x, c):
        return (s, c, u, x, g) if g != c else None

    def along(step):
        return lambda s, g, u, x, c: (s, g, u, (x + step) % at.chips, c) if g != c else None

    piece = at.move(lax.dynamic_index_in_dim(parts, at.chip, 0, keepdims=False), across)
    pieces = [piece]
    for step in range(1, at.chips):
        pieces.append(at.move(piece, along(step)))
    whole = parts
    for step, piece in enumerate(pieces):
        spot = (at.chip - step) % at.chips
        own = lax.dynamic_index_in_dim(parts, spot, 0, keepdims=False)
        whole = lax.dynamic_update_index_in_dim(whole, jnp.where(at.home, own, piece), spot, 0)
    return whole.reshape(weight.shape)


def group_rows(at, tokens, section):
    def across(s, g, u, x, c):
        return (s, 1 - g, u, x, c) if s == section else None

    own = lax.dynamic_index_in_dim(tokens, at.group, 0, keepdims=False)
    other = at.move(lax.dynamic_index_in_dim(tokens, 1 - at.group, 0, keepdims=False), across)
    lower = at.group == 0
    pair = jnp.stack([jnp.where(lower, own, other), jnp.where(lower, other, own)])
    whole = at.group_gather(pair)
    whole = whole.reshape((2, at.halves) + pair.shape)
    whole = jnp.swapaxes(whole, 1, 2)
    return whole.reshape(2, -1, tokens.shape[-1])


def spread_rows(at, rows, length):
    def across(s, g, u, x, c):
        return (s, 1 - g, u, x, c)

    row = lax.dynamic_index_in_dim(rows, at.core, 0, keepdims=False)
    tile = length // at.tensor

    def piece(group):
        return lax.dynamic_slice_in_dim(row, (group * at.halves + at.part) * tile, tile, 0)

    own = piece(at.group)
    other = at.move(piece(1 - at.group), across)
    lower = at.group == 0
    return jnp.stack([jnp.where(lower, own, other), jnp.where(lower, other, own)])


def sum_weight(at, gradient, across_first):
    parts = gradient.reshape((at.chips, -1) + gradient.shape[1:])

    def across(s, g, u, x, c):
        return (s, c, u, x, c) if g != c else None

    def along(step):
        def target(s, g, u, x, c):
            if across_first and g != c:
                return None
            return (s, g, u, (x + step) % at.chips, c)

        return target

    def fold_chips(parts):
        total = lax.dynamic_index_in_dim(parts, at.chip, 0, keepdims=False).astype(jnp.float32)
        for step in range(1, at.chips):
            piece = lax.dynamic_index_in_dim(
                parts, (at.chip + step) % at.chips, 0, keepdims=False
            )
            total = total + at.move(piece, along(step)).astype(jnp.float32)
        return total.astype(low_type)

    if across_first:
        total = fold_chips(
            (parts.astype(jnp.float32) + at.move(parts, across).astype(jnp.float32)).astype(
                low_type
            )
        )
    else:
        part = fold_chips(parts)
        total = (part.astype(jnp.float32) + at.move(part, across).astype(jnp.float32)).astype(
            low_type
        )
    halves = total.reshape((2, -1) + total.shape[1:])

    def over(s, g, u, x, c):
        return (s, g, u, x, 1 - c) if g == c else None

    own = lax.dynamic_index_in_dim(halves, at.core, 0, keepdims=False)
    other = at.move(lax.dynamic_index_in_dim(halves, 1 - at.core, 0, keepdims=False), over)
    return jnp.where(at.home, own, other).astype(jnp.float32)


def shards(
    tokens,
    timesteps,
    seg_starts,
    time_params,
    qkv_weight,
    qv_bias,
    out_weight,
    ffn_in,
    ffn_bias,
    ffn_out,
    ln_gains,
    row_biases,
    cotangent,
):
    at = Layout()
    width = tokens.shape[-1]
    length = tokens.shape[1] * at.tensor
    micro_count = 2
    tick_count = micro_count + at.sections - 1
    slots = micro_count + 1
    columns = qkv_weight.shape[3]

    def both_cores(value):
        def over(s, g, u, x, c):
            return (s, g, u, x, 1 - c)

        other = at.move(value, over)
        first = at.core == 0
        mine = jnp.stack([jnp.where(first, value, other), jnp.where(first, other, value)])
        return lax.dynamic_index_in_dim(mine, at.group, 1, keepdims=False)

    starts = both_cores(seg_starts)
    fractions_own = timesteps.astype(jnp.float32) / 5000.0
    fractions = both_cores(fractions_own)
    time_values = time_params.astype(jnp.float32)
    embedded = (
        tokens.astype(jnp.float32) + fractions_own[:, None, None] * time_values[0] + time_values[1]
    ).astype(low_type)
    rows_in = group_rows(at, embedded, 0)
    qv_low = group_weight(at, qv_bias[0].T).T.astype(jnp.float32)
    qkv_w = group_weight(at, qkv_weight[0].reshape(width, 3 * columns))
    out_w = group_weight(at, out_weight[0])
    in_w = group_weight(at, ffn_in[0])
    in_b = group_weight(at, ffn_bias[0])
    down_w = group_weight(at, ffn_out[0])
    rows_back = group_rows(at, cotangent, at.sections - 1)
    qkv_b = jnp.concatenate([qv_low[0], jnp.zeros((columns,), jnp.float32), qv_low[1]])
    params = (
        qkv_w,
        qkv_b,
        out_w,
        in_w,
        in_b.astype(jnp.float32),
        down_w,
        ln_gains[0].astype(jnp.float32),
        row_biases[0].astype(jnp.float32),
    )

    def hop(result, distance):
        def target(s, g, u, x, c):
            return (s + distance, g, u, x, c) if 0 <= s + distance < at.sections else None

        tile = length // at.size
        piece = at.move(lax.dynamic_slice_in_dim(result, at.rank * tile, tile, 0), target)
        return at.group_gather(piece).reshape(length, width)

    def place_of(tick_value, stage):
        place = tick_value - stage
        usable = jnp.logical_and(place >= 0, place < micro_count)
        return usable, jnp.clip(place, 0, micro_count - 1), jnp.where(usable, place, micro_count)

    def empty(values):
        return jax.tree.map(
            lambda value: jnp.zeros((slots,) + value.shape, value.dtype), values
        )

    blank = jnp.zeros((length, width), low_type)
    stash = forward_pass(
        at.sections,
        starts,
        qkv_b[None],
        in_b.astype(jnp.float32)[None],
        params[6],
        params[7],
        rows_in,
        qkv_w,
        out_w,
        in_w,
        down_w,
    )
    outputs = stash.pop("result")
    scales = stash.pop("scales")[..., 0]
    stash["scale_a"], stash["scale_z"] = scales[:, 0], scales[:, 1]
    stash = jax.tree.map(lambda v: jnp.concatenate([v, jnp.zeros_like(v[:1])]), stash)
    outputs = jnp.concatenate([outputs, outputs[:1]])
    layer_outs = spread_rows(at, outputs, length)

    def backward_tick(tick_value, arrived, stash, grads, totals):
        usable, position, slot = place_of(tick_value, at.sections - 1 - at.section)
        incoming = jnp.where(at.section == at.sections - 1, rows_back[position], arrived)
        grad_x, kept_now, sums = backward_layer(
            at, pick(dict(stash, result=outputs), slot), incoming, starts[position], params
        )
        totals = totals + jnp.where(usable, sums, 0.0)
        kept = store({name: stash[name] for name in kept_now}, kept_now, slot)
        return grad_x, dict(stash, **kept), store(grads, grad_x, slot), totals

    for name in ("grad_z", "grad_a"):
        stash[name] = empty(blank)
    totals = jnp.zeros((6, width), jnp.float32)

    def backward_loop(tick_value, carry):
        grad_x, stash, grads, totals = backward_tick(tick_value, *carry)
        return hop(grad_x, -1), stash, grads, totals

    carry = lax.fori_loop(
        0, tick_count - 1, backward_loop, (blank, stash, empty(blank), totals)
    )
    _, stash, grads, totals = backward_tick(tick_count - 1, *carry)
    input_grads = spread_rows(at, grads, length)

    def both(buffer):
        return buffer[:micro_count].reshape((micro_count * length,) + buffer.shape[2:])

    low_gz, grad_pre, low_ga, grad_qkv = (
        both(stash[name]) for name in ("grad_z", "slope", "grad_a", "qkv")
    )
    down_g = sum_weight(at, dot_first(both(stash["hidden"]), low_gz).astype(low_type), True)
    in_g = sum_weight(at, dot_first(both(stash["middle"]), grad_pre).astype(low_type), False)
    out_g = sum_weight(at, dot_first(both(stash["mixed"]), low_ga).astype(low_type), True)
    qkv_g = sum_weight(at, dot_first(both(stash["inputs"]), grad_qkv).astype(low_type), False)

    in_bias_g = jnp.sum(grad_pre, axis=0, dtype=jnp.float32)
    qkv_bias_g = jnp.sum(grad_qkv, axis=0, dtype=jnp.float32).reshape(3, columns)
    sliced = jnp.concatenate([qkv_bias_g[0], qkv_bias_g[2], in_bias_g])
    every = jnp.zeros((at.size,) + sliced.shape, jnp.float32)
    every = lax.dynamic_update_index_in_dim(every, sliced, at.rank, 0)
    row_terms = jnp.where(at.rank == 0, totals, 0.0)
    small = lax.psum(
        jnp.concatenate([row_terms.reshape(-1), every.reshape(-1)]), ("tensor", "dp")
    )
    row_sums = small[: row_terms.size].reshape(row_terms.shape)
    tensor = lax.axis_index("tensor")
    dp = lax.axis_index("dp")
    mine = lax.dynamic_index_in_dim(
        small[row_terms.size :].reshape(every.shape), tensor, 0, keepdims=False
    )

    def share(value, count, index):
        size = value.shape[-1] // count
        return lax.dynamic_slice_in_dim(value, index * size, size, value.ndim - 1)

    qv_g = share(mine[: 2 * columns].reshape(2, columns), at.dp, dp)
    in_bias_g = share(mine[2 * columns :], at.dp, dp)
    row_share = share(row_sums, at.tensor * at.dp, tensor * at.dp + dp)

    grad_rows = grads[:micro_count].astype(jnp.float32)
    row_grads = jnp.sum(grad_rows, axis=1)
    time_terms = jnp.stack([jnp.sum(fractions[:, None] * row_grads, 0), jnp.sum(row_grads, 0)])
    time_terms = jnp.where(jnp.logical_and(at.section == 0, at.rank == 0), time_terms, 0.0)
    grad_time = lax.psum(time_terms, AXES)
    return (
        layer_outs[None],
        input_grads[None],
        qkv_g.reshape(-1, 3, columns)[None],
        qv_g[None],
        out_g[None],
        in_g[None],
        in_bias_g[None],
        down_g[None],
        row_share[None, :2],
        row_share[None, 2:],
        grad_time,
    )


def solution(mesh):
    return jax.shard_map(
        shards,
        mesh=mesh,
        in_specs=(
            P("dp", "tensor", None),
            P("dp"),
            P("dp", None),
            P(),
            P("section", None, None, "tensor"),
            P("section", None, "tensor"),
            P("section", "tensor", None),
            P("section", None, "tensor"),
            P("section", "tensor"),
            P("section", "tensor", None),
            P("section", None, None),
            P("section", None, None),
            P("dp", "tensor", None),
        ),
        out_specs=(
            P("section", "dp", "tensor", None),
            P("section", "dp", "tensor", None),
            P("section", "dp", None, "tensor"),
            P("section", None, ("tensor", "dp")),
            P("section", ("tensor", "dp"), None),
            P("section", "dp", "tensor"),
            P("section", ("tensor", "dp")),
            P("section", ("tensor", "dp"), None),
            P("section", None, ("tensor", "dp")),
            P("section", None, ("tensor", "dp")),
            P(),
        ),
        check_vma=False,
    )
```

```python
import functools

import jax
import jax.numpy as jnp
from jax import lax
from jax.experimental import pallas as pl
from jax.experimental.pallas import tpu as pltpu
from jax.sharding import PartitionSpec as P

HEAD = 64
LANES = 128
MASKED = -1e30
eps_norm = 1e-05
AXES = ("section", "tensor", "dp")
low_type = jnp.bfloat16


class Layout:
    def __init__(self):
        self.sections = lax.axis_size("section")
        self.tensor = lax.axis_size("tensor")
        self.dp = lax.axis_size("dp")
        self.halves = self.tensor // 2
        self.chips = self.dp // 2
        self.size = self.tensor
        self.section = lax.axis_index("section")
        tensor, dp = lax.axis_index("tensor"), lax.axis_index("dp")
        self.group, self.part = tensor // self.halves, tensor % self.halves
        self.chip, self.core = dp // 2, dp % 2
        self.rank = self.core * self.halves + self.part
        self.home = self.group == self.core

    def move(self, value, target):
        pairs = []
        for s in range(self.sections):
            for t in range(self.tensor):
                for d in range(self.dp):
                    goal = target(s, t // self.halves, t % self.halves, d // 2, d % 2)
                    if goal is None:
                        continue
                    s2, g2, u2, x2, c2 = goal
                    here = (s * self.tensor + t) * self.dp + d
                    there = (s2 * self.tensor + g2 * self.halves + u2) * self.dp + x2 * 2 + c2
                    if here != there:
                        pairs.append((here, there))
        return lax.ppermute(value, AXES, pairs)

    def turn(self, value, step):
        def target(s, g, u, x, c):
            rank = (c * self.halves + u + step) % self.size
            return (s, g, rank % self.halves, x, rank // self.halves)

        return self.move(value, target)

    def group_sum(self, value):
        total = value.astype(jnp.float32)
        for step in range(1, self.size):
            total = total + self.turn(value, step).astype(jnp.float32)
        return total

    def group_gather(self, value):
        if self.size == 2:
            other = self.turn(value, 1)
            first = self.rank == 0
            return jnp.stack([jnp.where(first, value, other), jnp.where(first, other, value)])
        whole = jnp.zeros((self.size,) + value.shape, value.dtype)
        for step in range(self.size):
            piece = value if step == 0 else self.turn(value, step)
            whole = lax.dynamic_update_index_in_dim(
                whole, piece, (self.rank - step) % self.size, 0
            )
        return whole


def dot_rows(a, b):
    return lax.dot_general(a, b, (((1,), (1,)), ((), ())), preferred_element_type=jnp.float32)


def dot_plain(a, b):
    return lax.dot_general(a, b, (((1,), (0,)), ((), ())), preferred_element_type=jnp.float32)


def dot_first(a, b):
    return lax.dot_general(a, b, (((0,), (0,)), ((), ())), preferred_element_type=jnp.float32)


def tile_docs(starts_ref, length, count):
    place = lax.broadcasted_iota(jnp.int32, (length, LANES), 0)
    doc = jnp.zeros((length, LANES), jnp.int32)
    for j in range(count):
        doc = doc + (starts_ref[j] <= place).astype(jnp.int32)
    lane = lax.broadcasted_iota(jnp.int32, (length, LANES), 1)
    rel = lane % HEAD
    return lane < HEAD, rel, rel + 1 == doc


def three_parts(value):
    high = value.astype(low_type)
    rest = value - high.astype(jnp.float32)
    middle = rest.astype(low_type)
    return high, middle, (rest - middle.astype(jnp.float32)).astype(low_type)


def lanes(rel, count, value, base):
    high, middle, small = three_parts(value)
    return jnp.where(
        rel == count,
        high,
        jnp.where(rel == count + 1, middle, jnp.where(rel == count + 2, small, base)),
    )


def attend_kernel(starts_ref, q_ref, k_ref, v_ref, o_ref, l_ref, *, count, rows):
    length = q_ref.shape[0]
    first, rel, own = tile_docs(starts_ref, length, count)
    extra_k = jnp.where(own, 1.0, 0.0).astype(low_type)
    extra_q = jnp.where(
        jnp.logical_and(rel < count, jnp.logical_not(own)), MASKED, 0.0
    ).astype(low_type)
    q = q_ref[...] * low_type(HEAD**-0.5)
    k = k_ref[...]
    v = v_ref[...]
    ones = jnp.ones_like(v)
    heads = (
        (jnp.where(first, q, extra_q), jnp.where(first, k, extra_k), jnp.where(first, v, ones)),
        (jnp.where(first, extra_q, q), jnp.where(first, extra_k, k), jnp.where(first, ones, v)),
    )
    side = first[:rows]
    for start in range(0, length, rows):
        peaks, sums = [], []
        for q_head, k_head, v_head in heads:
            scores = dot_rows(q_head[start : start + rows], k_head)
            peak = jnp.max(scores, axis=-1, keepdims=True)
            powers = jnp.exp(scores - peak).astype(low_type)
            peaks.append(peak)
            sums.append(dot_plain(powers, v_head))
        mixed = jnp.where(side, sums[0], sums[1])
        totals = jnp.where(side, sums[1], sums[0])
        log_sums = jnp.where(side, peaks[1], peaks[0]) + jnp.log(totals)
        l_ref[start : start + rows] = lanes(
            rel[:rows], count, -log_sums, extra_q[start : start + rows]
        )
        o_ref[start : start + rows] = (mixed / pltpu.roll(totals, HEAD, 1)).astype(low_type)


def attend(qkv, starts):
    length, columns = qkv.shape[0], qkv.shape[1] // 3
    pairs = columns // LANES
    rows = min(512, length)

    def block(offset):
        return pl.BlockSpec((length, LANES), lambda j: (0, offset + j))

    return pl.pallas_call(
        functools.partial(attend_kernel, count=starts.shape[0], rows=rows),
        grid=(pairs,),
        in_specs=[
            pl.BlockSpec(memory_space=pltpu.SMEM),
            block(0),
            block(pairs),
            block(2 * pairs),
        ],
        out_specs=[block(0), block(0)],
        out_shape=[
            jax.ShapeDtypeStruct((length, columns), low_type),
            jax.ShapeDtypeStruct((length, columns), low_type),
        ],
        compiler_params=pltpu.CompilerParams(vmem_limit_bytes=48 * 1024 * 1024),
        cost_estimate=pl.CostEstimate(
            flops=16 * length * length * columns // 4,
            bytes_accessed=12 * length * columns,
            transcendentals=length * length * columns // HEAD,
        ),
        name="attend",
    )(starts, qkv, qkv, qkv)


def attend_back_kernel(
    starts_ref, q_ref, k_ref, v_ref, o_ref, l_ref, g_ref, dq_ref, dk_ref, dv_ref, *, count, rows
):
    length = q_ref.shape[0]
    first, rel, own = tile_docs(starts_ref, length, count)
    stat = jnp.logical_and(rel >= count, rel < count + 3)
    extra_k = jnp.where(jnp.logical_or(own, stat), 1.0, 0.0).astype(low_type)
    extra_v = jnp.where(stat, 1.0, 0.0).astype(low_type)
    extra_q = l_ref[...]
    g = g_ref[...]
    product = g.astype(jnp.float32) * o_ref[...].astype(jnp.float32)
    dots = [
        jnp.sum(jnp.where(first, product, 0.0), axis=-1, keepdims=True),
        jnp.sum(jnp.where(first, 0.0, product), axis=-1, keepdims=True),
    ]
    extra_g = lanes(rel, count, -jnp.where(first, dots[1], dots[0]), jnp.zeros_like(extra_q))
    q = q_ref[...] * low_type(HEAD**-0.5)
    k = k_ref[...]
    v = v_ref[...]
    heads = (
        tuple(
            jnp.where(first, a, b)
            for a, b in ((q, extra_q), (k, extra_k), (v, extra_v), (g, extra_g))
        ),
        tuple(
            jnp.where(first, b, a)
            for a, b in ((q, extra_q), (k, extra_k), (v, extra_v), (g, extra_g))
        ),
    )
    grad_k = [jnp.zeros((length, LANES), jnp.float32)] * 2
    grad_v = [jnp.zeros((length, LANES), jnp.float32)] * 2
    for start in range(0, length, rows):
        part = slice(start, start + rows)
        grad_q = []
        for i, (q_head, k_head, v_head, g_head) in enumerate(heads):
            probs = jnp.exp(dot_rows(k_head, q_head[part]))
            slopes = (probs * dot_rows(v_head, g_head[part])).astype(low_type)
            grad_v[i] = grad_v[i] + dot_plain(probs.astype(low_type), g[part])
            grad_k[i] = grad_k[i] + dot_plain(slopes, q[part])
            grad_q.append(dot_first(slopes, k))
        dq_ref[part] = (
            jnp.where(first[:rows], grad_q[0], grad_q[1]) * (HEAD**-0.5)
        ).astype(low_type)
    dk_ref[...] = jnp.where(first, grad_k[0], grad_k[1]).astype(low_type)
    dv_ref[...] = jnp.where(first, grad_v[0], grad_v[1]).astype(low_type)


def attend_back(qkv, starts, mixed, log_sums, grad_mixed):
    length, columns = mixed.shape
    pairs = columns // LANES
    rows = min(256, length)

    def block(offset):
        return pl.BlockSpec((length, LANES), lambda j: (0, offset + j))

    return pl.pallas_call(
        functools.partial(attend_back_kernel, count=starts.shape[0], rows=rows),
        grid=(pairs,),
        in_specs=[
            pl.BlockSpec(memory_space=pltpu.SMEM),
            block(0),
            block(pairs),
            block(2 * pairs),
            block(0),
            block(0),
            block(0),
        ],
        out_specs=[block(0)] * 3,
        out_shape=[jax.ShapeDtypeStruct((length, columns), low_type)] * 3,
        compiler_params=pltpu.CompilerParams(vmem_limit_bytes=48 * 1024 * 1024),
        cost_estimate=pl.CostEstimate(
            flops=40 * length * length * columns // 4,
            bytes_accessed=20 * length * columns,
            transcendentals=length * length * columns // HEAD,
        ),
        name="attend_back",
    )(starts, qkv, qkv, qkv, mixed, log_sums, grad_mixed)


MESH = pl.DeviceIdType.MESH


def rows_of(index, size):
    return pl.ds(pl.multiple_of(index * size, size), size)


def erf_pair(pre):
    bell = jnp.exp(-0.5 * pre * pre)
    size = jnp.abs(pre)
    t = 1.0 / (1.0 + 0.2316418882663604 * size)
    tail = bell * t * (
        0.127414796
        + t * (-0.142248368 + t * (0.7107068705 + t * (-0.7265760135 + t * 0.5307027145)))
    )
    return jnp.where(pre < 0.0, tail, 1.0 - tail), bell * 0.3989422804014327


def norm_rows(value):
    average = jnp.mean(value, axis=-1, keepdims=True)
    centered = value - average
    inv_scale = lax.rsqrt(jnp.mean(centered * centered, axis=-1, keepdims=True) + eps_norm)
    return centered * inv_scale, inv_scale


def doc_lanes(starts_ref, row, first_row, shape, count):
    place = lax.broadcasted_iota(jnp.int32, shape, 0) + first_row
    doc = jnp.zeros(shape, jnp.int32)
    for j in range(count):
        doc = doc + (starts_ref[row, j] <= place).astype(jnp.int32)
    lane = lax.broadcasted_iota(jnp.int32, shape, 1)
    rel = lane % HEAD
    return lane < HEAD, rel, rel + 1 == doc


def forward_kernel(
    sections,
    chunk,
    starts_ref,
    qkv_b,
    in_b,
    gains,
    biases,
    rows_in,
    qkv_w,
    out_w,
    in_w,
    down_w,
    qkv_out,
    stat_out,
    mixed_out,
    middle_out,
    hidden_out,
    slope_out,
    inputs_out,
    result_out,
    scale_out,
    wq,
    wo,
    wi,
    wd,
    hbuf,
    qkv,
    keys,
    values,
    mixed,
    stat,
    send_a,
    send_b,
    got_a,
    got_b,
    high_mid,
    low_mid,
    hidden,
    slope,
    result,
    scale_a,
    scale_z,
    w_sem,
    load_sem,
    hop_send,
    hop_got,
    pass_send,
    pass_got,
    keep_sem,
    qkv_sem,
    a_send,
    a_got,
    b_send,
    b_got,
    first_sem,
    second_sem,
    third_sem,
):
    section = lax.axis_index("section")
    dp = lax.axis_index("dp")
    core = lax.rem(dp, 2)
    peer = {"dp": dp + 1 - 2 * core}
    length = hbuf.shape[1]
    count = starts_ref.shape[1]
    width = hbuf.shape[2]
    columns = mixed.shape[1]
    pairs = columns // LANES
    chunks = length // chunk
    half = chunk // 2
    micro = hbuf.shape[0]

    weights = [
        pltpu.make_async_copy(source, target, w_sem.at[i])
        for i, (source, target) in enumerate(
            ((qkv_w, wq), (out_w, wo), (in_w, wi), (down_w, wd))
        )
    ]
    for copy in weights:
        copy.start()

    greet(section, sections, peer)

    def load(m, j):
        rows = rows_of(j, chunk)
        return pltpu.make_async_copy(
            rows_in.at[m, rows], hbuf.at[m, rows], load_sem.at[m, j]
        )

    def hop(m, j):
        rows = pl.ds(pl.multiple_of(core * half, half), half)
        target = pl.ds(pl.multiple_of(j * chunk + core * half, half), half)
        return pltpu.make_async_remote_copy(
            src_ref=result.at[rows],
            dst_ref=hbuf.at[m, target],
            send_sem=hop_send,
            recv_sem=hop_got.at[m, j],
            device_id={"section": section + 1},
            device_id_type=MESH,
        )

    def hand_over(m, j):
        rows = pl.ds(pl.multiple_of(j * chunk + core * half, half), half)
        return pltpu.make_async_remote_copy(
            src_ref=hbuf.at[m, rows],
            dst_ref=hbuf.at[m, rows],
            send_sem=pass_send.at[m, j],
            recv_sem=pass_got.at[m, j],
            device_id=peer,
            device_id_type=MESH,
        )

    def exchange_a(m, j):
        slot = lax.rem(j, 2)
        return pltpu.make_async_remote_copy(
            src_ref=send_a.at[slot],
            dst_ref=got_a.at[m, j],
            send_sem=a_send.at[slot],
            recv_sem=a_got.at[m, j],
            device_id=peer,
            device_id_type=MESH,
        )

    def exchange_b(m, j):
        slot = lax.rem(j, 2)
        return pltpu.make_async_remote_copy(
            src_ref=send_b.at[slot],
            dst_ref=got_b.at[m, j],
            send_sem=b_send.at[slot],
            recv_sem=b_got.at[m, j],
            device_id=peer,
            device_id_type=MESH,
        )

    def keep(m, j):
        rows = rows_of(j, chunk)
        return pltpu.make_async_copy(
            hbuf.at[m, rows], inputs_out.at[m, rows], keep_sem.at[m, j]
        )

    def keep_qkv(m, j):
        rows = rows_of(j, chunk)
        return pltpu.make_async_copy(qkv.at[rows], qkv_out.at[m, rows], qkv_sem.at[j])

    def keep_first(m, j):
        rows = rows_of(j, chunk)
        return [
            pltpu.make_async_copy(mixed, mixed_out.at[m, rows], first_sem.at[0]),
            pltpu.make_async_copy(stat, stat_out.at[m, rows], first_sem.at[1]),
        ]

    def keep_second(m, j):
        rows = rows_of(j, chunk)
        return [
            pltpu.make_async_copy(low_mid, middle_out.at[m, rows], second_sem.at[0]),
            pltpu.make_async_copy(hidden, hidden_out.at[m, rows], second_sem.at[1]),
            pltpu.make_async_copy(slope, slope_out.at[m, rows], second_sem.at[2]),
            pltpu.make_async_copy(scale_a, scale_out.at[m, 0, rows], second_sem.at[3]),
        ]

    def keep_third(m, j):
        rows = rows_of(j, chunk)
        return [
            pltpu.make_async_copy(result, result_out.at[m, rows], third_sem.at[0]),
            pltpu.make_async_copy(scale_z, scale_out.at[m, 1, rows], third_sem.at[1]),
        ]

    @pl.when(section == 0)
    def _():
        for m in range(micro):
            for j in range(chunks):
                load(m, j).start()

    weights[0].wait()
    shape = (chunk, LANES)

    def project(m, j):
        rows = rows_of(j, chunk)

        @pl.when(section == 0)
        def _():
            load(m, j).wait()

        @pl.when(section > 0)
        def _():
            hop(m, j).wait_recv()
            hand_over(m, j).start()
            hand_over(m, j).wait_recv()

        keep(m, j).start()

        @pl.when(m > 0)
        def _():
            keep_qkv(m - 1, j).wait()

        qkv[rows] = (dot_plain(hbuf[m, rows], wq[...]) + qkv_b[...]).astype(low_type)
        keep_qkv(m, j).start()
        first, rel, own = doc_lanes(starts_ref, m, j * chunk, shape, count)
        extra = jnp.where(own, 1.0, 0.0).astype(low_type)
        ones = jnp.ones(shape, low_type)
        for p in range(pairs):
            k = qkv[rows, columns + p * LANES : columns + (p + 1) * LANES]
            v = qkv[rows, 2 * columns + p * LANES : 2 * columns + (p + 1) * LANES]
            keys[2 * p, rows] = jnp.where(first, k, extra)
            keys[2 * p + 1, rows] = jnp.where(first, extra, k)
            values[2 * p, rows] = jnp.where(first, v, ones)
            values[2 * p + 1, rows] = jnp.where(first, ones, v)

    def mix(m, j):
        rows = rows_of(j, chunk)
        first, rel, own = doc_lanes(starts_ref, m, j * chunk, shape, count)
        extra = jnp.where(
            jnp.logical_and(rel < count, jnp.logical_not(own)), MASKED, 0.0
        ).astype(low_type)

        def scores(index):
            p = index // 2
            q = qkv[rows, p * LANES : (p + 1) * LANES] * low_type(HEAD**-0.5)
            q = jnp.where(first, q, extra) if index % 2 == 0 else jnp.where(first, extra, q)
            return dot_rows(q, keys[index])

        current = scores(0)
        peaks, sums = [], []
        for index in range(2 * pairs):
            later = scores(index + 1) if index + 1 < 2 * pairs else None
            peak = jnp.max(current, axis=-1, keepdims=True)
            powers = jnp.exp(current - peak).astype(low_type)
            peaks.append(peak)
            sums.append(dot_plain(powers, values[index]))
            current = later
            if index % 2 == 1:
                lane = slice((index // 2) * LANES, (index // 2 + 1) * LANES)
                total = jnp.where(first, sums[index], sums[index - 1])
                log_sum = jnp.where(first, peaks[index], peaks[index - 1]) + jnp.log(total)
                stat[:, lane] = lanes(rel, count, -log_sum, extra)
                mixed[:, lane] = (
                    jnp.where(first, sums[index - 1], sums[index]) / pltpu.roll(total, HEAD, 1)
                ).astype(low_type)
        for copy in keep_first(m, j):
            copy.start()
        send_a[lax.rem(j, 2)] = dot_plain(mixed[...], wo[...]).astype(low_type)
        exchange_a(m, j).start()

    def feed(m, j):
        rows = rows_of(j, chunk)
        slot = lax.rem(j, 2)
        exchange_a(m, j).wait()
        total = (
            send_a[slot].astype(jnp.float32)
            + got_a[m, j].astype(jnp.float32)
            + biases[0:1]
            + hbuf[m, rows].astype(jnp.float32)
        )
        unit, inv_scale = norm_rows(total)
        scale_a[...] = jnp.broadcast_to(inv_scale, shape)
        middle = unit * gains[0:1] + biases[1:2]
        high_mid[slot] = middle
        low_mid[...] = middle.astype(low_type)
        hidden_size = wi.shape[1]
        step = min(512, hidden_size)

        def before(start):
            part = slice(start, start + step)
            return dot_plain(low_mid[...], wi[:, part]) + in_b[:, part]

        pre = before(0)
        branch = jnp.zeros((chunk, width), jnp.float32)
        for start in range(0, hidden_size, step):
            part = slice(start, start + step)
            later = before(start + step) if start + step < hidden_size else None
            normal, density = erf_pair(pre)
            hidden[:, part] = (pre * normal).astype(low_type)
            slope[:, part] = (normal + pre * density).astype(low_type)
            branch = branch + dot_plain(hidden[:, part], wd[part])
            pre = later
        send_b[slot] = branch.astype(low_type)
        exchange_b(m, j).start()
        for copy in keep_second(m, j):
            copy.start()

    def finish(m, j):
        slot = lax.rem(j, 2)
        exchange_b(m, j).wait()
        total = (
            send_b[slot].astype(jnp.float32)
            + got_b[m, j].astype(jnp.float32)
            + biases[2:3]
            + high_mid[slot]
        )
        unit, inv_scale = norm_rows(total)
        scale_z[...] = jnp.broadcast_to(inv_scale, shape)
        result[...] = (unit * gains[1:2] + biases[3:4]).astype(low_type)

        @pl.when(section < sections - 1)
        def _():
            hop(m, j).start()

        for copy in keep_third(m, j):
            copy.start()

    def finish_wait(m, j):
        for copy in keep_third(m, j):
            copy.wait()

        @pl.when(section < sections - 1)
        def _():
            hop(m, j).wait_send()

    def one_row(m, carry):
        def first_step(j, carry):
            project(m, j)
            return carry

        lax.fori_loop(0, chunks, first_step, 0)

        @pl.when(m == 0)
        def _():
            for copy in weights[1:]:
                copy.wait()

        def step(i, carry):
            @pl.when(jnp.logical_and(i >= 1, i <= chunks))
            def _():
                for copy in keep_first(m, i - 1):
                    copy.wait()

            @pl.when(i < chunks)
            def _():
                mix(m, i)

            @pl.when(jnp.logical_and(i >= 2, i <= chunks + 1))
            def _():
                for copy in keep_second(m, i - 2):
                    copy.wait()

            @pl.when(jnp.logical_and(i >= 1, i <= chunks))
            def _():
                feed(m, i - 1)

            @pl.when(i >= 3)
            def _():
                finish_wait(m, i - 3)

            @pl.when(i >= 2)
            def _():
                finish(m, i - 2)

            return carry

        lax.fori_loop(0, chunks + 2, step, 0)
        finish_wait(m, chunks - 1)
        return carry

    lax.fori_loop(0, micro, one_row, 0)
    for j in range(chunks):
        keep_qkv(micro - 1, j).wait()
    for m in range(micro):
        for j in range(chunks):
            keep(m, j).wait()

    @pl.when(section > 0)
    def _():
        for m in range(micro):
            for j in range(chunks):
                hand_over(m, j).wait_send()


def forward_pass(sections, starts, qkv_b, in_b, gains, biases, rows_in, qkv_w, out_w, in_w, down_w):
    micro, length, width = rows_in.shape
    columns, hidden = out_w.shape[0], in_w.shape[1]
    chunk = min(256, length)
    chunks = length // chunk
    low, high = low_type, jnp.float32

    def out(*shape, dtype=low):
        return jax.ShapeDtypeStruct(shape, dtype)

    outs = dict(
        qkv=out(micro, length, 3 * columns),
        log_sums=out(micro, length, columns),
        mixed=out(micro, length, columns),
        middle=out(micro, length, width),
        hidden=out(micro, length, hidden),
        slope=out(micro, length, hidden),
        inputs=out(micro, length, width),
        result=out(micro, length, width),
        scales=out(micro, 2, length, LANES, dtype=high),
    )
    vmem = pl.BlockSpec(memory_space=pltpu.VMEM)
    anywhere = pl.BlockSpec(memory_space=pl.ANY)
    dma = pltpu.SemaphoreType.DMA
    results = pl.pallas_call(
        functools.partial(forward_kernel, sections, chunk),
        in_specs=[pl.BlockSpec(memory_space=pltpu.SMEM)] + [vmem] * 4 + [anywhere] * 5,
        out_specs=[anywhere] * len(outs),
        out_shape=list(outs.values()),
        scratch_shapes=[
            pltpu.VMEM(qkv_w.shape, low),
            pltpu.VMEM(out_w.shape, low),
            pltpu.VMEM(in_w.shape, low),
            pltpu.VMEM(down_w.shape, low),
            pltpu.VMEM((micro, length, width), low),
            pltpu.VMEM((length, 3 * columns), low),
            pltpu.VMEM((columns // HEAD, length, LANES), low),
            pltpu.VMEM((columns // HEAD, length, LANES), low),
            pltpu.VMEM((chunk, columns), low),
            pltpu.VMEM((chunk, columns), low),
            pltpu.VMEM((2, chunk, width), low),
            pltpu.VMEM((2, chunk, width), low),
            pltpu.VMEM((micro, chunks, chunk, width), low),
            pltpu.VMEM((micro, chunks, chunk, width), low),
            pltpu.VMEM((2, chunk, width), high),
            pltpu.VMEM((chunk, width), low),
            pltpu.VMEM((chunk, hidden), low),
            pltpu.VMEM((chunk, hidden), low),
            pltpu.VMEM((chunk, width), low),
            pltpu.VMEM((chunk, LANES), high),
            pltpu.VMEM((chunk, LANES), high),
            dma((4,)),
            dma((micro, chunks)),
            dma,
            dma((micro, chunks)),
            dma((micro, chunks)),
            dma((micro, chunks)),
            dma((micro, chunks)),
            dma((chunks,)),
            dma((2,)),
            dma((micro, chunks)),
            dma((2,)),
            dma((micro, chunks)),
            dma((2,)),
            dma((4,)),
            dma((2,)),
        ],
        compiler_params=pltpu.CompilerParams(
            collective_id=0, has_side_effects=True, vmem_limit_bytes=62 * 1024 * 1024
        ),
        name="forward_pass",
    )(starts, qkv_b, in_b, gains, biases, rows_in, qkv_w, out_w, in_w, down_w)
    return dict(zip(outs, results))


def greet(section, sections, peer):
    barrier = pltpu.get_barrier_semaphore()
    pl.semaphore_signal(barrier, inc=1, device_id=peer, device_id_type=MESH)

    @pl.when(section > 0)
    def _():
        pl.semaphore_signal(
            barrier, inc=1, device_id={"section": section - 1}, device_id_type=MESH
        )

    @pl.when(section < sections - 1)
    def _():
        pl.semaphore_signal(
            barrier, inc=1, device_id={"section": section + 1}, device_id_type=MESH
        )

    inner = jnp.logical_and(section > 0, section < sections - 1)

    @pl.when(inner)
    def _():
        pl.semaphore_wait(barrier, 3)

    @pl.when(jnp.logical_not(inner))
    def _():
        pl.semaphore_wait(barrier, 2)


def backward_kernel(
    sections,
    chunk,
    starts_ref,
    gains,
    biases,
    rows_back,
    qkv_w,
    out_w,
    in_w,
    down_w,
    qkv_in,
    stat_in,
    mixed_in,
    middle_in,
    slope_in,
    result_in,
    scale_in,
    row_sums,
    in_sums,
    qkv_sums,
    time_sums,
    gz_out,
    pre_out,
    ga_out,
    gqkv_out,
    grads_out,
    wq,
    wo,
    wi,
    wd,
    gbuf,
    high_ga,
    qkv,
    keys,
    values,
    grad_k,
    grad_v,
    grad_qkv,
    send_a,
    send_b,
    got_a,
    got_b,
    high_gz,
    low_gz,
    low_pre,
    low_ga,
    grad_mixed,
    grads,
    result,
    slope,
    scale_z,
    middle,
    scale_a,
    mixed,
    stat,
    w_sem,
    load_sem,
    hop_send,
    hop_got,
    pass_send,
    pass_got,
    a_send,
    a_got,
    b_send,
    b_got,
    qkv_sem,
    first_sem,
    second_sem,
    keep_sem,
    keep_ga_sem,
    keep_qkv_sem,
    grads_sem,
):
    section = lax.axis_index("section")
    dp = lax.axis_index("dp")
    core = lax.rem(dp, 2)
    peer = {"dp": dp + 1 - 2 * core}
    micro, length, width = gbuf.shape
    count = starts_ref.shape[1]
    columns = grad_mixed.shape[1]
    pairs = columns // LANES
    chunks = length // chunk
    half = chunk // 2
    last = sections - 1
    shape = (chunk, LANES)

    weights = [
        pltpu.make_async_copy(source, target, w_sem.at[i])
        for i, (source, target) in enumerate(
            ((down_w, wd), (in_w, wi), (out_w, wo), (qkv_w, wq))
        )
    ]
    for copy in weights:
        copy.start()

    def load(m, j):
        rows = rows_of(j, chunk)
        return pltpu.make_async_copy(
            rows_back.at[m, rows], gbuf.at[m, rows], load_sem.at[m, j]
        )

    def hop(m, j):
        target = pl.ds(pl.multiple_of(j * chunk + core * half, half), half)
        return pltpu.make_async_remote_copy(
            src_ref=grads.at[j, pl.ds(pl.multiple_of(core * half, half), half)],
            dst_ref=gbuf.at[m, target],
            send_sem=hop_send.at[j],
            recv_sem=hop_got.at[m, j],
            device_id={"section": section - 1},
            device_id_type=MESH,
        )

    def hand_over(m, j):
        rows = pl.ds(pl.multiple_of(j * chunk + core * half, half), half)
        return pltpu.make_async_remote_copy(
            src_ref=gbuf.at[m, rows],
            dst_ref=gbuf.at[m, rows],
            send_sem=pass_send.at[m, j],
            recv_sem=pass_got.at[m, j],
            device_id=peer,
            device_id_type=MESH,
        )

    def exchange(send, got, send_sem, got_sem, m, j):
        slot = lax.rem(j, 2)
        return pltpu.make_async_remote_copy(
            src_ref=send.at[slot],
            dst_ref=got.at[j],
            send_sem=send_sem.at[slot],
            recv_sem=got_sem.at[m, j],
            device_id=peer,
            device_id_type=MESH,
        )

    def exchange_a(m, j):
        return exchange(send_a, got_a, a_send, a_got, m, j)

    def exchange_b(m, j):
        return exchange(send_b, got_b, b_send, b_got, m, j)

    def load_qkv(m):
        return pltpu.make_async_copy(qkv_in.at[m], qkv, qkv_sem)

    def load_first(m, j):
        rows = rows_of(j, chunk)
        return [
            pltpu.make_async_copy(result_in.at[m, rows], result, first_sem.at[0]),
            pltpu.make_async_copy(slope_in.at[m, rows], slope, first_sem.at[1]),
            pltpu.make_async_copy(scale_in.at[m, 1, rows], scale_z, first_sem.at[2]),
        ]

    def load_second(m, j):
        rows = rows_of(j, chunk)
        return [
            pltpu.make_async_copy(middle_in.at[m, rows], middle, second_sem.at[0]),
            pltpu.make_async_copy(scale_in.at[m, 0, rows], scale_a, second_sem.at[1]),
            pltpu.make_async_copy(mixed_in.at[m, rows], mixed, second_sem.at[2]),
            pltpu.make_async_copy(stat_in.at[m, rows], stat, second_sem.at[3]),
        ]

    def keep_first(m, j):
        rows = rows_of(j, chunk)
        return [
            pltpu.make_async_copy(low_gz, gz_out.at[m, rows], keep_sem.at[0]),
            pltpu.make_async_copy(low_pre, pre_out.at[m, rows], keep_sem.at[1]),
        ]

    def keep_second(m, j):
        rows = rows_of(j, chunk)
        return pltpu.make_async_copy(low_ga, ga_out.at[m, rows], keep_ga_sem)

    def keep_qkv(m):
        return pltpu.make_async_copy(grad_qkv, gqkv_out.at[m], keep_qkv_sem)

    def keep_grads(m, j):
        return pltpu.make_async_copy(
            grads.at[j], grads_out.at[m, rows_of(j, chunk)], grads_sem.at[j]
        )

    load_qkv(0).start()
    for copy in load_first(0, 0) + load_second(0, 0):
        copy.start()

    @pl.when(section == last)
    def _():
        for m in range(micro):
            for j in range(chunks):
                load(m, j).start()

    row_sums[...] = jnp.zeros_like(row_sums)
    in_sums[...] = jnp.zeros_like(in_sums)
    qkv_sums[...] = jnp.zeros_like(qkv_sums)
    time_sums[...] = jnp.zeros_like(time_sums)
    greet(section, sections, peer)

    def add_row(index, value):
        row_sums[index : index + 1] += jnp.sum(value, axis=0, keepdims=True)

    def receive(m, j):
        @pl.when(section < last)
        def _():
            hop(m, j).wait_recv()
            hand_over(m, j).start()

    def norm_back_rows(gradient, unit, inv_scale, gain):
        weighted = gradient * gain
        return inv_scale * (
            weighted
            - jnp.mean(weighted, axis=-1, keepdims=True)
            - unit * jnp.mean(weighted * unit, axis=-1, keepdims=True)
        )

    def feed_back(m, j):
        rows = rows_of(j, chunk)
        slot = lax.rem(j, 2)

        @pl.when(section == last)
        def _():
            load(m, j).wait()

        @pl.when(section < last)
        def _():
            hand_over(m, j).wait_recv()

        for copy in load_first(m, j):
            copy.wait()
        gradient = gbuf[m, rows].astype(jnp.float32)
        unit = (result[...].astype(jnp.float32) - biases[3:4]) / gains[1:2]
        grad_z = norm_back_rows(gradient, unit, scale_z[:, :1], gains[1:2])
        add_row(1, gradient * unit)
        add_row(5, gradient)
        add_row(4, grad_z)
        high_gz[slot] = grad_z
        low_gz[...] = grad_z.astype(low_type)
        hidden_size = wi.shape[1]
        step = min(512, hidden_size)

        def before(start):
            return dot_rows(low_gz[...], wd[start : start + step])

        current = before(0)
        branch = jnp.zeros((chunk, width), jnp.float32)
        for start in range(0, hidden_size, step):
            part = slice(start, start + step)
            later = before(start + step) if start + step < hidden_size else None
            low = (current * slope[:, part].astype(jnp.float32)).astype(low_type)
            low_pre[:, part] = low
            in_sums[:, part] += jnp.sum(low.astype(jnp.float32), axis=0, keepdims=True)
            branch = branch + dot_rows(low, wi[:, part])
            current = later
        send_a[slot] = branch.astype(low_type)
        exchange_a(m, j).start()
        for copy in keep_first(m, j):
            copy.start()

    def norm_step(m, j):
        rows = rows_of(j, chunk)
        slot = lax.rem(j, 2)
        exchange_a(m, j).wait()
        for copy in load_second(m, j):
            copy.wait()
        gradient = (
            send_a[slot].astype(jnp.float32) + got_a[j].astype(jnp.float32) + high_gz[slot]
        )
        unit = (middle[...].astype(jnp.float32) - biases[1:2]) / gains[0:1]
        grad_a = norm_back_rows(gradient, unit, scale_a[:, :1], gains[0:1])
        add_row(0, gradient * unit)
        add_row(3, gradient)
        add_row(2, grad_a)
        high_ga[rows] = grad_a
        low_ga[...] = grad_a.astype(low_type)
        keep_second(m, j).start()
        grad_mixed[...] = dot_rows(low_ga[...], wo[...]).astype(low_type)

    def build(m):
        load_qkv(m).wait()

        def step(j, carry):
            rows = rows_of(j, chunk)
            first, rel, own = doc_lanes(starts_ref, m, j * chunk, shape, count)
            fixed = jnp.logical_and(rel >= count, rel < count + 3)
            extra_k = jnp.where(jnp.logical_or(own, fixed), 1.0, 0.0).astype(low_type)
            extra_v = jnp.where(fixed, 1.0, 0.0).astype(low_type)
            for p in range(pairs):
                lane = slice(p * LANES, (p + 1) * LANES)
                k = qkv[rows, columns + p * LANES : columns + (p + 1) * LANES]
                v = qkv[rows, 2 * columns + p * LANES : 2 * columns + (p + 1) * LANES]
                keys[2 * p, rows] = jnp.where(first, k, extra_k)
                keys[2 * p + 1, rows] = jnp.where(first, extra_k, k)
                values[2 * p, rows] = jnp.where(first, v, extra_v)
                values[2 * p + 1, rows] = jnp.where(first, extra_v, v)
                grad_k[rows, lane] = jnp.zeros(shape, jnp.float32)
                grad_v[rows, lane] = jnp.zeros(shape, jnp.float32)
            return carry

        lax.fori_loop(0, chunks, step, 0)

    def mix_back(m, j):
        rows = rows_of(j, chunk)
        lane_index = lax.broadcasted_iota(jnp.int32, shape, 1)
        first = lane_index < HEAD
        rel = lane_index % HEAD
        all_first = lax.broadcasted_iota(jnp.int32, (length, LANES), 1) < HEAD
        for p in range(pairs):
            lane = slice(p * LANES, (p + 1) * LANES)
            q = qkv[rows, lane] * low_type(HEAD**-0.5)
            k = qkv[:, columns + p * LANES : columns + (p + 1) * LANES]
            g = grad_mixed[:, lane]
            extra_q = stat[:, lane]
            product = g.astype(jnp.float32) * mixed[:, lane].astype(jnp.float32)
            dots = [
                jnp.sum(jnp.where(first, product, 0.0), axis=-1, keepdims=True),
                jnp.sum(jnp.where(first, 0.0, product), axis=-1, keepdims=True),
            ]
            extra_g = lanes(
                rel, count, -jnp.where(first, dots[1], dots[0]), jnp.zeros_like(extra_q)
            )
            parts = []
            for i in range(2):
                q_head = jnp.where(first, q, extra_q) if i == 0 else jnp.where(first, extra_q, q)
                g_head = jnp.where(first, g, extra_g) if i == 0 else jnp.where(first, extra_g, g)
                probs = jnp.exp(dot_rows(keys[2 * p + i], q_head))
                slopes = (probs * dot_rows(values[2 * p + i], g_head)).astype(low_type)
                parts.append(
                    (
                        dot_plain(probs.astype(low_type), g),
                        dot_plain(slopes, q),
                        dot_first(slopes, k),
                    )
                )
            grad_v[:, lane] += jnp.where(all_first, parts[0][0], parts[1][0])
            grad_k[:, lane] += jnp.where(all_first, parts[0][1], parts[1][1])
            grad_qkv[rows, lane] = (
                jnp.where(first, parts[0][2], parts[1][2]) * (HEAD**-0.5)
            ).astype(low_type)

    def project_back(m, j):
        rows = rows_of(j, chunk)
        low = grad_qkv[rows]
        qkv_sums[...] += jnp.sum(low.astype(jnp.float32), axis=0, keepdims=True)
        send_b[lax.rem(j, 2)] = dot_rows(low, wq[...]).astype(low_type)
        exchange_b(m, j).start()

    def finish(m, j):
        rows = rows_of(j, chunk)
        slot = lax.rem(j, 2)
        exchange_b(m, j).wait()

        @pl.when(m > 0)
        def _():
            keep_grads(m - 1, j).wait()

            @pl.when(section > 0)
            def _():
                hop(m - 1, j).wait_send()

        total = (
            send_b[slot].astype(jnp.float32) + got_b[j].astype(jnp.float32) + high_ga[rows]
        ).astype(low_type)
        grads[j] = total
        time_sums[m] += jnp.sum(total.astype(jnp.float32), axis=0, keepdims=True)

        @pl.when(section > 0)
        def _():
            hop(m, j).start()

        keep_grads(m, j).start()

    def one_row(m, carry):
        def step(i, carry):
            @pl.when(i < 2)
            def _():
                receive(m, i)

            @pl.when(jnp.logical_and(i >= 1, i < chunks))
            def _():
                for copy in keep_first(m, i - 1):
                    copy.wait()

            @pl.when(i < chunks)
            def _():
                @pl.when(jnp.logical_and(m == 0, i == 0))
                def _():
                    weights[0].wait()
                    weights[1].wait()

                feed_back(m, i)

                @pl.when(i + 1 < chunks)
                def _():
                    for copy in load_first(m, i + 1):
                        copy.start()

                @pl.when(jnp.logical_and(i + 1 == chunks, m + 1 < micro))
                def _():
                    for copy in load_first(m + 1, 0):
                        copy.start()

            @pl.when(i == 0)
            def _():
                @pl.when(m == 0)
                def _():
                    weights[2].wait()
                    weights[3].wait()

                build(m)

            @pl.when(i >= 1)
            def _():
                @pl.when(i >= 2)
                def _():
                    keep_second(m, i - 2).wait()

                norm_step(m, i - 1)

                @pl.when(i + 1 < chunks)
                def _():
                    receive(m, i + 1)

                mix_back(m, i - 1)

                @pl.when(i < chunks)
                def _():
                    for copy in load_second(m, i):
                        copy.start()

                @pl.when(jnp.logical_and(i == chunks, m + 1 < micro))
                def _():
                    for copy in load_second(m + 1, 0):
                        copy.start()

            return carry

        lax.fori_loop(0, chunks + 1, step, 0)
        for copy in keep_first(m, chunks - 1):
            copy.wait()
        keep_second(m, chunks - 1).wait()

        @pl.when(m + 1 < micro)
        def _():
            load_qkv(m + 1).start()

        grad_qkv[:, columns : 2 * columns] = grad_k[...].astype(low_type)
        grad_qkv[:, 2 * columns :] = grad_v[...].astype(low_type)
        keep_qkv(m).start()

        def last_step(i, carry):
            @pl.when(i < chunks)
            def _():
                project_back(m, i)

            @pl.when(i >= 1)
            def _():
                finish(m, i - 1)

            return carry

        lax.fori_loop(0, chunks + 1, last_step, 0)
        keep_qkv(m).wait()
        return carry

    lax.fori_loop(0, micro, one_row, 0)
    for j in range(chunks):
        keep_grads(micro - 1, j).wait()

    @pl.when(section > 0)
    def _():
        for j in range(chunks):
            hop(micro - 1, j).wait_send()

    @pl.when(section < last)
    def _():
        for m in range(micro):
            for j in range(chunks):
                hand_over(m, j).wait_send()


def backward_pass(sections, starts, gains, biases, rows_back, params, stash):
    qkv_w, out_w, in_w, down_w = params
    micro, length, width = rows_back.shape
    columns, hidden = out_w.shape[0], in_w.shape[1]
    chunk = min(256, length)
    chunks = length // chunk
    low, high = low_type, jnp.float32

    def out(*shape, dtype=low):
        return jax.ShapeDtypeStruct(shape, dtype)

    outs = dict(
        row_sums=out(6, width, dtype=high),
        in_sums=out(1, hidden, dtype=high),
        qkv_sums=out(1, 3 * columns, dtype=high),
        time_sums=out(micro, 1, width, dtype=high),
        grad_z=out(micro, length, width),
        grad_pre=out(micro, length, hidden),
        grad_a=out(micro, length, width),
        grad_qkv=out(micro, length, 3 * columns),
        grads=out(micro, length, width),
    )
    vmem = pl.BlockSpec(memory_space=pltpu.VMEM)
    anywhere = pl.BlockSpec(memory_space=pl.ANY)
    dma = pltpu.SemaphoreType.DMA
    results = pl.pallas_call(
        functools.partial(backward_kernel, sections, chunk),
        in_specs=[pl.BlockSpec(memory_space=pltpu.SMEM)] + [vmem] * 2 + [anywhere] * 12,
        out_specs=[vmem] * 4 + [anywhere] * 5,
        out_shape=list(outs.values()),
        scratch_shapes=[
            pltpu.VMEM(qkv_w.shape, low),
            pltpu.VMEM(out_w.shape, low),
            pltpu.VMEM(in_w.shape, low),
            pltpu.VMEM(down_w.shape, low),
            pltpu.VMEM((micro, length, width), low),
            pltpu.VMEM((length, width), high),
            pltpu.VMEM((length, 3 * columns), low),
            pltpu.VMEM((columns // HEAD, length, LANES), low),
            pltpu.VMEM((columns // HEAD, length, LANES), low),
            pltpu.VMEM((length, columns), high),
            pltpu.VMEM((length, columns), high),
            pltpu.VMEM((length, 3 * columns), low),
            pltpu.VMEM((2, chunk, width), low),
            pltpu.VMEM((2, chunk, width), low),
            pltpu.VMEM((chunks, chunk, width), low),
            pltpu.VMEM((chunks, chunk, width), low),
            pltpu.VMEM((2, chunk, width), high),
            pltpu.VMEM((chunk, width), low),
            pltpu.VMEM((chunk, hidden), low),
            pltpu.VMEM((chunk, width), low),
            pltpu.VMEM((chunk, columns), low),
            pltpu.VMEM((chunks, chunk, width), low),
            pltpu.VMEM((chunk, width), low),
            pltpu.VMEM((chunk, hidden), low),
            pltpu.VMEM((chunk, LANES), high),
            pltpu.VMEM((chunk, width), low),
            pltpu.VMEM((chunk, LANES), high),
            pltpu.VMEM((chunk, columns), low),
            pltpu.VMEM((chunk, columns), low),
            dma((4,)),
            dma((micro, chunks)),
            dma((chunks,)),
            dma((micro, chunks)),
            dma((micro, chunks)),
            dma((micro, chunks)),
            dma((2,)),
            dma((micro, chunks)),
            dma((2,)),
            dma((micro, chunks)),
            dma,
            dma((3,)),
            dma((4,)),
            dma((2,)),
            dma,
            dma,
            dma((chunks,)),
        ],
        compiler_params=pltpu.CompilerParams(
            collective_id=1, has_side_effects=True, vmem_limit_bytes=63 * 1024 * 1024
        ),
        name="backward_pass",
    )(
        starts,
        gains,
        biases,
        rows_back,
        qkv_w,
        out_w,
        in_w,
        down_w,
        stash["qkv"],
        stash["log_sums"],
        stash["mixed"],
        stash["middle"],
        stash["slope"],
        stash["result"],
        stash["scales"],
    )
    return dict(zip(outs, results))


def unit_norm(value):
    average = jnp.mean(value, axis=-1, keepdims=True)
    centered = value - average
    inv_scale = lax.rsqrt(jnp.mean(centered * centered, axis=-1, keepdims=True) + eps_norm)
    return centered * inv_scale, inv_scale


def norm_back(gradient, normed, inv_scale, gain_row):
    weighted = gradient * gain_row
    adjusted = (
        weighted
        - jnp.mean(weighted, axis=-1, keepdims=True)
        - normed * jnp.mean(weighted * normed, axis=-1, keepdims=True)
    )
    return inv_scale * adjusted


def gelu_pair(pre):
    normal = 0.5 * (1.0 + lax.erf(pre * 0.7071067811865476))
    density = jnp.exp(-0.5 * pre * pre) * 0.3989422804014327
    return pre * normal, normal + pre * density


def forward_layer(at, inputs, starts, params):
    qkv_w, qkv_b, out_w, in_w, in_b, down_w, gains, biases = params
    qkv = (dot_plain(inputs, qkv_w) + qkv_b).astype(low_type)
    mixed, log_sums = attend(qkv, starts)
    branch = at.group_sum(dot_plain(mixed, out_w).astype(low_type))
    unit_a, scale_a = unit_norm(branch + biases[0] + inputs.astype(jnp.float32))
    middle = unit_a * gains[0] + biases[1]
    low_middle = middle.astype(low_type)
    hidden, slope = gelu_pair(dot_plain(low_middle, in_w) + in_b)
    hidden = hidden.astype(low_type)
    branch_two = at.group_sum(dot_plain(hidden, down_w).astype(low_type))
    unit_z, scale_z = unit_norm(branch_two + biases[2] + middle)
    result = (unit_z * gains[1] + biases[3]).astype(low_type)
    saved = dict(
        inputs=inputs,
        qkv=qkv,
        mixed=mixed,
        log_sums=log_sums,
        scale_a=scale_a[:, 0],
        middle=low_middle,
        hidden=hidden,
        slope=slope.astype(low_type),
        scale_z=scale_z[:, 0],
    )
    return result, saved


def backward_layer(at, saved, incoming, starts, params):
    qkv_w, qkv_b, out_w, in_w, in_b, down_w, gains, biases = params
    gradient = incoming.astype(jnp.float32)
    unit_z = (saved["result"].astype(jnp.float32) - biases[3]) / gains[1]
    grad_z = norm_back(gradient, unit_z, saved["scale_z"][:, None], gains[1])
    low_gz = grad_z.astype(low_type)
    grad_pre = (dot_rows(low_gz, down_w) * saved["slope"].astype(jnp.float32)).astype(low_type)
    grad_mid = at.group_sum(dot_rows(grad_pre, in_w).astype(low_type)) + grad_z
    unit_a = (saved["middle"].astype(jnp.float32) - biases[1]) / gains[0]
    grad_a = norm_back(grad_mid, unit_a, saved["scale_a"][:, None], gains[0])
    low_ga = grad_a.astype(low_type)
    grad_mixed = dot_rows(low_ga, out_w).astype(low_type)
    grad_qkv = jnp.concatenate(
        attend_back(saved["qkv"], starts, saved["mixed"], saved["log_sums"], grad_mixed), 1
    )
    grad_x = at.group_sum(dot_rows(grad_qkv, qkv_w).astype(low_type)) + grad_a
    sums = jnp.stack(
        [
            jnp.sum(grad_mid * unit_a, axis=0),
            jnp.sum(gradient * unit_z, axis=0),
            jnp.sum(grad_a, axis=0),
            jnp.sum(grad_mid, axis=0),
            jnp.sum(grad_z, axis=0),
            jnp.sum(gradient, axis=0),
        ]
    )
    kept = dict(grad_z=low_gz, slope=grad_pre, grad_a=low_ga, qkv=grad_qkv)
    return grad_x.astype(low_type), kept, sums


def store(buffers, values, slot):
    return jax.tree.map(
        lambda buffer, value: lax.dynamic_update_index_in_dim(buffer, value, slot, 0),
        buffers,
        values,
    )


def pick(buffers, slot):
    return jax.tree.map(
        lambda buffer: lax.dynamic_index_in_dim(buffer, slot, 0, keepdims=False), buffers
    )


def group_weight(at, weight):
    parts = weight.reshape((at.chips, -1) + weight.shape[1:])

    def across(s, g, u, x, c):
        return (s, c, u, x, g) if g != c else None

    def along(step):
        return lambda s, g, u, x, c: (s, g, u, (x + step) % at.chips, c) if g != c else None

    piece = at.move(lax.dynamic_index_in_dim(parts, at.chip, 0, keepdims=False), across)
    pieces = [piece]
    for step in range(1, at.chips):
        pieces.append(at.move(piece, along(step)))
    whole = parts
    for step, piece in enumerate(pieces):
        spot = (at.chip - step) % at.chips
        own = lax.dynamic_index_in_dim(parts, spot, 0, keepdims=False)
        whole = lax.dynamic_update_index_in_dim(whole, jnp.where(at.home, own, piece), spot, 0)
    return whole.reshape(weight.shape)


def group_rows(at, tokens, section):
    def across(s, g, u, x, c):
        return (s, 1 - g, u, x, c) if s == section else None

    own = lax.dynamic_index_in_dim(tokens, at.group, 0, keepdims=False)
    other = at.move(lax.dynamic_index_in_dim(tokens, 1 - at.group, 0, keepdims=False), across)
    lower = at.group == 0
    pair = jnp.stack([jnp.where(lower, own, other), jnp.where(lower, other, own)])
    whole = at.group_gather(pair)
    whole = whole.reshape((2, at.halves) + pair.shape)
    whole = jnp.swapaxes(whole, 1, 2)
    return whole.reshape(2, -1, tokens.shape[-1])


def spread_rows(at, rows, length):
    def across(s, g, u, x, c):
        return (s, 1 - g, u, x, c)

    row = lax.dynamic_index_in_dim(rows, at.core, 0, keepdims=False)
    tile = length // at.tensor

    def piece(group):
        return lax.dynamic_slice_in_dim(row, (group * at.halves + at.part) * tile, tile, 0)

    own = piece(at.group)
    other = at.move(piece(1 - at.group), across)
    lower = at.group == 0
    return jnp.stack([jnp.where(lower, own, other), jnp.where(lower, other, own)])


def sum_weight(at, gradient, across_first):
    parts = gradient.reshape((at.chips, -1) + gradient.shape[1:])

    def across(s, g, u, x, c):
        return (s, c, u, x, c) if g != c else None

    def along(step):
        def target(s, g, u, x, c):
            if across_first and g != c:
                return None
            return (s, g, u, (x + step) % at.chips, c)

        return target

    def fold_chips(parts):
        total = lax.dynamic_index_in_dim(parts, at.chip, 0, keepdims=False).astype(jnp.float32)
        for step in range(1, at.chips):
            piece = lax.dynamic_index_in_dim(
                parts, (at.chip + step) % at.chips, 0, keepdims=False
            )
            total = total + at.move(piece, along(step)).astype(jnp.float32)
        return total.astype(low_type)

    if across_first:
        total = fold_chips(
            (parts.astype(jnp.float32) + at.move(parts, across).astype(jnp.float32)).astype(
                low_type
            )
        )
    else:
        part = fold_chips(parts)
        total = (part.astype(jnp.float32) + at.move(part, across).astype(jnp.float32)).astype(
            low_type
        )
    halves = total.reshape((2, -1) + total.shape[1:])

    def over(s, g, u, x, c):
        return (s, g, u, x, 1 - c) if g == c else None

    own = lax.dynamic_index_in_dim(halves, at.core, 0, keepdims=False)
    other = at.move(lax.dynamic_index_in_dim(halves, 1 - at.core, 0, keepdims=False), over)
    return jnp.where(at.home, own, other).astype(jnp.float32)


def layer_ticks(at, starts, rows_in, rows_back, params):
    qkv_w = params[0]
    micro_count, length, width = rows_in.shape
    tick_count = micro_count + at.sections - 1
    slots = micro_count + 1

    def hop(result, distance):
        def target(s, g, u, x, c):
            return (s + distance, g, u, x, c) if 0 <= s + distance < at.sections else None

        tile = length // at.size
        piece = at.move(lax.dynamic_slice_in_dim(result, at.rank * tile, tile, 0), target)
        return at.group_gather(piece).reshape(length, width)

    def place_of(tick_value, stage):
        place = tick_value - stage
        usable = jnp.logical_and(place >= 0, place < micro_count)
        return usable, jnp.clip(place, 0, micro_count - 1), jnp.where(usable, place, micro_count)

    def empty(values):
        return jax.tree.map(
            lambda value: jnp.zeros((slots,) + value.shape, value.dtype), values
        )

    def forward_tick(tick_value, arrived, stash, outputs):
        usable, position, slot = place_of(tick_value, at.section)
        inputs = jnp.where(at.section == 0, rows_in[position], arrived)
        result, saved = forward_layer(at, inputs, starts[position], params)
        if stash is None:
            return result, saved
        return result, store(stash, saved, slot), store(outputs, result, slot)

    blank = jnp.zeros((length, width), low_type)
    shapes = jax.eval_shape(lambda: forward_tick(0, blank, None, None))
    stash, outputs = empty(shapes[1]), empty(shapes[0])

    def forward_loop(tick_value, carry):
        result, stash, outputs = forward_tick(tick_value, *carry)
        return hop(result, 1), stash, outputs

    carry = lax.fori_loop(0, tick_count - 1, forward_loop, (blank, stash, outputs))
    _, stash, outputs = forward_tick(tick_count - 1, *carry)

    def backward_tick(tick_value, arrived, stash, grads, totals):
        usable, position, slot = place_of(tick_value, at.sections - 1 - at.section)
        incoming = jnp.where(at.section == at.sections - 1, rows_back[position], arrived)
        grad_x, kept_now, sums = backward_layer(
            at, pick(dict(stash, result=outputs), slot), incoming, starts[position], params
        )
        totals = totals + jnp.where(usable, sums, 0.0)
        kept = store({name: stash[name] for name in kept_now}, kept_now, slot)
        return grad_x, dict(stash, **kept), store(grads, grad_x, slot), totals

    for name in ("grad_z", "grad_a"):
        stash[name] = empty(blank)
    totals = jnp.zeros((6, width), jnp.float32)

    def backward_loop(tick_value, carry):
        grad_x, stash, grads, totals = backward_tick(tick_value, *carry)
        return hop(grad_x, -1), stash, grads, totals

    carry = lax.fori_loop(
        0, tick_count - 1, backward_loop, (blank, stash, empty(blank), totals)
    )
    _, stash, grads, totals = backward_tick(tick_count - 1, *carry)

    def both(buffer):
        return buffer[:micro_count]

    low_gz, grad_pre, low_ga, grad_qkv = (
        both(stash[name]) for name in ("grad_z", "slope", "grad_a", "qkv")
    )
    stash = {name: both(value) for name, value in stash.items()}
    stash["result"] = both(outputs)
    grads = both(grads)
    back = dict(
        row_sums=totals,
        in_sums=jnp.sum(grad_pre, axis=(0, 1), dtype=jnp.float32)[None],
        qkv_sums=jnp.sum(grad_qkv, axis=(0, 1), dtype=jnp.float32)[None],
        time_sums=jnp.sum(grads, axis=1, keepdims=True, dtype=jnp.float32),
        grad_z=low_gz,
        grad_pre=grad_pre,
        grad_a=low_ga,
        grad_qkv=grad_qkv,
        grads=grads,
    )
    return stash, back


def shards(
    tokens,
    timesteps,
    seg_starts,
    time_params,
    qkv_weight,
    qv_bias,
    out_weight,
    ffn_in,
    ffn_bias,
    ffn_out,
    ln_gains,
    row_biases,
    cotangent,
):
    at = Layout()
    width = tokens.shape[-1]
    length = tokens.shape[1] * at.tensor
    columns = qkv_weight.shape[3]

    def both_cores(value):
        def over(s, g, u, x, c):
            return (s, g, u, x, 1 - c)

        other = at.move(value, over)
        first = at.core == 0
        mine = jnp.stack([jnp.where(first, value, other), jnp.where(first, other, value)])
        return lax.dynamic_index_in_dim(mine, at.group, 1, keepdims=False)

    starts = both_cores(seg_starts)
    fractions_own = timesteps.astype(jnp.float32) / 5000.0
    fractions = both_cores(fractions_own)
    time_values = time_params.astype(jnp.float32)
    embedded = (
        tokens.astype(jnp.float32) + fractions_own[:, None, None] * time_values[0] + time_values[1]
    ).astype(low_type)
    rows_in = group_rows(at, embedded, 0)
    qv_low = group_weight(at, qv_bias[0].T).T.astype(jnp.float32)
    qkv_w = group_weight(at, qkv_weight[0].reshape(width, 3 * columns))
    out_w = group_weight(at, out_weight[0])
    in_w = group_weight(at, ffn_in[0])
    in_b = group_weight(at, ffn_bias[0])
    down_w = group_weight(at, ffn_out[0])
    rows_back = group_rows(at, cotangent, at.sections - 1)
    qkv_b = jnp.concatenate([qv_low[0], jnp.zeros((columns,), jnp.float32), qv_low[1]])
    params = (
        qkv_w,
        qkv_b,
        out_w,
        in_w,
        in_b.astype(jnp.float32),
        down_w,
        ln_gains[0].astype(jnp.float32),
        row_biases[0].astype(jnp.float32),
    )

    if at.size == 2:
        vectors = (starts, qkv_b[None], params[4][None], params[6], params[7])
        matrices = (qkv_w, out_w, in_w, down_w)
        stash = forward_pass(at.sections, *vectors, rows_in, *matrices)
        back = backward_pass(at.sections, starts, *params[6:], rows_back, matrices, stash)
    else:
        stash, back = layer_ticks(at, starts, rows_in, rows_back, params)
    layer_outs = spread_rows(at, stash["result"], length)
    input_grads = spread_rows(at, back["grads"], length)

    def product(left, right):
        left, right = (v.reshape(-1, v.shape[-1]) for v in (left, right))
        return dot_first(left, right).astype(low_type)

    down_g = sum_weight(at, product(stash["hidden"], back["grad_z"]), True)
    in_g = sum_weight(at, product(stash["middle"], back["grad_pre"]), False)
    out_g = sum_weight(at, product(stash["mixed"], back["grad_a"]), True)
    qkv_g = sum_weight(at, product(stash["inputs"], back["grad_qkv"]), False)
    qkv_bias_g = back["qkv_sums"].reshape(3, columns)
    sliced = jnp.concatenate([qkv_bias_g[0], qkv_bias_g[2], back["in_sums"][0]])
    every = jnp.zeros((at.size,) + sliced.shape, jnp.float32)
    every = lax.dynamic_update_index_in_dim(every, sliced, at.rank, 0)
    row_terms = jnp.where(at.rank == 0, back["row_sums"], 0.0)
    small = lax.psum(
        jnp.concatenate([row_terms.reshape(-1), every.reshape(-1)]), ("tensor", "dp")
    )
    row_sums = small[: row_terms.size].reshape(row_terms.shape)
    tensor = lax.axis_index("tensor")
    dp = lax.axis_index("dp")
    mine = lax.dynamic_index_in_dim(
        small[row_terms.size :].reshape(every.shape), tensor, 0, keepdims=False
    )

    def share(value, count, index):
        size = value.shape[-1] // count
        return lax.dynamic_slice_in_dim(value, index * size, size, value.ndim - 1)

    qv_g = share(mine[: 2 * columns].reshape(2, columns), at.dp, dp)
    in_bias_g = share(mine[2 * columns :], at.dp, dp)
    row_share = share(row_sums, at.tensor * at.dp, tensor * at.dp + dp)

    row_grads = back["time_sums"][:, 0]
    time_terms = jnp.stack([jnp.sum(fractions[:, None] * row_grads, 0), jnp.sum(row_grads, 0)])
    time_terms = jnp.where(jnp.logical_and(at.section == 0, at.rank == 0), time_terms, 0.0)
    grad_time = lax.psum(time_terms, AXES)
    return (
        layer_outs[None],
        input_grads[None],
        qkv_g.reshape(-1, 3, columns)[None],
        qv_g[None],
        out_g[None],
        in_g[None],
        in_bias_g[None],
        down_g[None],
        row_share[None, :2],
        row_share[None, 2:],
        grad_time,
    )


def solution(mesh):
    return jax.shard_map(
        shards,
        mesh=mesh,
        in_specs=(
            P("dp", "tensor", None),
            P("dp"),
            P("dp", None),
            P(),
            P("section", None, None, "tensor"),
            P("section", None, "tensor"),
            P("section", "tensor", None),
            P("section", None, "tensor"),
            P("section", "tensor"),
            P("section", "tensor", None),
            P("section", None, None),
            P("section", None, None),
            P("dp", "tensor", None),
        ),
        out_specs=(
            P("section", "dp", "tensor", None),
            P("section", "dp", "tensor", None),
            P("section", "dp", None, "tensor"),
            P("section", None, ("tensor", "dp")),
            P("section", ("tensor", "dp"), None),
            P("section", "dp", "tensor"),
            P("section", ("tensor", "dp")),
            P("section", ("tensor", "dp"), None),
            P("section", None, ("tensor", "dp")),
            P("section", None, ("tensor", "dp")),
            P(),
        ),
        check_vma=False,
    )
```

```python
import functools

import jax
import jax.numpy as jnp
from jax import lax
from jax.experimental import pallas as pl
from jax.experimental.pallas import tpu as pltpu
from jax.sharding import PartitionSpec as P

HEAD = 64
LANES = 128
MASKED = -1e30
eps_norm = 1e-05
AXES = ("section", "tensor", "dp")
low_type = jnp.bfloat16


class Layout:
    def __init__(self):
        self.sections = lax.axis_size("section")
        self.tensor = lax.axis_size("tensor")
        self.dp = lax.axis_size("dp")
        self.halves = self.tensor // 2
        self.chips = self.dp // 2
        self.size = self.tensor
        self.section = lax.axis_index("section")
        tensor, dp = lax.axis_index("tensor"), lax.axis_index("dp")
        self.group, self.part = tensor // self.halves, tensor % self.halves
        self.chip, self.core = dp // 2, dp % 2
        self.rank = self.core * self.halves + self.part
        self.home = self.group == self.core

    def move(self, value, target):
        pairs = []
        for s in range(self.sections):
            for t in range(self.tensor):
                for d in range(self.dp):
                    goal = target(s, t // self.halves, t % self.halves, d // 2, d % 2)
                    if goal is None:
                        continue
                    s2, g2, u2, x2, c2 = goal
                    here = (s * self.tensor + t) * self.dp + d
                    there = (s2 * self.tensor + g2 * self.halves + u2) * self.dp + x2 * 2 + c2
                    if here != there:
                        pairs.append((here, there))
        return lax.ppermute(value, AXES, pairs)

    def turn(self, value, step):
        def target(s, g, u, x, c):
            rank = (c * self.halves + u + step) % self.size
            return (s, g, rank % self.halves, x, rank // self.halves)

        return self.move(value, target)

    def group_sum(self, value):
        total = value.astype(jnp.float32)
        for step in range(1, self.size):
            total = total + self.turn(value, step).astype(jnp.float32)
        return total

    def group_gather(self, value):
        if self.size == 2:
            other = self.turn(value, 1)
            first = self.rank == 0
            return jnp.stack([jnp.where(first, value, other), jnp.where(first, other, value)])
        whole = jnp.zeros((self.size,) + value.shape, value.dtype)
        for step in range(self.size):
            piece = value if step == 0 else self.turn(value, step)
            whole = lax.dynamic_update_index_in_dim(
                whole, piece, (self.rank - step) % self.size, 0
            )
        return whole


def dot_rows(a, b):
    return lax.dot_general(a, b, (((1,), (1,)), ((), ())), preferred_element_type=jnp.float32)


def dot_plain(a, b):
    return lax.dot_general(a, b, (((1,), (0,)), ((), ())), preferred_element_type=jnp.float32)


def dot_first(a, b):
    return lax.dot_general(a, b, (((0,), (0,)), ((), ())), preferred_element_type=jnp.float32)


def tile_docs(starts_ref, length, count):
    place = lax.broadcasted_iota(jnp.int32, (length, LANES), 0)
    doc = jnp.zeros((length, LANES), jnp.int32)
    for j in range(count):
        doc = doc + (starts_ref[j] <= place).astype(jnp.int32)
    lane = lax.broadcasted_iota(jnp.int32, (length, LANES), 1)
    rel = lane % HEAD
    return lane < HEAD, rel, rel + 1 == doc


def three_parts(value):
    high = value.astype(low_type)
    rest = value - high.astype(jnp.float32)
    middle = rest.astype(low_type)
    return high, middle, (rest - middle.astype(jnp.float32)).astype(low_type)


def lanes(rel, count, value, base):
    high, middle, small = three_parts(value)
    return jnp.where(
        rel == count,
        high,
        jnp.where(rel == count + 1, middle, jnp.where(rel == count + 2, small, base)),
    )


def attend_kernel(starts_ref, q_ref, k_ref, v_ref, o_ref, l_ref, *, count, rows):
    length = q_ref.shape[0]
    first, rel, own = tile_docs(starts_ref, length, count)
    extra_k = jnp.where(own, 1.0, 0.0).astype(low_type)
    extra_q = jnp.where(
        jnp.logical_and(rel < count, jnp.logical_not(own)), MASKED, 0.0
    ).astype(low_type)
    q = q_ref[...] * low_type(HEAD**-0.5)
    k = k_ref[...]
    v = v_ref[...]
    ones = jnp.ones_like(v)
    heads = (
        (jnp.where(first, q, extra_q), jnp.where(first, k, extra_k), jnp.where(first, v, ones)),
        (jnp.where(first, extra_q, q), jnp.where(first, extra_k, k), jnp.where(first, ones, v)),
    )
    side = first[:rows]
    for start in range(0, length, rows):
        peaks, sums = [], []
        for q_head, k_head, v_head in heads:
            scores = dot_rows(q_head[start : start + rows], k_head)
            peak = jnp.max(scores, axis=-1, keepdims=True)
            powers = jnp.exp(scores - peak).astype(low_type)
            peaks.append(peak)
            sums.append(dot_plain(powers, v_head))
        mixed = jnp.where(side, sums[0], sums[1])
        totals = jnp.where(side, sums[1], sums[0])
        log_sums = jnp.where(side, peaks[1], peaks[0]) + jnp.log(totals)
        l_ref[start : start + rows] = lanes(
            rel[:rows], count, -log_sums, extra_q[start : start + rows]
        )
        o_ref[start : start + rows] = (mixed / pltpu.roll(totals, HEAD, 1)).astype(low_type)


def attend(qkv, starts):
    length, columns = qkv.shape[0], qkv.shape[1] // 3
    pairs = columns // LANES
    rows = min(512, length)

    def block(offset):
        return pl.BlockSpec((length, LANES), lambda j: (0, offset + j))

    return pl.pallas_call(
        functools.partial(attend_kernel, count=starts.shape[0], rows=rows),
        grid=(pairs,),
        in_specs=[
            pl.BlockSpec(memory_space=pltpu.SMEM),
            block(0),
            block(pairs),
            block(2 * pairs),
        ],
        out_specs=[block(0), block(0)],
        out_shape=[
            jax.ShapeDtypeStruct((length, columns), low_type),
            jax.ShapeDtypeStruct((length, columns), low_type),
        ],
        compiler_params=pltpu.CompilerParams(vmem_limit_bytes=48 * 1024 * 1024),
        cost_estimate=pl.CostEstimate(
            flops=16 * length * length * columns // 4,
            bytes_accessed=12 * length * columns,
            transcendentals=length * length * columns // HEAD,
        ),
        name="attend",
    )(starts, qkv, qkv, qkv)


def attend_back_kernel(
    starts_ref, q_ref, k_ref, v_ref, o_ref, l_ref, g_ref, dq_ref, dk_ref, dv_ref, *, count, rows
):
    length = q_ref.shape[0]
    first, rel, own = tile_docs(starts_ref, length, count)
    stat = jnp.logical_and(rel >= count, rel < count + 3)
    extra_k = jnp.where(jnp.logical_or(own, stat), 1.0, 0.0).astype(low_type)
    extra_v = jnp.where(stat, 1.0, 0.0).astype(low_type)
    extra_q = l_ref[...]
    g = g_ref[...]
    product = g.astype(jnp.float32) * o_ref[...].astype(jnp.float32)
    dots = [
        jnp.sum(jnp.where(first, product, 0.0), axis=-1, keepdims=True),
        jnp.sum(jnp.where(first, 0.0, product), axis=-1, keepdims=True),
    ]
    extra_g = lanes(rel, count, -jnp.where(first, dots[1], dots[0]), jnp.zeros_like(extra_q))
    q = q_ref[...] * low_type(HEAD**-0.5)
    k = k_ref[...]
    v = v_ref[...]
    heads = (
        tuple(
            jnp.where(first, a, b)
            for a, b in ((q, extra_q), (k, extra_k), (v, extra_v), (g, extra_g))
        ),
        tuple(
            jnp.where(first, b, a)
            for a, b in ((q, extra_q), (k, extra_k), (v, extra_v), (g, extra_g))
        ),
    )
    grad_k = [jnp.zeros((length, LANES), jnp.float32)] * 2
    grad_v = [jnp.zeros((length, LANES), jnp.float32)] * 2
    for start in range(0, length, rows):
        part = slice(start, start + rows)
        grad_q = []
        for i, (q_head, k_head, v_head, g_head) in enumerate(heads):
            probs = jnp.exp(dot_rows(k_head, q_head[part]))
            slopes = (probs * dot_rows(v_head, g_head[part])).astype(low_type)
            grad_v[i] = grad_v[i] + dot_plain(probs.astype(low_type), g[part])
            grad_k[i] = grad_k[i] + dot_plain(slopes, q[part])
            grad_q.append(dot_first(slopes, k))
        dq_ref[part] = (
            jnp.where(first[:rows], grad_q[0], grad_q[1]) * (HEAD**-0.5)
        ).astype(low_type)
    dk_ref[...] = jnp.where(first, grad_k[0], grad_k[1]).astype(low_type)
    dv_ref[...] = jnp.where(first, grad_v[0], grad_v[1]).astype(low_type)


def attend_back(qkv, starts, mixed, log_sums, grad_mixed):
    length, columns = mixed.shape
    pairs = columns // LANES
    rows = min(256, length)

    def block(offset):
        return pl.BlockSpec((length, LANES), lambda j: (0, offset + j))

    return pl.pallas_call(
        functools.partial(attend_back_kernel, count=starts.shape[0], rows=rows),
        grid=(pairs,),
        in_specs=[
            pl.BlockSpec(memory_space=pltpu.SMEM),
            block(0),
            block(pairs),
            block(2 * pairs),
            block(0),
            block(0),
            block(0),
        ],
        out_specs=[block(0)] * 3,
        out_shape=[jax.ShapeDtypeStruct((length, columns), low_type)] * 3,
        compiler_params=pltpu.CompilerParams(vmem_limit_bytes=48 * 1024 * 1024),
        cost_estimate=pl.CostEstimate(
            flops=40 * length * length * columns // 4,
            bytes_accessed=20 * length * columns,
            transcendentals=length * length * columns // HEAD,
        ),
        name="attend_back",
    )(starts, qkv, qkv, qkv, mixed, log_sums, grad_mixed)


MESH = pl.DeviceIdType.MESH


def rows_of(index, size):
    return pl.ds(pl.multiple_of(index * size, size), size)


def erf_pair(pre):
    bell = jnp.exp(-0.5 * pre * pre)
    size = jnp.abs(pre)
    t = 1.0 / (1.0 + 0.2316418882663604 * size)
    tail = bell * t * (
        0.127414796
        + t * (-0.142248368 + t * (0.7107068705 + t * (-0.7265760135 + t * 0.5307027145)))
    )
    return jnp.where(pre < 0.0, tail, 1.0 - tail), bell * 0.3989422804014327


def norm_rows(value):
    average = jnp.mean(value, axis=-1, keepdims=True)
    centered = value - average
    inv_scale = lax.rsqrt(jnp.mean(centered * centered, axis=-1, keepdims=True) + eps_norm)
    return centered * inv_scale, inv_scale


def doc_lanes(starts_ref, row, first_row, shape, count):
    place = lax.broadcasted_iota(jnp.int32, shape, 0) + first_row
    doc = jnp.zeros(shape, jnp.int32)
    for j in range(count):
        doc = doc + (starts_ref[row, j] <= place).astype(jnp.int32)
    lane = lax.broadcasted_iota(jnp.int32, shape, 1)
    rel = lane % HEAD
    return lane < HEAD, rel, rel + 1 == doc


def forward_kernel(
    sections,
    chunk,
    starts_ref,
    bias_in,
    gains,
    biases,
    tokens_in,
    cotangent_in,
    qkv_w,
    out_w,
    in_w,
    down_w,
    qkv_out,
    stat_out,
    mixed_out,
    middle_out,
    hidden_out,
    slope_out,
    inputs_out,
    result_out,
    scale_out,
    placed_out,
    back_out,
    wq_out,
    wo_out,
    wi_out,
    wd_out,
    wq,
    wo,
    wi,
    wd,
    bias,
    hbuf,
    qkv,
    keys,
    values,
    mixed,
    stat,
    send_a,
    send_b,
    got_a,
    got_b,
    high_mid,
    low_mid,
    hidden,
    slope,
    result,
    scale_a,
    scale_z,
    w_sem,
    y_send,
    y_got,
    x_send,
    x_got,
    bias_sem,
    token_local,
    token_send,
    token_got,
    cot_local,
    cot_send,
    cot_got,
    hop_send,
    hop_got,
    pass_send,
    pass_got,
    keep_sem,
    qkv_sem,
    a_send,
    a_got,
    b_send,
    b_got,
    first_sem,
    second_sem,
    third_sem,
    scale_sem,
    out_local,
    out_send,
    out_got,
):
    at = Seat()
    section, core, peer = at.section, at.core, at.peer
    last = sections - 1
    micro, length, width = hbuf.shape
    count = starts_ref.shape[1]
    columns = mixed.shape[1]
    pairs = columns // LANES
    chunks = length // chunk
    half = chunk // 2
    shape = (chunk, LANES)
    given, held = (qkv_w, out_w, in_w, down_w), (wq, wo, wi, wd)
    own_weights = [
        pltpu.make_async_copy(source, target, w_sem.at[i])
        for i, (source, target) in enumerate(zip(given, held))
    ]
    pieces = weight_pieces(*held)

    def swap(k):
        index, where = pieces[k]
        return remote(
            where(given[index], at.chip),
            where(held[index], at.chip),
            y_send.at[k],
            y_got.at[k],
            at.swap,
        )

    def relay(k):
        index, where = pieces[k]
        part = where(held[index], at.chip)
        return remote(part, part, x_send.at[k], x_got.at[k], at.beside)

    def pieces_of(*indices):
        return [k for k, (index, _) in enumerate(pieces) if index in indices]

    def pass_on(group):
        for k in group:
            swap(k).wait_recv()
            relay(k).start()

    def ready(index):
        @pl.when(at.home)
        def _():
            own_weights[index].wait()

        @pl.when(at.away)
        def _():
            for k in pieces_of(index):
                relay(k).wait_recv()

    def swap_bias():
        return remote(bias_in, bias, bias_sem.at[0], bias_sem.at[1], at.swap)

    tokens = RowPieces(at, tokens_in, hbuf, token_local, token_send, token_got)
    cotangents = RowPieces(at, cotangent_in, back_out, cot_local, cot_send, cot_got)
    placed = OutPieces(at, result, placed_out, out_local, out_send, out_got)

    @pl.when(at.home)
    def _():
        for copy in own_weights:
            copy.start()
        bias[...] = bias_in[...]

    greet(section, sections, (at.peer, at.across, at.swap, at.beside))

    @pl.when(section == 0)
    def _():
        tokens.own.start()
        tokens.to_peer.start()

        @pl.when(core == 0)
        def _():
            tokens.to_across.start()

    @pl.when(at.away)
    def _():
        swap_bias().start()
        for k in pieces_of(0, 1):
            swap(k).start()

    @pl.when(jnp.logical_and(section == 0, core > 0))
    def _():
        tokens.to_across.start()

    @pl.when(at.away)
    def _():
        for k in pieces_of(2, 3):
            swap(k).start()
        swap_bias().wait()
        pass_on(pieces_of(0))

        @pl.when(section > 0)
        def _():
            pass_on(pieces_of(1, 2, 3))

    @pl.when(section == last)
    def _():
        cotangents.own.start()
        cotangents.to_peer.start()
        cotangents.to_across.start()
        cotangents.to_across.wait()
        cotangents.forward.start()
        cotangents.own.wait()
        cotangents.to_peer.wait()
        cotangents.forward.wait()

    def hop(m, j):
        rows = pl.ds(pl.multiple_of(core * half, half), half)
        target = pl.ds(pl.multiple_of(j * chunk + core * half, half), half)
        return pltpu.make_async_remote_copy(
            src_ref=result.at[j, rows],
            dst_ref=hbuf.at[m, target],
            send_sem=hop_send.at[j],
            recv_sem=hop_got.at[m, j],
            device_id={"section": section + 1},
            device_id_type=MESH,
        )

    def hand_over(m, j):
        rows = pl.ds(pl.multiple_of(j * chunk + core * half, half), half)
        return pltpu.make_async_remote_copy(
            src_ref=hbuf.at[m, rows],
            dst_ref=hbuf.at[m, rows],
            send_sem=pass_send.at[m, j],
            recv_sem=pass_got.at[m, j],
            device_id=peer,
            device_id_type=MESH,
        )

    def exchange_a(m, j):
        slot = j
        return pltpu.make_async_remote_copy(
            src_ref=send_a.at[slot],
            dst_ref=got_a.at[j],
            send_sem=a_send.at[slot],
            recv_sem=a_got.at[m, j],
            device_id=peer,
            device_id_type=MESH,
        )

    def exchange_b(m, j):
        slot = lax.rem(j, 2)
        return pltpu.make_async_remote_copy(
            src_ref=send_b.at[slot],
            dst_ref=got_b.at[j],
            send_sem=b_send.at[slot],
            recv_sem=b_got.at[m, j],
            device_id=peer,
            device_id_type=MESH,
        )

    def keep(m, j):
        rows = rows_of(j, chunk)
        return pltpu.make_async_copy(
            hbuf.at[m, rows], inputs_out.at[m, rows], keep_sem.at[m, j]
        )

    def keep_qkv(m, j):
        rows = rows_of(j, chunk)
        return pltpu.make_async_copy(qkv.at[rows], qkv_out.at[m, rows], qkv_sem.at[j])

    def keep_first(m, j):
        rows = rows_of(j, chunk)
        return [
            pltpu.make_async_copy(mixed, mixed_out.at[m, rows], first_sem.at[0]),
            pltpu.make_async_copy(stat, stat_out.at[m, rows], first_sem.at[1]),
        ]

    def keep_second(m, j):
        rows = rows_of(j, chunk)
        return [
            pltpu.make_async_copy(low_mid, middle_out.at[m, rows], second_sem.at[0]),
            pltpu.make_async_copy(hidden, hidden_out.at[m, rows], second_sem.at[1]),
            pltpu.make_async_copy(slope, slope_out.at[m, rows], second_sem.at[2]),
            pltpu.make_async_copy(scale_a, scale_out.at[m, 0, rows], second_sem.at[3]),
        ]

    def keep_third(m, j):
        rows = rows_of(j, chunk)
        return [
            pltpu.make_async_copy(result.at[j], result_out.at[m, rows], third_sem.at[j]),
            pltpu.make_async_copy(scale_z.at[j], scale_out.at[m, 1, rows], scale_sem.at[j]),
        ]

    def project(m, j):
        rows = rows_of(j, chunk)

        @pl.when(section > 0)
        def _():
            hop(m, j).wait_recv()
            hand_over(m, j).start()
            hand_over(m, j).wait_recv()

        keep(m, j).start()

        @pl.when(m > 0)
        def _():
            keep_qkv(m - 1, j).wait()

        for third in range(3):
            part = slice(third * columns, (third + 1) * columns)
            qkv[rows, part] = (dot_plain(hbuf[m, rows], wq[third]) + bias[:, part]).astype(low_type)
        keep_qkv(m, j).start()
        first, rel, own = doc_lanes(starts_ref, m, j * chunk, shape, count)
        extra = jnp.where(own, 1.0, 0.0).astype(low_type)
        ones = jnp.ones(shape, low_type)
        for p in range(pairs):
            k = qkv[rows, columns + p * LANES : columns + (p + 1) * LANES]
            v = qkv[rows, 2 * columns + p * LANES : 2 * columns + (p + 1) * LANES]
            keys[2 * p, rows] = jnp.where(first, k, extra)
            keys[2 * p + 1, rows] = jnp.where(first, extra, k)
            values[2 * p, rows] = jnp.where(first, v, ones)
            values[2 * p + 1, rows] = jnp.where(first, ones, v)

    def mix(m, j):
        rows = rows_of(j, chunk)
        first, rel, own = doc_lanes(starts_ref, m, j * chunk, shape, count)
        extra = jnp.where(
            jnp.logical_and(rel < count, jnp.logical_not(own)), MASKED, 0.0
        ).astype(low_type)

        def scores(index):
            p = index // 2
            q = qkv[rows, p * LANES : (p + 1) * LANES] * low_type(HEAD**-0.5)
            q = jnp.where(first, q, extra) if index % 2 == 0 else jnp.where(first, extra, q)
            return dot_rows(q, keys[index])

        current = scores(0)
        peaks, sums = [], []
        for index in range(2 * pairs):
            later = scores(index + 1) if index + 1 < 2 * pairs else None
            peak = jnp.max(current, axis=-1, keepdims=True)
            powers = jnp.exp(current - peak).astype(low_type)
            peaks.append(peak)
            sums.append(dot_plain(powers, values[index]))
            current = later
            if index % 2 == 1:
                lane = slice((index // 2) * LANES, (index // 2 + 1) * LANES)
                total = jnp.where(first, sums[index], sums[index - 1])
                log_sum = jnp.where(first, peaks[index], peaks[index - 1]) + jnp.log(total)
                stat[:, lane] = lanes(rel, count, -log_sum, extra)
                mixed[:, lane] = (
                    jnp.where(first, sums[index - 1], sums[index]) / pltpu.roll(total, HEAD, 1)
                ).astype(low_type)
        for copy in keep_first(m, j):
            copy.start()
        send_a[j] = dot_plain(mixed[...], wo[...]).astype(low_type)
        exchange_a(m, j).start()

    def feed(m, j):
        rows = rows_of(j, chunk)
        slot = lax.rem(j, 2)
        exchange_a(m, j).wait()
        total = (
            send_a[j].astype(jnp.float32)
            + got_a[j].astype(jnp.float32)
            + biases[0:1]
            + hbuf[m, rows].astype(jnp.float32)
        )
        unit, inv_scale = norm_rows(total)
        scale_a[...] = jnp.broadcast_to(inv_scale, shape)
        middle = unit * gains[0:1] + biases[1:2]
        high_mid[slot] = middle
        low_mid[...] = middle.astype(low_type)
        hidden_size = wi.shape[1]
        step = min(512, hidden_size)

        def before(start):
            part = slice(start, start + step)
            return dot_plain(low_mid[...], wi[:, part]) + bias[:, 3 * columns + start : 3 * columns + start + step]

        pre = before(0)
        branch = jnp.zeros((chunk, width), jnp.float32)
        for start in range(0, hidden_size, step):
            part = slice(start, start + step)
            later = before(start + step) if start + step < hidden_size else None
            normal, density = erf_pair(pre)
            hidden[:, part] = (pre * normal).astype(low_type)
            slope[:, part] = (normal + pre * density).astype(low_type)
            branch = branch + dot_plain(hidden[:, part], wd[part])
            pre = later
        send_b[slot] = branch.astype(low_type)
        exchange_b(m, j).start()
        for copy in keep_second(m, j):
            copy.start()

    def finish(m, j):
        slot = lax.rem(j, 2)
        exchange_b(m, j).wait()
        total = (
            send_b[slot].astype(jnp.float32)
            + got_b[j].astype(jnp.float32)
            + biases[2:3]
            + high_mid[slot]
        )
        unit, inv_scale = norm_rows(total)
        @pl.when(m > 0)
        def _():
            finish_wait(m - 1, j)

        scale_z[j] = jnp.broadcast_to(inv_scale, shape)
        result[j] = (unit * gains[1:2] + biases[3:4]).astype(low_type)

        @pl.when(section < sections - 1)
        def _():
            hop(m, j).start()

        placed.start(m, j)
        for copy in keep_third(m, j):
            copy.start()

    def finish_wait(m, j):
        for copy in keep_third(m, j):
            copy.wait()

        placed.wait(m, j)

        @pl.when(section < sections - 1)
        def _():
            hop(m, j).wait_send()

    def one_row(m, carry):
        @pl.when(jnp.logical_and(section == 0, core == m))
        def _():
            tokens.own.wait()
            tokens.to_across.wait_recv()
            tokens.forward.start()

        @pl.when(jnp.logical_and(section == 0, core != m))
        def _():
            tokens.to_peer.wait_recv()
            tokens.forward.wait_recv()

        @pl.when(m == 0)
        def _():
            ready(0)

        def first_step(j, carry):
            project(m, j)
            return carry

        lax.fori_loop(0, chunks, first_step, 0)

        @pl.when(m == 0)
        def _():
            @pl.when(jnp.logical_and(section == 0, at.away))
            def _():
                pass_on(pieces_of(1))

            ready(1)

        lag = jnp.where(jnp.logical_and(section == 0, m == 0), chunks, 1)

        def step(i, carry):
            j = i - lag

            @pl.when(jnp.logical_and(i >= 1, i <= chunks))
            def _():
                for copy in keep_first(m, i - 1):
                    copy.wait()

            @pl.when(i < chunks)
            def _():
                mix(m, i)

            @pl.when(jnp.logical_and(section == 0, at.away))
            def _():
                share = len(pieces_of(2, 3)) // 4
                for turn in range(4):

                    @pl.when(jnp.logical_and(m == 0, i == turn))
                    def _():
                        pass_on(pieces_of(2, 3)[turn * share : (turn + 1) * share])

            @pl.when(jnp.logical_and(m == 0, j == 0))
            def _():
                ready(2)
                ready(3)

            @pl.when(jnp.logical_and(j >= 1, j <= chunks))
            def _():
                for copy in keep_second(m, j - 1):
                    copy.wait()

            @pl.when(jnp.logical_and(j >= 0, j < chunks))
            def _():
                feed(m, j)

            @pl.when(j >= 1)
            def _():
                finish(m, j - 1)

            return carry

        lax.fori_loop(0, chunks + lag + 1, step, 0)

        @pl.when(m == 0)
        def _():
            for copy in keep_weights:
                copy.start()

        return carry

    keep_weights = [
        pltpu.make_async_copy(source, target, w_sem.at[i])
        for i, (source, target) in enumerate(zip(held, (wq_out, wo_out, wi_out, wd_out)))
    ]
    lax.fori_loop(0, micro, one_row, 0)
    for copy in keep_weights:
        copy.wait()
    for j in range(chunks):
        finish_wait(micro - 1, j)
        keep_qkv(micro - 1, j).wait()
    for m in range(micro):
        for j in range(chunks):
            keep(m, j).wait()
    placed.wait_got()

    @pl.when(at.away)
    def _():
        for k in range(len(pieces)):
            swap(k).wait_send()
            relay(k).wait_send()

    @pl.when(section == 0)
    def _():
        tokens.to_peer.wait_send()
        tokens.to_across.wait_send()
        tokens.forward.wait_send()

    @pl.when(section > 0)
    def _():
        for m in range(micro):
            for j in range(chunks):
                hand_over(m, j).wait_send()


def forward_pass(sections, starts, bias, gains, biases, tokens, cotangent, weights):
    wq, wo, wi, wd = weights
    micro, tile, width = tokens.shape
    length = 2 * tile
    columns, hidden = wo.shape[0], wi.shape[1]
    chunk = min(256, length // 4)
    chunks = length // chunk
    low, high = low_type, jnp.float32

    def out(*shape, dtype=low):
        return jax.ShapeDtypeStruct(shape, dtype)

    outs = dict(
        qkv=out(micro, length, 3 * columns),
        log_sums=out(micro, length, columns),
        mixed=out(micro, length, columns),
        middle=out(micro, length, width),
        hidden=out(micro, length, hidden),
        slope=out(micro, length, hidden),
        inputs=out(micro, length, width),
        result=out(micro, length, width),
        scales=out(micro, 2, length, LANES, dtype=high),
        placed=out(*tokens.shape),
        rows_back=out(micro, length, width),
        wq=out(*wq.shape),
        wo=out(*wo.shape),
        wi=out(*wi.shape),
        wd=out(*wd.shape),
    )
    vmem = pl.BlockSpec(memory_space=pltpu.VMEM)
    anywhere = pl.BlockSpec(memory_space=pl.ANY)
    dma = pltpu.SemaphoreType.DMA
    pieces = len(weight_pieces(*weights))
    results = pl.pallas_call(
        functools.partial(forward_kernel, sections, chunk),
        in_specs=[pl.BlockSpec(memory_space=pltpu.SMEM)] + [vmem] * 3 + [anywhere] * 6,
        out_specs=[anywhere] * len(outs),
        out_shape=list(outs.values()),
        scratch_shapes=[
            pltpu.VMEM(wq.shape, low),
            pltpu.VMEM(wo.shape, low),
            pltpu.VMEM(wi.shape, low),
            pltpu.VMEM(wd.shape, low),
            pltpu.VMEM(bias.shape, high),
            pltpu.VMEM((micro, length, width), low),
            pltpu.VMEM((length, 3 * columns), low),
            pltpu.VMEM((columns // HEAD, length, LANES), low),
            pltpu.VMEM((columns // HEAD, length, LANES), low),
            pltpu.VMEM((chunk, columns), low),
            pltpu.VMEM((chunk, columns), low),
            pltpu.VMEM((chunks, chunk, width), low),
            pltpu.VMEM((2, chunk, width), low),
            pltpu.VMEM((chunks, chunk, width), low),
            pltpu.VMEM((chunks, chunk, width), low),
            pltpu.VMEM((2, chunk, width), high),
            pltpu.VMEM((chunk, width), low),
            pltpu.VMEM((chunk, hidden), low),
            pltpu.VMEM((chunk, hidden), low),
            pltpu.VMEM((chunks, chunk, width), low),
            pltpu.VMEM((chunk, LANES), high),
            pltpu.VMEM((chunks, chunk, LANES), high),
            dma((4,)),
            dma((pieces,)),
            dma((pieces,)),
            dma((pieces,)),
            dma((pieces,)),
            dma((2,)),
            dma,
            dma((3,)),
            dma((3,)),
            dma,
            dma((3,)),
            dma((3,)),
            dma((chunks,)),
            dma((micro, chunks)),
            dma((micro, chunks)),
            dma((micro, chunks)),
            dma((micro, chunks)),
            dma((chunks,)),
            dma((chunks,)),
            dma((micro, chunks)),
            dma((2,)),
            dma((micro, chunks)),
            dma((2,)),
            dma((4,)),
            dma((chunks,)),
            dma((chunks,)),
            dma((chunks,)),
            dma((chunks,)),
            dma((chunks // 2,)),
        ],
        compiler_params=pltpu.CompilerParams(
            collective_id=0, has_side_effects=True, vmem_limit_bytes=62 * 1024 * 1024
        ),
        name="forward_pass",
    )(starts, bias, gains, biases, tokens, cotangent, *weights)
    return dict(zip(outs, results))


def greet(section, sections, partners):
    barrier = pltpu.get_barrier_semaphore()
    for partner in partners:
        pl.semaphore_signal(barrier, inc=1, device_id=partner, device_id_type=MESH)

    @pl.when(section > 0)
    def _():
        pl.semaphore_signal(
            barrier, inc=1, device_id={"section": section - 1}, device_id_type=MESH
        )

    @pl.when(section < sections - 1)
    def _():
        pl.semaphore_signal(
            barrier, inc=1, device_id={"section": section + 1}, device_id_type=MESH
        )

    inner = jnp.logical_and(section > 0, section < sections - 1)

    @pl.when(inner)
    def _():
        pl.semaphore_wait(barrier, len(partners) + 2)

    @pl.when(jnp.logical_not(inner))
    def _():
        pl.semaphore_wait(barrier, len(partners) + 1)


class Seat:
    def __init__(self):
        self.section = lax.axis_index("section")
        self.group = lax.axis_index("tensor")
        dp = lax.axis_index("dp")
        self.core = lax.rem(dp, 2)
        self.chip = dp // 2
        other = dp + 1 - 2 * self.core
        self.peer = {"dp": other}
        self.across = {"tensor": 1 - self.group}
        self.swap = {"tensor": 1 - self.group, "dp": other}
        self.beside = {"dp": dp + 2 - 4 * self.chip}
        self.home = self.group == self.core
        self.away = self.group != self.core


def remote(source, target, send_sem, recv_sem, device):
    return pltpu.make_async_remote_copy(
        src_ref=source,
        dst_ref=target,
        send_sem=send_sem,
        recv_sem=recv_sem,
        device_id=device,
        device_id_type=MESH,
    )


class RowPieces:
    def __init__(self, at, source, target, local, send, got):
        tile = source.shape[1]

        def half(group):
            return pl.ds(pl.multiple_of(group * tile, tile), tile)

        own = target.at[at.core, half(at.group)]
        other = target.at[at.core, half(1 - at.group)]
        mine = source.at[at.group]
        self.own = pltpu.make_async_copy(mine, own, local)
        self.to_peer = remote(mine, own, send.at[0], got.at[0], at.peer)
        self.to_across = remote(source.at[1 - at.group], own, send.at[1], got.at[1], at.across)
        self.forward = remote(other, other, send.at[2], got.at[2], at.peer)


class OutPieces:
    def __init__(self, at, rows, target, local, send, got):
        self.at, self.rows, self.target = at, rows, target
        self.local, self.send, self.got = local, send, got
        self.chunks, self.chunk = rows.shape[0], rows.shape[1]
        self.per = self.chunks // 2

    def copies(self, m, j):
        place = rows_of(lax.rem(j, self.per), self.chunk)
        spot = self.target.at[self.at.group, place]
        near = pltpu.make_async_copy(self.rows.at[j], spot, self.local.at[j])
        far = remote(
            self.rows.at[j],
            spot,
            self.send.at[j],
            self.got.at[lax.rem(j, self.per)],
            self.at.across,
        )
        mine = self.at.core == m
        stays = j // self.per == self.at.group
        return (
            (jnp.logical_and(mine, stays), near, near.wait),
            (jnp.logical_and(mine, jnp.logical_not(stays)), far, far.wait_send),
        )

    def start(self, m, j):
        for condition, copy, _ in self.copies(m, j):
            pl.when(condition)(copy.start)

    def wait(self, m, j):
        for condition, _, wait in self.copies(m, j):
            pl.when(condition)(wait)

    def wait_got(self):
        for j in range(self.per):
            remote(
                self.rows.at[j],
                self.target.at[1 - self.at.group, pl.ds(j * self.chunk, self.chunk)],
                self.send.at[j],
                self.got.at[j],
                self.at.across,
            ).wait_recv()


def weight_pieces(wq, wo, wi, wd):
    pieces = []

    def split(index, rows, count, lead=()):
        size = rows // 2 // count
        for i in range(count):

            def where(ref, chip, i=i):
                start = pl.multiple_of(chip * (rows // 2) + i * size, size)
                return ref.at[lead + (pl.ds(start, size),)]

            pieces.append((index, where))

    for k in range(wq.shape[0]):
        split(0, wq.shape[1], 1, (k,))
    split(1, wo.shape[0], 1)
    split(2, wi.shape[0], 4)
    split(3, wd.shape[0], 4)
    return pieces


def backward_kernel(
    sections,
    chunk,
    starts_ref,
    gains,
    biases,
    rows_back,
    qkv_w,
    out_w,
    in_w,
    down_w,
    qkv_in,
    stat_in,
    mixed_in,
    middle_in,
    slope_in,
    result_in,
    scale_in,
    row_sums,
    in_sums,
    qkv_sums,
    time_sums,
    gz_out,
    pre_out,
    ga_out,
    gqkv_out,
    grads_out,
    wq,
    wo,
    wi,
    wd,
    gbuf,
    high_ga,
    qkv,
    keys,
    values,
    grad_k,
    grad_v,
    grad_qkv,
    send_a,
    send_b,
    got_a,
    got_b,
    high_gz,
    low_gz,
    low_pre,
    low_ga,
    grad_mixed,
    grads,
    result,
    slope,
    scale_z,
    middle,
    scale_a,
    mixed,
    stat,
    w_sem,
    load_sem,
    hop_send,
    hop_got,
    pass_send,
    pass_got,
    a_send,
    a_got,
    b_send,
    b_got,
    qkv_sem,
    first_sem,
    second_sem,
    keep_sem,
    keep_ga_sem,
    keep_qkv_sem,
    grads_sem,
    out_send,
    out_got,
):
    at = Seat()
    section, core, peer = at.section, at.core, at.peer
    micro, length, width = gbuf.shape
    count = starts_ref.shape[1]
    columns = grad_mixed.shape[1]
    pairs = columns // LANES
    chunks = length // chunk
    half = chunk // 2
    last = sections - 1
    shape = (chunk, LANES)

    weights = [
        pltpu.make_async_copy(source, target, w_sem.at[i])
        for i, (source, target) in enumerate(
            ((down_w, wd), (in_w, wi), (out_w, wo), (qkv_w, wq))
        )
    ]
    for copy in weights:
        copy.start()

    def load(m, j):
        rows = rows_of(j, chunk)
        return pltpu.make_async_copy(
            rows_back.at[m, rows], gbuf.at[m, rows], load_sem.at[m, j]
        )

    def hop(m, j):
        target = pl.ds(pl.multiple_of(j * chunk + core * half, half), half)
        return pltpu.make_async_remote_copy(
            src_ref=grads.at[j, pl.ds(pl.multiple_of(core * half, half), half)],
            dst_ref=gbuf.at[m, target],
            send_sem=hop_send.at[j],
            recv_sem=hop_got.at[m, j],
            device_id={"section": section - 1},
            device_id_type=MESH,
        )

    def hand_over(m, j):
        rows = pl.ds(pl.multiple_of(j * chunk + core * half, half), half)
        return pltpu.make_async_remote_copy(
            src_ref=gbuf.at[m, rows],
            dst_ref=gbuf.at[m, rows],
            send_sem=pass_send.at[m, j],
            recv_sem=pass_got.at[m, j],
            device_id=peer,
            device_id_type=MESH,
        )

    def exchange(send, got, send_sem, got_sem, m, j):
        slot = lax.rem(j, 2)
        return pltpu.make_async_remote_copy(
            src_ref=send.at[slot],
            dst_ref=got.at[j],
            send_sem=send_sem.at[slot],
            recv_sem=got_sem.at[m, j],
            device_id=peer,
            device_id_type=MESH,
        )

    def exchange_a(m, j):
        return exchange(send_a, got_a, a_send, a_got, m, j)

    def exchange_b(m, j):
        return exchange(send_b, got_b, b_send, b_got, m, j)

    def load_qkv(m):
        return pltpu.make_async_copy(qkv_in.at[m], qkv, qkv_sem)

    def load_first(m, j):
        rows = rows_of(j, chunk)
        return [
            pltpu.make_async_copy(result_in.at[m, rows], result, first_sem.at[0]),
            pltpu.make_async_copy(slope_in.at[m, rows], slope, first_sem.at[1]),
            pltpu.make_async_copy(scale_in.at[m, 1, rows], scale_z, first_sem.at[2]),
        ]

    def load_second(m, j):
        rows = rows_of(j, chunk)
        return [
            pltpu.make_async_copy(middle_in.at[m, rows], middle, second_sem.at[0]),
            pltpu.make_async_copy(scale_in.at[m, 0, rows], scale_a, second_sem.at[1]),
            pltpu.make_async_copy(mixed_in.at[m, rows], mixed, second_sem.at[2]),
            pltpu.make_async_copy(stat_in.at[m, rows], stat, second_sem.at[3]),
        ]

    def keep_first(m, j):
        rows = rows_of(j, chunk)
        return [
            pltpu.make_async_copy(low_gz, gz_out.at[m, rows], keep_sem.at[0]),
            pltpu.make_async_copy(low_pre, pre_out.at[m, rows], keep_sem.at[1]),
        ]

    def keep_second(m, j):
        rows = rows_of(j, chunk)
        return pltpu.make_async_copy(low_ga, ga_out.at[m, rows], keep_ga_sem)

    def keep_qkv(m):
        return pltpu.make_async_copy(grad_qkv, gqkv_out.at[m], keep_qkv_sem)

    placed = OutPieces(at, grads, grads_out, grads_sem, out_send, out_got)

    load_qkv(0).start()
    for copy in load_first(0, 0) + load_second(0, 0):
        copy.start()

    @pl.when(section == last)
    def _():
        for m in range(micro):
            for j in range(chunks):
                load(m, j).start()

    row_sums[...] = jnp.zeros_like(row_sums)
    in_sums[...] = jnp.zeros_like(in_sums)
    qkv_sums[...] = jnp.zeros_like(qkv_sums)
    time_sums[...] = jnp.zeros_like(time_sums)
    greet(section, sections, (at.peer, at.across))

    def add_row(index, value):
        row_sums[index : index + 1] += jnp.sum(value, axis=0, keepdims=True)

    def receive(m, j):
        @pl.when(section < last)
        def _():
            hop(m, j).wait_recv()
            hand_over(m, j).start()

    def norm_back_rows(gradient, unit, inv_scale, gain):
        weighted = gradient * gain
        return inv_scale * (
            weighted
            - jnp.mean(weighted, axis=-1, keepdims=True)
            - unit * jnp.mean(weighted * unit, axis=-1, keepdims=True)
        )

    def feed_back(m, j):
        rows = rows_of(j, chunk)
        slot = lax.rem(j, 2)

        @pl.when(section == last)
        def _():
            load(m, j).wait()

        @pl.when(section < last)
        def _():
            hand_over(m, j).wait_recv()

        for copy in load_first(m, j):
            copy.wait()
        gradient = gbuf[m, rows].astype(jnp.float32)
        unit = (result[...].astype(jnp.float32) - biases[3:4]) / gains[1:2]
        grad_z = norm_back_rows(gradient, unit, scale_z[:, :1], gains[1:2])
        add_row(1, gradient * unit)
        add_row(5, gradient)
        add_row(4, grad_z)
        high_gz[slot] = grad_z
        low_gz[...] = grad_z.astype(low_type)
        hidden_size = wi.shape[1]
        step = min(512, hidden_size)

        def before(start):
            return dot_rows(low_gz[...], wd[start : start + step])

        current = before(0)
        branch = jnp.zeros((chunk, width), jnp.float32)
        for start in range(0, hidden_size, step):
            part = slice(start, start + step)
            later = before(start + step) if start + step < hidden_size else None
            low = (current * slope[:, part].astype(jnp.float32)).astype(low_type)
            low_pre[:, part] = low
            in_sums[:, part] += jnp.sum(low.astype(jnp.float32), axis=0, keepdims=True)
            branch = branch + dot_rows(low, wi[:, part])
            current = later
        send_a[slot] = branch.astype(low_type)
        exchange_a(m, j).start()
        for copy in keep_first(m, j):
            copy.start()

    def norm_step(m, j):
        rows = rows_of(j, chunk)
        slot = lax.rem(j, 2)
        exchange_a(m, j).wait()
        for copy in load_second(m, j):
            copy.wait()
        gradient = (
            send_a[slot].astype(jnp.float32) + got_a[j].astype(jnp.float32) + high_gz[slot]
        )
        unit = (middle[...].astype(jnp.float32) - biases[1:2]) / gains[0:1]
        grad_a = norm_back_rows(gradient, unit, scale_a[:, :1], gains[0:1])
        add_row(0, gradient * unit)
        add_row(3, gradient)
        add_row(2, grad_a)
        high_ga[rows] = grad_a
        low_ga[...] = grad_a.astype(low_type)
        keep_second(m, j).start()
        grad_mixed[...] = dot_rows(low_ga[...], wo[...]).astype(low_type)

    def build(m):
        load_qkv(m).wait()

        def step(j, carry):
            rows = rows_of(j, chunk)
            first, rel, own = doc_lanes(starts_ref, m, j * chunk, shape, count)
            fixed = jnp.logical_and(rel >= count, rel < count + 3)
            extra_k = jnp.where(jnp.logical_or(own, fixed), 1.0, 0.0).astype(low_type)
            extra_v = jnp.where(fixed, 1.0, 0.0).astype(low_type)
            for p in range(pairs):
                lane = slice(p * LANES, (p + 1) * LANES)
                k = qkv[rows, columns + p * LANES : columns + (p + 1) * LANES]
                v = qkv[rows, 2 * columns + p * LANES : 2 * columns + (p + 1) * LANES]
                keys[2 * p, rows] = jnp.where(first, k, extra_k)
                keys[2 * p + 1, rows] = jnp.where(first, extra_k, k)
                values[2 * p, rows] = jnp.where(first, v, extra_v)
                values[2 * p + 1, rows] = jnp.where(first, extra_v, v)
                grad_k[rows, lane] = jnp.zeros(shape, jnp.float32)
                grad_v[rows, lane] = jnp.zeros(shape, jnp.float32)
            return carry

        lax.fori_loop(0, chunks, step, 0)

    def mix_back(m, j):
        rows = rows_of(j, chunk)
        lane_index = lax.broadcasted_iota(jnp.int32, shape, 1)
        first = lane_index < HEAD
        rel = lane_index % HEAD
        all_first = lax.broadcasted_iota(jnp.int32, (length, LANES), 1) < HEAD
        for p in range(pairs):
            lane = slice(p * LANES, (p + 1) * LANES)
            q = qkv[rows, lane] * low_type(HEAD**-0.5)
            k = qkv[:, columns + p * LANES : columns + (p + 1) * LANES]
            g = grad_mixed[:, lane]
            extra_q = stat[:, lane]
            product = g.astype(jnp.float32) * mixed[:, lane].astype(jnp.float32)
            dots = [
                jnp.sum(jnp.where(first, product, 0.0), axis=-1, keepdims=True),
                jnp.sum(jnp.where(first, 0.0, product), axis=-1, keepdims=True),
            ]
            extra_g = lanes(
                rel, count, -jnp.where(first, dots[1], dots[0]), jnp.zeros_like(extra_q)
            )
            parts = []
            for i in range(2):
                q_head = jnp.where(first, q, extra_q) if i == 0 else jnp.where(first, extra_q, q)
                g_head = jnp.where(first, g, extra_g) if i == 0 else jnp.where(first, extra_g, g)
                probs = jnp.exp(dot_rows(keys[2 * p + i], q_head))
                slopes = (probs * dot_rows(values[2 * p + i], g_head)).astype(low_type)
                parts.append(
                    (
                        dot_plain(probs.astype(low_type), g),
                        dot_plain(slopes, q),
                        dot_first(slopes, k),
                    )
                )
            grad_v[:, lane] += jnp.where(all_first, parts[0][0], parts[1][0])
            grad_k[:, lane] += jnp.where(all_first, parts[0][1], parts[1][1])
            grad_qkv[rows, lane] = (
                jnp.where(first, parts[0][2], parts[1][2]) * (HEAD**-0.5)
            ).astype(low_type)

    def project_back(m, j):
        rows = rows_of(j, chunk)
        low = grad_qkv[rows]
        qkv_sums[...] += jnp.sum(low.astype(jnp.float32), axis=0, keepdims=True)
        total = dot_rows(low[:, :columns], wq[0])
        for third in range(1, 3):
            total = total + dot_rows(low[:, third * columns : (third + 1) * columns], wq[third])
        send_b[lax.rem(j, 2)] = total.astype(low_type)
        exchange_b(m, j).start()

    def finish(m, j):
        rows = rows_of(j, chunk)
        slot = lax.rem(j, 2)
        exchange_b(m, j).wait()

        @pl.when(m > 0)
        def _():
            placed.wait(m - 1, j)

            @pl.when(section > 0)
            def _():
                hop(m - 1, j).wait_send()

        total = (
            send_b[slot].astype(jnp.float32) + got_b[j].astype(jnp.float32) + high_ga[rows]
        ).astype(low_type)
        grads[j] = total
        time_sums[m] += jnp.sum(total.astype(jnp.float32), axis=0, keepdims=True)

        @pl.when(section > 0)
        def _():
            hop(m, j).start()

        placed.start(m, j)

    def one_row(m, carry):
        def step(i, carry):
            @pl.when(i < 2)
            def _():
                receive(m, i)

            @pl.when(jnp.logical_and(i >= 1, i < chunks))
            def _():
                for copy in keep_first(m, i - 1):
                    copy.wait()

            @pl.when(i < chunks)
            def _():
                @pl.when(jnp.logical_and(m == 0, i == 0))
                def _():
                    weights[0].wait()
                    weights[1].wait()

                feed_back(m, i)

                @pl.when(i + 1 < chunks)
                def _():
                    for copy in load_first(m, i + 1):
                        copy.start()

                @pl.when(jnp.logical_and(i + 1 == chunks, m + 1 < micro))
                def _():
                    for copy in load_first(m + 1, 0):
                        copy.start()

            @pl.when(i == 0)
            def _():
                @pl.when(m == 0)
                def _():
                    weights[2].wait()
                    weights[3].wait()

                build(m)

            @pl.when(i >= 1)
            def _():
                @pl.when(i >= 2)
                def _():
                    keep_second(m, i - 2).wait()

                norm_step(m, i - 1)

                @pl.when(i + 1 < chunks)
                def _():
                    receive(m, i + 1)

                mix_back(m, i - 1)

                @pl.when(i < chunks)
                def _():
                    for copy in load_second(m, i):
                        copy.start()

                @pl.when(jnp.logical_and(i == chunks, m + 1 < micro))
                def _():
                    for copy in load_second(m + 1, 0):
                        copy.start()

            return carry

        lax.fori_loop(0, chunks + 1, step, 0)
        for copy in keep_first(m, chunks - 1):
            copy.wait()
        keep_second(m, chunks - 1).wait()

        @pl.when(m + 1 < micro)
        def _():
            load_qkv(m + 1).start()

        grad_qkv[:, columns : 2 * columns] = grad_k[...].astype(low_type)
        grad_qkv[:, 2 * columns :] = grad_v[...].astype(low_type)
        keep_qkv(m).start()

        def last_step(i, carry):
            @pl.when(i < chunks)
            def _():
                project_back(m, i)

            @pl.when(i >= 1)
            def _():
                finish(m, i - 1)

            return carry

        lax.fori_loop(0, chunks + 1, last_step, 0)
        keep_qkv(m).wait()
        return carry

    lax.fori_loop(0, micro, one_row, 0)
    for j in range(chunks):
        placed.wait(micro - 1, j)

    @pl.when(section > 0)
    def _():
        for j in range(chunks):
            hop(micro - 1, j).wait_send()

    @pl.when(section < last)
    def _():
        for m in range(micro):
            for j in range(chunks):
                hand_over(m, j).wait_send()
    placed.wait_got()


def backward_pass(sections, starts, gains, biases, rows_back, params, stash):
    qkv_w, out_w, in_w, down_w = params
    micro, length, width = rows_back.shape
    columns, hidden = out_w.shape[0], in_w.shape[1]
    chunk = min(256, length // 4)
    chunks = length // chunk
    low, high = low_type, jnp.float32

    def out(*shape, dtype=low):
        return jax.ShapeDtypeStruct(shape, dtype)

    outs = dict(
        row_sums=out(6, width, dtype=high),
        in_sums=out(1, hidden, dtype=high),
        qkv_sums=out(1, 3 * columns, dtype=high),
        time_sums=out(micro, 1, width, dtype=high),
        grad_z=out(micro, length, width),
        grad_pre=out(micro, length, hidden),
        grad_a=out(micro, length, width),
        grad_qkv=out(micro, length, 3 * columns),
        grads=out(micro, length // 2, width),
    )
    vmem = pl.BlockSpec(memory_space=pltpu.VMEM)
    anywhere = pl.BlockSpec(memory_space=pl.ANY)
    dma = pltpu.SemaphoreType.DMA
    results = pl.pallas_call(
        functools.partial(backward_kernel, sections, chunk),
        in_specs=[pl.BlockSpec(memory_space=pltpu.SMEM)] + [vmem] * 2 + [anywhere] * 12,
        out_specs=[vmem] * 4 + [anywhere] * 5,
        out_shape=list(outs.values()),
        scratch_shapes=[
            pltpu.VMEM(qkv_w.shape, low),
            pltpu.VMEM(out_w.shape, low),
            pltpu.VMEM(in_w.shape, low),
            pltpu.VMEM(down_w.shape, low),
            pltpu.VMEM((micro, length, width), low),
            pltpu.VMEM((length, width), high),
            pltpu.VMEM((length, 3 * columns), low),
            pltpu.VMEM((columns // HEAD, length, LANES), low),
            pltpu.VMEM((columns // HEAD, length, LANES), low),
            pltpu.VMEM((length, columns), high),
            pltpu.VMEM((length, columns), high),
            pltpu.VMEM((length, 3 * columns), low),
            pltpu.VMEM((2, chunk, width), low),
            pltpu.VMEM((2, chunk, width), low),
            pltpu.VMEM((chunks, chunk, width), low),
            pltpu.VMEM((chunks, chunk, width), low),
            pltpu.VMEM((2, chunk, width), high),
            pltpu.VMEM((chunk, width), low),
            pltpu.VMEM((chunk, hidden), low),
            pltpu.VMEM((chunk, width), low),
            pltpu.VMEM((chunk, columns), low),
            pltpu.VMEM((chunks, chunk, width), low),
            pltpu.VMEM((chunk, width), low),
            pltpu.VMEM((chunk, hidden), low),
            pltpu.VMEM((chunk, LANES), high),
            pltpu.VMEM((chunk, width), low),
            pltpu.VMEM((chunk, LANES), high),
            pltpu.VMEM((chunk, columns), low),
            pltpu.VMEM((chunk, columns), low),
            dma((4,)),
            dma((micro, chunks)),
            dma((chunks,)),
            dma((micro, chunks)),
            dma((micro, chunks)),
            dma((micro, chunks)),
            dma((2,)),
            dma((micro, chunks)),
            dma((2,)),
            dma((micro, chunks)),
            dma,
            dma((3,)),
            dma((4,)),
            dma((2,)),
            dma,
            dma,
            dma((chunks,)),
            dma((chunks,)),
            dma((chunks // 2,)),
        ],
        compiler_params=pltpu.CompilerParams(
            collective_id=1, has_side_effects=True, vmem_limit_bytes=63 * 1024 * 1024
        ),
        name="backward_pass",
    )(
        starts,
        gains,
        biases,
        rows_back,
        qkv_w,
        out_w,
        in_w,
        down_w,
        stash["qkv"],
        stash["log_sums"],
        stash["mixed"],
        stash["middle"],
        stash["slope"],
        stash["result"],
        stash["scales"],
    )
    return dict(zip(outs, results))


def gradient_kernel(
    sections,
    plan,
    fractions_ref,
    row_sums,
    in_sums,
    qkv_sums,
    time_sums,
    *refs,
):
    count = len(plan)
    lefts, rights = refs[:count], refs[count : 2 * count]
    refs = refs[2 * count :]
    outs, (small_out, other_out, time_out) = refs[:count], refs[count : count + 3]
    refs = refs[count + 3 :]
    tiles, firsts, seconds, shares, finals = (
        refs[i * count : (i + 1) * count] for i in range(5)
    )
    (
        held,
        big,
        middle,
        small_in,
        small_group,
        small_beside,
        left_sem,
        right_sem,
        first_send,
        first_got,
        second_send,
        second_got,
        share_send,
        share_got,
        final_sem,
        small_send,
        small_got,
    ) = refs[5 * count :]
    at = Seat()
    section, chip, core = at.section, at.chip, at.core

    def block(order):
        owner = 1 - chip if order < 2 else chip
        return 2 * owner + order % 2

    steps = []
    for w, (rows, _, width, _) in enumerate(plan):
        for order in range(4):
            for start in range(0, rows, width):
                steps.append((w, order, start, width))

    def load_left(index):
        w, order, start, width = steps[index]
        first = pl.multiple_of(block(order) * plan[w][0] + start, width)
        return pltpu.make_async_copy(
            lefts[w].at[:, pl.ds(first, width)],
            held.at[index % 2, :, pl.ds(0, width)],
            left_sem.at[index % 2],
        )

    def room(w):
        columns = plan[w][1]
        return (big if w % 2 == 0 else middle).at[:, pl.ds(0, columns)]

    def load_right(w):
        return pltpu.make_async_copy(rights[w], room(w), right_sem.at[w % 2])

    def send_first(w, order):
        if plan[w][3]:
            return remote(
                tiles[w].at[order],
                firsts[w].at[order],
                first_send.at[w, order],
                first_got.at[w, order],
                at.across,
            )
        return remote(
            tiles[w].at[order],
            firsts[w].at[order],
            first_send.at[w, order],
            first_got.at[w, order],
            at.beside,
        )

    def send_second(w, order):
        if plan[w][3]:
            return remote(
                tiles[w].at[order],
                seconds[w].at[order],
                second_send.at[w, order],
                second_got.at[w, order],
                at.beside,
            )
        return remote(
            tiles[w].at[2 + order],
            seconds[w].at[order],
            second_send.at[w, order],
            second_got.at[w, order],
            at.across,
        )

    def send_share(w):
        return remote(
            tiles[w].at[3 - core], shares[w], share_send.at[w], share_got.at[w], at.peer
        )

    def store_final(w):
        return pltpu.make_async_copy(finals[w], outs[w], final_sem.at[w])

    def put_final(w, value):
        if len(finals[w].shape) == 3:
            size = finals[w].shape[2]
            for i in range(finals[w].shape[0]):
                finals[w][i] = value[:, i * size : (i + 1) * size]
        else:
            finals[w][...] = value
        store_final(w).start()

    def high(value):
        return value.astype(jnp.float32)

    load_right(0).start()
    load_right(1).start()
    load_left(0).start()
    small_in[...] = jnp.zeros_like(small_in)
    small_in[0:6] = row_sums[...]
    weighted = jnp.zeros_like(time_sums[0])
    plain = jnp.zeros_like(time_sums[0])
    for m in range(time_sums.shape[0]):
        weighted = weighted + fractions_ref[m] * time_sums[m]
        plain = plain + time_sums[m]
    from_first = jnp.where(section == 0, 1.0, 0.0)
    small_in[8:9] = weighted * from_first
    small_in[9:10] = plain * from_first
    width = small_in.shape[1]
    for i in range(in_sums.shape[1] // width):
        small_in[16 + i : 17 + i] = in_sums[:, i * width : (i + 1) * width]
    third = qkv_sums.shape[1] // 3
    small_in[20:21, :third] = qkv_sums[:, :third]
    small_in[20:21, third : 2 * third] = qkv_sums[:, 2 * third :]
    greet(section, sections, (at.peer, at.across, at.beside))

    small_across = remote(
        small_in, small_group, small_send.at[0], small_got.at[0], at.across
    )
    small_chips = remote(
        small_in, small_beside, small_send.at[1], small_got.at[1], at.beside
    )
    small_cores = remote(small_out, other_out, small_send.at[2], small_got.at[2], at.peer)
    time_hop = remote(
        time_out, time_out, small_send.at[3], small_got.at[3], {"section": section + 1}
    )
    small_across.start()
    seen = 0
    for w, (rows, columns, step_width, across_first) in enumerate(plan):
        load_right(w).wait()
        for order in range(4):
            while seen < len(steps) and steps[seen][:2] == (w, order):
                load_left(seen).wait()
                if seen + 1 < len(steps):
                    load_left(seen + 1).start()
                start = steps[seen][2]
                tiles[w][order, start : start + step_width] = dot_first(
                    held[seen % 2, :, :step_width], room(w)[...]
                ).astype(low_type)
                seen += 1
            if across_first:
                pl.when(at.away)(send_first(w, order).start)
            elif order < 2:
                send_first(w, order).start()
        if w + 2 < count:
            load_right(w + 2).start()
        if w == 0:
            small_across.wait()
            small_in[...] += small_group[...]
            small_chips.start()
        if w == 1:
            small_chips.wait()
            small_out[...] = small_in[...] + small_beside[...]
            small_cores.start()

    @pl.when(section == 0)
    def _():
        time_out[...] = small_out[8:16]

    for w, (_, _, _, across_first) in enumerate(plan):
        if across_first:

            @pl.when(at.home)
            def _(w=w):
                for order in range(2):
                    send_first(w, order).wait_recv()
                    tiles[w][order] = (
                        high(tiles[w][order]) + high(firsts[w][order])
                    ).astype(low_type)
                    send_second(w, order).start()

        else:

            @pl.when(at.away)
            def _(w=w):
                for order in range(2):
                    send_first(w, order).wait_recv()
                    tiles[w][2 + order] = (
                        high(tiles[w][2 + order]) + high(firsts[w][order])
                    ).astype(low_type)
                    send_second(w, order).start()

    @pl.when(at.home)
    def _():
        for w, (_, _, _, across_first) in enumerate(plan):
            for order in range(2):
                send_first(w, order + 2 if across_first else order).wait_recv()
                send_second(w, order).wait_recv()

            def total(side):
                first = firsts[w][2 + side] if across_first else firsts[w][side]
                return high(tiles[w][2 + side]) + high(first) + high(seconds[w][side])

            tiles[w][3 - core] = total(1 - core).astype(low_type)
            send_share(w).start()
            put_final(w, total(core))

    @pl.when(at.away)
    def _():
        for w in range(count):
            send_share(w).wait_recv()
            put_final(w, high(shares[w][...]))

    small_cores.wait()

    @pl.when(section > 0)
    def _():
        time_hop.wait_recv()

    @pl.when(section < sections - 1)
    def _():
        time_hop.start()
        time_hop.wait_send()

    for w, (_, _, _, across_first) in enumerate(plan):
        store_final(w).wait()
        if across_first:

            @pl.when(at.away)
            def _(w=w):
                for order in range(4):
                    send_first(w, order).wait_send()

            @pl.when(at.home)
            def _(w=w):
                for order in range(2):
                    send_second(w, order).wait_send()

        else:
            for order in range(2):
                send_first(w, order).wait_send()

            @pl.when(at.away)
            def _(w=w):
                for order in range(2):
                    send_second(w, order).wait_send()

        pl.when(at.home)(send_share(w).wait_send)


def gradient_pass(sections, fractions, back, lefts, rights, across_first, splits):
    plan = []
    finals = []
    for left, right, first, split in zip(lefts, rights, across_first, splits):
        rows = left.shape[1] // 4
        columns = right.shape[1]
        plan.append((rows, columns, min(256, rows), first))
        finals.append((split, rows, columns // split) if split > 1 else (rows, columns))
    length = lefts[0].shape[0]
    low, high = low_type, jnp.float32
    width = back["row_sums"].shape[1]
    count = len(plan)
    widest = max(columns for _, columns, _, _ in plan[0::2])
    middle = max(columns for _, columns, _, _ in plan[1::2])
    vmem = pl.BlockSpec(memory_space=pltpu.VMEM)
    anywhere = pl.BlockSpec(memory_space=pl.ANY)
    dma = pltpu.SemaphoreType.DMA
    small = (24, width)

    def buffers(number):
        return [
            pltpu.VMEM((number, rows, columns), low) for rows, columns, _, _ in plan
        ]

    return pl.pallas_call(
        functools.partial(gradient_kernel, sections, tuple(plan)),
        in_specs=[pl.BlockSpec(memory_space=pltpu.SMEM)] + [vmem] * 4 + [anywhere] * (2 * count),
        out_specs=[anywhere] * count + [vmem] * 3,
        out_shape=[jax.ShapeDtypeStruct(shape, high) for shape in finals]
        + [jax.ShapeDtypeStruct(shape, high) for shape in (small, small, (8, width))],
        scratch_shapes=buffers(4)
        + [
            pltpu.VMEM((4 if first else 2, rows, columns), low)
            for rows, columns, _, first in plan
        ]
        + buffers(2)
        + [pltpu.VMEM((rows, columns), low) for rows, columns, _, _ in plan]
        + [pltpu.VMEM(shape, high) for shape in finals]
        + [
            pltpu.VMEM((2, length, max(step for _, _, step, _ in plan)), low),
            pltpu.VMEM((length, widest), low),
            pltpu.VMEM((length, middle), low),
            pltpu.VMEM(small, high),
            pltpu.VMEM(small, high),
            pltpu.VMEM(small, high),
            dma((2,)),
            dma((2,)),
            dma((count, 4)),
            dma((count, 4)),
            dma((count, 2)),
            dma((count, 2)),
            dma((count,)),
            dma((count,)),
            dma((count,)),
            dma((4,)),
            dma((4,)),
        ],
        compiler_params=pltpu.CompilerParams(
            collective_id=2, has_side_effects=True, vmem_limit_bytes=62 * 1024 * 1024
        ),
        name="gradient_pass",
    )(
        fractions,
        back["row_sums"],
        back["in_sums"],
        back["qkv_sums"],
        back["time_sums"],
        *lefts,
        *rights,
    )


def unit_norm(value):
    average = jnp.mean(value, axis=-1, keepdims=True)
    centered = value - average
    inv_scale = lax.rsqrt(jnp.mean(centered * centered, axis=-1, keepdims=True) + eps_norm)
    return centered * inv_scale, inv_scale


def norm_back(gradient, normed, inv_scale, gain_row):
    weighted = gradient * gain_row
    adjusted = (
        weighted
        - jnp.mean(weighted, axis=-1, keepdims=True)
        - normed * jnp.mean(weighted * normed, axis=-1, keepdims=True)
    )
    return inv_scale * adjusted


def gelu_pair(pre):
    normal = 0.5 * (1.0 + lax.erf(pre * 0.7071067811865476))
    density = jnp.exp(-0.5 * pre * pre) * 0.3989422804014327
    return pre * normal, normal + pre * density


def forward_layer(at, inputs, starts, params):
    qkv_w, qkv_b, out_w, in_w, in_b, down_w, gains, biases = params
    qkv = (dot_plain(inputs, qkv_w) + qkv_b).astype(low_type)
    mixed, log_sums = attend(qkv, starts)
    branch = at.group_sum(dot_plain(mixed, out_w).astype(low_type))
    unit_a, scale_a = unit_norm(branch + biases[0] + inputs.astype(jnp.float32))
    middle = unit_a * gains[0] + biases[1]
    low_middle = middle.astype(low_type)
    hidden, slope = gelu_pair(dot_plain(low_middle, in_w) + in_b)
    hidden = hidden.astype(low_type)
    branch_two = at.group_sum(dot_plain(hidden, down_w).astype(low_type))
    unit_z, scale_z = unit_norm(branch_two + biases[2] + middle)
    result = (unit_z * gains[1] + biases[3]).astype(low_type)
    saved = dict(
        inputs=inputs,
        qkv=qkv,
        mixed=mixed,
        log_sums=log_sums,
        scale_a=scale_a[:, 0],
        middle=low_middle,
        hidden=hidden,
        slope=slope.astype(low_type),
        scale_z=scale_z[:, 0],
    )
    return result, saved


def backward_layer(at, saved, incoming, starts, params):
    qkv_w, qkv_b, out_w, in_w, in_b, down_w, gains, biases = params
    gradient = incoming.astype(jnp.float32)
    unit_z = (saved["result"].astype(jnp.float32) - biases[3]) / gains[1]
    grad_z = norm_back(gradient, unit_z, saved["scale_z"][:, None], gains[1])
    low_gz = grad_z.astype(low_type)
    grad_pre = (dot_rows(low_gz, down_w) * saved["slope"].astype(jnp.float32)).astype(low_type)
    grad_mid = at.group_sum(dot_rows(grad_pre, in_w).astype(low_type)) + grad_z
    unit_a = (saved["middle"].astype(jnp.float32) - biases[1]) / gains[0]
    grad_a = norm_back(grad_mid, unit_a, saved["scale_a"][:, None], gains[0])
    low_ga = grad_a.astype(low_type)
    grad_mixed = dot_rows(low_ga, out_w).astype(low_type)
    grad_qkv = jnp.concatenate(
        attend_back(saved["qkv"], starts, saved["mixed"], saved["log_sums"], grad_mixed), 1
    )
    grad_x = at.group_sum(dot_rows(grad_qkv, qkv_w).astype(low_type)) + grad_a
    sums = jnp.stack(
        [
            jnp.sum(grad_mid * unit_a, axis=0),
            jnp.sum(gradient * unit_z, axis=0),
            jnp.sum(grad_a, axis=0),
            jnp.sum(grad_mid, axis=0),
            jnp.sum(grad_z, axis=0),
            jnp.sum(gradient, axis=0),
        ]
    )
    kept = dict(grad_z=low_gz, slope=grad_pre, grad_a=low_ga, qkv=grad_qkv)
    return grad_x.astype(low_type), kept, sums


def store(buffers, values, slot):
    return jax.tree.map(
        lambda buffer, value: lax.dynamic_update_index_in_dim(buffer, value, slot, 0),
        buffers,
        values,
    )


def pick(buffers, slot):
    return jax.tree.map(
        lambda buffer: lax.dynamic_index_in_dim(buffer, slot, 0, keepdims=False), buffers
    )


def group_weight(at, weight):
    parts = weight.reshape((at.chips, -1) + weight.shape[1:])

    def across(s, g, u, x, c):
        return (s, c, u, x, g) if g != c else None

    def along(step):
        return lambda s, g, u, x, c: (s, g, u, (x + step) % at.chips, c) if g != c else None

    piece = at.move(lax.dynamic_index_in_dim(parts, at.chip, 0, keepdims=False), across)
    pieces = [piece]
    for step in range(1, at.chips):
        pieces.append(at.move(piece, along(step)))
    whole = parts
    for step, piece in enumerate(pieces):
        spot = (at.chip - step) % at.chips
        own = lax.dynamic_index_in_dim(parts, spot, 0, keepdims=False)
        whole = lax.dynamic_update_index_in_dim(whole, jnp.where(at.home, own, piece), spot, 0)
    return whole.reshape(weight.shape)


def group_rows(at, tokens, section):
    def across(s, g, u, x, c):
        return (s, 1 - g, u, x, c) if s == section else None

    own = lax.dynamic_index_in_dim(tokens, at.group, 0, keepdims=False)
    other = at.move(lax.dynamic_index_in_dim(tokens, 1 - at.group, 0, keepdims=False), across)
    lower = at.group == 0
    pair = jnp.stack([jnp.where(lower, own, other), jnp.where(lower, other, own)])
    whole = at.group_gather(pair)
    whole = whole.reshape((2, at.halves) + pair.shape)
    whole = jnp.swapaxes(whole, 1, 2)
    return whole.reshape(2, -1, tokens.shape[-1])


def spread_rows(at, rows, length):
    def across(s, g, u, x, c):
        return (s, 1 - g, u, x, c)

    row = lax.dynamic_index_in_dim(rows, at.core, 0, keepdims=False)
    tile = length // at.tensor

    def piece(group):
        return lax.dynamic_slice_in_dim(row, (group * at.halves + at.part) * tile, tile, 0)

    own = piece(at.group)
    other = at.move(piece(1 - at.group), across)
    lower = at.group == 0
    return jnp.stack([jnp.where(lower, own, other), jnp.where(lower, other, own)])


def sum_weight(at, gradient, across_first):
    parts = gradient.reshape((at.chips, -1) + gradient.shape[1:])

    def across(s, g, u, x, c):
        return (s, c, u, x, c) if g != c else None

    def along(step):
        def target(s, g, u, x, c):
            if across_first and g != c:
                return None
            return (s, g, u, (x + step) % at.chips, c)

        return target

    def fold_chips(parts):
        total = lax.dynamic_index_in_dim(parts, at.chip, 0, keepdims=False).astype(jnp.float32)
        for step in range(1, at.chips):
            piece = lax.dynamic_index_in_dim(
                parts, (at.chip + step) % at.chips, 0, keepdims=False
            )
            total = total + at.move(piece, along(step)).astype(jnp.float32)
        return total.astype(low_type)

    if across_first:
        total = fold_chips(
            (parts.astype(jnp.float32) + at.move(parts, across).astype(jnp.float32)).astype(
                low_type
            )
        )
    else:
        part = fold_chips(parts)
        total = (part.astype(jnp.float32) + at.move(part, across).astype(jnp.float32)).astype(
            low_type
        )
    halves = total.reshape((2, -1) + total.shape[1:])

    def over(s, g, u, x, c):
        return (s, g, u, x, 1 - c) if g == c else None

    own = lax.dynamic_index_in_dim(halves, at.core, 0, keepdims=False)
    other = at.move(lax.dynamic_index_in_dim(halves, 1 - at.core, 0, keepdims=False), over)
    return jnp.where(at.home, own, other).astype(jnp.float32)


def layer_ticks(at, starts, rows_in, rows_back, params):
    qkv_w = params[0]
    micro_count, length, width = rows_in.shape
    tick_count = micro_count + at.sections - 1
    slots = micro_count + 1

    def hop(result, distance):
        def target(s, g, u, x, c):
            return (s + distance, g, u, x, c) if 0 <= s + distance < at.sections else None

        tile = length // at.size
        piece = at.move(lax.dynamic_slice_in_dim(result, at.rank * tile, tile, 0), target)
        return at.group_gather(piece).reshape(length, width)

    def place_of(tick_value, stage):
        place = tick_value - stage
        usable = jnp.logical_and(place >= 0, place < micro_count)
        return usable, jnp.clip(place, 0, micro_count - 1), jnp.where(usable, place, micro_count)

    def empty(values):
        return jax.tree.map(
            lambda value: jnp.zeros((slots,) + value.shape, value.dtype), values
        )

    def forward_tick(tick_value, arrived, stash, outputs):
        usable, position, slot = place_of(tick_value, at.section)
        inputs = jnp.where(at.section == 0, rows_in[position], arrived)
        result, saved = forward_layer(at, inputs, starts[position], params)
        if stash is None:
            return result, saved
        return result, store(stash, saved, slot), store(outputs, result, slot)

    blank = jnp.zeros((length, width), low_type)
    shapes = jax.eval_shape(lambda: forward_tick(0, blank, None, None))
    stash, outputs = empty(shapes[1]), empty(shapes[0])

    def forward_loop(tick_value, carry):
        result, stash, outputs = forward_tick(tick_value, *carry)
        return hop(result, 1), stash, outputs

    carry = lax.fori_loop(0, tick_count - 1, forward_loop, (blank, stash, outputs))
    _, stash, outputs = forward_tick(tick_count - 1, *carry)

    def backward_tick(tick_value, arrived, stash, grads, totals):
        usable, position, slot = place_of(tick_value, at.sections - 1 - at.section)
        incoming = jnp.where(at.section == at.sections - 1, rows_back[position], arrived)
        grad_x, kept_now, sums = backward_layer(
            at, pick(dict(stash, result=outputs), slot), incoming, starts[position], params
        )
        totals = totals + jnp.where(usable, sums, 0.0)
        kept = store({name: stash[name] for name in kept_now}, kept_now, slot)
        return grad_x, dict(stash, **kept), store(grads, grad_x, slot), totals

    for name in ("grad_z", "grad_a"):
        stash[name] = empty(blank)
    totals = jnp.zeros((6, width), jnp.float32)

    def backward_loop(tick_value, carry):
        grad_x, stash, grads, totals = backward_tick(tick_value, *carry)
        return hop(grad_x, -1), stash, grads, totals

    carry = lax.fori_loop(
        0, tick_count - 1, backward_loop, (blank, stash, empty(blank), totals)
    )
    _, stash, grads, totals = backward_tick(tick_count - 1, *carry)

    def both(buffer):
        return buffer[:micro_count]

    low_gz, grad_pre, low_ga, grad_qkv = (
        both(stash[name]) for name in ("grad_z", "slope", "grad_a", "qkv")
    )
    stash = {name: both(value) for name, value in stash.items()}
    stash["result"] = both(outputs)
    grads = both(grads)
    back = dict(
        row_sums=totals,
        in_sums=jnp.sum(grad_pre, axis=(0, 1), dtype=jnp.float32)[None],
        qkv_sums=jnp.sum(grad_qkv, axis=(0, 1), dtype=jnp.float32)[None],
        time_sums=jnp.sum(grads, axis=1, keepdims=True, dtype=jnp.float32),
        grad_z=low_gz,
        grad_pre=grad_pre,
        grad_a=low_ga,
        grad_qkv=grad_qkv,
        grads=grads,
    )
    return stash, back


def shards(
    tokens,
    timesteps,
    seg_starts,
    time_params,
    qkv_weight,
    qv_bias,
    out_weight,
    ffn_in,
    ffn_bias,
    ffn_out,
    ln_gains,
    row_biases,
    cotangent,
):
    at = Layout()
    width = tokens.shape[-1]
    length = tokens.shape[1] * at.tensor
    columns = qkv_weight.shape[3]

    def both_cores(value):
        def over(s, g, u, x, c):
            return (s, g, u, x, 1 - c)

        other = at.move(value, over)
        first = at.core == 0
        mine = jnp.stack([jnp.where(first, value, other), jnp.where(first, other, value)])
        return lax.dynamic_index_in_dim(mine, at.group, 1, keepdims=False)

    starts = both_cores(seg_starts)
    fractions_own = timesteps.astype(jnp.float32) / 5000.0
    fractions = both_cores(fractions_own)
    time_values = time_params.astype(jnp.float32)
    embedded = (
        tokens.astype(jnp.float32) + fractions_own[:, None, None] * time_values[0] + time_values[1]
    ).astype(low_type)
    gains, biases = ln_gains[0].astype(jnp.float32), row_biases[0].astype(jnp.float32)
    if at.size == 2 and at.chips == 2:
        bias = jnp.concatenate(
            [qv_bias[0, 0], jnp.zeros((columns,), low_type), qv_bias[0, 1], ffn_bias[0]]
        ).astype(jnp.float32)
        weights = (
            jnp.transpose(qkv_weight[0], (1, 0, 2)),
            out_weight[0],
            ffn_in[0],
            ffn_out[0],
        )
        stash = forward_pass(
            at.sections, starts, bias[None], gains, biases, embedded, cotangent, weights
        )
        weights = tuple(stash[name] for name in ("wq", "wo", "wi", "wd"))
        back = backward_pass(
            at.sections, starts, gains, biases, stash["rows_back"], weights, stash
        )
        layer_outs, input_grads = stash["placed"], back["grads"]
    else:
        rows_in = group_rows(at, embedded, 0)
        qv_low = group_weight(at, qv_bias[0].T).T.astype(jnp.float32)
        params = (
            group_weight(at, qkv_weight[0].reshape(width, 3 * columns)),
            jnp.concatenate([qv_low[0], jnp.zeros((columns,), jnp.float32), qv_low[1]]),
            group_weight(at, out_weight[0]),
            group_weight(at, ffn_in[0]),
            group_weight(at, ffn_bias[0]).astype(jnp.float32),
            group_weight(at, ffn_out[0]),
            gains,
            biases,
        )
        rows_back = group_rows(at, cotangent, at.sections - 1)
        stash, back = layer_ticks(at, starts, rows_in, rows_back, params)
        layer_outs = spread_rows(at, stash["result"], length)
        input_grads = spread_rows(at, back["grads"], length)

    tensor = lax.axis_index("tensor")
    dp = lax.axis_index("dp")

    def flat(value):
        return value.reshape(-1, value.shape[-1])

    if at.size == 2 and at.chips == 2:
        in_g, down_g, qkv_g, out_g, sums, other, time_rows = gradient_pass(
            at.sections,
            fractions,
            back,
            [flat(stash[name]) for name in ("middle", "hidden", "inputs", "mixed")],
            [flat(back[name]) for name in ("grad_pre", "grad_z", "grad_qkv", "grad_a")],
            (False, True, False, True),
            (1, 1, 3, 1),
        )
        qkv_g = jnp.transpose(qkv_g, (1, 0, 2))
        slices = jnp.where(at.home, sums, other)
        mine = jnp.concatenate([slices[20], slices[16:20].reshape(-1)])
        mine = mine[: 2 * columns + back["in_sums"].shape[1]]
        row_sums = sums[:6]
        grad_time = time_rows[:2]
    else:
        def product(left, right):
            left, right = (v.reshape(-1, v.shape[-1]) for v in (left, right))
            return dot_first(left, right).astype(low_type)

        down_g = sum_weight(at, product(stash["hidden"], back["grad_z"]), True)
        in_g = sum_weight(at, product(stash["middle"], back["grad_pre"]), False)
        out_g = sum_weight(at, product(stash["mixed"], back["grad_a"]), True)
        qkv_g = sum_weight(at, product(stash["inputs"], back["grad_qkv"]), False)
        qkv_bias_g = back["qkv_sums"].reshape(3, columns)
        sliced = jnp.concatenate([qkv_bias_g[0], qkv_bias_g[2], back["in_sums"][0]])
        every = jnp.zeros((at.size,) + sliced.shape, jnp.float32)
        every = lax.dynamic_update_index_in_dim(every, sliced, at.rank, 0)
        row_terms = jnp.where(at.rank == 0, back["row_sums"], 0.0)
        small = lax.psum(
            jnp.concatenate([row_terms.reshape(-1), every.reshape(-1)]), ("tensor", "dp")
        )
        row_sums = small[: row_terms.size].reshape(row_terms.shape)
        mine = lax.dynamic_index_in_dim(
            small[row_terms.size :].reshape(every.shape), tensor, 0, keepdims=False
        )
        row_grads = back["time_sums"][:, 0]
        time_terms = jnp.stack([jnp.sum(fractions[:, None] * row_grads, 0), jnp.sum(row_grads, 0)])
        time_terms = jnp.where(jnp.logical_and(at.section == 0, at.rank == 0), time_terms, 0.0)
        grad_time = lax.psum(time_terms, AXES)

    def share(value, count, index):
        size = value.shape[-1] // count
        return lax.dynamic_slice_in_dim(value, index * size, size, value.ndim - 1)

    qv_g = share(mine[: 2 * columns].reshape(2, columns), at.dp, dp)
    in_bias_g = share(mine[2 * columns :], at.dp, dp)
    row_share = share(row_sums, at.tensor * at.dp, tensor * at.dp + dp)

    return (
        layer_outs[None],
        input_grads[None],
        qkv_g.reshape(-1, 3, columns)[None],
        qv_g[None],
        out_g[None],
        in_g[None],
        in_bias_g[None],
        down_g[None],
        row_share[None, :2],
        row_share[None, 2:],
        grad_time,
    )


def solution(mesh):
    return jax.shard_map(
        shards,
        mesh=mesh,
        in_specs=(
            P("dp", "tensor", None),
            P("dp"),
            P("dp", None),
            P(),
            P("section", None, None, "tensor"),
            P("section", None, "tensor"),
            P("section", "tensor", None),
            P("section", None, "tensor"),
            P("section", "tensor"),
            P("section", "tensor", None),
            P("section", None, None),
            P("section", None, None),
            P("dp", "tensor", None),
        ),
        out_specs=(
            P("section", "dp", "tensor", None),
            P("section", "dp", "tensor", None),
            P("section", "dp", None, "tensor"),
            P("section", None, ("tensor", "dp")),
            P("section", ("tensor", "dp"), None),
            P("section", "dp", "tensor"),
            P("section", ("tensor", "dp")),
            P("section", ("tensor", "dp"), None),
            P("section", None, ("tensor", "dp")),
            P("section", None, ("tensor", "dp")),
            P(),
        ),
        check_vma=False,
    )
```

```python
import functools

import jax
import jax.numpy as jnp
from jax import lax
from jax.experimental import pallas as pl
from jax.experimental.pallas import tpu as pltpu
from jax.sharding import PartitionSpec as P

HEAD = 64
LANES = 128
MASKED = -1e30
eps_norm = 1e-05
AXES = ("section", "tensor", "dp")
low_type = jnp.bfloat16


class Layout:
    def __init__(self):
        self.sections = lax.axis_size("section")
        self.tensor = lax.axis_size("tensor")
        self.dp = lax.axis_size("dp")
        self.halves = self.tensor // 2
        self.chips = self.dp // 2
        self.size = self.tensor
        self.section = lax.axis_index("section")
        tensor, dp = lax.axis_index("tensor"), lax.axis_index("dp")
        self.group, self.part = tensor // self.halves, tensor % self.halves
        self.chip, self.core = dp // 2, dp % 2
        self.rank = self.core * self.halves + self.part
        self.home = self.group == self.core

    def move(self, value, target):
        pairs = []
        for s in range(self.sections):
            for t in range(self.tensor):
                for d in range(self.dp):
                    goal = target(s, t // self.halves, t % self.halves, d // 2, d % 2)
                    if goal is None:
                        continue
                    s2, g2, u2, x2, c2 = goal
                    here = (s * self.tensor + t) * self.dp + d
                    there = (s2 * self.tensor + g2 * self.halves + u2) * self.dp + x2 * 2 + c2
                    if here != there:
                        pairs.append((here, there))
        return lax.ppermute(value, AXES, pairs)

    def turn(self, value, step):
        def target(s, g, u, x, c):
            rank = (c * self.halves + u + step) % self.size
            return (s, g, rank % self.halves, x, rank // self.halves)

        return self.move(value, target)

    def group_sum(self, value):
        total = value.astype(jnp.float32)
        for step in range(1, self.size):
            total = total + self.turn(value, step).astype(jnp.float32)
        return total

    def group_gather(self, value):
        if self.size == 2:
            other = self.turn(value, 1)
            first = self.rank == 0
            return jnp.stack([jnp.where(first, value, other), jnp.where(first, other, value)])
        whole = jnp.zeros((self.size,) + value.shape, value.dtype)
        for step in range(self.size):
            piece = value if step == 0 else self.turn(value, step)
            whole = lax.dynamic_update_index_in_dim(
                whole, piece, (self.rank - step) % self.size, 0
            )
        return whole


def dot_rows(a, b):
    return lax.dot_general(a, b, (((1,), (1,)), ((), ())), preferred_element_type=jnp.float32)


def dot_plain(a, b):
    return lax.dot_general(a, b, (((1,), (0,)), ((), ())), preferred_element_type=jnp.float32)


def dot_first(a, b):
    return lax.dot_general(a, b, (((0,), (0,)), ((), ())), preferred_element_type=jnp.float32)


def tile_docs(starts_ref, length, count):
    place = lax.broadcasted_iota(jnp.int32, (length, LANES), 0)
    doc = jnp.zeros((length, LANES), jnp.int32)
    for j in range(count):
        doc = doc + (starts_ref[j] <= place).astype(jnp.int32)
    lane = lax.broadcasted_iota(jnp.int32, (length, LANES), 1)
    rel = lane % HEAD
    return lane < HEAD, rel, rel + 1 == doc


def three_parts(value):
    high = value.astype(low_type)
    rest = value - high.astype(jnp.float32)
    middle = rest.astype(low_type)
    return high, middle, (rest - middle.astype(jnp.float32)).astype(low_type)


def lanes(rel, count, value, base):
    high, middle, small = three_parts(value)
    return jnp.where(
        rel == count,
        high,
        jnp.where(rel == count + 1, middle, jnp.where(rel == count + 2, small, base)),
    )


def attend_kernel(starts_ref, q_ref, k_ref, v_ref, o_ref, l_ref, *, count, rows):
    length = q_ref.shape[0]
    first, rel, own = tile_docs(starts_ref, length, count)
    extra_k = jnp.where(own, 1.0, 0.0).astype(low_type)
    extra_q = jnp.where(
        jnp.logical_and(rel < count, jnp.logical_not(own)), MASKED, 0.0
    ).astype(low_type)
    q = q_ref[...] * low_type(HEAD**-0.5)
    k = k_ref[...]
    v = v_ref[...]
    ones = jnp.ones_like(v)
    heads = (
        (jnp.where(first, q, extra_q), jnp.where(first, k, extra_k), jnp.where(first, v, ones)),
        (jnp.where(first, extra_q, q), jnp.where(first, extra_k, k), jnp.where(first, ones, v)),
    )
    side = first[:rows]
    for start in range(0, length, rows):
        peaks, sums = [], []
        for q_head, k_head, v_head in heads:
            scores = dot_rows(q_head[start : start + rows], k_head)
            peak = jnp.max(scores, axis=-1, keepdims=True)
            powers = jnp.exp(scores - peak).astype(low_type)
            peaks.append(peak)
            sums.append(dot_plain(powers, v_head))
        mixed = jnp.where(side, sums[0], sums[1])
        totals = jnp.where(side, sums[1], sums[0])
        log_sums = jnp.where(side, peaks[1], peaks[0]) + jnp.log(totals)
        l_ref[start : start + rows] = lanes(
            rel[:rows], count, -log_sums, extra_q[start : start + rows]
        )
        o_ref[start : start + rows] = (mixed / pltpu.roll(totals, HEAD, 1)).astype(low_type)


def attend(qkv, starts):
    length, columns = qkv.shape[0], qkv.shape[1] // 3
    pairs = columns // LANES
    rows = min(512, length)

    def block(offset):
        return pl.BlockSpec((length, LANES), lambda j: (0, offset + j))

    return pl.pallas_call(
        functools.partial(attend_kernel, count=starts.shape[0], rows=rows),
        grid=(pairs,),
        in_specs=[
            pl.BlockSpec(memory_space=pltpu.SMEM),
            block(0),
            block(pairs),
            block(2 * pairs),
        ],
        out_specs=[block(0), block(0)],
        out_shape=[
            jax.ShapeDtypeStruct((length, columns), low_type),
            jax.ShapeDtypeStruct((length, columns), low_type),
        ],
        compiler_params=pltpu.CompilerParams(vmem_limit_bytes=48 * 1024 * 1024),
        cost_estimate=pl.CostEstimate(
            flops=16 * length * length * columns // 4,
            bytes_accessed=12 * length * columns,
            transcendentals=length * length * columns // HEAD,
        ),
        name="attend",
    )(starts, qkv, qkv, qkv)


def attend_back_kernel(
    starts_ref, q_ref, k_ref, v_ref, o_ref, l_ref, g_ref, dq_ref, dk_ref, dv_ref, *, count, rows
):
    length = q_ref.shape[0]
    first, rel, own = tile_docs(starts_ref, length, count)
    stat = jnp.logical_and(rel >= count, rel < count + 3)
    extra_k = jnp.where(jnp.logical_or(own, stat), 1.0, 0.0).astype(low_type)
    extra_v = jnp.where(stat, 1.0, 0.0).astype(low_type)
    extra_q = l_ref[...]
    g = g_ref[...]
    product = g.astype(jnp.float32) * o_ref[...].astype(jnp.float32)
    dots = [
        jnp.sum(jnp.where(first, product, 0.0), axis=-1, keepdims=True),
        jnp.sum(jnp.where(first, 0.0, product), axis=-1, keepdims=True),
    ]
    extra_g = lanes(rel, count, -jnp.where(first, dots[1], dots[0]), jnp.zeros_like(extra_q))
    q = q_ref[...] * low_type(HEAD**-0.5)
    k = k_ref[...]
    v = v_ref[...]
    heads = (
        tuple(
            jnp.where(first, a, b)
            for a, b in ((q, extra_q), (k, extra_k), (v, extra_v), (g, extra_g))
        ),
        tuple(
            jnp.where(first, b, a)
            for a, b in ((q, extra_q), (k, extra_k), (v, extra_v), (g, extra_g))
        ),
    )
    grad_k = [jnp.zeros((length, LANES), jnp.float32)] * 2
    grad_v = [jnp.zeros((length, LANES), jnp.float32)] * 2
    for start in range(0, length, rows):
        part = slice(start, start + rows)
        grad_q = []
        for i, (q_head, k_head, v_head, g_head) in enumerate(heads):
            probs = jnp.exp(dot_rows(k_head, q_head[part]))
            slopes = (probs * dot_rows(v_head, g_head[part])).astype(low_type)
            grad_v[i] = grad_v[i] + dot_plain(probs.astype(low_type), g[part])
            grad_k[i] = grad_k[i] + dot_plain(slopes, q[part])
            grad_q.append(dot_first(slopes, k))
        dq_ref[part] = (
            jnp.where(first[:rows], grad_q[0], grad_q[1]) * (HEAD**-0.5)
        ).astype(low_type)
    dk_ref[...] = jnp.where(first, grad_k[0], grad_k[1]).astype(low_type)
    dv_ref[...] = jnp.where(first, grad_v[0], grad_v[1]).astype(low_type)


def attend_back(qkv, starts, mixed, log_sums, grad_mixed):
    length, columns = mixed.shape
    pairs = columns // LANES
    rows = min(256, length)

    def block(offset):
        return pl.BlockSpec((length, LANES), lambda j: (0, offset + j))

    return pl.pallas_call(
        functools.partial(attend_back_kernel, count=starts.shape[0], rows=rows),
        grid=(pairs,),
        in_specs=[
            pl.BlockSpec(memory_space=pltpu.SMEM),
            block(0),
            block(pairs),
            block(2 * pairs),
            block(0),
            block(0),
            block(0),
        ],
        out_specs=[block(0)] * 3,
        out_shape=[jax.ShapeDtypeStruct((length, columns), low_type)] * 3,
        compiler_params=pltpu.CompilerParams(vmem_limit_bytes=48 * 1024 * 1024),
        cost_estimate=pl.CostEstimate(
            flops=40 * length * length * columns // 4,
            bytes_accessed=20 * length * columns,
            transcendentals=length * length * columns // HEAD,
        ),
        name="attend_back",
    )(starts, qkv, qkv, qkv, mixed, log_sums, grad_mixed)


MESH = pl.DeviceIdType.MESH


def rows_of(index, size):
    return pl.ds(pl.multiple_of(index * size, size), size)


def erf_pair(pre):
    bell = jnp.exp(-0.5 * pre * pre)
    size = jnp.abs(pre)
    t = 1.0 / (1.0 + 0.2316418882663604 * size)
    tail = bell * t * (
        0.127414796
        + t * (-0.142248368 + t * (0.7107068705 + t * (-0.7265760135 + t * 0.5307027145)))
    )
    return jnp.where(pre < 0.0, tail, 1.0 - tail), bell * 0.3989422804014327


def norm_rows(value):
    average = jnp.mean(value, axis=-1, keepdims=True)
    centered = value - average
    inv_scale = lax.rsqrt(jnp.mean(centered * centered, axis=-1, keepdims=True) + eps_norm)
    return centered * inv_scale, inv_scale


def doc_lanes(starts, first_row, shape):
    place = lax.broadcasted_iota(jnp.int32, shape, 0) + first_row
    doc = jnp.zeros(shape, jnp.int32)
    for start in starts:
        doc = doc + (start <= place).astype(jnp.int32)
    lane = lax.broadcasted_iota(jnp.int32, shape, 1)
    rel = lane % HEAD
    return lane < HEAD, rel, rel + 1 == doc


def forward_kernel(
    sections,
    chunk,
    own_ref,
    other_ref,
    qv_in,
    hidden_bias_in,
    gains_in,
    biases_in,
    time_in,
    tokens_in,
    cotangent_in,
    qkv_w,
    out_w,
    in_w,
    down_w,
    qkv_out,
    stat_out,
    mixed_out,
    middle_out,
    hidden_out,
    slope_out,
    inputs_out,
    result_out,
    scale_out,
    placed_out,
    back_out,
    wq_out,
    wo_out,
    wi_out,
    wd_out,
    wq,
    wo,
    wi,
    wd,
    bias_own,
    bias,
    gains,
    biases,
    hbuf,
    qkv,
    keys,
    values,
    mixed,
    stat,
    send_a,
    send_b,
    got_a,
    got_b,
    high_mid,
    low_mid,
    hidden,
    slope,
    result,
    scale_a,
    scale_z,
    w_sem,
    y_send,
    y_got,
    x_send,
    x_got,
    round_up,
    round_down,
    round_tokens,
    round_send,
    round_got,
    bias_sem,
    token_local,
    token_send,
    token_got,
    cot_local,
    cot_send,
    cot_got,
    hop_send,
    hop_got,
    pass_send,
    pass_got,
    keep_sem,
    qkv_sem,
    a_send,
    a_got,
    b_send,
    b_got,
    first_sem,
    second_sem,
    third_sem,
    scale_sem,
    out_local,
    out_send,
    out_got,
):
    at = Seat()
    section, core, peer = at.section, at.core, at.peer
    last = sections - 1
    micro, length, width = hbuf.shape
    count = own_ref.shape[1] - 1
    columns = mixed.shape[2]
    pairs = columns // LANES
    chunks = length // chunk
    half = chunk // 2
    shape = (chunk, LANES)
    given, held = (qkv_w, out_w, in_w, down_w), (wq, wo, wi, wd)
    own_weights = [
        pltpu.make_async_copy(source, target, w_sem.at[i])
        for i, (source, target) in enumerate(zip(given, held))
    ]
    pieces = weight_pieces(*held)

    def swap(k):
        index, where = pieces[k]
        return remote(
            where(given[index], at.chip),
            where(held[index], at.chip),
            y_send.at[k],
            y_got.at[k],
            at.swap,
        )

    def relay(k):
        index, where = pieces[k]
        part = where(held[index], at.chip)
        return remote(part, part, x_send.at[k], x_got.at[k], at.beside)

    size = wd.shape[0] // 8
    rounds = round_up.shape[0]

    def round_rows(ref, n):
        return ref.at[pl.ds((n % 2) * 4 * size + (4 - rounds // 2 + n // 2) * size, size)]

    def go_up(n):
        return remote(
            round_rows(down_w, n),
            round_up.at[n],
            round_send.at[0, n],
            round_got.at[0, n],
            {"section": section + 1},
        )

    def go_over(n):
        return remote(
            round_up.at[n], round_down.at[n], round_send.at[1, n], round_got.at[1, n], at.swap
        )

    def go_down(n):
        return remote(
            round_down.at[n],
            round_rows(wd, n),
            round_send.at[2, n],
            round_got.at[2, n],
            {"section": section - 1},
        )

    def tokens_over():
        return remote(
            tokens_in.at[1 - at.group],
            round_tokens,
            round_send.at[3, 0],
            round_got.at[3, 0],
            at.across,
        )

    def tokens_down():
        tile = tokens_in.shape[1]
        rows = pl.ds(pl.multiple_of((1 - at.group) * tile, tile), tile)
        return remote(
            round_tokens,
            hbuf.at[core, rows],
            round_send.at[3, 1],
            round_got.at[3, 1],
            {"section": section - 1},
        )

    def pieces_of(*indices):
        return [k for k, (index, _) in enumerate(pieces) if index in indices]

    def pass_on(group):
        for k in group:
            swap(k).wait_recv()
            relay(k).start()

    def begin(group):
        for k in group:
            swap(k).start()

    direct = pieces_of(0, 1, 2, 3)[: -(rounds // 2)]
    detour = pieces_of(3)[-(rounds // 2) :]

    def ready(index):
        @pl.when(at.home)
        def _():
            own_weights[index].wait()

        @pl.when(at.away)
        def _():
            for k in pieces_of(index):
                if k in direct:
                    relay(k).wait_recv()
            if index == 3:

                @pl.when(section > 0)
                def _():
                    for k in detour:
                        relay(k).wait_recv()

                @pl.when(section == 0)
                def _():
                    for n in range(rounds):
                        go_down(n).wait_recv()

    def swap_bias():
        return remote(bias_own, bias, bias_sem.at[0], bias_sem.at[1], at.swap)

    tokens = RowPieces(at, tokens_in, hbuf, token_local, token_send, token_got)
    cotangents = RowPieces(at, cotangent_in, back_out, cot_local, cot_send, cot_got)
    placed = OutPieces(at, result, placed_out, out_local, out_send, out_got)

    @pl.when(at.home)
    def _():
        for copy in own_weights:
            copy.start()

    gains[...] = gains_in[...].astype(jnp.float32)
    biases[...] = biases_in[...].astype(jnp.float32)
    qv = qv_in[...].astype(jnp.float32)
    bias_own[:, :columns] = qv[0:1]
    bias_own[:, columns : 2 * columns] = jnp.zeros_like(qv[0:1])
    bias_own[:, 2 * columns : 3 * columns] = qv[1:2]
    bias_own[:, 3 * columns :] = hidden_bias_in[...].astype(jnp.float32)

    @pl.when(at.home)
    def _():
        bias[...] = bias_own[...]

    greet(section, sections, (at.peer, at.across, at.swap, at.beside))

    @pl.when(section == 0)
    def _():
        tokens.own.start()
        tokens.to_peer.start()

    guide = jnp.logical_and(section == 1, core == 0)
    pl.when(guide)(lambda: tokens_over().start())

    @pl.when(at.away)
    def _():
        swap_bias().start()

        @pl.when(section == 0)
        def _():
            begin(direct)
            for n in range(rounds):
                go_up(n).start()

        @pl.when(section > 1)
        def _():
            begin(direct + detour)

        @pl.when(section == 1)
        def _():
            for n in range(rounds + 1):
                if n < rounds:
                    go_up(n).wait_recv()
                    go_over(n).start()
                if n > 0:
                    go_over(n - 1).wait_recv()
                    go_down(n - 1).start()
                if n == 1:

                    @pl.when(guide)
                    def _():
                        tokens_over().wait_recv()
                        tokens_down().start()

            begin(direct + detour)

        swap_bias().wait()
        pass_on(direct[:4])

        @pl.when(section > 0)
        def _():
            pass_on(direct[4:] + detour)

    @pl.when(jnp.logical_and(guide, at.home))
    def _():
        tokens_over().wait_recv()
        tokens_down().start()

    @pl.when(section == last)
    def _():
        cotangents.own.start()
        cotangents.to_peer.start()
        cotangents.to_across.start()
        cotangents.to_across.wait()
        cotangents.forward.start()
        cotangents.own.wait()
        cotangents.to_peer.wait()
        cotangents.forward.wait()

    def hop(m, j):
        rows = pl.ds(pl.multiple_of(core * half, half), half)
        target = pl.ds(pl.multiple_of(j * chunk + core * half, half), half)
        return pltpu.make_async_remote_copy(
            src_ref=result.at[j, rows],
            dst_ref=hbuf.at[m, target],
            send_sem=hop_send.at[j],
            recv_sem=hop_got.at[m, j],
            device_id={"section": section + 1},
            device_id_type=MESH,
        )

    def hand_over(m, j):
        rows = pl.ds(pl.multiple_of(j * chunk + core * half, half), half)
        return pltpu.make_async_remote_copy(
            src_ref=hbuf.at[m, rows],
            dst_ref=hbuf.at[m, rows],
            send_sem=pass_send.at[m, j],
            recv_sem=pass_got.at[m, j],
            device_id=peer,
            device_id_type=MESH,
        )

    def exchange_a(m, j):
        slot = j
        return pltpu.make_async_remote_copy(
            src_ref=send_a.at[slot],
            dst_ref=got_a.at[j],
            send_sem=a_send.at[slot],
            recv_sem=a_got.at[m, j],
            device_id=peer,
            device_id_type=MESH,
        )

    def exchange_b(m, j):
        slot = lax.rem(j, 2)
        return pltpu.make_async_remote_copy(
            src_ref=send_b.at[slot],
            dst_ref=got_b.at[j],
            send_sem=b_send.at[slot],
            recv_sem=b_got.at[m, j],
            device_id=peer,
            device_id_type=MESH,
        )

    def keep(m, j):
        rows = rows_of(j, chunk)
        return pltpu.make_async_copy(
            hbuf.at[m, rows], inputs_out.at[m, rows], keep_sem.at[m, j]
        )

    def keep_qkv(m, j):
        rows = rows_of(j, chunk)
        return pltpu.make_async_copy(qkv.at[rows], qkv_out.at[m, rows], qkv_sem.at[j])

    def keep_first(m, j):
        rows = rows_of(j, chunk)
        return [
            pltpu.make_async_copy(mixed.at[j], mixed_out.at[m, rows], first_sem.at[0]),
            pltpu.make_async_copy(stat, stat_out.at[m, rows], first_sem.at[1]),
        ]

    def keep_second(m, j):
        rows = rows_of(j, chunk)
        return [
            pltpu.make_async_copy(low_mid, middle_out.at[m, rows], second_sem.at[0]),
            pltpu.make_async_copy(hidden, hidden_out.at[m, rows], second_sem.at[1]),
            pltpu.make_async_copy(slope, slope_out.at[m, rows], second_sem.at[2]),
            pltpu.make_async_copy(scale_a, scale_out.at[m, 0, rows], second_sem.at[3]),
        ]

    def keep_third(m, j):
        rows = rows_of(j, chunk)
        return [
            pltpu.make_async_copy(result.at[j], result_out.at[m, rows], third_sem.at[j]),
            pltpu.make_async_copy(scale_z.at[j], scale_out.at[m, 1, rows], scale_sem.at[j]),
        ]

    def arrive(m, j):
        hop(m, j).wait_recv()
        hand_over(m, j).start()

    def project(m, j):
        rows = rows_of(j, chunk)

        starts, moment = row_facts(at, own_ref, other_ref, m)

        @pl.when(section == 0)
        def _():
            fraction = jnp.full((1, width), moment.astype(jnp.float32)) / 5000.0
            times = time_in[...].astype(jnp.float32)
            hbuf[m, rows] = (
                hbuf[m, rows].astype(jnp.float32) + fraction * times[0:1] + times[1:2]
            ).astype(low_type)

        @pl.when(section > 0)
        def _():
            @pl.when(j + 1 < chunks)
            def _():
                arrive(m, j + 1)

            hand_over(m, j).wait_recv()

        keep(m, j).start()

        @pl.when(m > 0)
        def _():
            keep_qkv(m - 1, j).wait()

        for third in range(3):
            part = slice(third * columns, (third + 1) * columns)
            qkv[rows, part] = (dot_plain(hbuf[m, rows], wq[third]) + bias[:, part]).astype(low_type)
        keep_qkv(m, j).start()
        first, rel, own = doc_lanes(starts, j * chunk, shape)
        extra = jnp.where(own, 1.0, 0.0).astype(low_type)
        ones = jnp.ones(shape, low_type)
        for p in range(pairs):
            k = qkv[rows, columns + p * LANES : columns + (p + 1) * LANES]
            v = qkv[rows, 2 * columns + p * LANES : 2 * columns + (p + 1) * LANES]
            keys[2 * p, rows] = jnp.where(first, k, extra)
            keys[2 * p + 1, rows] = jnp.where(first, extra, k)
            values[2 * p, rows] = jnp.where(first, v, ones)
            values[2 * p + 1, rows] = jnp.where(first, ones, v)

    def mix(m, j):
        rows = rows_of(j, chunk)
        starts, _ = row_facts(at, own_ref, other_ref, m)
        first, rel, own = doc_lanes(starts, j * chunk, shape)
        extra = jnp.where(
            jnp.logical_and(rel < count, jnp.logical_not(own)), MASKED, 0.0
        ).astype(low_type)

        def scores(index):
            p = index // 2
            q = qkv[rows, p * LANES : (p + 1) * LANES] * low_type(HEAD**-0.5)
            q = jnp.where(first, q, extra) if index % 2 == 0 else jnp.where(first, extra, q)
            return dot_rows(q, keys[index])

        current = scores(0)
        peaks, sums = [], []
        for index in range(2 * pairs):
            later = scores(index + 1) if index + 1 < 2 * pairs else None
            peak = jnp.max(current, axis=-1, keepdims=True)
            powers = jnp.exp(current - peak).astype(low_type)
            peaks.append(peak)
            sums.append(dot_plain(powers, values[index]))
            current = later
            if index % 2 == 1:
                lane = slice((index // 2) * LANES, (index // 2 + 1) * LANES)
                total = jnp.where(first, sums[index], sums[index - 1])
                log_sum = jnp.where(first, peaks[index], peaks[index - 1]) + jnp.log(total)
                stat[:, lane] = lanes(rel, count, -log_sum, extra)
                mixed[j, :, lane] = (
                    jnp.where(first, sums[index - 1], sums[index]) / pltpu.roll(total, HEAD, 1)
                ).astype(low_type)
        for copy in keep_first(m, j):
            copy.start()

    def branch(m, j):
        send_a[j] = dot_plain(mixed[j], wo[...]).astype(low_type)
        exchange_a(m, j).start()

    def feed(m, j):
        rows = rows_of(j, chunk)
        slot = lax.rem(j, 2)
        exchange_a(m, j).wait()
        total = (
            send_a[j].astype(jnp.float32)
            + got_a[j].astype(jnp.float32)
            + biases[0:1]
            + hbuf[m, rows].astype(jnp.float32)
        )
        unit, inv_scale = norm_rows(total)
        scale_a[...] = jnp.broadcast_to(inv_scale, shape)
        middle = unit * gains[0:1] + biases[1:2]
        high_mid[slot] = middle
        low_mid[...] = middle.astype(low_type)
        hidden_size = wi.shape[1]
        step = min(1024, hidden_size)

        def before(start):
            part = slice(start, start + step)
            return dot_plain(low_mid[...], wi[:, part]) + bias[:, 3 * columns + start : 3 * columns + start + step]

        pre = before(0)
        branch = jnp.zeros((chunk, width), jnp.float32)
        for start in range(0, hidden_size, step):
            part = slice(start, start + step)
            later = before(start + step) if start + step < hidden_size else None
            normal, density = erf_pair(pre)
            hidden[:, part] = (pre * normal).astype(low_type)
            slope[:, part] = (normal + pre * density).astype(low_type)
            branch = branch + dot_plain(hidden[:, part], wd[part])
            pre = later
        send_b[slot] = branch.astype(low_type)
        exchange_b(m, j).start()
        for copy in keep_second(m, j):
            copy.start()

    def finish(m, j):
        slot = lax.rem(j, 2)
        exchange_b(m, j).wait()
        total = (
            send_b[slot].astype(jnp.float32)
            + got_b[j].astype(jnp.float32)
            + biases[2:3]
            + high_mid[slot]
        )
        unit, inv_scale = norm_rows(total)
        @pl.when(m > 0)
        def _():
            finish_wait(m - 1, j)

        scale_z[j] = jnp.broadcast_to(inv_scale, shape)
        result[j] = (unit * gains[1:2] + biases[3:4]).astype(low_type)

        @pl.when(section < sections - 1)
        def _():
            hop(m, j).start()

        placed.start(m, j)
        for copy in keep_third(m, j):
            copy.start()

    def finish_wait(m, j):
        for copy in keep_third(m, j):
            copy.wait()

        placed.wait(m, j)

        @pl.when(section < sections - 1)
        def _():
            hop(m, j).wait_send()

    def one_row(m, carry):
        @pl.when(jnp.logical_and(section == 0, core == m))
        def _():
            tokens.own.wait()

            @pl.when(core == 0)
            def _():
                tokens_down().wait_recv()

            @pl.when(core > 0)
            def _():
                tokens.to_across.wait_recv()

            tokens.forward.start()

        @pl.when(jnp.logical_and(section == 0, core != m))
        def _():
            tokens.to_peer.wait_recv()
            tokens.forward.wait_recv()

        @pl.when(m == 0)
        def _():
            ready(0)

        @pl.when(jnp.logical_and(section == 0, core == m))
        def _():
            tokens.forward.wait_send()

        @pl.when(section > 0)
        def _():
            arrive(m, 0)

        opening = jnp.logical_and(m == 0, jnp.logical_and(section == 0, at.away))

        @pl.when(opening)
        def _():
            pass_on(direct[4:5])

        def first_step(j, carry):
            project(m, j)

            @pl.when(jnp.logical_and(opening, j == 0))
            def _():
                pass_on(direct[5:6])

            return carry

        lax.fori_loop(0, chunks, first_step, 0)

        @pl.when(jnp.logical_and(m == 0, section > 0))
        def _():
            ready(1)

        @pl.when(opening)
        def _():
            pass_on(direct[6:7])

        lag = jnp.where(jnp.logical_and(section == 0, m == 0), chunks, 1)

        def step(i, carry):
            j = i - lag

            @pl.when(jnp.logical_and(i >= 1, i <= chunks))
            def _():
                for copy in keep_first(m, i - 1):
                    copy.wait()

            @pl.when(i < chunks)
            def _():
                mix(m, i)

                @pl.when(lag == 1)
                def _():
                    branch(m, i)

            for turn, k in enumerate(direct[7:]):

                @pl.when(jnp.logical_and(opening, i == turn))
                def _(k=k):
                    pass_on([k])

            @pl.when(
                jnp.logical_and(
                    jnp.logical_and(section == 0, core > 0),
                    jnp.logical_and(m == 0, i == chunks - 1),
                )
            )
            def _():
                tokens.to_across.start()

            @pl.when(jnp.logical_and(lag > 1, j == 0))
            def _():
                ready(1)
                for turn in range(chunks):
                    branch(m, turn)

            @pl.when(jnp.logical_and(m == 0, j == 0))
            def _():
                ready(2)
                ready(3)

            @pl.when(jnp.logical_and(j >= 1, j <= chunks))
            def _():
                for copy in keep_second(m, j - 1):
                    copy.wait()

            @pl.when(j >= 1)
            def _():
                finish(m, j - 1)

            @pl.when(jnp.logical_and(j >= 0, j < chunks))
            def _():
                feed(m, j)

            return carry

        lax.fori_loop(0, chunks + lag + 1, step, 0)

        @pl.when(m == 0)
        def _():
            for copy in keep_weights:
                copy.start()

        return carry

    keep_weights = [
        pltpu.make_async_copy(source, target, w_sem.at[i])
        for i, (source, target) in enumerate(zip(held, (wq_out, wo_out, wi_out, wd_out)))
    ]
    lax.fori_loop(0, micro, one_row, 0)
    for copy in keep_weights:
        copy.wait()
    for j in range(chunks):
        finish_wait(micro - 1, j)
        keep_qkv(micro - 1, j).wait()
    for m in range(micro):
        for j in range(chunks):
            keep(m, j).wait()
    placed.wait_got()

    @pl.when(at.away)
    def _():
        for k in direct:
            swap(k).wait_send()
            relay(k).wait_send()

        @pl.when(section > 0)
        def _():
            for k in detour:
                swap(k).wait_send()
                relay(k).wait_send()

        for n in range(rounds):

            @pl.when(section == 0)
            def _(n=n):
                go_up(n).wait_send()

            @pl.when(section == 1)
            def _(n=n):
                go_over(n).wait_send()
                go_down(n).wait_send()

    @pl.when(guide)
    def _():
        tokens_over().wait_send()
        tokens_down().wait_send()

    @pl.when(section == 0)
    def _():
        tokens.to_peer.wait_send()

        @pl.when(core > 0)
        def _():
            tokens.to_across.wait_send()

    @pl.when(section > 0)
    def _():
        for m in range(micro):
            for j in range(chunks):
                hand_over(m, j).wait_send()


def forward_pass(sections, facts, vectors, tokens, cotangent, weights):
    wq, wo, wi, wd = weights
    micro, tile, width = tokens.shape
    length = 2 * tile
    columns, hidden = wo.shape[0], wi.shape[1]
    chunk = min(256, length // 4)
    chunks = length // chunk
    low, high = low_type, jnp.float32

    def out(*shape, dtype=low):
        return jax.ShapeDtypeStruct(shape, dtype)

    outs = dict(
        qkv=out(micro, length, 3 * columns),
        log_sums=out(micro, length, columns),
        mixed=out(micro, length, columns),
        middle=out(micro, length, width),
        hidden=out(micro, length, hidden),
        slope=out(micro, length, hidden),
        inputs=out(micro, length, width),
        result=out(micro, length, width),
        scales=out(micro, 2, length, LANES, dtype=high),
        placed=out(*tokens.shape),
        rows_back=out(micro, length, width),
        wq=out(*wq.shape),
        wo=out(*wo.shape),
        wi=out(*wi.shape),
        wd=out(*wd.shape),
    )
    vmem = pl.BlockSpec(memory_space=pltpu.VMEM)
    anywhere = pl.BlockSpec(memory_space=pl.ANY)
    dma = pltpu.SemaphoreType.DMA
    pieces = len(weight_pieces(*weights))
    rounds = 4
    results = pl.pallas_call(
        functools.partial(forward_kernel, sections, chunk),
        in_specs=[pl.BlockSpec(memory_space=pltpu.SMEM)] * 2 + [vmem] * 5 + [anywhere] * 6,
        out_specs=[anywhere] * len(outs),
        out_shape=list(outs.values()),
        scratch_shapes=[
            pltpu.VMEM(wq.shape, low),
            pltpu.VMEM(wo.shape, low),
            pltpu.VMEM(wi.shape, low),
            pltpu.VMEM(wd.shape, low),
            pltpu.VMEM((1, 3 * columns + hidden), high),
            pltpu.VMEM((1, 3 * columns + hidden), high),
            pltpu.VMEM(vectors[2].shape, high),
            pltpu.VMEM(vectors[3].shape, high),
            pltpu.VMEM((micro, length, width), low),
            pltpu.VMEM((length, 3 * columns), low),
            pltpu.VMEM((columns // HEAD, length, LANES), low),
            pltpu.VMEM((columns // HEAD, length, LANES), low),
            pltpu.VMEM((chunks, chunk, columns), low),
            pltpu.VMEM((chunk, columns), low),
            pltpu.VMEM((chunks, chunk, width), low),
            pltpu.VMEM((2, chunk, width), low),
            pltpu.VMEM((chunks, chunk, width), low),
            pltpu.VMEM((chunks, chunk, width), low),
            pltpu.VMEM((2, chunk, width), high),
            pltpu.VMEM((chunk, width), low),
            pltpu.VMEM((chunk, hidden), low),
            pltpu.VMEM((chunk, hidden), low),
            pltpu.VMEM((chunks, chunk, width), low),
            pltpu.VMEM((chunk, LANES), high),
            pltpu.VMEM((chunks, chunk, LANES), high),
            dma((4,)),
            dma((pieces,)),
            dma((pieces,)),
            dma((pieces,)),
            dma((pieces,)),
            pltpu.VMEM((rounds, hidden // 8, width), low),
            pltpu.VMEM((rounds, hidden // 8, width), low),
            pltpu.VMEM((tile, width), low),
            dma((4, rounds)),
            dma((4, rounds)),
            dma((2,)),
            dma,
            dma((3,)),
            dma((3,)),
            dma,
            dma((3,)),
            dma((3,)),
            dma((chunks,)),
            dma((micro, chunks)),
            dma((micro, chunks)),
            dma((micro, chunks)),
            dma((micro, chunks)),
            dma((chunks,)),
            dma((chunks,)),
            dma((micro, chunks)),
            dma((2,)),
            dma((micro, chunks)),
            dma((2,)),
            dma((4,)),
            dma((chunks,)),
            dma((chunks,)),
            dma((chunks,)),
            dma((chunks,)),
            dma((chunks // 2,)),
        ],
        compiler_params=pltpu.CompilerParams(
            collective_id=0, has_side_effects=True, vmem_limit_bytes=62 * 1024 * 1024
        ),
        name="forward_pass",
    )(*facts, *vectors, tokens, cotangent, *weights)
    return dict(zip(outs, results))


def greet(section, sections, partners):
    barrier = pltpu.get_barrier_semaphore()
    for partner in partners:
        pl.semaphore_signal(barrier, inc=1, device_id=partner, device_id_type=MESH)

    @pl.when(section > 0)
    def _():
        pl.semaphore_signal(
            barrier, inc=1, device_id={"section": section - 1}, device_id_type=MESH
        )

    @pl.when(section < sections - 1)
    def _():
        pl.semaphore_signal(
            barrier, inc=1, device_id={"section": section + 1}, device_id_type=MESH
        )

    inner = jnp.logical_and(section > 0, section < sections - 1)

    @pl.when(inner)
    def _():
        pl.semaphore_wait(barrier, len(partners) + 2)

    @pl.when(jnp.logical_not(inner))
    def _():
        pl.semaphore_wait(barrier, len(partners) + 1)


class Seat:
    def __init__(self):
        self.section = lax.axis_index("section")
        self.group = lax.axis_index("tensor")
        dp = lax.axis_index("dp")
        self.core = lax.rem(dp, 2)
        self.chip = dp // 2
        other = dp + 1 - 2 * self.core
        self.peer = {"dp": other}
        self.across = {"tensor": 1 - self.group}
        self.swap = {"tensor": 1 - self.group, "dp": other}
        self.beside = {"dp": dp + 2 - 4 * self.chip}
        self.home = self.group == self.core
        self.away = self.group != self.core


def row_facts(at, own_ref, other_ref, m):
    facts = [
        jnp.where(at.core == m, own_ref[at.group, j], other_ref[at.group, j])
        for j in range(own_ref.shape[1])
    ]
    return facts[:-1], facts[-1]


def remote(source, target, send_sem, recv_sem, device):
    return pltpu.make_async_remote_copy(
        src_ref=source,
        dst_ref=target,
        send_sem=send_sem,
        recv_sem=recv_sem,
        device_id=device,
        device_id_type=MESH,
    )


class RowPieces:
    def __init__(self, at, source, target, local, send, got):
        tile = source.shape[1]

        def half(group):
            return pl.ds(pl.multiple_of(group * tile, tile), tile)

        own = target.at[at.core, half(at.group)]
        other = target.at[at.core, half(1 - at.group)]
        mine = source.at[at.group]
        self.own = pltpu.make_async_copy(mine, own, local)
        self.to_peer = remote(mine, own, send.at[0], got.at[0], at.peer)
        self.to_across = remote(source.at[1 - at.group], own, send.at[1], got.at[1], at.across)
        self.forward = remote(other, other, send.at[2], got.at[2], at.peer)


class OutPieces:
    def __init__(self, at, rows, target, local, send, got):
        self.at, self.rows, self.target = at, rows, target
        self.local, self.send, self.got = local, send, got
        self.chunks, self.chunk = rows.shape[0], rows.shape[1]
        self.per = self.chunks // 2

    def copies(self, m, j):
        place = rows_of(lax.rem(j, self.per), self.chunk)
        spot = self.target.at[self.at.group, place]
        near = pltpu.make_async_copy(self.rows.at[j], spot, self.local.at[j])
        far = remote(
            self.rows.at[j],
            spot,
            self.send.at[j],
            self.got.at[lax.rem(j, self.per)],
            self.at.across,
        )
        mine = self.at.core == m
        stays = j // self.per == self.at.group
        return (
            (jnp.logical_and(mine, stays), near, near.wait),
            (jnp.logical_and(mine, jnp.logical_not(stays)), far, far.wait_send),
        )

    def start(self, m, j):
        for condition, copy, _ in self.copies(m, j):
            pl.when(condition)(copy.start)

    def wait(self, m, j):
        for condition, _, wait in self.copies(m, j):
            pl.when(condition)(wait)

    def wait_got(self):
        for j in range(self.per):
            remote(
                self.rows.at[j],
                self.target.at[1 - self.at.group, pl.ds(j * self.chunk, self.chunk)],
                self.send.at[j],
                self.got.at[j],
                self.at.across,
            ).wait_recv()


def weight_pieces(wq, wo, wi, wd):
    pieces = []

    def split(index, rows, count, lead=()):
        size = rows // 2 // count
        for i in range(count):

            def where(ref, chip, i=i):
                start = pl.multiple_of(chip * (rows // 2) + i * size, size)
                return ref.at[lead + (pl.ds(start, size),)]

            pieces.append((index, where))

    for k in range(wq.shape[0]):
        split(0, wq.shape[1], 1, (k,))
    split(1, wo.shape[0], 1)
    split(2, wi.shape[0], 4)
    split(3, wd.shape[0], 4)
    return pieces


def backward_kernel(
    sections,
    chunk,
    own_ref,
    other_ref,
    gains_in,
    biases_in,
    rows_back,
    qkv_w,
    out_w,
    in_w,
    down_w,
    qkv_in,
    stat_in,
    mixed_in,
    middle_in,
    slope_in,
    result_in,
    scale_in,
    row_sums,
    in_sums,
    qkv_sums,
    time_sums,
    gz_out,
    pre_out,
    ga_out,
    gqkv_out,
    grads_out,
    wq,
    wo,
    wi,
    wd,
    gains,
    biases,
    gbuf,
    high_ga,
    qkv,
    keys,
    values,
    grad_k,
    grad_v,
    grad_qkv,
    send_a,
    send_b,
    got_a,
    got_b,
    high_gz,
    low_gz,
    low_pre,
    low_ga,
    grad_mixed,
    grads,
    result,
    slope,
    scale_z,
    middle,
    scale_a,
    mixed,
    stat,
    w_sem,
    load_sem,
    hop_send,
    hop_got,
    pass_send,
    pass_got,
    a_send,
    a_got,
    b_send,
    b_got,
    qkv_sem,
    first_sem,
    second_sem,
    keep_sem,
    keep_ga_sem,
    keep_qkv_sem,
    grads_sem,
    out_send,
    out_got,
):
    at = Seat()
    section, core, peer = at.section, at.core, at.peer
    micro, length, width = gbuf.shape
    count = own_ref.shape[1] - 1
    columns = grad_mixed.shape[1]
    pairs = columns // LANES
    chunks = length // chunk
    half = chunk // 2
    last = sections - 1
    shape = (chunk, LANES)

    weights = [
        pltpu.make_async_copy(source, target, w_sem.at[i])
        for i, (source, target) in enumerate(
            ((down_w, wd), (in_w, wi), (out_w, wo), (qkv_w, wq))
        )
    ]
    for copy in weights:
        copy.start()

    def load(m, j):
        rows = rows_of(j, chunk)
        return pltpu.make_async_copy(
            rows_back.at[m, rows], gbuf.at[m, rows], load_sem.at[m, j]
        )

    def hop(m, j):
        target = pl.ds(pl.multiple_of(j * chunk + core * half, half), half)
        return pltpu.make_async_remote_copy(
            src_ref=grads.at[j, pl.ds(pl.multiple_of(core * half, half), half)],
            dst_ref=gbuf.at[m, target],
            send_sem=hop_send.at[j],
            recv_sem=hop_got.at[m, j],
            device_id={"section": section - 1},
            device_id_type=MESH,
        )

    def hand_over(m, j):
        rows = pl.ds(pl.multiple_of(j * chunk + core * half, half), half)
        return pltpu.make_async_remote_copy(
            src_ref=gbuf.at[m, rows],
            dst_ref=gbuf.at[m, rows],
            send_sem=pass_send.at[m, j],
            recv_sem=pass_got.at[m, j],
            device_id=peer,
            device_id_type=MESH,
        )

    def exchange(send, got, send_sem, got_sem, m, j):
        slot = lax.rem(j, 2)
        return pltpu.make_async_remote_copy(
            src_ref=send.at[slot],
            dst_ref=got.at[j],
            send_sem=send_sem.at[slot],
            recv_sem=got_sem.at[m, j],
            device_id=peer,
            device_id_type=MESH,
        )

    def exchange_a(m, j):
        return exchange(send_a, got_a, a_send, a_got, m, j)

    def exchange_b(m, j):
        return exchange(send_b, got_b, b_send, b_got, m, j)

    def load_qkv(m):
        return pltpu.make_async_copy(qkv_in.at[m], qkv, qkv_sem)

    def load_first(m, j):
        rows = rows_of(j, chunk)
        slot = lax.rem(j, 2)
        return [
            pltpu.make_async_copy(result_in.at[m, rows], result.at[slot], first_sem.at[slot, 0]),
            pltpu.make_async_copy(slope_in.at[m, rows], slope.at[slot], first_sem.at[slot, 1]),
            pltpu.make_async_copy(scale_in.at[m, 1, rows], scale_z.at[slot], first_sem.at[slot, 2]),
        ]

    def load_second(m, j):
        rows = rows_of(j, chunk)
        return [
            pltpu.make_async_copy(middle_in.at[m, rows], middle, second_sem.at[0]),
            pltpu.make_async_copy(scale_in.at[m, 0, rows], scale_a, second_sem.at[1]),
            pltpu.make_async_copy(mixed_in.at[m, rows], mixed, second_sem.at[2]),
            pltpu.make_async_copy(stat_in.at[m, rows], stat, second_sem.at[3]),
        ]

    def keep_first(m, j):
        rows = rows_of(j, chunk)
        slot = lax.rem(j, 2)
        return [
            pltpu.make_async_copy(low_gz.at[slot], gz_out.at[m, rows], keep_sem.at[slot, 0]),
            pltpu.make_async_copy(low_pre.at[slot], pre_out.at[m, rows], keep_sem.at[slot, 1]),
        ]

    def keep_second(m, j):
        rows = rows_of(j, chunk)
        return pltpu.make_async_copy(low_ga, ga_out.at[m, rows], keep_ga_sem)

    def keep_qkv(m):
        return pltpu.make_async_copy(grad_qkv, gqkv_out.at[m], keep_qkv_sem)

    placed = OutPieces(at, grads, grads_out, grads_sem, out_send, out_got)

    load_qkv(0).start()
    for copy in load_first(0, 0) + load_first(0, 1) + load_second(0, 0):
        copy.start()

    @pl.when(section == last)
    def _():
        for m in range(micro):
            for j in range(chunks):
                load(m, j).start()

    gains[...] = gains_in[...].astype(jnp.float32)
    biases[...] = biases_in[...].astype(jnp.float32)
    row_sums[...] = jnp.zeros_like(row_sums)
    in_sums[...] = jnp.zeros_like(in_sums)
    qkv_sums[...] = jnp.zeros_like(qkv_sums)
    time_sums[...] = jnp.zeros_like(time_sums)
    greet(section, sections, (at.peer, at.across))

    def add_row(index, value):
        row_sums[index : index + 1] += jnp.sum(value, axis=0, keepdims=True)

    def receive(m, j):
        @pl.when(section < last)
        def _():
            hop(m, j).wait_recv()
            hand_over(m, j).start()

    def norm_back_rows(gradient, unit, inv_scale, gain):
        weighted = gradient * gain
        return inv_scale * (
            weighted
            - jnp.mean(weighted, axis=-1, keepdims=True)
            - unit * jnp.mean(weighted * unit, axis=-1, keepdims=True)
        )

    def feed_back(m, j):
        rows = rows_of(j, chunk)
        slot = lax.rem(j, 2)

        @pl.when(section == last)
        def _():
            load(m, j).wait()

        @pl.when(section < last)
        def _():
            hand_over(m, j).wait_recv()

        for copy in load_first(m, j):
            copy.wait()
        gradient = gbuf[m, rows].astype(jnp.float32)
        unit = (result[slot].astype(jnp.float32) - biases[3:4]) / gains[1:2]
        grad_z = norm_back_rows(gradient, unit, scale_z[slot, :, :1], gains[1:2])
        add_row(1, gradient * unit)
        add_row(5, gradient)
        add_row(4, grad_z)
        high_gz[slot] = grad_z
        low_gz[slot] = grad_z.astype(low_type)
        hidden_size = wi.shape[1]
        step = min(1024, hidden_size)

        def before(start):
            return dot_rows(low_gz[slot], wd[start : start + step])

        current = before(0)
        branch = jnp.zeros((chunk, width), jnp.float32)
        for start in range(0, hidden_size, step):
            part = slice(start, start + step)
            later = before(start + step) if start + step < hidden_size else None
            low = (current * slope[slot, :, part].astype(jnp.float32)).astype(low_type)
            low_pre[slot, :, part] = low
            in_sums[:, part] += jnp.sum(low.astype(jnp.float32), axis=0, keepdims=True)
            branch = branch + dot_rows(low, wi[:, part])
            current = later
        send_a[slot] = branch.astype(low_type)
        exchange_a(m, j).start()
        for copy in keep_first(m, j):
            copy.start()

    def norm_step(m, j):
        rows = rows_of(j, chunk)
        slot = lax.rem(j, 2)
        exchange_a(m, j).wait()
        for copy in load_second(m, j):
            copy.wait()
        gradient = (
            send_a[slot].astype(jnp.float32) + got_a[j].astype(jnp.float32) + high_gz[slot]
        )
        unit = (middle[...].astype(jnp.float32) - biases[1:2]) / gains[0:1]
        grad_a = norm_back_rows(gradient, unit, scale_a[:, :1], gains[0:1])
        add_row(0, gradient * unit)
        add_row(3, gradient)
        add_row(2, grad_a)
        high_ga[rows] = grad_a
        low_ga[...] = grad_a.astype(low_type)
        keep_second(m, j).start()
        grad_mixed[...] = dot_rows(low_ga[...], wo[...]).astype(low_type)

    def build(m):
        load_qkv(m).wait()

        starts, _ = row_facts(at, own_ref, other_ref, m)

        def step(j, carry):
            rows = rows_of(j, chunk)
            first, rel, own = doc_lanes(starts, j * chunk, shape)
            fixed = jnp.logical_and(rel >= count, rel < count + 3)
            extra_k = jnp.where(jnp.logical_or(own, fixed), 1.0, 0.0).astype(low_type)
            extra_v = jnp.where(fixed, 1.0, 0.0).astype(low_type)
            for p in range(pairs):
                lane = slice(p * LANES, (p + 1) * LANES)
                k = qkv[rows, columns + p * LANES : columns + (p + 1) * LANES]
                v = qkv[rows, 2 * columns + p * LANES : 2 * columns + (p + 1) * LANES]
                keys[2 * p, rows] = jnp.where(first, k, extra_k)
                keys[2 * p + 1, rows] = jnp.where(first, extra_k, k)
                values[2 * p, rows] = jnp.where(first, v, extra_v)
                values[2 * p + 1, rows] = jnp.where(first, extra_v, v)
                grad_k[rows, lane] = jnp.zeros(shape, jnp.float32)
                grad_v[rows, lane] = jnp.zeros(shape, jnp.float32)
            return carry

        lax.fori_loop(0, chunks, step, 0)

    def mix_back(m, j):
        rows = rows_of(j, chunk)
        lane_index = lax.broadcasted_iota(jnp.int32, shape, 1)
        first = lane_index < HEAD
        rel = lane_index % HEAD
        all_first = lax.broadcasted_iota(jnp.int32, (length, LANES), 1) < HEAD
        for p in range(pairs):
            lane = slice(p * LANES, (p + 1) * LANES)
            q = qkv[rows, lane] * low_type(HEAD**-0.5)
            k = qkv[:, columns + p * LANES : columns + (p + 1) * LANES]
            g = grad_mixed[:, lane]
            extra_q = stat[:, lane]
            product = g.astype(jnp.float32) * mixed[:, lane].astype(jnp.float32)
            dots = [
                jnp.sum(jnp.where(first, product, 0.0), axis=-1, keepdims=True),
                jnp.sum(jnp.where(first, 0.0, product), axis=-1, keepdims=True),
            ]
            extra_g = lanes(
                rel, count, -jnp.where(first, dots[1], dots[0]), jnp.zeros_like(extra_q)
            )
            parts = []
            for i in range(2):
                q_head = jnp.where(first, q, extra_q) if i == 0 else jnp.where(first, extra_q, q)
                g_head = jnp.where(first, g, extra_g) if i == 0 else jnp.where(first, extra_g, g)
                probs = jnp.exp(dot_rows(keys[2 * p + i], q_head))
                slopes = (probs * dot_rows(values[2 * p + i], g_head)).astype(low_type)
                parts.append(
                    (
                        dot_plain(probs.astype(low_type), g),
                        dot_plain(slopes, q),
                        dot_first(slopes, k),
                    )
                )
            grad_v[:, lane] += jnp.where(all_first, parts[0][0], parts[1][0])
            grad_k[:, lane] += jnp.where(all_first, parts[0][1], parts[1][1])
            grad_qkv[rows, lane] = (
                jnp.where(first, parts[0][2], parts[1][2]) * (HEAD**-0.5)
            ).astype(low_type)

    def project_back(m, j):
        rows = rows_of(j, chunk)
        low = grad_qkv[rows]
        qkv_sums[...] += jnp.sum(low.astype(jnp.float32), axis=0, keepdims=True)
        total = dot_rows(low[:, :columns], wq[0])
        for third in range(1, 3):
            total = total + dot_rows(low[:, third * columns : (third + 1) * columns], wq[third])
        send_b[lax.rem(j, 2)] = total.astype(low_type)
        exchange_b(m, j).start()

    def finish(m, j):
        rows = rows_of(j, chunk)
        slot = lax.rem(j, 2)
        exchange_b(m, j).wait()

        @pl.when(m > 0)
        def _():
            placed.wait(m - 1, j)

            @pl.when(section > 0)
            def _():
                hop(m - 1, j).wait_send()

        total = (
            send_b[slot].astype(jnp.float32) + got_b[j].astype(jnp.float32) + high_ga[rows]
        ).astype(low_type)
        grads[j] = total
        time_sums[m] += jnp.sum(total.astype(jnp.float32), axis=0, keepdims=True)

        @pl.when(section > 0)
        def _():
            hop(m, j).start()

        placed.start(m, j)

    def one_row(m, carry):
        @pl.when(m == 0)
        def _():
            weights[0].wait()
            weights[1].wait()

        receive(m, 0)

        def first_step(j, carry):
            @pl.when(j >= 2)
            def _():
                for copy in keep_first(m, j - 2):
                    copy.wait()

            feed_back(m, j)

            @pl.when(j + 2 < chunks)
            def _():
                for copy in load_first(m, j + 2):
                    copy.start()

            @pl.when(jnp.logical_and(j + 2 >= chunks, m + 1 < micro))
            def _():
                for copy in load_first(m + 1, j + 2 - chunks):
                    copy.start()

            return carry

        def reached(i):
            return jnp.minimum(i * (i + 1) // 2, chunks)

        def step(i, carry):
            @pl.when(i >= 1)
            def _():
                @pl.when(i >= 2)
                def _():
                    keep_second(m, i - 2).wait()

                norm_step(m, i - 1)

                @pl.when(i == 1)
                def _():
                    receive(m, 1)

                @pl.when(i == 2)
                def _():
                    receive(m, 3)

                mix_back(m, i - 1)

                @pl.when(i < chunks)
                def _():
                    for copy in load_second(m, i):
                        copy.start()

                @pl.when(jnp.logical_and(i == chunks, m + 1 < micro))
                def _():
                    for copy in load_second(m + 1, 0):
                        copy.start()

                @pl.when(i == 1)
                def _():
                    receive(m, 2)

            lax.fori_loop(reached(i), reached(i + 1), first_step, 0)

            @pl.when(i == 0)
            def _():
                @pl.when(m == 0)
                def _():
                    weights[2].wait()
                    weights[3].wait()

                build(m)

            return carry

        lax.fori_loop(0, chunks + 1, step, 0)
        for copy in keep_first(m, chunks - 2) + keep_first(m, chunks - 1):
            copy.wait()
        keep_second(m, chunks - 1).wait()

        @pl.when(m + 1 < micro)
        def _():
            load_qkv(m + 1).start()

        grad_qkv[:, columns : 2 * columns] = grad_k[...].astype(low_type)
        grad_qkv[:, 2 * columns :] = grad_v[...].astype(low_type)
        keep_qkv(m).start()

        shift = jnp.where(jnp.logical_and(section == 0, at.group == 0), chunks // 2, 0)

        def last_step(i, carry):
            @pl.when(i < chunks)
            def _():
                project_back(m, lax.rem(i + shift, chunks))

            @pl.when(i >= 1)
            def _():
                finish(m, lax.rem(i - 1 + shift, chunks))

            return carry

        lax.fori_loop(0, chunks + 1, last_step, 0)
        keep_qkv(m).wait()
        return carry

    lax.fori_loop(0, micro, one_row, 0)
    for j in range(chunks):
        placed.wait(micro - 1, j)

    @pl.when(section > 0)
    def _():
        for j in range(chunks):
            hop(micro - 1, j).wait_send()

    @pl.when(section < last)
    def _():
        for m in range(micro):
            for j in range(chunks):
                hand_over(m, j).wait_send()
    placed.wait_got()


def backward_pass(sections, facts, gains, biases, rows_back, params, stash):
    qkv_w, out_w, in_w, down_w = params
    micro, length, width = rows_back.shape
    columns, hidden = out_w.shape[0], in_w.shape[1]
    chunk = min(256, length // 4)
    chunks = length // chunk
    low, high = low_type, jnp.float32

    def out(*shape, dtype=low):
        return jax.ShapeDtypeStruct(shape, dtype)

    outs = dict(
        row_sums=out(6, width, dtype=high),
        in_sums=out(1, hidden, dtype=high),
        qkv_sums=out(1, 3 * columns, dtype=high),
        time_sums=out(micro, 1, width, dtype=high),
        grad_z=out(micro, length, width),
        grad_pre=out(micro, length, hidden),
        grad_a=out(micro, length, width),
        grad_qkv=out(micro, length, 3 * columns),
        grads=out(micro, length // 2, width),
    )
    vmem = pl.BlockSpec(memory_space=pltpu.VMEM)
    anywhere = pl.BlockSpec(memory_space=pl.ANY)
    dma = pltpu.SemaphoreType.DMA
    results = pl.pallas_call(
        functools.partial(backward_kernel, sections, chunk),
        in_specs=[pl.BlockSpec(memory_space=pltpu.SMEM)] * 2 + [vmem] * 2 + [anywhere] * 12,
        out_specs=[vmem] * 4 + [anywhere] * 5,
        out_shape=list(outs.values()),
        scratch_shapes=[
            pltpu.VMEM(qkv_w.shape, low),
            pltpu.VMEM(out_w.shape, low),
            pltpu.VMEM(in_w.shape, low),
            pltpu.VMEM(down_w.shape, low),
            pltpu.VMEM(gains.shape, high),
            pltpu.VMEM(biases.shape, high),
            pltpu.VMEM((micro, length, width), low),
            pltpu.VMEM((length, width), high),
            pltpu.VMEM((length, 3 * columns), low),
            pltpu.VMEM((columns // HEAD, length, LANES), low),
            pltpu.VMEM((columns // HEAD, length, LANES), low),
            pltpu.VMEM((length, columns), high),
            pltpu.VMEM((length, columns), high),
            pltpu.VMEM((length, 3 * columns), low),
            pltpu.VMEM((2, chunk, width), low),
            pltpu.VMEM((2, chunk, width), low),
            pltpu.VMEM((chunks, chunk, width), low),
            pltpu.VMEM((chunks, chunk, width), low),
            pltpu.VMEM((2, chunk, width), high),
            pltpu.VMEM((2, chunk, width), low),
            pltpu.VMEM((2, chunk, hidden), low),
            pltpu.VMEM((chunk, width), low),
            pltpu.VMEM((chunk, columns), low),
            pltpu.VMEM((chunks, chunk, width), low),
            pltpu.VMEM((2, chunk, width), low),
            pltpu.VMEM((2, chunk, hidden), low),
            pltpu.VMEM((2, chunk, LANES), high),
            pltpu.VMEM((chunk, width), low),
            pltpu.VMEM((chunk, LANES), high),
            pltpu.VMEM((chunk, columns), low),
            pltpu.VMEM((chunk, columns), low),
            dma((4,)),
            dma((micro, chunks)),
            dma((chunks,)),
            dma((micro, chunks)),
            dma((micro, chunks)),
            dma((micro, chunks)),
            dma((2,)),
            dma((micro, chunks)),
            dma((2,)),
            dma((micro, chunks)),
            dma,
            dma((2, 3)),
            dma((4,)),
            dma((2, 2)),
            dma,
            dma,
            dma((chunks,)),
            dma((chunks,)),
            dma((chunks // 2,)),
        ],
        compiler_params=pltpu.CompilerParams(
            collective_id=1, has_side_effects=True, vmem_limit_bytes=63 * 1024 * 1024
        ),
        name="backward_pass",
    )(
        *facts,
        gains,
        biases,
        rows_back,
        qkv_w,
        out_w,
        in_w,
        down_w,
        stash["qkv"],
        stash["log_sums"],
        stash["mixed"],
        stash["middle"],
        stash["slope"],
        stash["result"],
        stash["scales"],
    )
    return dict(zip(outs, results))


def gradient_kernel(
    sections,
    plan,
    own_ref,
    other_ref,
    row_sums,
    in_sums,
    qkv_sums,
    time_sums,
    *refs,
):
    count = len(plan)
    number = 1 + max(part[0] for part in plan)
    lefts, rights = refs[:number], refs[number : 2 * number]
    refs = refs[2 * number :]
    outs = refs[:number]
    gains_out, biases_out, qv_out, in_out, time_rows_out = refs[number : number + 5]
    refs = refs[number + 5 :]
    tiles, firsts, seconds, shares, finals = (
        refs[i * count : (i + 1) * count] for i in range(5)
    )
    (
        held,
        right,
        small_in,
        small_group,
        small_beside,
        small_out,
        other_out,
        time_out,
        left_sem,
        right_sem,
        first_send,
        first_got,
        second_send,
        second_got,
        share_send,
        share_got,
        final_sem,
        small_send,
        small_got,
    ) = refs[5 * count :]
    at = Seat()
    section, chip, core = at.section, at.chip, at.core

    def block(order):
        owner = 1 - chip if order < 2 else chip
        return 2 * owner + order % 2

    steps = []
    for w, (_, rows, _, _, _) in enumerate(plan):
        width = min(256, rows)
        for order in range(4):
            for start in range(0, rows, width):
                steps.append((w, order, start, width))

    def load_left(index):
        w, order, start, width = steps[index]
        number, rows, _, _, _ = plan[w]
        first = pl.multiple_of(block(order) * rows + start, width)
        return pltpu.make_async_copy(
            lefts[number].at[:, pl.ds(first, width)],
            held.at[index % 2, :, pl.ds(0, width)],
            left_sem.at[index % 2],
        )

    def room(w):
        return right.at[w % 2, :, pl.ds(0, plan[w][3])]

    def load_right(w):
        number, _, first, columns, _ = plan[w]
        return pltpu.make_async_copy(
            rights[number].at[:, pl.ds(first, columns)], room(w), right_sem.at[w % 2]
        )

    def send_first(w, order):
        if plan[w][4]:
            return remote(
                tiles[w].at[order],
                firsts[w].at[order],
                first_send.at[w, order],
                first_got.at[w, order],
                at.across,
            )
        return remote(
            tiles[w].at[order],
            firsts[w].at[order],
            first_send.at[w, order],
            first_got.at[w, order],
            at.beside,
        )

    def send_second(w, order):
        if plan[w][4]:
            return remote(
                tiles[w].at[order],
                seconds[w].at[order],
                second_send.at[w, order],
                second_got.at[w, order],
                at.beside,
            )
        return remote(
            tiles[w].at[2 + order],
            seconds[w].at[order],
            second_send.at[w, order],
            second_got.at[w, order],
            at.across,
        )

    def send_share(w):
        return remote(
            tiles[w].at[3 - core], shares[w], share_send.at[w], share_got.at[w], at.peer
        )

    def store_final(w):
        number, _, first, columns, _ = plan[w]
        target = outs[number]
        if len(target.shape) == 2:
            places = [(finals[w], target.at[:, pl.ds(first, columns)])]
        else:
            size = target.shape[2]
            places = [
                (finals[w].at[:, pl.ds(i * size, size)], target.at[first // size + i])
                for i in range(columns // size)
            ]
        return [
            pltpu.make_async_copy(source, place, final_sem.at[w, i])
            for i, (source, place) in enumerate(places)
        ]

    def put_final(w, value):
        finals[w][...] = value.astype(finals[w].dtype)
        for copy in store_final(w):
            copy.start()

    def high(value):
        return value.astype(jnp.float32)

    load_right(0).start()
    load_right(1).start()
    load_left(0).start()
    small_in[...] = jnp.zeros_like(small_in)
    small_in[0:6] = row_sums[...]
    weighted = jnp.zeros_like(time_sums[0])
    plain = jnp.zeros_like(time_sums[0])
    for m in range(time_sums.shape[0]):
        _, moment = row_facts(at, own_ref, other_ref, m)
        fraction = jnp.full((1, time_sums.shape[2]), moment.astype(jnp.float32)) / 5000.0
        weighted = weighted + fraction * time_sums[m]
        plain = plain + time_sums[m]
    from_first = jnp.where(section == 0, 1.0, 0.0)
    small_in[8:9] = weighted * from_first
    small_in[9:10] = plain * from_first
    width = small_in.shape[1]
    for i in range(in_sums.shape[1] // width):
        small_in[16 + i : 17 + i] = in_sums[:, i * width : (i + 1) * width]
    third = qkv_sums.shape[1] // 3
    small_in[20:21, :third] = qkv_sums[:, :third]
    small_in[20:21, third : 2 * third] = qkv_sums[:, 2 * third :]
    greet(section, sections, (at.peer, at.across, at.beside))

    small_across = remote(
        small_in, small_group, small_send.at[0], small_got.at[0], at.across
    )
    small_chips = remote(
        small_in, small_beside, small_send.at[1], small_got.at[1], at.beside
    )
    small_cores = remote(small_out, other_out, small_send.at[2], small_got.at[2], at.peer)
    time_hop = remote(
        time_out, time_out, small_send.at[3], small_got.at[3], {"section": section + 1}
    )
    small_across.start()
    seen = 0
    for w, (_, _, _, columns, across_first) in enumerate(plan):
        load_right(w).wait()
        for order in range(4):
            while seen < len(steps) and steps[seen][:2] == (w, order):
                load_left(seen).wait()
                if seen + 1 < len(steps):
                    load_left(seen + 1).start()
                _, _, start, step_width = steps[seen]
                tiles[w][order, start : start + step_width] = dot_first(
                    held[seen % 2, :, :step_width], right[w % 2, :, :columns]
                ).astype(low_type)
                seen += 1
            if across_first:
                pl.when(at.away)(send_first(w, order).start)
            elif order < 2:
                send_first(w, order).start()
        if w + 2 < count:
            load_right(w + 2).start()
        if w == 0:
            small_across.wait()
            small_in[...] += small_group[...]
            small_chips.start()
        if w == 1:
            small_chips.wait()
            small_out[...] = small_in[...] + small_beside[...]
            small_cores.start()

    @pl.when(section == 0)
    def _():
        time_out[...] = small_out[8:16]

    for w, (_, _, _, _, across_first) in enumerate(plan):
        if across_first:

            @pl.when(at.home)
            def _(w=w):
                for order in range(2):
                    send_first(w, order).wait_recv()
                    tiles[w][order] = (
                        high(tiles[w][order]) + high(firsts[w][order])
                    ).astype(low_type)
                    send_second(w, order).start()

        else:

            @pl.when(at.away)
            def _(w=w):
                for order in range(2):
                    send_first(w, order).wait_recv()
                    tiles[w][2 + order] = (
                        high(tiles[w][2 + order]) + high(firsts[w][order])
                    ).astype(low_type)
                    send_second(w, order).start()

    @pl.when(at.home)
    def _():
        for w, (_, _, _, _, across_first) in enumerate(plan):
            for order in range(2):
                send_first(w, order + 2 if across_first else order).wait_recv()
                send_second(w, order).wait_recv()

            def total(side):
                first = firsts[w][2 + side] if across_first else firsts[w][side]
                return high(tiles[w][2 + side]) + high(first) + high(seconds[w][side])

            tiles[w][3 - core] = total(1 - core).astype(low_type)
            send_share(w).start()
            put_final(w, total(core))

    @pl.when(at.away)
    def _():
        for w in range(count):
            send_share(w).wait_recv()
            put_final(w, shares[w][...])

    small_cores.wait()
    device = 4 * at.group + 2 * chip + core
    lane = pl.ds(pl.multiple_of(device * LANES, LANES), LANES)
    gains_out[...] = small_out[0:2, lane]
    biases_out[...] = small_out[2:6, lane]

    def place(source):
        quarter = 2 * chip + core
        size = third // 4
        qv_out[0:1] = source[20:21, pl.ds(pl.multiple_of(quarter * size, size), size)]
        qv_out[1:2] = source[20:21, pl.ds(pl.multiple_of(third + quarter * size, size), size)]
        size = in_out.shape[1]
        per = width // size
        spot = pl.ds(pl.multiple_of(lax.rem(quarter, per) * size, size), size)
        for i in range(4 // per):

            @pl.when(quarter // per == i)
            def _(i=i):
                in_out[...] = source[16 + i : 17 + i, spot]

    pl.when(at.home)(functools.partial(place, small_out))
    pl.when(at.away)(functools.partial(place, other_out))

    @pl.when(section > 0)
    def _():
        time_hop.wait_recv()

    @pl.when(section < sections - 1)
    def _():
        time_hop.start()
        time_hop.wait_send()

    time_rows_out[...] = time_out[0:2]
    for w, (_, _, _, _, across_first) in enumerate(plan):
        for copy in store_final(w):
            copy.wait()
        if across_first:

            @pl.when(at.away)
            def _(w=w):
                for order in range(4):
                    send_first(w, order).wait_send()

            @pl.when(at.home)
            def _(w=w):
                for order in range(2):
                    send_second(w, order).wait_send()

        else:
            for order in range(2):
                send_first(w, order).wait_send()

            @pl.when(at.away)
            def _(w=w):
                for order in range(2):
                    send_second(w, order).wait_send()

        pl.when(at.home)(send_share(w).wait_send)


def gradient_pass(sections, facts, back, lefts, rights, splits, order):
    plan = tuple(
        (number, lefts[number].shape[1] // 4, first, columns, across)
        for number, first, columns, across in order
    )
    finals = [
        (left.shape[1] // 4, right.shape[1])
        if split == 1
        else (split, left.shape[1] // 4, right.shape[1] // split)
        for left, right, split in zip(lefts, rights, splits)
    ]
    length = lefts[0].shape[0]
    low, high = low_type, jnp.float32
    width = back["row_sums"].shape[1]
    count = len(plan)
    vmem = pl.BlockSpec(memory_space=pltpu.VMEM)
    anywhere = pl.BlockSpec(memory_space=pl.ANY)
    dma = pltpu.SemaphoreType.DMA
    small = (24, width)
    hidden = back["in_sums"].shape[1]
    smalls = [
        (2, width // 8),
        (4, width // 8),
        (2, back["qkv_sums"].shape[1] // 12),
        (1, hidden // 4),
        (2, width),
    ]

    def buffers(size):
        return [pltpu.VMEM((size(part), part[1], part[3]), low) for part in plan]

    return pl.pallas_call(
        functools.partial(gradient_kernel, sections, plan),
        in_specs=[pl.BlockSpec(memory_space=pltpu.SMEM)] * 2
        + [vmem] * 4
        + [anywhere] * (2 * len(lefts)),
        out_specs=[anywhere] * len(lefts) + [vmem] * len(smalls),
        out_shape=[jax.ShapeDtypeStruct(shape, low) for shape in finals]
        + [jax.ShapeDtypeStruct(shape, high) for shape in smalls],
        scratch_shapes=buffers(lambda part: 4)
        + buffers(lambda part: 4 if part[4] else 2)
        + buffers(lambda part: 2)
        + [pltpu.VMEM((part[1], part[3]), low) for part in plan]
        + [pltpu.VMEM((part[1], part[3]), low) for part in plan]
        + [
            pltpu.VMEM((2, length, min(256, max(part[1] for part in plan))), low),
            pltpu.VMEM((2, length, max(part[3] for part in plan)), low),
        ]
        + [pltpu.VMEM(small, high)] * 5
        + [
            pltpu.VMEM((8, width), high),
            dma((2,)),
            dma((2,)),
            dma((count, 4)),
            dma((count, 4)),
            dma((count, 2)),
            dma((count, 2)),
            dma((count,)),
            dma((count,)),
            dma((count, 2)),
            dma((4,)),
            dma((4,)),
        ],
        compiler_params=pltpu.CompilerParams(
            collective_id=2, has_side_effects=True, vmem_limit_bytes=62 * 1024 * 1024
        ),
        name="gradient_pass",
    )(
        *facts,
        back["row_sums"],
        back["in_sums"],
        back["qkv_sums"],
        back["time_sums"],
        *lefts,
        *rights,
    )


def unit_norm(value):
    average = jnp.mean(value, axis=-1, keepdims=True)
    centered = value - average
    inv_scale = lax.rsqrt(jnp.mean(centered * centered, axis=-1, keepdims=True) + eps_norm)
    return centered * inv_scale, inv_scale


def norm_back(gradient, normed, inv_scale, gain_row):
    weighted = gradient * gain_row
    adjusted = (
        weighted
        - jnp.mean(weighted, axis=-1, keepdims=True)
        - normed * jnp.mean(weighted * normed, axis=-1, keepdims=True)
    )
    return inv_scale * adjusted


def gelu_pair(pre):
    normal = 0.5 * (1.0 + lax.erf(pre * 0.7071067811865476))
    density = jnp.exp(-0.5 * pre * pre) * 0.3989422804014327
    return pre * normal, normal + pre * density


def forward_layer(at, inputs, starts, params):
    qkv_w, qkv_b, out_w, in_w, in_b, down_w, gains, biases = params
    qkv = (dot_plain(inputs, qkv_w) + qkv_b).astype(low_type)
    mixed, log_sums = attend(qkv, starts)
    branch = at.group_sum(dot_plain(mixed, out_w).astype(low_type))
    unit_a, scale_a = unit_norm(branch + biases[0] + inputs.astype(jnp.float32))
    middle = unit_a * gains[0] + biases[1]
    low_middle = middle.astype(low_type)
    hidden, slope = gelu_pair(dot_plain(low_middle, in_w) + in_b)
    hidden = hidden.astype(low_type)
    branch_two = at.group_sum(dot_plain(hidden, down_w).astype(low_type))
    unit_z, scale_z = unit_norm(branch_two + biases[2] + middle)
    result = (unit_z * gains[1] + biases[3]).astype(low_type)
    saved = dict(
        inputs=inputs,
        qkv=qkv,
        mixed=mixed,
        log_sums=log_sums,
        scale_a=scale_a[:, 0],
        middle=low_middle,
        hidden=hidden,
        slope=slope.astype(low_type),
        scale_z=scale_z[:, 0],
    )
    return result, saved


def backward_layer(at, saved, incoming, starts, params):
    qkv_w, qkv_b, out_w, in_w, in_b, down_w, gains, biases = params
    gradient = incoming.astype(jnp.float32)
    unit_z = (saved["result"].astype(jnp.float32) - biases[3]) / gains[1]
    grad_z = norm_back(gradient, unit_z, saved["scale_z"][:, None], gains[1])
    low_gz = grad_z.astype(low_type)
    grad_pre = (dot_rows(low_gz, down_w) * saved["slope"].astype(jnp.float32)).astype(low_type)
    grad_mid = at.group_sum(dot_rows(grad_pre, in_w).astype(low_type)) + grad_z
    unit_a = (saved["middle"].astype(jnp.float32) - biases[1]) / gains[0]
    grad_a = norm_back(grad_mid, unit_a, saved["scale_a"][:, None], gains[0])
    low_ga = grad_a.astype(low_type)
    grad_mixed = dot_rows(low_ga, out_w).astype(low_type)
    grad_qkv = jnp.concatenate(
        attend_back(saved["qkv"], starts, saved["mixed"], saved["log_sums"], grad_mixed), 1
    )
    grad_x = at.group_sum(dot_rows(grad_qkv, qkv_w).astype(low_type)) + grad_a
    sums = jnp.stack(
        [
            jnp.sum(grad_mid * unit_a, axis=0),
            jnp.sum(gradient * unit_z, axis=0),
            jnp.sum(grad_a, axis=0),
            jnp.sum(grad_mid, axis=0),
            jnp.sum(grad_z, axis=0),
            jnp.sum(gradient, axis=0),
        ]
    )
    kept = dict(grad_z=low_gz, slope=grad_pre, grad_a=low_ga, qkv=grad_qkv)
    return grad_x.astype(low_type), kept, sums


def store(buffers, values, slot):
    return jax.tree.map(
        lambda buffer, value: lax.dynamic_update_index_in_dim(buffer, value, slot, 0),
        buffers,
        values,
    )


def pick(buffers, slot):
    return jax.tree.map(
        lambda buffer: lax.dynamic_index_in_dim(buffer, slot, 0, keepdims=False), buffers
    )


def group_weight(at, weight):
    parts = weight.reshape((at.chips, -1) + weight.shape[1:])

    def across(s, g, u, x, c):
        return (s, c, u, x, g) if g != c else None

    def along(step):
        return lambda s, g, u, x, c: (s, g, u, (x + step) % at.chips, c) if g != c else None

    piece = at.move(lax.dynamic_index_in_dim(parts, at.chip, 0, keepdims=False), across)
    pieces = [piece]
    for step in range(1, at.chips):
        pieces.append(at.move(piece, along(step)))
    whole = parts
    for step, piece in enumerate(pieces):
        spot = (at.chip - step) % at.chips
        own = lax.dynamic_index_in_dim(parts, spot, 0, keepdims=False)
        whole = lax.dynamic_update_index_in_dim(whole, jnp.where(at.home, own, piece), spot, 0)
    return whole.reshape(weight.shape)


def group_rows(at, tokens, section):
    def across(s, g, u, x, c):
        return (s, 1 - g, u, x, c) if s == section else None

    own = lax.dynamic_index_in_dim(tokens, at.group, 0, keepdims=False)
    other = at.move(lax.dynamic_index_in_dim(tokens, 1 - at.group, 0, keepdims=False), across)
    lower = at.group == 0
    pair = jnp.stack([jnp.where(lower, own, other), jnp.where(lower, other, own)])
    whole = at.group_gather(pair)
    whole = whole.reshape((2, at.halves) + pair.shape)
    whole = jnp.swapaxes(whole, 1, 2)
    return whole.reshape(2, -1, tokens.shape[-1])


def spread_rows(at, rows, length):
    def across(s, g, u, x, c):
        return (s, 1 - g, u, x, c)

    row = lax.dynamic_index_in_dim(rows, at.core, 0, keepdims=False)
    tile = length // at.tensor

    def piece(group):
        return lax.dynamic_slice_in_dim(row, (group * at.halves + at.part) * tile, tile, 0)

    own = piece(at.group)
    other = at.move(piece(1 - at.group), across)
    lower = at.group == 0
    return jnp.stack([jnp.where(lower, own, other), jnp.where(lower, other, own)])


def sum_weight(at, gradient, across_first):
    parts = gradient.reshape((at.chips, -1) + gradient.shape[1:])

    def across(s, g, u, x, c):
        return (s, c, u, x, c) if g != c else None

    def along(step):
        def target(s, g, u, x, c):
            if across_first and g != c:
                return None
            return (s, g, u, (x + step) % at.chips, c)

        return target

    def fold_chips(parts):
        total = lax.dynamic_index_in_dim(parts, at.chip, 0, keepdims=False).astype(jnp.float32)
        for step in range(1, at.chips):
            piece = lax.dynamic_index_in_dim(
                parts, (at.chip + step) % at.chips, 0, keepdims=False
            )
            total = total + at.move(piece, along(step)).astype(jnp.float32)
        return total.astype(low_type)

    if across_first:
        total = fold_chips(
            (parts.astype(jnp.float32) + at.move(parts, across).astype(jnp.float32)).astype(
                low_type
            )
        )
    else:
        part = fold_chips(parts)
        total = (part.astype(jnp.float32) + at.move(part, across).astype(jnp.float32)).astype(
            low_type
        )
    halves = total.reshape((2, -1) + total.shape[1:])

    def over(s, g, u, x, c):
        return (s, g, u, x, 1 - c) if g == c else None

    own = lax.dynamic_index_in_dim(halves, at.core, 0, keepdims=False)
    other = at.move(lax.dynamic_index_in_dim(halves, 1 - at.core, 0, keepdims=False), over)
    return jnp.where(at.home, own, other).astype(jnp.float32)


def layer_ticks(at, starts, rows_in, rows_back, params):
    qkv_w = params[0]
    micro_count, length, width = rows_in.shape
    tick_count = micro_count + at.sections - 1
    slots = micro_count + 1

    def hop(result, distance):
        def target(s, g, u, x, c):
            return (s + distance, g, u, x, c) if 0 <= s + distance < at.sections else None

        tile = length // at.size
        piece = at.move(lax.dynamic_slice_in_dim(result, at.rank * tile, tile, 0), target)
        return at.group_gather(piece).reshape(length, width)

    def place_of(tick_value, stage):
        place = tick_value - stage
        usable = jnp.logical_and(place >= 0, place < micro_count)
        return usable, jnp.clip(place, 0, micro_count - 1), jnp.where(usable, place, micro_count)

    def empty(values):
        return jax.tree.map(
            lambda value: jnp.zeros((slots,) + value.shape, value.dtype), values
        )

    def forward_tick(tick_value, arrived, stash, outputs):
        usable, position, slot = place_of(tick_value, at.section)
        inputs = jnp.where(at.section == 0, rows_in[position], arrived)
        result, saved = forward_layer(at, inputs, starts[position], params)
        if stash is None:
            return result, saved
        return result, store(stash, saved, slot), store(outputs, result, slot)

    blank = jnp.zeros((length, width), low_type)
    shapes = jax.eval_shape(lambda: forward_tick(0, blank, None, None))
    stash, outputs = empty(shapes[1]), empty(shapes[0])

    def forward_loop(tick_value, carry):
        result, stash, outputs = forward_tick(tick_value, *carry)
        return hop(result, 1), stash, outputs

    carry = lax.fori_loop(0, tick_count - 1, forward_loop, (blank, stash, outputs))
    _, stash, outputs = forward_tick(tick_count - 1, *carry)

    def backward_tick(tick_value, arrived, stash, grads, totals):
        usable, position, slot = place_of(tick_value, at.sections - 1 - at.section)
        incoming = jnp.where(at.section == at.sections - 1, rows_back[position], arrived)
        grad_x, kept_now, sums = backward_layer(
            at, pick(dict(stash, result=outputs), slot), incoming, starts[position], params
        )
        totals = totals + jnp.where(usable, sums, 0.0)
        kept = store({name: stash[name] for name in kept_now}, kept_now, slot)
        return grad_x, dict(stash, **kept), store(grads, grad_x, slot), totals

    for name in ("grad_z", "grad_a"):
        stash[name] = empty(blank)
    totals = jnp.zeros((6, width), jnp.float32)

    def backward_loop(tick_value, carry):
        grad_x, stash, grads, totals = backward_tick(tick_value, *carry)
        return hop(grad_x, -1), stash, grads, totals

    carry = lax.fori_loop(
        0, tick_count - 1, backward_loop, (blank, stash, empty(blank), totals)
    )
    _, stash, grads, totals = backward_tick(tick_count - 1, *carry)

    def both(buffer):
        return buffer[:micro_count]

    low_gz, grad_pre, low_ga, grad_qkv = (
        both(stash[name]) for name in ("grad_z", "slope", "grad_a", "qkv")
    )
    stash = {name: both(value) for name, value in stash.items()}
    stash["result"] = both(outputs)
    grads = both(grads)
    back = dict(
        row_sums=totals,
        in_sums=jnp.sum(grad_pre, axis=(0, 1), dtype=jnp.float32)[None],
        qkv_sums=jnp.sum(grad_qkv, axis=(0, 1), dtype=jnp.float32)[None],
        time_sums=jnp.sum(grads, axis=1, keepdims=True, dtype=jnp.float32),
        grad_z=low_gz,
        grad_pre=grad_pre,
        grad_a=low_ga,
        grad_qkv=grad_qkv,
        grads=grads,
    )
    return stash, back


def shards(
    tokens,
    timesteps,
    seg_starts,
    time_params,
    qkv_weight,
    qv_bias,
    out_weight,
    ffn_in,
    ffn_bias,
    ffn_out,
    ln_gains,
    row_biases,
    cotangent,
):
    at = Layout()
    width = tokens.shape[-1]
    length = tokens.shape[1] * at.tensor
    columns = qkv_weight.shape[3]

    def over(s, g, u, x, c):
        return (s, g, u, x, 1 - c)

    own_facts = jnp.concatenate([seg_starts, timesteps[:, None]], 1)
    other_facts = at.move(own_facts, over)
    if at.size == 2 and at.chips == 2:
        facts = (own_facts, other_facts)
        vectors = (qv_bias[0], ffn_bias, ln_gains[0], row_biases[0], time_params)
        weights = (
            jnp.transpose(qkv_weight[0], (1, 0, 2)),
            out_weight[0],
            ffn_in[0],
            ffn_out[0],
        )
        stash = forward_pass(at.sections, facts, vectors, tokens, cotangent, weights)
        weights = tuple(stash[name] for name in ("wq", "wo", "wi", "wd"))
        back = backward_pass(
            at.sections, facts, ln_gains[0], row_biases[0], stash["rows_back"], weights, stash
        )

        def flat(value):
            return value.reshape(-1, value.shape[-1])

        hidden = ffn_in.shape[2]
        in_g, down_g, qkv_g, out_g, gains_g, biases_g, qv_g, hidden_g, time_g = gradient_pass(
            at.sections,
            facts,
            back,
            [flat(stash[name]) for name in ("middle", "hidden", "inputs", "mixed")],
            [flat(back[name]) for name in ("grad_pre", "grad_z", "grad_qkv", "grad_a")],
            (1, 1, 3, 1),
            (
                (0, hidden // 2, hidden // 2, False),
                (0, 0, hidden // 2, True),
                (1, width // 2, width // 2, False),
                (1, 0, width // 2, True),
                (2, columns, 2 * columns, False),
                (2, 0, columns, True),
                (3, 0, width, True),
            ),
        )
        in_g, down_g, qkv_g, out_g = (
            value.astype(jnp.float32) for value in (in_g, down_g, qkv_g, out_g)
        )
        return (
            stash["placed"][None],
            back["grads"][None],
            jnp.transpose(qkv_g, (1, 0, 2))[None],
            qv_g[None],
            out_g[None],
            in_g[None],
            hidden_g,
            down_g[None],
            gains_g[None],
            biases_g[None],
            time_g,
        )

    first = at.core == 0
    facts = jnp.stack(
        [jnp.where(first, own_facts, other_facts), jnp.where(first, other_facts, own_facts)]
    )
    facts = lax.dynamic_index_in_dim(facts, at.group, 1, keepdims=False)
    starts, fractions = facts[:, :-1], facts[:, -1].astype(jnp.float32) / 5000.0
    own_fractions = timesteps.astype(jnp.float32) / 5000.0
    time_values = time_params.astype(jnp.float32)
    embedded = (
        tokens.astype(jnp.float32) + own_fractions[:, None, None] * time_values[0] + time_values[1]
    ).astype(low_type)
    gains, biases = ln_gains[0].astype(jnp.float32), row_biases[0].astype(jnp.float32)
    tensor = lax.axis_index("tensor")
    dp = lax.axis_index("dp")
    rows_in = group_rows(at, embedded, 0)
    qv_low = group_weight(at, qv_bias[0].T).T.astype(jnp.float32)
    params = (
        group_weight(at, qkv_weight[0].reshape(width, 3 * columns)),
        jnp.concatenate([qv_low[0], jnp.zeros((columns,), jnp.float32), qv_low[1]]),
        group_weight(at, out_weight[0]),
        group_weight(at, ffn_in[0]),
        group_weight(at, ffn_bias[0]).astype(jnp.float32),
        group_weight(at, ffn_out[0]),
        gains,
        biases,
    )
    rows_back = group_rows(at, cotangent, at.sections - 1)
    stash, back = layer_ticks(at, starts, rows_in, rows_back, params)
    layer_outs = spread_rows(at, stash["result"], length)
    input_grads = spread_rows(at, back["grads"], length)

    def product(left, right):
        left, right = (v.reshape(-1, v.shape[-1]) for v in (left, right))
        return dot_first(left, right).astype(low_type)

    down_g = sum_weight(at, product(stash["hidden"], back["grad_z"]), True)
    in_g = sum_weight(at, product(stash["middle"], back["grad_pre"]), False)
    out_g = sum_weight(at, product(stash["mixed"], back["grad_a"]), True)
    qkv_g = sum_weight(at, product(stash["inputs"], back["grad_qkv"]), False)
    qkv_bias_g = back["qkv_sums"].reshape(3, columns)
    sliced = jnp.concatenate([qkv_bias_g[0], qkv_bias_g[2], back["in_sums"][0]])
    every = jnp.zeros((at.size,) + sliced.shape, jnp.float32)
    every = lax.dynamic_update_index_in_dim(every, sliced, at.rank, 0)
    row_terms = jnp.where(at.rank == 0, back["row_sums"], 0.0)
    small = lax.psum(
        jnp.concatenate([row_terms.reshape(-1), every.reshape(-1)]), ("tensor", "dp")
    )
    row_sums = small[: row_terms.size].reshape(row_terms.shape)
    mine = lax.dynamic_index_in_dim(
        small[row_terms.size :].reshape(every.shape), tensor, 0, keepdims=False
    )
    row_grads = back["time_sums"][:, 0]
    time_terms = jnp.stack([jnp.sum(fractions[:, None] * row_grads, 0), jnp.sum(row_grads, 0)])
    time_terms = jnp.where(jnp.logical_and(at.section == 0, at.rank == 0), time_terms, 0.0)
    grad_time = lax.psum(time_terms, AXES)

    def share(value, count, index):
        size = value.shape[-1] // count
        return lax.dynamic_slice_in_dim(value, index * size, size, value.ndim - 1)

    qv_g = share(mine[: 2 * columns].reshape(2, columns), at.dp, dp)
    in_bias_g = share(mine[2 * columns :], at.dp, dp)
    row_share = share(row_sums, at.tensor * at.dp, tensor * at.dp + dp)

    return (
        layer_outs[None],
        input_grads[None],
        qkv_g.reshape(-1, 3, columns)[None],
        qv_g[None],
        out_g[None],
        in_g[None],
        in_bias_g[None],
        down_g[None],
        row_share[None, :2],
        row_share[None, 2:],
        grad_time,
    )


def solution(mesh):
    return jax.shard_map(
        shards,
        mesh=mesh,
        in_specs=(
            P("dp", "tensor", None),
            P("dp"),
            P("dp", None),
            P(),
            P("section", None, None, "tensor"),
            P("section", None, "tensor"),
            P("section", "tensor", None),
            P("section", None, "tensor"),
            P("section", "tensor"),
            P("section", "tensor", None),
            P("section", None, None),
            P("section", None, None),
            P("dp", "tensor", None),
        ),
        out_specs=(
            P("section", "dp", "tensor", None),
            P("section", "dp", "tensor", None),
            P("section", "dp", None, "tensor"),
            P("section", None, ("tensor", "dp")),
            P("section", ("tensor", "dp"), None),
            P("section", "dp", "tensor"),
            P("section", ("tensor", "dp")),
            P("section", ("tensor", "dp"), None),
            P("section", None, ("tensor", "dp")),
            P("section", None, ("tensor", "dp")),
            P(),
        ),
        check_vma=False,
    )
```

```python
import functools

import jax
import jax.numpy as jnp
from jax import lax
from jax.experimental import pallas as pl
from jax.experimental.pallas import tpu as pltpu
from jax.sharding import PartitionSpec as P

HEAD = 64
LANES = 128
MASKED = -1e30
eps_norm = 1e-05
AXES = ("section", "tensor", "dp")
low_type = jnp.bfloat16


class Layout:
    def __init__(self):
        self.sections = lax.axis_size("section")
        self.tensor = lax.axis_size("tensor")
        self.dp = lax.axis_size("dp")
        self.halves = self.tensor // 2
        self.chips = self.dp // 2
        self.size = self.tensor
        self.section = lax.axis_index("section")
        tensor, dp = lax.axis_index("tensor"), lax.axis_index("dp")
        self.group, self.part = tensor // self.halves, tensor % self.halves
        self.chip, self.core = dp // 2, dp % 2
        self.rank = self.core * self.halves + self.part
        self.home = self.group == self.core

    def move(self, value, target):
        pairs = []
        for s in range(self.sections):
            for t in range(self.tensor):
                for d in range(self.dp):
                    goal = target(s, t // self.halves, t % self.halves, d // 2, d % 2)
                    if goal is None:
                        continue
                    s2, g2, u2, x2, c2 = goal
                    here = (s * self.tensor + t) * self.dp + d
                    there = (s2 * self.tensor + g2 * self.halves + u2) * self.dp + x2 * 2 + c2
                    if here != there:
                        pairs.append((here, there))
        return lax.ppermute(value, AXES, pairs)

    def turn(self, value, step):
        def target(s, g, u, x, c):
            rank = (c * self.halves + u + step) % self.size
            return (s, g, rank % self.halves, x, rank // self.halves)

        return self.move(value, target)

    def group_sum(self, value):
        total = value.astype(jnp.float32)
        for step in range(1, self.size):
            total = total + self.turn(value, step).astype(jnp.float32)
        return total

    def group_gather(self, value):
        if self.size == 2:
            other = self.turn(value, 1)
            first = self.rank == 0
            return jnp.stack([jnp.where(first, value, other), jnp.where(first, other, value)])
        whole = jnp.zeros((self.size,) + value.shape, value.dtype)
        for step in range(self.size):
            piece = value if step == 0 else self.turn(value, step)
            whole = lax.dynamic_update_index_in_dim(
                whole, piece, (self.rank - step) % self.size, 0
            )
        return whole


def dot_rows(a, b):
    return lax.dot_general(a, b, (((1,), (1,)), ((), ())), preferred_element_type=jnp.float32)


def dot_plain(a, b):
    return lax.dot_general(a, b, (((1,), (0,)), ((), ())), preferred_element_type=jnp.float32)


def dot_first(a, b):
    return lax.dot_general(a, b, (((0,), (0,)), ((), ())), preferred_element_type=jnp.float32)


def tile_docs(starts_ref, length, count):
    place = lax.broadcasted_iota(jnp.int32, (length, LANES), 0)
    doc = jnp.zeros((length, LANES), jnp.int32)
    for j in range(count):
        doc = doc + (starts_ref[j] <= place).astype(jnp.int32)
    lane = lax.broadcasted_iota(jnp.int32, (length, LANES), 1)
    rel = lane % HEAD
    return lane < HEAD, rel, rel + 1 == doc


def three_parts(value):
    high = value.astype(low_type)
    rest = value - high.astype(jnp.float32)
    middle = rest.astype(low_type)
    return high, middle, (rest - middle.astype(jnp.float32)).astype(low_type)


def lanes(rel, count, value, base):
    high, middle, small = three_parts(value)
    return jnp.where(
        rel == count,
        high,
        jnp.where(rel == count + 1, middle, jnp.where(rel == count + 2, small, base)),
    )


def attend_kernel(starts_ref, q_ref, k_ref, v_ref, o_ref, l_ref, *, count, rows):
    length = q_ref.shape[0]
    first, rel, own = tile_docs(starts_ref, length, count)
    extra_k = jnp.where(own, 1.0, 0.0).astype(low_type)
    extra_q = jnp.where(
        jnp.logical_and(rel < count, jnp.logical_not(own)), MASKED, 0.0
    ).astype(low_type)
    q = q_ref[...] * low_type(HEAD**-0.5)
    k = k_ref[...]
    v = v_ref[...]
    ones = jnp.ones_like(v)
    heads = (
        (jnp.where(first, q, extra_q), jnp.where(first, k, extra_k), jnp.where(first, v, ones)),
        (jnp.where(first, extra_q, q), jnp.where(first, extra_k, k), jnp.where(first, ones, v)),
    )
    side = first[:rows]
    for start in range(0, length, rows):
        peaks, sums = [], []
        for q_head, k_head, v_head in heads:
            scores = dot_rows(q_head[start : start + rows], k_head)
            peak = jnp.max(scores, axis=-1, keepdims=True)
            powers = jnp.exp(scores - peak).astype(low_type)
            peaks.append(peak)
            sums.append(dot_plain(powers, v_head))
        mixed = jnp.where(side, sums[0], sums[1])
        totals = jnp.where(side, sums[1], sums[0])
        log_sums = jnp.where(side, peaks[1], peaks[0]) + jnp.log(totals)
        l_ref[start : start + rows] = lanes(
            rel[:rows], count, -log_sums, extra_q[start : start + rows]
        )
        o_ref[start : start + rows] = (mixed / pltpu.roll(totals, HEAD, 1)).astype(low_type)


def attend(qkv, starts):
    length, columns = qkv.shape[0], qkv.shape[1] // 3
    pairs = columns // LANES
    rows = min(512, length)

    def block(offset):
        return pl.BlockSpec((length, LANES), lambda j: (0, offset + j))

    return pl.pallas_call(
        functools.partial(attend_kernel, count=starts.shape[0], rows=rows),
        grid=(pairs,),
        in_specs=[
            pl.BlockSpec(memory_space=pltpu.SMEM),
            block(0),
            block(pairs),
            block(2 * pairs),
        ],
        out_specs=[block(0), block(0)],
        out_shape=[
            jax.ShapeDtypeStruct((length, columns), low_type),
            jax.ShapeDtypeStruct((length, columns), low_type),
        ],
        compiler_params=pltpu.CompilerParams(vmem_limit_bytes=48 * 1024 * 1024),
        cost_estimate=pl.CostEstimate(
            flops=16 * length * length * columns // 4,
            bytes_accessed=12 * length * columns,
            transcendentals=length * length * columns // HEAD,
        ),
        name="attend",
    )(starts, qkv, qkv, qkv)


def attend_back_kernel(
    starts_ref, q_ref, k_ref, v_ref, o_ref, l_ref, g_ref, dq_ref, dk_ref, dv_ref, *, count, rows
):
    length = q_ref.shape[0]
    first, rel, own = tile_docs(starts_ref, length, count)
    stat = jnp.logical_and(rel >= count, rel < count + 3)
    extra_k = jnp.where(jnp.logical_or(own, stat), 1.0, 0.0).astype(low_type)
    extra_v = jnp.where(stat, 1.0, 0.0).astype(low_type)
    extra_q = l_ref[...]
    g = g_ref[...]
    product = g.astype(jnp.float32) * o_ref[...].astype(jnp.float32)
    dots = [
        jnp.sum(jnp.where(first, product, 0.0), axis=-1, keepdims=True),
        jnp.sum(jnp.where(first, 0.0, product), axis=-1, keepdims=True),
    ]
    extra_g = lanes(rel, count, -jnp.where(first, dots[1], dots[0]), jnp.zeros_like(extra_q))
    q = q_ref[...] * low_type(HEAD**-0.5)
    k = k_ref[...]
    v = v_ref[...]
    heads = (
        tuple(
            jnp.where(first, a, b)
            for a, b in ((q, extra_q), (k, extra_k), (v, extra_v), (g, extra_g))
        ),
        tuple(
            jnp.where(first, b, a)
            for a, b in ((q, extra_q), (k, extra_k), (v, extra_v), (g, extra_g))
        ),
    )
    grad_k = [jnp.zeros((length, LANES), jnp.float32)] * 2
    grad_v = [jnp.zeros((length, LANES), jnp.float32)] * 2
    for start in range(0, length, rows):
        part = slice(start, start + rows)
        grad_q = []
        for i, (q_head, k_head, v_head, g_head) in enumerate(heads):
            probs = jnp.exp(dot_rows(k_head, q_head[part]))
            slopes = (probs * dot_rows(v_head, g_head[part])).astype(low_type)
            grad_v[i] = grad_v[i] + dot_plain(probs.astype(low_type), g[part])
            grad_k[i] = grad_k[i] + dot_plain(slopes, q[part])
            grad_q.append(dot_first(slopes, k))
        dq_ref[part] = (
            jnp.where(first[:rows], grad_q[0], grad_q[1]) * (HEAD**-0.5)
        ).astype(low_type)
    dk_ref[...] = jnp.where(first, grad_k[0], grad_k[1]).astype(low_type)
    dv_ref[...] = jnp.where(first, grad_v[0], grad_v[1]).astype(low_type)


def attend_back(qkv, starts, mixed, log_sums, grad_mixed):
    length, columns = mixed.shape
    pairs = columns // LANES
    rows = min(256, length)

    def block(offset):
        return pl.BlockSpec((length, LANES), lambda j: (0, offset + j))

    return pl.pallas_call(
        functools.partial(attend_back_kernel, count=starts.shape[0], rows=rows),
        grid=(pairs,),
        in_specs=[
            pl.BlockSpec(memory_space=pltpu.SMEM),
            block(0),
            block(pairs),
            block(2 * pairs),
            block(0),
            block(0),
            block(0),
        ],
        out_specs=[block(0)] * 3,
        out_shape=[jax.ShapeDtypeStruct((length, columns), low_type)] * 3,
        compiler_params=pltpu.CompilerParams(vmem_limit_bytes=48 * 1024 * 1024),
        cost_estimate=pl.CostEstimate(
            flops=40 * length * length * columns // 4,
            bytes_accessed=20 * length * columns,
            transcendentals=length * length * columns // HEAD,
        ),
        name="attend_back",
    )(starts, qkv, qkv, qkv, mixed, log_sums, grad_mixed)


MESH = pl.DeviceIdType.MESH


def rows_of(index, size):
    return pl.ds(pl.multiple_of(index * size, size), size)


def erf_pair(pre):
    bell = jnp.exp(-0.5 * pre * pre)
    size = jnp.abs(pre)
    t = 1.0 / (1.0 + 0.2316418882663604 * size)
    tail = bell * t * (
        0.127414796
        + t * (-0.142248368 + t * (0.7107068705 + t * (-0.7265760135 + t * 0.5307027145)))
    )
    return jnp.where(pre < 0.0, tail, 1.0 - tail), bell * 0.3989422804014327


def norm_rows(value):
    average = jnp.mean(value, axis=-1, keepdims=True)
    centered = value - average
    inv_scale = lax.rsqrt(jnp.mean(centered * centered, axis=-1, keepdims=True) + eps_norm)
    return centered * inv_scale, inv_scale


def doc_lanes(starts, first_row, shape):
    place = lax.broadcasted_iota(jnp.int32, shape, 0) + first_row
    doc = jnp.zeros(shape, jnp.int32)
    for start in starts:
        doc = doc + (start <= place).astype(jnp.int32)
    lane = lax.broadcasted_iota(jnp.int32, shape, 1)
    rel = lane % HEAD
    return lane < HEAD, rel, rel + 1 == doc


def forward_kernel(
    sections,
    chunk,
    own_ref,
    other_ref,
    qv_in,
    hidden_bias_in,
    gains_in,
    biases_in,
    time_in,
    tokens_in,
    cotangent_in,
    qkv_w,
    out_w,
    in_w,
    down_w,
    qkv_out,
    stat_out,
    mixed_out,
    middle_out,
    hidden_out,
    slope_out,
    inputs_out,
    result_out,
    scale_out,
    placed_out,
    back_out,
    wq_out,
    wo_out,
    wi_out,
    wd_out,
    wq,
    wo,
    wi,
    wd,
    bias_own,
    bias,
    gains,
    biases,
    hbuf,
    qkv,
    keys,
    values,
    mixed,
    stat,
    send_a,
    send_b,
    got_a,
    got_b,
    high_mid,
    low_mid,
    hidden,
    slope,
    result,
    scale_a,
    scale_z,
    w_sem,
    y_send,
    y_got,
    x_send,
    x_got,
    round_up,
    round_down,
    round_tokens,
    round_send,
    round_got,
    bias_sem,
    token_local,
    token_send,
    token_got,
    cot_local,
    cot_send,
    cot_got,
    hop_send,
    hop_got,
    pass_send,
    pass_got,
    keep_sem,
    qkv_sem,
    a_send,
    a_got,
    b_send,
    b_got,
    first_sem,
    second_sem,
    third_sem,
    scale_sem,
    out_local,
    out_send,
    out_got,
):
    at = Seat()
    section, core, peer = at.section, at.core, at.peer
    last = sections - 1
    micro, length, width = hbuf.shape
    count = own_ref.shape[1] - 1
    columns = mixed.shape[2]
    pairs = columns // LANES
    chunks = length // chunk
    half = chunk // 2
    shape = (chunk, LANES)
    given, held = (qkv_w, out_w, in_w, down_w), (wq, wo, wi, wd)
    own_weights = [
        pltpu.make_async_copy(source, target, w_sem.at[i])
        for i, (source, target) in enumerate(zip(given, held))
    ]
    pieces = weight_pieces(*held)

    def swap(k):
        index, where = pieces[k]
        return remote(
            where(given[index], at.chip),
            where(held[index], at.chip),
            y_send.at[k],
            y_got.at[k],
            at.swap,
        )

    def relay(k):
        index, where = pieces[k]
        part = where(held[index], at.chip)
        return remote(part, part, x_send.at[k], x_got.at[k], at.beside)

    size = wd.shape[0] // 8
    rounds = round_up.shape[0]

    def round_rows(ref, n):
        return ref.at[pl.ds((n % 2) * 4 * size + (4 - rounds // 2 + n // 2) * size, size)]

    def go_up(n):
        return remote(
            round_rows(down_w, n),
            round_up.at[n],
            round_send.at[0, n],
            round_got.at[0, n],
            {"section": section + 1},
        )

    def go_over(n):
        return remote(
            round_up.at[n], round_down.at[n], round_send.at[1, n], round_got.at[1, n], at.swap
        )

    def go_down(n):
        return remote(
            round_down.at[n],
            round_rows(wd, n),
            round_send.at[2, n],
            round_got.at[2, n],
            {"section": section - 1},
        )

    def tokens_over():
        return remote(
            tokens_in.at[1 - at.group],
            round_tokens,
            round_send.at[3, 0],
            round_got.at[3, 0],
            at.across,
        )

    def tokens_down():
        tile = tokens_in.shape[1]
        rows = pl.ds(pl.multiple_of((1 - at.group) * tile, tile), tile)
        return remote(
            round_tokens,
            hbuf.at[core, rows],
            round_send.at[3, 1],
            round_got.at[3, 1],
            {"section": section - 1},
        )

    def pieces_of(*indices):
        return [k for k, (index, _) in enumerate(pieces) if index in indices]

    def pass_on(group):
        for k in group:
            swap(k).wait_recv()
            relay(k).start()

    def begin(group):
        for k in group:
            swap(k).start()

    direct = pieces_of(0, 1, 2, 3)[: -(rounds // 2)]
    detour = pieces_of(3)[-(rounds // 2) :]

    def ready(index):
        @pl.when(at.home)
        def _():
            own_weights[index].wait()

        @pl.when(at.away)
        def _():
            for k in pieces_of(index):
                if k in direct:
                    relay(k).wait_recv()
            if index == 3:

                @pl.when(section > 0)
                def _():
                    for k in detour:
                        relay(k).wait_recv()

                @pl.when(section == 0)
                def _():
                    for n in range(rounds):
                        go_down(n).wait_recv()

    def swap_bias():
        return remote(bias_own, bias, bias_sem.at[0], bias_sem.at[1], at.swap)

    tokens = RowPieces(at, tokens_in, hbuf, token_local, token_send, token_got)
    cotangents = RowPieces(at, cotangent_in, back_out, cot_local, cot_send, cot_got)
    placed = OutPieces(at, result, placed_out, out_local, out_send, out_got)

    @pl.when(at.home)
    def _():
        for copy in own_weights:
            copy.start()

    gains[...] = gains_in[...].astype(jnp.float32)
    biases[...] = biases_in[...].astype(jnp.float32)
    qv = qv_in[...].astype(jnp.float32)
    bias_own[:, :columns] = qv[0:1]
    bias_own[:, columns : 2 * columns] = jnp.zeros_like(qv[0:1])
    bias_own[:, 2 * columns : 3 * columns] = qv[1:2]
    bias_own[:, 3 * columns :] = hidden_bias_in[...].astype(jnp.float32)

    @pl.when(at.home)
    def _():
        bias[...] = bias_own[...]

    greet(section, sections, (at.peer, at.across, at.swap, at.beside))

    @pl.when(section == 0)
    def _():
        tokens.own.start()
        tokens.to_peer.start()

    guide = jnp.logical_and(section == 1, core == 0)
    pl.when(guide)(lambda: tokens_over().start())

    @pl.when(at.away)
    def _():
        swap_bias().start()

        @pl.when(section == 0)
        def _():
            begin(direct)
            for n in range(rounds):
                go_up(n).start()

        @pl.when(section > 1)
        def _():
            begin(direct + detour)

        @pl.when(section == 1)
        def _():
            for n in range(rounds + 1):
                if n < rounds:
                    go_up(n).wait_recv()
                    go_over(n).start()
                if n > 0:
                    go_over(n - 1).wait_recv()
                    go_down(n - 1).start()
                if n == 1:

                    @pl.when(guide)
                    def _():
                        tokens_over().wait_recv()
                        tokens_down().start()

            begin(direct + detour)

        swap_bias().wait()
        pass_on(direct[:4])

        @pl.when(section > 0)
        def _():
            pass_on(direct[4:] + detour)

    @pl.when(jnp.logical_and(guide, at.home))
    def _():
        tokens_over().wait_recv()
        tokens_down().start()

    @pl.when(section == last)
    def _():
        cotangents.own.start()
        cotangents.to_peer.start()
        cotangents.to_across.start()
        cotangents.to_across.wait()
        cotangents.forward.start()
        cotangents.own.wait()
        cotangents.to_peer.wait()
        cotangents.forward.wait()

    def hop(m, j):
        rows = pl.ds(pl.multiple_of(core * half, half), half)
        target = pl.ds(pl.multiple_of(j * chunk + core * half, half), half)
        return pltpu.make_async_remote_copy(
            src_ref=result.at[j, rows],
            dst_ref=hbuf.at[m, target],
            send_sem=hop_send.at[j],
            recv_sem=hop_got.at[m, j],
            device_id={"section": section + 1},
            device_id_type=MESH,
        )

    def hand_over(m, j):
        rows = pl.ds(pl.multiple_of(j * chunk + core * half, half), half)
        return pltpu.make_async_remote_copy(
            src_ref=hbuf.at[m, rows],
            dst_ref=hbuf.at[m, rows],
            send_sem=pass_send.at[m, j],
            recv_sem=pass_got.at[m, j],
            device_id=peer,
            device_id_type=MESH,
        )

    def exchange_a(m, j):
        slot = j
        return pltpu.make_async_remote_copy(
            src_ref=send_a.at[slot],
            dst_ref=got_a.at[j],
            send_sem=a_send.at[slot],
            recv_sem=a_got.at[m, j],
            device_id=peer,
            device_id_type=MESH,
        )

    def exchange_b(m, j):
        slot = lax.rem(j, 2)
        return pltpu.make_async_remote_copy(
            src_ref=send_b.at[slot],
            dst_ref=got_b.at[j],
            send_sem=b_send.at[slot],
            recv_sem=b_got.at[m, j],
            device_id=peer,
            device_id_type=MESH,
        )

    def keep(m, j):
        rows = rows_of(j, chunk)
        return pltpu.make_async_copy(
            hbuf.at[m, rows], inputs_out.at[m, rows], keep_sem.at[m, j]
        )

    def keep_qkv(m, j):
        rows = rows_of(j, chunk)
        return pltpu.make_async_copy(qkv.at[rows], qkv_out.at[m, rows], qkv_sem.at[j])

    def keep_first(m, j):
        rows = rows_of(j, chunk)
        return [
            pltpu.make_async_copy(mixed.at[j], mixed_out.at[m, rows], first_sem.at[0]),
            pltpu.make_async_copy(stat, stat_out.at[m, rows], first_sem.at[1]),
        ]

    def keep_second(m, j):
        rows = rows_of(j, chunk)
        return [
            pltpu.make_async_copy(low_mid, middle_out.at[m, rows], second_sem.at[0]),
            pltpu.make_async_copy(hidden, hidden_out.at[m, rows], second_sem.at[1]),
            pltpu.make_async_copy(slope, slope_out.at[m, rows], second_sem.at[2]),
            pltpu.make_async_copy(scale_a, scale_out.at[m, 0, rows], second_sem.at[3]),
        ]

    def keep_third(m, j):
        rows = rows_of(j, chunk)
        return [
            pltpu.make_async_copy(result.at[j], result_out.at[m, rows], third_sem.at[j]),
            pltpu.make_async_copy(scale_z.at[j], scale_out.at[m, 1, rows], scale_sem.at[j]),
        ]

    def arrive(m, j):
        hop(m, j).wait_recv()
        hand_over(m, j).start()

    def project(m, j):
        rows = rows_of(j, chunk)

        starts, moment = row_facts(at, own_ref, other_ref, m)

        @pl.when(section == 0)
        def _():
            fraction = jnp.full((1, width), moment.astype(jnp.float32)) / 5000.0
            times = time_in[...].astype(jnp.float32)
            hbuf[m, rows] = (
                hbuf[m, rows].astype(jnp.float32) + fraction * times[0:1] + times[1:2]
            ).astype(low_type)

        @pl.when(section > 0)
        def _():
            @pl.when(j + 1 < chunks)
            def _():
                arrive(m, j + 1)

            hand_over(m, j).wait_recv()

        keep(m, j).start()

        @pl.when(m > 0)
        def _():
            keep_qkv(m - 1, j).wait()

        for third in range(3):
            part = slice(third * columns, (third + 1) * columns)
            qkv[rows, part] = (dot_plain(hbuf[m, rows], wq[third]) + bias[:, part]).astype(low_type)
        keep_qkv(m, j).start()
        first, rel, own = doc_lanes(starts, j * chunk, shape)
        extra = jnp.where(own, 1.0, 0.0).astype(low_type)
        ones = jnp.ones(shape, low_type)
        for p in range(pairs):
            k = qkv[rows, columns + p * LANES : columns + (p + 1) * LANES]
            v = qkv[rows, 2 * columns + p * LANES : 2 * columns + (p + 1) * LANES]
            keys[2 * p, rows] = jnp.where(first, k, extra)
            keys[2 * p + 1, rows] = jnp.where(first, extra, k)
            values[2 * p, rows] = jnp.where(first, v, ones)
            values[2 * p + 1, rows] = jnp.where(first, ones, v)

    def mix(m, j):
        rows = rows_of(j, chunk)
        starts, _ = row_facts(at, own_ref, other_ref, m)
        first, rel, own = doc_lanes(starts, j * chunk, shape)
        extra = jnp.where(
            jnp.logical_and(rel < count, jnp.logical_not(own)), MASKED, 0.0
        ).astype(low_type)

        def scores(index):
            p = index // 2
            q = qkv[rows, p * LANES : (p + 1) * LANES] * low_type(HEAD**-0.5)
            q = jnp.where(first, q, extra) if index % 2 == 0 else jnp.where(first, extra, q)
            return dot_rows(q, keys[index])

        current = scores(0)
        peaks, sums = [], []
        for index in range(2 * pairs):
            later = scores(index + 1) if index + 1 < 2 * pairs else None
            peak = jnp.max(current, axis=-1, keepdims=True)
            powers = jnp.exp(current - peak).astype(low_type)
            peaks.append(peak)
            sums.append(dot_plain(powers, values[index]))
            current = later
            if index % 2 == 1:
                lane = slice((index // 2) * LANES, (index // 2 + 1) * LANES)
                total = jnp.where(first, sums[index], sums[index - 1])
                log_sum = jnp.where(first, peaks[index], peaks[index - 1]) + jnp.log(total)
                stat[:, lane] = lanes(rel, count, -log_sum, extra)
                mixed[j, :, lane] = (
                    jnp.where(first, sums[index - 1], sums[index]) / pltpu.roll(total, HEAD, 1)
                ).astype(low_type)
        for copy in keep_first(m, j):
            copy.start()

    def branch(m, j):
        send_a[j] = dot_plain(mixed[j], wo[...]).astype(low_type)
        exchange_a(m, j).start()

    def feed(m, j):
        rows = rows_of(j, chunk)
        slot = lax.rem(j, 2)
        exchange_a(m, j).wait()
        total = (
            send_a[j].astype(jnp.float32)
            + got_a[j].astype(jnp.float32)
            + biases[0:1]
            + hbuf[m, rows].astype(jnp.float32)
        )
        unit, inv_scale = norm_rows(total)
        scale_a[...] = jnp.broadcast_to(inv_scale, shape)
        middle = unit * gains[0:1] + biases[1:2]
        high_mid[slot] = middle
        low_mid[...] = middle.astype(low_type)
        hidden_size = wi.shape[1]
        step = min(1024, hidden_size)

        def before(start):
            part = slice(start, start + step)
            return dot_plain(low_mid[...], wi[:, part]) + bias[:, 3 * columns + start : 3 * columns + start + step]

        pre = before(0)
        branch = jnp.zeros((chunk, width), jnp.float32)
        for start in range(0, hidden_size, step):
            part = slice(start, start + step)
            later = before(start + step) if start + step < hidden_size else None
            normal, density = erf_pair(pre)
            hidden[:, part] = (pre * normal).astype(low_type)
            slope[:, part] = (normal + pre * density).astype(low_type)
            branch = branch + dot_plain(hidden[:, part], wd[part])
            pre = later
        send_b[slot] = branch.astype(low_type)
        exchange_b(m, j).start()
        for copy in keep_second(m, j):
            copy.start()

    def finish(m, j):
        slot = lax.rem(j, 2)
        exchange_b(m, j).wait()
        total = (
            send_b[slot].astype(jnp.float32)
            + got_b[j].astype(jnp.float32)
            + biases[2:3]
            + high_mid[slot]
        )
        unit, inv_scale = norm_rows(total)
        @pl.when(m > 0)
        def _():
            finish_wait(m - 1, j)

        scale_z[j] = jnp.broadcast_to(inv_scale, shape)
        result[j] = (unit * gains[1:2] + biases[3:4]).astype(low_type)

        @pl.when(section < sections - 1)
        def _():
            hop(m, j).start()

        placed.start(m, j)
        for copy in keep_third(m, j):
            copy.start()

    def finish_wait(m, j):
        for copy in keep_third(m, j):
            copy.wait()

        placed.wait(m, j)

        @pl.when(section < sections - 1)
        def _():
            hop(m, j).wait_send()

    def one_row(m, carry):
        @pl.when(jnp.logical_and(section == 0, core == m))
        def _():
            tokens.own.wait()

            @pl.when(core == 0)
            def _():
                tokens_down().wait_recv()

            @pl.when(core > 0)
            def _():
                tokens.to_across.wait_recv()

            tokens.forward.start()

        @pl.when(jnp.logical_and(section == 0, core != m))
        def _():
            tokens.to_peer.wait_recv()
            tokens.forward.wait_recv()

        @pl.when(m == 0)
        def _():
            ready(0)

        @pl.when(jnp.logical_and(section == 0, core == m))
        def _():
            tokens.forward.wait_send()

        @pl.when(section > 0)
        def _():
            arrive(m, 0)

        opening = jnp.logical_and(m == 0, jnp.logical_and(section == 0, at.away))

        @pl.when(opening)
        def _():
            pass_on(direct[4:5])

        def first_step(j, carry):
            project(m, j)

            @pl.when(jnp.logical_and(opening, j == 0))
            def _():
                pass_on(direct[5:6])

            return carry

        lax.fori_loop(0, chunks, first_step, 0)

        @pl.when(jnp.logical_and(m == 0, section > 0))
        def _():
            ready(1)

        @pl.when(opening)
        def _():
            pass_on(direct[6:7])

        lag = jnp.where(jnp.logical_and(section == 0, m == 0), chunks, 1)

        def step(i, carry):
            j = i - lag

            @pl.when(jnp.logical_and(i >= 1, i <= chunks))
            def _():
                for copy in keep_first(m, i - 1):
                    copy.wait()

            @pl.when(i < chunks)
            def _():
                mix(m, i)

                @pl.when(lag == 1)
                def _():
                    branch(m, i)

            for turn, k in enumerate(direct[7:]):

                @pl.when(jnp.logical_and(opening, i == turn))
                def _(k=k):
                    pass_on([k])

            @pl.when(
                jnp.logical_and(
                    jnp.logical_and(section == 0, core > 0),
                    jnp.logical_and(m == 0, i == chunks - 1),
                )
            )
            def _():
                tokens.to_across.start()

            @pl.when(jnp.logical_and(lag > 1, j == 0))
            def _():
                ready(1)
                for turn in range(chunks):
                    branch(m, turn)

            @pl.when(jnp.logical_and(m == 0, j == 0))
            def _():
                ready(2)
                ready(3)

            @pl.when(jnp.logical_and(j >= 1, j <= chunks))
            def _():
                for copy in keep_second(m, j - 1):
                    copy.wait()

            @pl.when(j >= 1)
            def _():
                finish(m, j - 1)

            @pl.when(jnp.logical_and(j >= 0, j < chunks))
            def _():
                feed(m, j)

            return carry

        lax.fori_loop(0, chunks + lag + 1, step, 0)

        @pl.when(m == 0)
        def _():
            for copy in keep_weights:
                copy.start()

        return carry

    keep_weights = [
        pltpu.make_async_copy(source, target, w_sem.at[i])
        for i, (source, target) in enumerate(zip(held, (wq_out, wo_out, wi_out, wd_out)))
    ]
    lax.fori_loop(0, micro, one_row, 0)
    for copy in keep_weights:
        copy.wait()
    for j in range(chunks):
        finish_wait(micro - 1, j)
        keep_qkv(micro - 1, j).wait()
    for m in range(micro):
        for j in range(chunks):
            keep(m, j).wait()
    placed.wait_got()

    @pl.when(at.away)
    def _():
        for k in direct:
            swap(k).wait_send()
            relay(k).wait_send()

        @pl.when(section > 0)
        def _():
            for k in detour:
                swap(k).wait_send()
                relay(k).wait_send()

        for n in range(rounds):

            @pl.when(section == 0)
            def _(n=n):
                go_up(n).wait_send()

            @pl.when(section == 1)
            def _(n=n):
                go_over(n).wait_send()
                go_down(n).wait_send()

    @pl.when(guide)
    def _():
        tokens_over().wait_send()
        tokens_down().wait_send()

    @pl.when(section == 0)
    def _():
        tokens.to_peer.wait_send()

        @pl.when(core > 0)
        def _():
            tokens.to_across.wait_send()

    @pl.when(section > 0)
    def _():
        for m in range(micro):
            for j in range(chunks):
                hand_over(m, j).wait_send()


def forward_pass(sections, facts, vectors, tokens, cotangent, weights):
    wq, wo, wi, wd = weights
    micro, tile, width = tokens.shape
    length = 2 * tile
    columns, hidden = wo.shape[0], wi.shape[1]
    chunk = min(256, length // 4)
    chunks = length // chunk
    low, high = low_type, jnp.float32

    def out(*shape, dtype=low):
        return jax.ShapeDtypeStruct(shape, dtype)

    outs = dict(
        qkv=out(micro, length, 3 * columns),
        log_sums=out(micro, length, columns),
        mixed=out(micro, length, columns),
        middle=out(micro, length, width),
        hidden=out(micro, length, hidden),
        slope=out(micro, length, hidden),
        inputs=out(micro, length, width),
        result=out(micro, length, width),
        scales=out(micro, 2, length, LANES, dtype=high),
        placed=out(*tokens.shape),
        rows_back=out(micro, length, width),
        wq=out(*wq.shape),
        wo=out(*wo.shape),
        wi=out(*wi.shape),
        wd=out(*wd.shape),
    )
    vmem = pl.BlockSpec(memory_space=pltpu.VMEM)
    anywhere = pl.BlockSpec(memory_space=pl.ANY)
    dma = pltpu.SemaphoreType.DMA
    pieces = len(weight_pieces(*weights))
    rounds = 4
    results = pl.pallas_call(
        functools.partial(forward_kernel, sections, chunk),
        in_specs=[pl.BlockSpec(memory_space=pltpu.SMEM)] * 2 + [vmem] * 5 + [anywhere] * 6,
        out_specs=[anywhere] * len(outs),
        out_shape=list(outs.values()),
        scratch_shapes=[
            pltpu.VMEM(wq.shape, low),
            pltpu.VMEM(wo.shape, low),
            pltpu.VMEM(wi.shape, low),
            pltpu.VMEM(wd.shape, low),
            pltpu.VMEM((1, 3 * columns + hidden), high),
            pltpu.VMEM((1, 3 * columns + hidden), high),
            pltpu.VMEM(vectors[2].shape, high),
            pltpu.VMEM(vectors[3].shape, high),
            pltpu.VMEM((micro, length, width), low),
            pltpu.VMEM((length, 3 * columns), low),
            pltpu.VMEM((columns // HEAD, length, LANES), low),
            pltpu.VMEM((columns // HEAD, length, LANES), low),
            pltpu.VMEM((chunks, chunk, columns), low),
            pltpu.VMEM((chunk, columns), low),
            pltpu.VMEM((chunks, chunk, width), low),
            pltpu.VMEM((2, chunk, width), low),
            pltpu.VMEM((chunks, chunk, width), low),
            pltpu.VMEM((chunks, chunk, width), low),
            pltpu.VMEM((2, chunk, width), high),
            pltpu.VMEM((chunk, width), low),
            pltpu.VMEM((chunk, hidden), low),
            pltpu.VMEM((chunk, hidden), low),
            pltpu.VMEM((chunks, chunk, width), low),
            pltpu.VMEM((chunk, LANES), high),
            pltpu.VMEM((chunks, chunk, LANES), high),
            dma((4,)),
            dma((pieces,)),
            dma((pieces,)),
            dma((pieces,)),
            dma((pieces,)),
            pltpu.VMEM((rounds, hidden // 8, width), low),
            pltpu.VMEM((rounds, hidden // 8, width), low),
            pltpu.VMEM((tile, width), low),
            dma((4, rounds)),
            dma((4, rounds)),
            dma((2,)),
            dma,
            dma((3,)),
            dma((3,)),
            dma,
            dma((3,)),
            dma((3,)),
            dma((chunks,)),
            dma((micro, chunks)),
            dma((micro, chunks)),
            dma((micro, chunks)),
            dma((micro, chunks)),
            dma((chunks,)),
            dma((chunks,)),
            dma((micro, chunks)),
            dma((2,)),
            dma((micro, chunks)),
            dma((2,)),
            dma((4,)),
            dma((chunks,)),
            dma((chunks,)),
            dma((chunks,)),
            dma((chunks,)),
            dma((chunks // 2,)),
        ],
        compiler_params=pltpu.CompilerParams(
            collective_id=0, has_side_effects=True, vmem_limit_bytes=62 * 1024 * 1024
        ),
        name="forward_pass",
    )(*facts, *vectors, tokens, cotangent, *weights)
    return dict(zip(outs, results))


def greet(section, sections, partners):
    barrier = pltpu.get_barrier_semaphore()
    for partner in partners:
        pl.semaphore_signal(barrier, inc=1, device_id=partner, device_id_type=MESH)

    @pl.when(section > 0)
    def _():
        pl.semaphore_signal(
            barrier, inc=1, device_id={"section": section - 1}, device_id_type=MESH
        )

    @pl.when(section < sections - 1)
    def _():
        pl.semaphore_signal(
            barrier, inc=1, device_id={"section": section + 1}, device_id_type=MESH
        )

    inner = jnp.logical_and(section > 0, section < sections - 1)

    @pl.when(inner)
    def _():
        pl.semaphore_wait(barrier, len(partners) + 2)

    @pl.when(jnp.logical_not(inner))
    def _():
        pl.semaphore_wait(barrier, len(partners) + 1)


class Seat:
    def __init__(self):
        self.section = lax.axis_index("section")
        self.group = lax.axis_index("tensor")
        dp = lax.axis_index("dp")
        self.core = lax.rem(dp, 2)
        self.chip = dp // 2
        other = dp + 1 - 2 * self.core
        self.peer = {"dp": other}
        self.across = {"tensor": 1 - self.group}
        self.swap = {"tensor": 1 - self.group, "dp": other}
        self.beside = {"dp": dp + 2 - 4 * self.chip}
        self.home = self.group == self.core
        self.away = self.group != self.core


def row_facts(at, own_ref, other_ref, m):
    facts = [
        jnp.where(at.core == m, own_ref[at.group, j], other_ref[at.group, j])
        for j in range(own_ref.shape[1])
    ]
    return facts[:-1], facts[-1]


def remote(source, target, send_sem, recv_sem, device):
    return pltpu.make_async_remote_copy(
        src_ref=source,
        dst_ref=target,
        send_sem=send_sem,
        recv_sem=recv_sem,
        device_id=device,
        device_id_type=MESH,
    )


class RowPieces:
    def __init__(self, at, source, target, local, send, got):
        tile = source.shape[1]

        def half(group):
            return pl.ds(pl.multiple_of(group * tile, tile), tile)

        own = target.at[at.core, half(at.group)]
        other = target.at[at.core, half(1 - at.group)]
        mine = source.at[at.group]
        self.own = pltpu.make_async_copy(mine, own, local)
        self.to_peer = remote(mine, own, send.at[0], got.at[0], at.peer)
        self.to_across = remote(source.at[1 - at.group], own, send.at[1], got.at[1], at.across)
        self.forward = remote(other, other, send.at[2], got.at[2], at.peer)


class OutPieces:
    def __init__(self, at, rows, target, local, send, got):
        self.at, self.rows, self.target = at, rows, target
        self.local, self.send, self.got = local, send, got
        self.chunks, self.chunk = rows.shape[0], rows.shape[1]
        self.per = self.chunks // 2

    def copies(self, m, j):
        place = rows_of(lax.rem(j, self.per), self.chunk)
        spot = self.target.at[self.at.group, place]
        near = pltpu.make_async_copy(self.rows.at[j], spot, self.local.at[j])
        far = remote(
            self.rows.at[j],
            spot,
            self.send.at[j],
            self.got.at[lax.rem(j, self.per)],
            self.at.across,
        )
        mine = self.at.core == m
        stays = j // self.per == self.at.group
        return (
            (jnp.logical_and(mine, stays), near, near.wait),
            (jnp.logical_and(mine, jnp.logical_not(stays)), far, far.wait_send),
        )

    def start(self, m, j):
        for condition, copy, _ in self.copies(m, j):
            pl.when(condition)(copy.start)

    def wait(self, m, j):
        for condition, _, wait in self.copies(m, j):
            pl.when(condition)(wait)

    def wait_got(self):
        for j in range(self.per):
            remote(
                self.rows.at[j],
                self.target.at[1 - self.at.group, pl.ds(j * self.chunk, self.chunk)],
                self.send.at[j],
                self.got.at[j],
                self.at.across,
            ).wait_recv()


def weight_pieces(wq, wo, wi, wd):
    pieces = []

    def split(index, rows, count, lead=()):
        size = rows // 2 // count
        for i in range(count):

            def where(ref, chip, i=i):
                start = pl.multiple_of(chip * (rows // 2) + i * size, size)
                return ref.at[lead + (pl.ds(start, size),)]

            pieces.append((index, where))

    for k in range(wq.shape[0]):
        split(0, wq.shape[1], 1, (k,))
    split(1, wo.shape[0], 1)
    split(2, wi.shape[0], 4)
    split(3, wd.shape[0], 4)
    return pieces


def backward_kernel(
    sections,
    chunk,
    own_ref,
    other_ref,
    gains_in,
    biases_in,
    rows_back,
    qkv_w,
    out_w,
    in_w,
    down_w,
    qkv_in,
    stat_in,
    mixed_in,
    middle_in,
    hidden_in,
    slope_in,
    result_in,
    scale_in,
    row_sums,
    in_sums,
    qkv_sums,
    time_sums,
    gz_out,
    pre_out,
    ga_out,
    gqkv_out,
    grads_out,
    own_in,
    own_down,
    in_first_b,
    in_first_a,
    down_first_b,
    down_first_a,
    wq,
    wo,
    wi,
    wd,
    gains,
    biases,
    gbuf,
    high_ga,
    qkv,
    keys,
    values,
    grad_k,
    grad_v,
    grad_qkv,
    send_a,
    send_b,
    got_a,
    got_b,
    low_gz,
    low_pre,
    low_ga,
    grad_mixed,
    grads,
    result,
    slope,
    scale_z,
    middle,
    scale_a,
    mixed,
    stat,
    w_sem,
    load_sem,
    hop_send,
    hop_got,
    pass_send,
    pass_got,
    a_send,
    a_got,
    b_send,
    b_got,
    qkv_sem,
    first_sem,
    second_sem,
    keep_sem,
    keep_ga_sem,
    keep_qkv_sem,
    grads_sem,
    out_send,
    out_got,
    stage,
    right_sem,
    left_sem,
    store_sem,
    part_send,
    part_got,
):
    at = Seat()
    section, core, peer = at.section, at.core, at.peer
    micro, length, width = gbuf.shape
    count = own_ref.shape[1] - 1
    columns = grad_mixed.shape[1]
    pairs = columns // LANES
    chunks = length // chunk
    half = chunk // 2
    last = sections - 1
    shape = (chunk, LANES)

    weights = [
        pltpu.make_async_copy(source, target, w_sem.at[i])
        for i, (source, target) in enumerate(
            ((down_w, wd), (in_w, wi), (out_w, wo), (qkv_w, wq))
        )
    ]
    for copy in weights:
        copy.start()

    def load(m, j):
        rows = rows_of(j, chunk)
        return pltpu.make_async_copy(
            rows_back.at[m, rows], gbuf.at[m, rows], load_sem.at[m, j]
        )

    def hop(m, j):
        target = pl.ds(pl.multiple_of(j * chunk + core * half, half), half)
        return pltpu.make_async_remote_copy(
            src_ref=grads.at[j, pl.ds(pl.multiple_of(core * half, half), half)],
            dst_ref=gbuf.at[m, target],
            send_sem=hop_send.at[j],
            recv_sem=hop_got.at[m, j],
            device_id={"section": section - 1},
            device_id_type=MESH,
        )

    def hand_over(m, j):
        rows = pl.ds(pl.multiple_of(j * chunk + core * half, half), half)
        return pltpu.make_async_remote_copy(
            src_ref=gbuf.at[m, rows],
            dst_ref=gbuf.at[m, rows],
            send_sem=pass_send.at[m, j],
            recv_sem=pass_got.at[m, j],
            device_id=peer,
            device_id_type=MESH,
        )

    def exchange(send, got, send_sem, got_sem, m, j):
        slot = lax.rem(j, send.shape[0])
        return pltpu.make_async_remote_copy(
            src_ref=send.at[slot],
            dst_ref=got.at[j],
            send_sem=send_sem.at[slot],
            recv_sem=got_sem.at[m, j],
            device_id=peer,
            device_id_type=MESH,
        )

    def exchange_a(m, j):
        return exchange(send_a, got_a, a_send, a_got, m, j)

    def exchange_b(m, j):
        return exchange(send_b, got_b, b_send, b_got, m, j)

    def load_qkv(m):
        return pltpu.make_async_copy(qkv_in.at[m], qkv, qkv_sem)

    def load_first(m, j):
        rows = rows_of(j, chunk)
        slot = lax.rem(j, 2)
        return [
            pltpu.make_async_copy(result_in.at[m, rows], result.at[slot], first_sem.at[slot, 0]),
            pltpu.make_async_copy(slope_in.at[m, rows], slope.at[slot], first_sem.at[slot, 1]),
            pltpu.make_async_copy(scale_in.at[m, 1, rows], scale_z.at[slot], first_sem.at[slot, 2]),
        ]

    def load_second(m, j):
        rows = rows_of(j, chunk)
        return [
            pltpu.make_async_copy(middle_in.at[m, rows], middle, second_sem.at[0]),
            pltpu.make_async_copy(scale_in.at[m, 0, rows], scale_a, second_sem.at[1]),
            pltpu.make_async_copy(mixed_in.at[m, rows], mixed, second_sem.at[2]),
            pltpu.make_async_copy(stat_in.at[m, rows], stat, second_sem.at[3]),
        ]

    def keep_first(m, j):
        rows = rows_of(j, chunk)
        slot = lax.rem(j, 2)
        return [
            pltpu.make_async_copy(low_gz.at[j], gz_out.at[m, rows], keep_sem.at[slot, 0]),
            pltpu.make_async_copy(low_pre.at[slot], pre_out.at[m, rows], keep_sem.at[slot, 1]),
        ]

    def keep_second(m, j):
        rows = rows_of(j, chunk)
        return pltpu.make_async_copy(low_ga, ga_out.at[m, rows], keep_ga_sem)

    def keep_qkv(m):
        return pltpu.make_async_copy(grad_qkv, gqkv_out.at[m], keep_qkv_sem)

    placed = OutPieces(at, grads, grads_out, grads_sem, out_send, out_got)

    load_qkv(0).start()
    for copy in load_first(0, 0) + load_first(0, 1) + load_second(0, 0):
        copy.start()

    @pl.when(section == last)
    def _():
        for m in range(micro):
            for j in range(chunks):
                load(m, j).start()

    gains[...] = gains_in[...].astype(jnp.float32)
    biases[...] = biases_in[...].astype(jnp.float32)
    row_sums[...] = jnp.zeros_like(row_sums)
    in_sums[...] = jnp.zeros_like(in_sums)
    qkv_sums[...] = jnp.zeros_like(qkv_sums)
    time_sums[...] = jnp.zeros_like(time_sums)
    greet(section, sections, (at.peer, at.across, at.beside))

    def add_row(index, value):
        row_sums[index : index + 1] += jnp.sum(value, axis=0, keepdims=True)

    def receive(m, j):
        @pl.when(section < last)
        def _():
            hop(m, j).wait_recv()
            hand_over(m, j).start()

    def norm_back_rows(gradient, unit, inv_scale, gain):
        weighted = gradient * gain
        return inv_scale * (
            weighted
            - jnp.mean(weighted, axis=-1, keepdims=True)
            - unit * jnp.mean(weighted * unit, axis=-1, keepdims=True)
        )

    def feed_back(m, j):
        rows = rows_of(j, chunk)
        slot = lax.rem(j, 2)

        @pl.when(section == last)
        def _():
            load(m, j).wait()

        @pl.when(section < last)
        def _():
            hand_over(m, j).wait_recv()

        for copy in load_first(m, j):
            copy.wait()
        gradient = gbuf[m, rows].astype(jnp.float32)
        unit = (result[slot].astype(jnp.float32) - biases[3:4]) / gains[1:2]
        grad_z = norm_back_rows(gradient, unit, scale_z[slot, :, :1], gains[1:2])
        add_row(1, gradient * unit)
        add_row(5, gradient)
        add_row(4, grad_z)
        low_gz[j] = grad_z.astype(low_type)
        hidden_size = wi.shape[1]
        step = min(1024, hidden_size)

        def before(start):
            return dot_rows(low_gz[j], wd[start : start + step])

        current = before(0)
        branch = jnp.zeros((chunk, width), jnp.float32)
        for start in range(0, hidden_size, step):
            part = slice(start, start + step)
            later = before(start + step) if start + step < hidden_size else None
            low = (current * slope[slot, :, part].astype(jnp.float32)).astype(low_type)
            low_pre[slot, :, part] = low
            in_sums[:, part] += jnp.sum(low.astype(jnp.float32), axis=0, keepdims=True)
            branch = branch + dot_rows(low, wi[:, part])
            current = later
        send_a[j] = branch.astype(low_type)
        exchange_a(m, j).start()
        for copy in keep_first(m, j):
            copy.start()

    def norm_step(m, j):
        rows = rows_of(j, chunk)
        exchange_a(m, j).wait()
        for copy in load_second(m, j):
            copy.wait()
        gradient = (
            send_a[j].astype(jnp.float32)
            + got_a[j].astype(jnp.float32)
            + low_gz[j].astype(jnp.float32)
        )
        unit = (middle[...].astype(jnp.float32) - biases[1:2]) / gains[0:1]
        grad_a = norm_back_rows(gradient, unit, scale_a[:, :1], gains[0:1])
        add_row(0, gradient * unit)
        add_row(3, gradient)
        add_row(2, grad_a)
        high_ga[rows] = grad_a.astype(low_type)
        low_ga[...] = grad_a.astype(low_type)
        keep_second(m, j).start()
        grad_mixed[...] = dot_rows(low_ga[...], wo[...]).astype(low_type)

    def build(m):
        load_qkv(m).wait()

        starts, _ = row_facts(at, own_ref, other_ref, m)

        def step(j, carry):
            rows = rows_of(j, chunk)
            first, rel, own = doc_lanes(starts, j * chunk, shape)
            fixed = jnp.logical_and(rel >= count, rel < count + 3)
            extra_k = jnp.where(jnp.logical_or(own, fixed), 1.0, 0.0).astype(low_type)
            extra_v = jnp.where(fixed, 1.0, 0.0).astype(low_type)
            for p in range(pairs):
                lane = slice(p * LANES, (p + 1) * LANES)
                k = qkv[rows, columns + p * LANES : columns + (p + 1) * LANES]
                v = qkv[rows, 2 * columns + p * LANES : 2 * columns + (p + 1) * LANES]
                keys[2 * p, rows] = jnp.where(first, k, extra_k)
                keys[2 * p + 1, rows] = jnp.where(first, extra_k, k)
                values[2 * p, rows] = jnp.where(first, v, extra_v)
                values[2 * p + 1, rows] = jnp.where(first, extra_v, v)
                grad_k[rows, lane] = jnp.zeros(shape, jnp.float32)
                grad_v[rows, lane] = jnp.zeros(shape, jnp.float32)
            return carry

        lax.fori_loop(0, chunks, step, 0)

    def mix_back(m, j):
        rows = rows_of(j, chunk)
        lane_index = lax.broadcasted_iota(jnp.int32, shape, 1)
        first = lane_index < HEAD
        rel = lane_index % HEAD
        all_first = lax.broadcasted_iota(jnp.int32, (length, LANES), 1) < HEAD
        for p in range(pairs):
            lane = slice(p * LANES, (p + 1) * LANES)
            q = qkv[rows, lane] * low_type(HEAD**-0.5)
            k = qkv[:, columns + p * LANES : columns + (p + 1) * LANES]
            g = grad_mixed[:, lane]
            extra_q = stat[:, lane]
            product = g.astype(jnp.float32) * mixed[:, lane].astype(jnp.float32)
            dots = [
                jnp.sum(jnp.where(first, product, 0.0), axis=-1, keepdims=True),
                jnp.sum(jnp.where(first, 0.0, product), axis=-1, keepdims=True),
            ]
            extra_g = lanes(
                rel, count, -jnp.where(first, dots[1], dots[0]), jnp.zeros_like(extra_q)
            )
            parts = []
            for i in range(2):
                q_head = jnp.where(first, q, extra_q) if i == 0 else jnp.where(first, extra_q, q)
                g_head = jnp.where(first, g, extra_g) if i == 0 else jnp.where(first, extra_g, g)
                probs = jnp.exp(dot_rows(keys[2 * p + i], q_head))
                slopes = (probs * dot_rows(values[2 * p + i], g_head)).astype(low_type)
                parts.append(
                    (
                        dot_plain(probs.astype(low_type), g),
                        dot_plain(slopes, q),
                        dot_first(slopes, k),
                    )
                )
            grad_v[:, lane] += jnp.where(all_first, parts[0][0], parts[1][0])
            grad_k[:, lane] += jnp.where(all_first, parts[0][1], parts[1][1])
            grad_qkv[rows, lane] = (
                jnp.where(first, parts[0][2], parts[1][2]) * (HEAD**-0.5)
            ).astype(low_type)

    def project_back(m, j):
        rows = rows_of(j, chunk)
        low = grad_qkv[rows]
        qkv_sums[...] += jnp.sum(low.astype(jnp.float32), axis=0, keepdims=True)
        total = dot_rows(low[:, :columns], wq[0])
        for third in range(1, 3):
            total = total + dot_rows(low[:, third * columns : (third + 1) * columns], wq[third])
        send_b[lax.rem(j, 2)] = total.astype(low_type)
        exchange_b(m, j).start()

    def finish(m, j):
        rows = rows_of(j, chunk)
        slot = lax.rem(j, 2)
        exchange_b(m, j).wait()

        @pl.when(m > 0)
        def _():
            placed.wait(m - 1, j)

            @pl.when(section > 0)
            def _():
                hop(m - 1, j).wait_send()

        total = (
            send_b[slot].astype(jnp.float32) + got_b[j].astype(jnp.float32) + high_ga[rows].astype(jnp.float32)
        ).astype(low_type)
        grads[j] = total
        time_sums[m] += jnp.sum(total.astype(jnp.float32), axis=0, keepdims=True)

        @pl.when(section > 0)
        def _():
            hop(m, j).start()

        placed.start(m, j)

    def block(order):
        owner = jnp.where(order < 2, 1 - at.chip, at.chip)
        return 2 * owner + lax.rem(order, 2)

    def feed_products():
        @pl.when(section < last)
        def _():
            for m in range(micro):
                for j in range(chunks):
                    hand_over(m, j).wait_send()

        width_half = width
        block_in, block_down = own_in.shape[1], own_down.shape[1]
        phases = (
            (middle_in, pre_out, width_half, block_in),
            (middle_in, pre_out, 0, block_in),
            (hidden_in, gz_out, 0, block_down),
        )

        def room(phase, m):
            if phase % 2 == 0:
                return gbuf.at[m]
            return wi.at[:, pl.ds(m * width, width)]

        def load_right(phase):
            _, right, first, _ = phases[phase]
            return [
                pltpu.make_async_copy(
                    right.at[m, :, pl.ds(first, width)],
                    room(phase, m),
                    right_sem.at[phase % 2, m],
                )
                for m in range(micro)
            ]

        def spot(t):
            return pl.ds(pl.multiple_of(lax.rem(t, 2) * chunk, chunk), chunk)

        for copy in load_right(0):
            copy.start()
        for phase, (left, right, first, rows) in enumerate(phases):
            subs = rows // chunk
            if phase + 1 < len(phases):
                for copy in load_right(phase + 1):
                    copy.start()

            def load_left(t, left=left, rows=rows, subs=subs):
                start = block(t // subs) * rows + lax.rem(t, subs) * chunk
                return [
                    pltpu.make_async_copy(
                        left.at[m, :, pl.ds(pl.multiple_of(start, chunk), chunk)],
                        wd.at[pl.ds(m * length, length), spot(t)],
                        left_sem.at[lax.rem(t, 2), m],
                    )
                    for m in range(micro)
                ]

            def store(t, phase=phase, first=first, subs=subs):
                order = t // subs
                if phase < 2:
                    target = own_in.at[order, :, pl.ds(first, width)]
                else:
                    target = own_down.at[order, rows_of(lax.rem(t, subs), chunk)]
                slot = lax.rem(t, 2)
                return pltpu.make_async_copy(stage.at[slot], target, store_sem.at[slot])

            def after(t, phase=phase, subs=subs, store=store):
                store(t).wait()
                order = t // subs

                @pl.when(lax.rem(t, subs) == subs - 1)
                def _():
                    if phase != 1:

                        @pl.when(order < 2)
                        def _():
                            (part_in_b if phase == 0 else part_down_b)(order).start()

                    if phase > 0:

                        @pl.when(at.away)
                        def _():
                            (part_in_a if phase == 1 else part_down_a)(order).start()

            for copy in load_left(0):
                copy.start()
            for copy in load_right(phase):
                copy.wait()

            def step(
                t, carry, load_left=load_left, store=store, after=after, subs=subs, phase=phase
            ):
                for copy in load_left(t):
                    copy.wait()

                @pl.when(t + 1 < 4 * subs)
                def _():
                    for copy in load_left(t + 1):
                        copy.start()

                value = dot_first(wd[:length, spot(t)], room(phase, 0)[...])
                for m in range(1, micro):
                    value = value + dot_first(
                        wd[m * length : (m + 1) * length, spot(t)], room(phase, m)[...]
                    )

                @pl.when(t > 0)
                def _():
                    after(t - 1)

                stage[lax.rem(t, 2)] = value.astype(low_type)
                store(t).start()
                return carry

            lax.fori_loop(0, 4 * subs, step, 0)
            after(4 * subs - 1)

    def part_in_b(order):
        return remote(
            own_in.at[order, :, pl.ds(width, width)],
            in_first_b.at[order],
            part_send.at[order],
            part_got.at[order],
            at.beside,
        )

    def part_in_a(order):
        return remote(
            own_in.at[order, :, pl.ds(0, width)],
            in_first_a.at[order],
            part_send.at[2 + order],
            part_got.at[2 + order],
            at.across,
        )

    def part_down_b(order):
        return remote(
            own_down.at[order, :, pl.ds(width // 2, width // 2)],
            down_first_b.at[order],
            part_send.at[6 + order],
            part_got.at[6 + order],
            at.beside,
        )

    def part_down_a(order):
        return remote(
            own_down.at[order, :, pl.ds(0, width // 2)],
            down_first_a.at[order],
            part_send.at[8 + order],
            part_got.at[8 + order],
            at.across,
        )

    def one_row(m, carry):
        early = jnp.logical_and(section == 0, m == micro - 1)

        @pl.when(m == 0)
        def _():
            weights[0].wait()
            weights[1].wait()

        receive(m, 0)

        def first_step(j, carry):
            @pl.when(j >= 2)
            def _():
                for copy in keep_first(m, j - 2):
                    copy.wait()

            feed_back(m, j)

            @pl.when(j + 2 < chunks)
            def _():
                for copy in load_first(m, j + 2):
                    copy.start()

            @pl.when(jnp.logical_and(j + 2 >= chunks, m + 1 < micro))
            def _():
                for copy in load_first(m + 1, j + 2 - chunks):
                    copy.start()

            return carry

        def reached(i):
            return jnp.minimum(i * (i + 1) // 2, chunks)

        def step(i, carry):
            @pl.when(i >= 1)
            def _():
                @pl.when(i >= 2)
                def _():
                    keep_second(m, i - 2).wait()

                norm_step(m, i - 1)

                @pl.when(i == 1)
                def _():
                    receive(m, 1)

                @pl.when(i == 2)
                def _():
                    receive(m, 3)

                mix_back(m, i - 1)

                @pl.when(i < chunks)
                def _():
                    for copy in load_second(m, i):
                        copy.start()

                @pl.when(jnp.logical_and(i == chunks, m + 1 < micro))
                def _():
                    for copy in load_second(m + 1, 0):
                        copy.start()

                @pl.when(i == 1)
                def _():
                    receive(m, 2)

            lax.fori_loop(reached(i), reached(i + 1), first_step, 0)

            @pl.when(i == 0)
            def _():
                @pl.when(m == 0)
                def _():
                    weights[2].wait()
                    weights[3].wait()

                build(m)

            @pl.when(jnp.logical_and(early, i == 2))
            def _():
                for copy in keep_first(m, chunks - 2) + keep_first(m, chunks - 1):
                    copy.wait()
                feed_products()

            return carry

        lax.fori_loop(0, chunks + 1, step, 0)

        @pl.when(jnp.logical_not(early))
        def _():
            for copy in keep_first(m, chunks - 2) + keep_first(m, chunks - 1):
                copy.wait()

        keep_second(m, chunks - 1).wait()

        @pl.when(m + 1 < micro)
        def _():
            load_qkv(m + 1).start()

        grad_qkv[:, columns : 2 * columns] = grad_k[...].astype(low_type)
        grad_qkv[:, 2 * columns :] = grad_v[...].astype(low_type)
        keep_qkv(m).start()

        shift = jnp.where(jnp.logical_and(section == 0, at.group == 0), chunks // 2, 0)

        def last_step(i, carry):
            @pl.when(i < chunks)
            def _():
                project_back(m, lax.rem(i + shift, chunks))

            @pl.when(i >= 1)
            def _():
                finish(m, lax.rem(i - 1 + shift, chunks))

            return carry

        lax.fori_loop(0, chunks + 1, last_step, 0)
        keep_qkv(m).wait()
        return carry

    lax.fori_loop(0, micro, one_row, 0)
    for j in range(chunks):
        placed.wait(micro - 1, j)

    @pl.when(section > 0)
    def _():
        for j in range(chunks):
            hop(micro - 1, j).wait_send()

    pl.when(section > 0)(feed_products)
    for order in range(2):
        part_in_b(order).wait()
        part_down_b(order).wait()
    for order in range(4):

        @pl.when(at.away)
        def _(order=order):
            part_in_a(order).wait_send()
            part_down_a(order).wait_send()

        @pl.when(at.home)
        def _(order=order):
            part_in_a(order).wait_recv()
            part_down_a(order).wait_recv()

    placed.wait_got()


def backward_pass(sections, facts, gains, biases, rows_back, params, stash):
    qkv_w, out_w, in_w, down_w = params
    micro, length, width = rows_back.shape
    columns, hidden = out_w.shape[0], in_w.shape[1]
    chunk = min(256, length // 4)
    chunks = length // chunk
    low, high = low_type, jnp.float32

    def out(*shape, dtype=low):
        return jax.ShapeDtypeStruct(shape, dtype)

    outs = dict(
        row_sums=out(6, width, dtype=high),
        in_sums=out(1, hidden, dtype=high),
        qkv_sums=out(1, 3 * columns, dtype=high),
        time_sums=out(micro, 1, width, dtype=high),
        grad_z=out(micro, length, width),
        grad_pre=out(micro, length, hidden),
        grad_a=out(micro, length, width),
        grad_qkv=out(micro, length, 3 * columns),
        grads=out(micro, length // 2, width),
        own_in=out(4, width // 4, hidden),
        own_down=out(4, hidden // 4, width),
        in_first_b=out(2, width // 4, hidden // 2),
        in_first_a=out(4, width // 4, hidden // 2),
        down_first_b=out(2, hidden // 4, width // 2),
        down_first_a=out(4, hidden // 4, width // 2),
    )
    vmem = pl.BlockSpec(memory_space=pltpu.VMEM)
    anywhere = pl.BlockSpec(memory_space=pl.ANY)
    dma = pltpu.SemaphoreType.DMA
    results = pl.pallas_call(
        functools.partial(backward_kernel, sections, chunk),
        in_specs=[pl.BlockSpec(memory_space=pltpu.SMEM)] * 2 + [vmem] * 2 + [anywhere] * 13,
        out_specs=[vmem] * 4 + [anywhere] * 11,
        out_shape=list(outs.values()),
        scratch_shapes=[
            pltpu.VMEM(qkv_w.shape, low),
            pltpu.VMEM(out_w.shape, low),
            pltpu.VMEM(in_w.shape, low),
            pltpu.VMEM(down_w.shape, low),
            pltpu.VMEM(gains.shape, high),
            pltpu.VMEM(biases.shape, high),
            pltpu.VMEM((micro, length, width), low),
            pltpu.VMEM((length, width), low),
            pltpu.VMEM((length, 3 * columns), low),
            pltpu.VMEM((columns // HEAD, length, LANES), low),
            pltpu.VMEM((columns // HEAD, length, LANES), low),
            pltpu.VMEM((length, columns), high),
            pltpu.VMEM((length, columns), high),
            pltpu.VMEM((length, 3 * columns), low),
            pltpu.VMEM((chunks, chunk, width), low),
            pltpu.VMEM((2, chunk, width), low),
            pltpu.VMEM((chunks, chunk, width), low),
            pltpu.VMEM((chunks, chunk, width), low),
            pltpu.VMEM((chunks, chunk, width), low),
            pltpu.VMEM((2, chunk, hidden), low),
            pltpu.VMEM((chunk, width), low),
            pltpu.VMEM((chunk, columns), low),
            pltpu.VMEM((chunks, chunk, width), low),
            pltpu.VMEM((2, chunk, width), low),
            pltpu.VMEM((2, chunk, hidden), low),
            pltpu.VMEM((2, chunk, LANES), high),
            pltpu.VMEM((chunk, width), low),
            pltpu.VMEM((chunk, LANES), high),
            pltpu.VMEM((chunk, columns), low),
            pltpu.VMEM((chunk, columns), low),
            dma((4,)),
            dma((micro, chunks)),
            dma((chunks,)),
            dma((micro, chunks)),
            dma((micro, chunks)),
            dma((micro, chunks)),
            dma((chunks,)),
            dma((micro, chunks)),
            dma((2,)),
            dma((micro, chunks)),
            dma,
            dma((2, 3)),
            dma((4,)),
            dma((2, 2)),
            dma,
            dma,
            dma((chunks,)),
            dma((chunks,)),
            dma((chunks // 2,)),
            pltpu.VMEM((2, chunk, width), low),
            dma((2, micro)),
            dma((2, micro)),
            dma((2,)),
            dma((12,)),
            dma((12,)),
        ],
        compiler_params=pltpu.CompilerParams(
            collective_id=1, has_side_effects=True, vmem_limit_bytes=63 * 1024 * 1024
        ),
        name="backward_pass",
    )(
        *facts,
        gains,
        biases,
        rows_back,
        qkv_w,
        out_w,
        in_w,
        down_w,
        stash["qkv"],
        stash["log_sums"],
        stash["mixed"],
        stash["middle"],
        stash["hidden"],
        stash["slope"],
        stash["result"],
        stash["scales"],
    )
    return dict(zip(outs, results))


def gradient_kernel(
    sections,
    plan,
    ready,
    own_ref,
    other_ref,
    row_sums,
    in_sums,
    qkv_sums,
    time_sums,
    *refs,
):
    count = len(plan)
    done = len(ready)
    number = 1 + max(part[0] for part in plan)
    made = {w: i for i, w in enumerate(sorted({part[0] for part in plan[done:]}))}
    products, arrived = refs[: 1 + max(ready)], refs[1 + max(ready) : 1 + max(ready) + done]
    refs = refs[1 + max(ready) + done :]
    lefts, rights = refs[: len(made)], refs[len(made) : 2 * len(made)]
    refs = refs[2 * len(made) :]
    outs = refs[:number]
    gains_out, biases_out, qv_out, in_out, time_rows_out = refs[number : number + 5]
    refs = refs[number + 5 :]
    tiles, firsts, seconds, shares, finals = (
        refs[i * count : (i + 1) * count] for i in range(5)
    )
    (
        held,
        right,
        small_in,
        small_group,
        small_beside,
        small_out,
        other_out,
        time_out,
        left_sem,
        right_sem,
        first_send,
        first_got,
        second_send,
        second_got,
        share_send,
        share_got,
        final_sem,
        ready_sem,
        small_send,
        small_got,
    ) = refs[5 * count :]
    at = Seat()
    section, chip, core = at.section, at.chip, at.core

    def block(order):
        owner = 1 - chip if order < 2 else chip
        return 2 * owner + order % 2

    steps = []
    for w, (_, rows, _, _, _) in enumerate(plan):
        if w < done:
            continue
        width = min(256, rows)
        for order in range(4):
            for start in range(0, rows, width):
                steps.append((w, order, start, width))

    def load_left(index):
        w, order, start, width = steps[index]
        number, rows, _, _, _ = plan[w]
        first = pl.multiple_of(block(order) * rows + start, width)
        return pltpu.make_async_copy(
            lefts[made[number]].at[:, pl.ds(first, width)],
            held.at[index % 2, :, pl.ds(0, width)],
            left_sem.at[index % 2],
        )

    def room(w):
        return right.at[w % 2, :, pl.ds(0, plan[w][3])]

    def load_right(w):
        number, _, first, columns, _ = plan[w]
        return pltpu.make_async_copy(
            rights[made[number]].at[:, pl.ds(first, columns)], room(w), right_sem.at[w % 2]
        )

    def send_first(w, order):
        if plan[w][4]:
            return remote(
                tiles[w].at[order],
                firsts[w].at[order],
                first_send.at[w, order],
                first_got.at[w, order],
                at.across,
            )
        return remote(
            tiles[w].at[order],
            firsts[w].at[order],
            first_send.at[w, order],
            first_got.at[w, order],
            at.beside,
        )

    def send_second(w, order):
        if plan[w][4]:
            return remote(
                tiles[w].at[order],
                seconds[w].at[order],
                second_send.at[w, order],
                second_got.at[w, order],
                at.beside,
            )
        return remote(
            tiles[w].at[2 + order],
            seconds[w].at[order],
            second_send.at[w, order],
            second_got.at[w, order],
            at.across,
        )

    def send_share(w):
        return remote(
            tiles[w].at[3 - core], shares[w], share_send.at[w], share_got.at[w], at.peer
        )

    def store_final(w):
        number, _, first, columns, _ = plan[w]
        target = outs[number]
        if len(target.shape) == 2:
            places = [(finals[w], target.at[:, pl.ds(first, columns)])]
        else:
            size = target.shape[2]
            places = [
                (finals[w].at[:, pl.ds(i * size, size)], target.at[first // size + i])
                for i in range(columns // size)
            ]
        return [
            pltpu.make_async_copy(source, place, final_sem.at[w, i])
            for i, (source, place) in enumerate(places)
        ]

    def put_final(w, value):
        finals[w][...] = value.astype(finals[w].dtype)
        for copy in store_final(w):
            copy.start()

    def high(value):
        return value.astype(jnp.float32)

    def load_ready(w):
        number, _, first, columns, _ = plan[w]
        return [
            pltpu.make_async_copy(
                products[number].at[:, :, pl.ds(first, columns)], tiles[w], ready_sem.at[w, 0]
            ),
            pltpu.make_async_copy(arrived[w], firsts[w], ready_sem.at[w, 1]),
        ]

    for w in range(done):
        for copy in load_ready(w):
            copy.start()
    load_right(done).start()
    load_right(done + 1).start()
    load_left(0).start()
    small_in[...] = jnp.zeros_like(small_in)
    small_in[0:6] = row_sums[...]
    weighted = jnp.zeros_like(time_sums[0])
    plain = jnp.zeros_like(time_sums[0])
    for m in range(time_sums.shape[0]):
        _, moment = row_facts(at, own_ref, other_ref, m)
        fraction = jnp.full((1, time_sums.shape[2]), moment.astype(jnp.float32)) / 5000.0
        weighted = weighted + fraction * time_sums[m]
        plain = plain + time_sums[m]
    from_first = jnp.where(section == 0, 1.0, 0.0)
    small_in[8:9] = weighted * from_first
    small_in[9:10] = plain * from_first
    width = small_in.shape[1]
    for i in range(in_sums.shape[1] // width):
        small_in[16 + i : 17 + i] = in_sums[:, i * width : (i + 1) * width]
    third = qkv_sums.shape[1] // 3
    small_in[20:21, :third] = qkv_sums[:, :third]
    small_in[20:21, third : 2 * third] = qkv_sums[:, 2 * third :]
    greet(section, sections, (at.peer, at.across, at.beside))

    small_across = remote(
        small_in, small_group, small_send.at[0], small_got.at[0], at.across
    )
    small_chips = remote(
        small_in, small_beside, small_send.at[1], small_got.at[1], at.beside
    )
    small_cores = remote(small_out, other_out, small_send.at[2], small_got.at[2], at.peer)
    time_hop = remote(
        time_out, time_out, small_send.at[3], small_got.at[3], {"section": section + 1}
    )
    small_across.start()

    def second_stage(w):
        shift, condition = (0, at.home) if plan[w][4] else (2, at.away)

        @pl.when(condition)
        def _():
            for order in range(2):
                if w >= done:
                    send_first(w, order).wait_recv()
                tiles[w][shift + order] = (
                    high(tiles[w][shift + order]) + high(firsts[w][order])
                ).astype(low_type)
                send_second(w, order).start()

    for w in range(done):
        for copy in load_ready(w):
            copy.wait()
        second_stage(w)
    seen = 0
    for w, (_, _, _, columns, across_first) in enumerate(plan):
        if w < done:
            continue
        load_right(w).wait()
        for order in range(4):
            while seen < len(steps) and steps[seen][:2] == (w, order):
                load_left(seen).wait()
                if seen + 1 < len(steps):
                    load_left(seen + 1).start()
                _, _, start, step_width = steps[seen]
                tiles[w][order, start : start + step_width] = dot_first(
                    held[seen % 2, :, :step_width], right[w % 2, :, :columns]
                ).astype(low_type)
                seen += 1
            if across_first:
                pl.when(at.away)(send_first(w, order).start)
            elif order < 2:
                send_first(w, order).start()
        if w + 2 < count:
            load_right(w + 2).start()
        if w == done:
            small_across.wait()
            small_in[...] += small_group[...]
            small_chips.start()
        if w == done + 1:
            small_chips.wait()
            small_out[...] = small_in[...] + small_beside[...]
            small_cores.start()

    @pl.when(section == 0)
    def _():
        time_out[...] = small_out[8:16]

    for w in range(done, count):
        second_stage(w)

    @pl.when(at.home)
    def _():
        for w, (_, _, _, _, across_first) in enumerate(plan):
            for order in range(2):
                if w >= done:
                    send_first(w, order + 2 if across_first else order).wait_recv()
                send_second(w, order).wait_recv()

            def total(side):
                first = firsts[w][2 + side] if across_first else firsts[w][side]
                return high(tiles[w][2 + side]) + high(first) + high(seconds[w][side])

            tiles[w][3 - core] = total(1 - core).astype(low_type)
            send_share(w).start()
            put_final(w, total(core))

    @pl.when(at.away)
    def _():
        for w in range(count):
            send_share(w).wait_recv()
            put_final(w, shares[w][...])

    small_cores.wait()
    device = 4 * at.group + 2 * chip + core
    lane = pl.ds(pl.multiple_of(device * LANES, LANES), LANES)
    gains_out[...] = small_out[0:2, lane]
    biases_out[...] = small_out[2:6, lane]

    def place(source):
        quarter = 2 * chip + core
        size = third // 4
        qv_out[0:1] = source[20:21, pl.ds(pl.multiple_of(quarter * size, size), size)]
        qv_out[1:2] = source[20:21, pl.ds(pl.multiple_of(third + quarter * size, size), size)]
        size = in_out.shape[1]
        per = width // size
        spot = pl.ds(pl.multiple_of(lax.rem(quarter, per) * size, size), size)
        for i in range(4 // per):

            @pl.when(quarter // per == i)
            def _(i=i):
                in_out[...] = source[16 + i : 17 + i, spot]

    pl.when(at.home)(functools.partial(place, small_out))
    pl.when(at.away)(functools.partial(place, other_out))

    @pl.when(section > 0)
    def _():
        time_hop.wait_recv()

    @pl.when(section < sections - 1)
    def _():
        time_hop.start()
        time_hop.wait_send()

    time_rows_out[...] = time_out[0:2]
    for w, (_, _, _, _, across_first) in enumerate(plan):
        for copy in store_final(w):
            copy.wait()
        if across_first:

            @pl.when(at.away)
            def _(w=w):
                for order in range(4):
                    if w >= done:
                        send_first(w, order).wait_send()

            @pl.when(at.home)
            def _(w=w):
                for order in range(2):
                    send_second(w, order).wait_send()

        else:
            for order in range(2):
                if w >= done:
                    send_first(w, order).wait_send()

            @pl.when(at.away)
            def _(w=w):
                for order in range(2):
                    send_second(w, order).wait_send()

        pl.when(at.home)(send_share(w).wait_send)


def gradient_pass(sections, facts, back, products, arrived, lefts, rights, splits, order):
    blocks = [product.shape[1:] for product in products]
    blocks += [(left.shape[1] // 4, right.shape[1]) for left, right in zip(lefts, rights)]
    plan = tuple(
        (number, blocks[number][0], first, columns, across)
        for number, first, columns, across in order
    )
    ready = tuple(part[0] for part in plan[: len(arrived)])
    finals = [
        (rows, columns) if split == 1 else (split, rows, columns // split)
        for (rows, columns), split in zip(blocks, splits)
    ]
    length = lefts[0].shape[0]
    low, high = low_type, jnp.float32
    width = back["row_sums"].shape[1]
    count = len(plan)
    vmem = pl.BlockSpec(memory_space=pltpu.VMEM)
    anywhere = pl.BlockSpec(memory_space=pl.ANY)
    dma = pltpu.SemaphoreType.DMA
    small = (24, width)
    hidden = back["in_sums"].shape[1]
    smalls = [
        (2, width // 8),
        (4, width // 8),
        (2, back["qkv_sums"].shape[1] // 12),
        (1, hidden // 4),
        (2, width),
    ]

    def buffers(size):
        return [pltpu.VMEM((size(part), part[1], part[3]), low) for part in plan]

    return pl.pallas_call(
        functools.partial(gradient_kernel, sections, plan, ready),
        in_specs=[pl.BlockSpec(memory_space=pltpu.SMEM)] * 2
        + [vmem] * 4
        + [anywhere] * (len(products) + len(arrived) + 2 * len(lefts)),
        out_specs=[anywhere] * len(finals) + [vmem] * len(smalls),
        out_shape=[jax.ShapeDtypeStruct(shape, low) for shape in finals]
        + [jax.ShapeDtypeStruct(shape, high) for shape in smalls],
        scratch_shapes=buffers(lambda part: 4)
        + buffers(lambda part: 4 if part[4] else 2)
        + buffers(lambda part: 2)
        + [pltpu.VMEM((part[1], part[3]), low) for part in plan]
        + [pltpu.VMEM((part[1], part[3]), low) for part in plan]
        + [
            pltpu.VMEM((2, length, min(256, max(part[1] for part in plan))), low),
            pltpu.VMEM((2, length, max(part[3] for part in plan[len(ready) :])), low),
        ]
        + [pltpu.VMEM(small, high)] * 5
        + [
            pltpu.VMEM((8, width), high),
            dma((2,)),
            dma((2,)),
            dma((count, 4)),
            dma((count, 4)),
            dma((count, 2)),
            dma((count, 2)),
            dma((count,)),
            dma((count,)),
            dma((count, 2)),
            dma((count, 2)),
            dma((4,)),
            dma((4,)),
        ],
        compiler_params=pltpu.CompilerParams(
            collective_id=2, has_side_effects=True, vmem_limit_bytes=62 * 1024 * 1024
        ),
        name="gradient_pass",
    )(
        *facts,
        back["row_sums"],
        back["in_sums"],
        back["qkv_sums"],
        back["time_sums"],
        *products,
        *arrived,
        *lefts,
        *rights,
    )


def unit_norm(value):
    average = jnp.mean(value, axis=-1, keepdims=True)
    centered = value - average
    inv_scale = lax.rsqrt(jnp.mean(centered * centered, axis=-1, keepdims=True) + eps_norm)
    return centered * inv_scale, inv_scale


def norm_back(gradient, normed, inv_scale, gain_row):
    weighted = gradient * gain_row
    adjusted = (
        weighted
        - jnp.mean(weighted, axis=-1, keepdims=True)
        - normed * jnp.mean(weighted * normed, axis=-1, keepdims=True)
    )
    return inv_scale * adjusted


def gelu_pair(pre):
    normal = 0.5 * (1.0 + lax.erf(pre * 0.7071067811865476))
    density = jnp.exp(-0.5 * pre * pre) * 0.3989422804014327
    return pre * normal, normal + pre * density


def forward_layer(at, inputs, starts, params):
    qkv_w, qkv_b, out_w, in_w, in_b, down_w, gains, biases = params
    qkv = (dot_plain(inputs, qkv_w) + qkv_b).astype(low_type)
    mixed, log_sums = attend(qkv, starts)
    branch = at.group_sum(dot_plain(mixed, out_w).astype(low_type))
    unit_a, scale_a = unit_norm(branch + biases[0] + inputs.astype(jnp.float32))
    middle = unit_a * gains[0] + biases[1]
    low_middle = middle.astype(low_type)
    hidden, slope = gelu_pair(dot_plain(low_middle, in_w) + in_b)
    hidden = hidden.astype(low_type)
    branch_two = at.group_sum(dot_plain(hidden, down_w).astype(low_type))
    unit_z, scale_z = unit_norm(branch_two + biases[2] + middle)
    result = (unit_z * gains[1] + biases[3]).astype(low_type)
    saved = dict(
        inputs=inputs,
        qkv=qkv,
        mixed=mixed,
        log_sums=log_sums,
        scale_a=scale_a[:, 0],
        middle=low_middle,
        hidden=hidden,
        slope=slope.astype(low_type),
        scale_z=scale_z[:, 0],
    )
    return result, saved


def backward_layer(at, saved, incoming, starts, params):
    qkv_w, qkv_b, out_w, in_w, in_b, down_w, gains, biases = params
    gradient = incoming.astype(jnp.float32)
    unit_z = (saved["result"].astype(jnp.float32) - biases[3]) / gains[1]
    grad_z = norm_back(gradient, unit_z, saved["scale_z"][:, None], gains[1])
    low_gz = grad_z.astype(low_type)
    grad_pre = (dot_rows(low_gz, down_w) * saved["slope"].astype(jnp.float32)).astype(low_type)
    grad_mid = at.group_sum(dot_rows(grad_pre, in_w).astype(low_type)) + grad_z
    unit_a = (saved["middle"].astype(jnp.float32) - biases[1]) / gains[0]
    grad_a = norm_back(grad_mid, unit_a, saved["scale_a"][:, None], gains[0])
    low_ga = grad_a.astype(low_type)
    grad_mixed = dot_rows(low_ga, out_w).astype(low_type)
    grad_qkv = jnp.concatenate(
        attend_back(saved["qkv"], starts, saved["mixed"], saved["log_sums"], grad_mixed), 1
    )
    grad_x = at.group_sum(dot_rows(grad_qkv, qkv_w).astype(low_type)) + grad_a
    sums = jnp.stack(
        [
            jnp.sum(grad_mid * unit_a, axis=0),
            jnp.sum(gradient * unit_z, axis=0),
            jnp.sum(grad_a, axis=0),
            jnp.sum(grad_mid, axis=0),
            jnp.sum(grad_z, axis=0),
            jnp.sum(gradient, axis=0),
        ]
    )
    kept = dict(grad_z=low_gz, slope=grad_pre, grad_a=low_ga, qkv=grad_qkv)
    return grad_x.astype(low_type), kept, sums


def store(buffers, values, slot):
    return jax.tree.map(
        lambda buffer, value: lax.dynamic_update_index_in_dim(buffer, value, slot, 0),
        buffers,
        values,
    )


def pick(buffers, slot):
    return jax.tree.map(
        lambda buffer: lax.dynamic_index_in_dim(buffer, slot, 0, keepdims=False), buffers
    )


def group_weight(at, weight):
    parts = weight.reshape((at.chips, -1) + weight.shape[1:])

    def across(s, g, u, x, c):
        return (s, c, u, x, g) if g != c else None

    def along(step):
        return lambda s, g, u, x, c: (s, g, u, (x + step) % at.chips, c) if g != c else None

    piece = at.move(lax.dynamic_index_in_dim(parts, at.chip, 0, keepdims=False), across)
    pieces = [piece]
    for step in range(1, at.chips):
        pieces.append(at.move(piece, along(step)))
    whole = parts
    for step, piece in enumerate(pieces):
        spot = (at.chip - step) % at.chips
        own = lax.dynamic_index_in_dim(parts, spot, 0, keepdims=False)
        whole = lax.dynamic_update_index_in_dim(whole, jnp.where(at.home, own, piece), spot, 0)
    return whole.reshape(weight.shape)


def group_rows(at, tokens, section):
    def across(s, g, u, x, c):
        return (s, 1 - g, u, x, c) if s == section else None

    own = lax.dynamic_index_in_dim(tokens, at.group, 0, keepdims=False)
    other = at.move(lax.dynamic_index_in_dim(tokens, 1 - at.group, 0, keepdims=False), across)
    lower = at.group == 0
    pair = jnp.stack([jnp.where(lower, own, other), jnp.where(lower, other, own)])
    whole = at.group_gather(pair)
    whole = whole.reshape((2, at.halves) + pair.shape)
    whole = jnp.swapaxes(whole, 1, 2)
    return whole.reshape(2, -1, tokens.shape[-1])


def spread_rows(at, rows, length):
    def across(s, g, u, x, c):
        return (s, 1 - g, u, x, c)

    row = lax.dynamic_index_in_dim(rows, at.core, 0, keepdims=False)
    tile = length // at.tensor

    def piece(group):
        return lax.dynamic_slice_in_dim(row, (group * at.halves + at.part) * tile, tile, 0)

    own = piece(at.group)
    other = at.move(piece(1 - at.group), across)
    lower = at.group == 0
    return jnp.stack([jnp.where(lower, own, other), jnp.where(lower, other, own)])


def sum_weight(at, gradient, across_first):
    parts = gradient.reshape((at.chips, -1) + gradient.shape[1:])

    def across(s, g, u, x, c):
        return (s, c, u, x, c) if g != c else None

    def along(step):
        def target(s, g, u, x, c):
            if across_first and g != c:
                return None
            return (s, g, u, (x + step) % at.chips, c)

        return target

    def fold_chips(parts):
        total = lax.dynamic_index_in_dim(parts, at.chip, 0, keepdims=False).astype(jnp.float32)
        for step in range(1, at.chips):
            piece = lax.dynamic_index_in_dim(
                parts, (at.chip + step) % at.chips, 0, keepdims=False
            )
            total = total + at.move(piece, along(step)).astype(jnp.float32)
        return total.astype(low_type)

    if across_first:
        total = fold_chips(
            (parts.astype(jnp.float32) + at.move(parts, across).astype(jnp.float32)).astype(
                low_type
            )
        )
    else:
        part = fold_chips(parts)
        total = (part.astype(jnp.float32) + at.move(part, across).astype(jnp.float32)).astype(
            low_type
        )
    halves = total.reshape((2, -1) + total.shape[1:])

    def over(s, g, u, x, c):
        return (s, g, u, x, 1 - c) if g == c else None

    own = lax.dynamic_index_in_dim(halves, at.core, 0, keepdims=False)
    other = at.move(lax.dynamic_index_in_dim(halves, 1 - at.core, 0, keepdims=False), over)
    return jnp.where(at.home, own, other).astype(jnp.float32)


def layer_ticks(at, starts, rows_in, rows_back, params):
    qkv_w = params[0]
    micro_count, length, width = rows_in.shape
    tick_count = micro_count + at.sections - 1
    slots = micro_count + 1

    def hop(result, distance):
        def target(s, g, u, x, c):
            return (s + distance, g, u, x, c) if 0 <= s + distance < at.sections else None

        tile = length // at.size
        piece = at.move(lax.dynamic_slice_in_dim(result, at.rank * tile, tile, 0), target)
        return at.group_gather(piece).reshape(length, width)

    def place_of(tick_value, stage):
        place = tick_value - stage
        usable = jnp.logical_and(place >= 0, place < micro_count)
        return usable, jnp.clip(place, 0, micro_count - 1), jnp.where(usable, place, micro_count)

    def empty(values):
        return jax.tree.map(
            lambda value: jnp.zeros((slots,) + value.shape, value.dtype), values
        )

    def forward_tick(tick_value, arrived, stash, outputs):
        usable, position, slot = place_of(tick_value, at.section)
        inputs = jnp.where(at.section == 0, rows_in[position], arrived)
        result, saved = forward_layer(at, inputs, starts[position], params)
        if stash is None:
            return result, saved
        return result, store(stash, saved, slot), store(outputs, result, slot)

    blank = jnp.zeros((length, width), low_type)
    shapes = jax.eval_shape(lambda: forward_tick(0, blank, None, None))
    stash, outputs = empty(shapes[1]), empty(shapes[0])

    def forward_loop(tick_value, carry):
        result, stash, outputs = forward_tick(tick_value, *carry)
        return hop(result, 1), stash, outputs

    carry = lax.fori_loop(0, tick_count - 1, forward_loop, (blank, stash, outputs))
    _, stash, outputs = forward_tick(tick_count - 1, *carry)

    def backward_tick(tick_value, arrived, stash, grads, totals):
        usable, position, slot = place_of(tick_value, at.sections - 1 - at.section)
        incoming = jnp.where(at.section == at.sections - 1, rows_back[position], arrived)
        grad_x, kept_now, sums = backward_layer(
            at, pick(dict(stash, result=outputs), slot), incoming, starts[position], params
        )
        totals = totals + jnp.where(usable, sums, 0.0)
        kept = store({name: stash[name] for name in kept_now}, kept_now, slot)
        return grad_x, dict(stash, **kept), store(grads, grad_x, slot), totals

    for name in ("grad_z", "grad_a"):
        stash[name] = empty(blank)
    totals = jnp.zeros((6, width), jnp.float32)

    def backward_loop(tick_value, carry):
        grad_x, stash, grads, totals = backward_tick(tick_value, *carry)
        return hop(grad_x, -1), stash, grads, totals

    carry = lax.fori_loop(
        0, tick_count - 1, backward_loop, (blank, stash, empty(blank), totals)
    )
    _, stash, grads, totals = backward_tick(tick_count - 1, *carry)

    def both(buffer):
        return buffer[:micro_count]

    low_gz, grad_pre, low_ga, grad_qkv = (
        both(stash[name]) for name in ("grad_z", "slope", "grad_a", "qkv")
    )
    stash = {name: both(value) for name, value in stash.items()}
    stash["result"] = both(outputs)
    grads = both(grads)
    back = dict(
        row_sums=totals,
        in_sums=jnp.sum(grad_pre, axis=(0, 1), dtype=jnp.float32)[None],
        qkv_sums=jnp.sum(grad_qkv, axis=(0, 1), dtype=jnp.float32)[None],
        time_sums=jnp.sum(grads, axis=1, keepdims=True, dtype=jnp.float32),
        grad_z=low_gz,
        grad_pre=grad_pre,
        grad_a=low_ga,
        grad_qkv=grad_qkv,
        grads=grads,
    )
    return stash, back


def shards(
    tokens,
    timesteps,
    seg_starts,
    time_params,
    qkv_weight,
    qv_bias,
    out_weight,
    ffn_in,
    ffn_bias,
    ffn_out,
    ln_gains,
    row_biases,
    cotangent,
):
    at = Layout()
    width = tokens.shape[-1]
    length = tokens.shape[1] * at.tensor
    columns = qkv_weight.shape[3]

    def over(s, g, u, x, c):
        return (s, g, u, x, 1 - c)

    own_facts = jnp.concatenate([seg_starts, timesteps[:, None]], 1)
    other_facts = at.move(own_facts, over)
    if at.size == 2 and at.chips == 2 and ffn_in.shape[2] == 2 * width == 2 * length:
        facts = (own_facts, other_facts)
        vectors = (qv_bias[0], ffn_bias, ln_gains[0], row_biases[0], time_params)
        weights = (
            jnp.transpose(qkv_weight[0], (1, 0, 2)),
            out_weight[0],
            ffn_in[0],
            ffn_out[0],
        )
        stash = forward_pass(at.sections, facts, vectors, tokens, cotangent, weights)
        weights = tuple(stash[name] for name in ("wq", "wo", "wi", "wd"))
        back = backward_pass(
            at.sections, facts, ln_gains[0], row_biases[0], stash["rows_back"], weights, stash
        )

        def flat(value):
            return value.reshape(-1, value.shape[-1])

        hidden = ffn_in.shape[2]
        in_g, down_g, qkv_g, out_g, gains_g, biases_g, qv_g, hidden_g, time_g = gradient_pass(
            at.sections,
            facts,
            back,
            (back["own_in"], back["own_down"]),
            [back[name] for name in ("in_first_b", "in_first_a", "down_first_b", "down_first_a")],
            [flat(stash[name]) for name in ("inputs", "mixed")],
            [flat(back[name]) for name in ("grad_qkv", "grad_a")],
            (1, 1, 3, 1),
            (
                (0, hidden // 2, hidden // 2, False),
                (0, 0, hidden // 2, True),
                (1, width // 2, width // 2, False),
                (1, 0, width // 2, True),
                (2, columns, 2 * columns, False),
                (2, 0, columns, True),
                (3, 0, width, True),
            ),
        )
        in_g, down_g, qkv_g, out_g = (
            value.astype(jnp.float32) for value in (in_g, down_g, qkv_g, out_g)
        )
        return (
            stash["placed"][None],
            back["grads"][None],
            jnp.transpose(qkv_g, (1, 0, 2))[None],
            qv_g[None],
            out_g[None],
            in_g[None],
            hidden_g,
            down_g[None],
            gains_g[None],
            biases_g[None],
            time_g,
        )

    first = at.core == 0
    facts = jnp.stack(
        [jnp.where(first, own_facts, other_facts), jnp.where(first, other_facts, own_facts)]
    )
    facts = lax.dynamic_index_in_dim(facts, at.group, 1, keepdims=False)
    starts, fractions = facts[:, :-1], facts[:, -1].astype(jnp.float32) / 5000.0
    own_fractions = timesteps.astype(jnp.float32) / 5000.0
    time_values = time_params.astype(jnp.float32)
    embedded = (
        tokens.astype(jnp.float32) + own_fractions[:, None, None] * time_values[0] + time_values[1]
    ).astype(low_type)
    gains, biases = ln_gains[0].astype(jnp.float32), row_biases[0].astype(jnp.float32)
    tensor = lax.axis_index("tensor")
    dp = lax.axis_index("dp")
    rows_in = group_rows(at, embedded, 0)
    qv_low = group_weight(at, qv_bias[0].T).T.astype(jnp.float32)
    params = (
        group_weight(at, qkv_weight[0].reshape(width, 3 * columns)),
        jnp.concatenate([qv_low[0], jnp.zeros((columns,), jnp.float32), qv_low[1]]),
        group_weight(at, out_weight[0]),
        group_weight(at, ffn_in[0]),
        group_weight(at, ffn_bias[0]).astype(jnp.float32),
        group_weight(at, ffn_out[0]),
        gains,
        biases,
    )
    rows_back = group_rows(at, cotangent, at.sections - 1)
    stash, back = layer_ticks(at, starts, rows_in, rows_back, params)
    layer_outs = spread_rows(at, stash["result"], length)
    input_grads = spread_rows(at, back["grads"], length)

    def product(left, right):
        left, right = (v.reshape(-1, v.shape[-1]) for v in (left, right))
        return dot_first(left, right).astype(low_type)

    down_g = sum_weight(at, product(stash["hidden"], back["grad_z"]), True)
    in_g = sum_weight(at, product(stash["middle"], back["grad_pre"]), False)
    out_g = sum_weight(at, product(stash["mixed"], back["grad_a"]), True)
    qkv_g = sum_weight(at, product(stash["inputs"], back["grad_qkv"]), False)
    qkv_bias_g = back["qkv_sums"].reshape(3, columns)
    sliced = jnp.concatenate([qkv_bias_g[0], qkv_bias_g[2], back["in_sums"][0]])
    every = jnp.zeros((at.size,) + sliced.shape, jnp.float32)
    every = lax.dynamic_update_index_in_dim(every, sliced, at.rank, 0)
    row_terms = jnp.where(at.rank == 0, back["row_sums"], 0.0)
    small = lax.psum(
        jnp.concatenate([row_terms.reshape(-1), every.reshape(-1)]), ("tensor", "dp")
    )
    row_sums = small[: row_terms.size].reshape(row_terms.shape)
    mine = lax.dynamic_index_in_dim(
        small[row_terms.size :].reshape(every.shape), tensor, 0, keepdims=False
    )
    row_grads = back["time_sums"][:, 0]
    time_terms = jnp.stack([jnp.sum(fractions[:, None] * row_grads, 0), jnp.sum(row_grads, 0)])
    time_terms = jnp.where(jnp.logical_and(at.section == 0, at.rank == 0), time_terms, 0.0)
    grad_time = lax.psum(time_terms, AXES)

    def share(value, count, index):
        size = value.shape[-1] // count
        return lax.dynamic_slice_in_dim(value, index * size, size, value.ndim - 1)

    qv_g = share(mine[: 2 * columns].reshape(2, columns), at.dp, dp)
    in_bias_g = share(mine[2 * columns :], at.dp, dp)
    row_share = share(row_sums, at.tensor * at.dp, tensor * at.dp + dp)

    return (
        layer_outs[None],
        input_grads[None],
        qkv_g.reshape(-1, 3, columns)[None],
        qv_g[None],
        out_g[None],
        in_g[None],
        in_bias_g[None],
        down_g[None],
        row_share[None, :2],
        row_share[None, 2:],
        grad_time,
    )


def solution(mesh):
    return jax.shard_map(
        shards,
        mesh=mesh,
        in_specs=(
            P("dp", "tensor", None),
            P("dp"),
            P("dp", None),
            P(),
            P("section", None, None, "tensor"),
            P("section", None, "tensor"),
            P("section", "tensor", None),
            P("section", None, "tensor"),
            P("section", "tensor"),
            P("section", "tensor", None),
            P("section", None, None),
            P("section", None, None),
            P("dp", "tensor", None),
        ),
        out_specs=(
            P("section", "dp", "tensor", None),
            P("section", "dp", "tensor", None),
            P("section", "dp", None, "tensor"),
            P("section", None, ("tensor", "dp")),
            P("section", ("tensor", "dp"), None),
            P("section", "dp", "tensor"),
            P("section", ("tensor", "dp")),
            P("section", ("tensor", "dp"), None),
            P("section", None, ("tensor", "dp")),
            P("section", None, ("tensor", "dp")),
            P(),
        ),
        check_vma=False,
    )
```

```python
import functools

import jax
import jax.numpy as jnp
from jax import lax
from jax.experimental import pallas as pl
from jax.experimental.pallas import tpu as pltpu
from jax.sharding import PartitionSpec as P

HEAD = 64
LANES = 128
MASKED = -1e30
eps_norm = 1e-05
AXES = ("section", "tensor", "dp")
low_type = jnp.bfloat16


class Layout:
    def __init__(self):
        self.sections = lax.axis_size("section")
        self.tensor = lax.axis_size("tensor")
        self.dp = lax.axis_size("dp")
        self.halves = self.tensor // 2
        self.chips = self.dp // 2
        self.size = self.tensor
        self.section = lax.axis_index("section")
        tensor, dp = lax.axis_index("tensor"), lax.axis_index("dp")
        self.group, self.part = tensor // self.halves, tensor % self.halves
        self.chip, self.core = dp // 2, dp % 2
        self.rank = self.core * self.halves + self.part
        self.home = self.group == self.core

    def move(self, value, target):
        pairs = []
        for s in range(self.sections):
            for t in range(self.tensor):
                for d in range(self.dp):
                    goal = target(s, t // self.halves, t % self.halves, d // 2, d % 2)
                    if goal is None:
                        continue
                    s2, g2, u2, x2, c2 = goal
                    here = (s * self.tensor + t) * self.dp + d
                    there = (s2 * self.tensor + g2 * self.halves + u2) * self.dp + x2 * 2 + c2
                    if here != there:
                        pairs.append((here, there))
        return lax.ppermute(value, AXES, pairs)

    def turn(self, value, step):
        def target(s, g, u, x, c):
            rank = (c * self.halves + u + step) % self.size
            return (s, g, rank % self.halves, x, rank // self.halves)

        return self.move(value, target)

    def group_sum(self, value):
        total = value.astype(jnp.float32)
        for step in range(1, self.size):
            total = total + self.turn(value, step).astype(jnp.float32)
        return total

    def group_gather(self, value):
        if self.size == 2:
            other = self.turn(value, 1)
            first = self.rank == 0
            return jnp.stack([jnp.where(first, value, other), jnp.where(first, other, value)])
        whole = jnp.zeros((self.size,) + value.shape, value.dtype)
        for step in range(self.size):
            piece = value if step == 0 else self.turn(value, step)
            whole = lax.dynamic_update_index_in_dim(
                whole, piece, (self.rank - step) % self.size, 0
            )
        return whole


def dot_rows(a, b):
    return lax.dot_general(a, b, (((1,), (1,)), ((), ())), preferred_element_type=jnp.float32)


def dot_plain(a, b):
    return lax.dot_general(a, b, (((1,), (0,)), ((), ())), preferred_element_type=jnp.float32)


def dot_first(a, b):
    return lax.dot_general(a, b, (((0,), (0,)), ((), ())), preferred_element_type=jnp.float32)


def tile_docs(starts_ref, length, count):
    place = lax.broadcasted_iota(jnp.int32, (length, LANES), 0)
    doc = jnp.zeros((length, LANES), jnp.int32)
    for j in range(count):
        doc = doc + (starts_ref[j] <= place).astype(jnp.int32)
    lane = lax.broadcasted_iota(jnp.int32, (length, LANES), 1)
    rel = lane % HEAD
    return lane < HEAD, rel, rel + 1 == doc


def three_parts(value):
    high = value.astype(low_type)
    rest = value - high.astype(jnp.float32)
    middle = rest.astype(low_type)
    return high, middle, (rest - middle.astype(jnp.float32)).astype(low_type)


def lanes(rel, count, value, base):
    high, middle, small = three_parts(value)
    return jnp.where(
        rel == count,
        high,
        jnp.where(rel == count + 1, middle, jnp.where(rel == count + 2, small, base)),
    )


def attend_kernel(starts_ref, q_ref, k_ref, v_ref, o_ref, l_ref, *, count, rows):
    length = q_ref.shape[0]
    first, rel, own = tile_docs(starts_ref, length, count)
    extra_k = jnp.where(own, 1.0, 0.0).astype(low_type)
    extra_q = jnp.where(
        jnp.logical_and(rel < count, jnp.logical_not(own)), MASKED, 0.0
    ).astype(low_type)
    q = q_ref[...] * low_type(HEAD**-0.5)
    k = k_ref[...]
    v = v_ref[...]
    ones = jnp.ones_like(v)
    heads = (
        (jnp.where(first, q, extra_q), jnp.where(first, k, extra_k), jnp.where(first, v, ones)),
        (jnp.where(first, extra_q, q), jnp.where(first, extra_k, k), jnp.where(first, ones, v)),
    )
    side = first[:rows]
    for start in range(0, length, rows):
        peaks, sums = [], []
        for q_head, k_head, v_head in heads:
            scores = dot_rows(q_head[start : start + rows], k_head)
            peak = jnp.max(scores, axis=-1, keepdims=True)
            powers = jnp.exp(scores - peak).astype(low_type)
            peaks.append(peak)
            sums.append(dot_plain(powers, v_head))
        mixed = jnp.where(side, sums[0], sums[1])
        totals = jnp.where(side, sums[1], sums[0])
        log_sums = jnp.where(side, peaks[1], peaks[0]) + jnp.log(totals)
        l_ref[start : start + rows] = lanes(
            rel[:rows], count, -log_sums, extra_q[start : start + rows]
        )
        o_ref[start : start + rows] = (mixed / pltpu.roll(totals, HEAD, 1)).astype(low_type)


def attend(qkv, starts):
    length, columns = qkv.shape[0], qkv.shape[1] // 3
    pairs = columns // LANES
    rows = min(512, length)

    def block(offset):
        return pl.BlockSpec((length, LANES), lambda j: (0, offset + j))

    return pl.pallas_call(
        functools.partial(attend_kernel, count=starts.shape[0], rows=rows),
        grid=(pairs,),
        in_specs=[
            pl.BlockSpec(memory_space=pltpu.SMEM),
            block(0),
            block(pairs),
            block(2 * pairs),
        ],
        out_specs=[block(0), block(0)],
        out_shape=[
            jax.ShapeDtypeStruct((length, columns), low_type),
            jax.ShapeDtypeStruct((length, columns), low_type),
        ],
        compiler_params=pltpu.CompilerParams(vmem_limit_bytes=48 * 1024 * 1024),
        cost_estimate=pl.CostEstimate(
            flops=16 * length * length * columns // 4,
            bytes_accessed=12 * length * columns,
            transcendentals=length * length * columns // HEAD,
        ),
        name="attend",
    )(starts, qkv, qkv, qkv)


def attend_back_kernel(
    starts_ref, q_ref, k_ref, v_ref, o_ref, l_ref, g_ref, dq_ref, dk_ref, dv_ref, *, count, rows
):
    length = q_ref.shape[0]
    first, rel, own = tile_docs(starts_ref, length, count)
    stat = jnp.logical_and(rel >= count, rel < count + 3)
    extra_k = jnp.where(jnp.logical_or(own, stat), 1.0, 0.0).astype(low_type)
    extra_v = jnp.where(stat, 1.0, 0.0).astype(low_type)
    extra_q = l_ref[...]
    g = g_ref[...]
    product = g.astype(jnp.float32) * o_ref[...].astype(jnp.float32)
    dots = [
        jnp.sum(jnp.where(first, product, 0.0), axis=-1, keepdims=True),
        jnp.sum(jnp.where(first, 0.0, product), axis=-1, keepdims=True),
    ]
    extra_g = lanes(rel, count, -jnp.where(first, dots[1], dots[0]), jnp.zeros_like(extra_q))
    q = q_ref[...] * low_type(HEAD**-0.5)
    k = k_ref[...]
    v = v_ref[...]
    heads = (
        tuple(
            jnp.where(first, a, b)
            for a, b in ((q, extra_q), (k, extra_k), (v, extra_v), (g, extra_g))
        ),
        tuple(
            jnp.where(first, b, a)
            for a, b in ((q, extra_q), (k, extra_k), (v, extra_v), (g, extra_g))
        ),
    )
    grad_k = [jnp.zeros((length, LANES), jnp.float32)] * 2
    grad_v = [jnp.zeros((length, LANES), jnp.float32)] * 2
    for start in range(0, length, rows):
        part = slice(start, start + rows)
        grad_q = []
        for i, (q_head, k_head, v_head, g_head) in enumerate(heads):
            probs = jnp.exp(dot_rows(k_head, q_head[part]))
            slopes = (probs * dot_rows(v_head, g_head[part])).astype(low_type)
            grad_v[i] = grad_v[i] + dot_plain(probs.astype(low_type), g[part])
            grad_k[i] = grad_k[i] + dot_plain(slopes, q[part])
            grad_q.append(dot_first(slopes, k))
        dq_ref[part] = (
            jnp.where(first[:rows], grad_q[0], grad_q[1]) * (HEAD**-0.5)
        ).astype(low_type)
    dk_ref[...] = jnp.where(first, grad_k[0], grad_k[1]).astype(low_type)
    dv_ref[...] = jnp.where(first, grad_v[0], grad_v[1]).astype(low_type)


def attend_back(qkv, starts, mixed, log_sums, grad_mixed):
    length, columns = mixed.shape
    pairs = columns // LANES
    rows = min(256, length)

    def block(offset):
        return pl.BlockSpec((length, LANES), lambda j: (0, offset + j))

    return pl.pallas_call(
        functools.partial(attend_back_kernel, count=starts.shape[0], rows=rows),
        grid=(pairs,),
        in_specs=[
            pl.BlockSpec(memory_space=pltpu.SMEM),
            block(0),
            block(pairs),
            block(2 * pairs),
            block(0),
            block(0),
            block(0),
        ],
        out_specs=[block(0)] * 3,
        out_shape=[jax.ShapeDtypeStruct((length, columns), low_type)] * 3,
        compiler_params=pltpu.CompilerParams(vmem_limit_bytes=48 * 1024 * 1024),
        cost_estimate=pl.CostEstimate(
            flops=40 * length * length * columns // 4,
            bytes_accessed=20 * length * columns,
            transcendentals=length * length * columns // HEAD,
        ),
        name="attend_back",
    )(starts, qkv, qkv, qkv, mixed, log_sums, grad_mixed)


MESH = pl.DeviceIdType.MESH


def rows_of(index, size):
    return pl.ds(pl.multiple_of(index * size, size), size)


def erf_pair(pre):
    bell = jnp.exp(-0.5 * pre * pre)
    size = jnp.abs(pre)
    t = 1.0 / (1.0 + 0.2316418882663604 * size)
    tail = bell * t * (
        0.127414796
        + t * (-0.142248368 + t * (0.7107068705 + t * (-0.7265760135 + t * 0.5307027145)))
    )
    return jnp.where(pre < 0.0, tail, 1.0 - tail), bell * 0.3989422804014327


def norm_rows(value):
    average = jnp.mean(value, axis=-1, keepdims=True)
    centered = value - average
    inv_scale = lax.rsqrt(jnp.mean(centered * centered, axis=-1, keepdims=True) + eps_norm)
    return centered * inv_scale, inv_scale


def doc_lanes(starts, first_row, shape):
    place = lax.broadcasted_iota(jnp.int32, shape, 0) + first_row
    doc = jnp.zeros(shape, jnp.int32)
    for start in starts:
        doc = doc + (start <= place).astype(jnp.int32)
    lane = lax.broadcasted_iota(jnp.int32, shape, 1)
    rel = lane % HEAD
    return lane < HEAD, rel, rel + 1 == doc


def forward_kernel(
    sections,
    chunk,
    own_ref,
    other_ref,
    qv_in,
    hidden_bias_in,
    gains_in,
    biases_in,
    time_in,
    tokens_in,
    cotangent_in,
    qkv_w,
    out_w,
    in_w,
    down_w,
    qkv_out,
    stat_out,
    mixed_out,
    middle_out,
    hidden_out,
    slope_out,
    inputs_out,
    result_out,
    scale_out,
    placed_out,
    back_out,
    wq_out,
    wo_out,
    wi_out,
    wd_out,
    wq,
    wo,
    wi,
    wd,
    bias_own,
    bias,
    gains,
    biases,
    hbuf,
    qkv,
    keys,
    values,
    mixed,
    stat,
    send_a,
    send_b,
    got_a,
    got_b,
    high_mid,
    low_mid,
    hidden,
    slope,
    result,
    scale_a,
    scale_z,
    w_sem,
    y_send,
    y_got,
    x_send,
    x_got,
    round_up,
    round_down,
    round_tokens,
    round_send,
    round_got,
    bias_sem,
    token_local,
    token_send,
    token_got,
    cot_local,
    cot_send,
    cot_got,
    hop_send,
    hop_got,
    pass_send,
    pass_got,
    keep_sem,
    qkv_sem,
    a_send,
    a_got,
    b_send,
    b_got,
    first_sem,
    second_sem,
    third_sem,
    scale_sem,
    out_local,
    out_send,
    out_got,
):
    at = Seat()
    section, core, peer = at.section, at.core, at.peer
    last = sections - 1
    micro, length, width = hbuf.shape
    count = own_ref.shape[1] - 1
    columns = mixed.shape[2]
    pairs = columns // LANES
    chunks = length // chunk
    half = chunk // 2
    shape = (chunk, LANES)
    given, held = (qkv_w, out_w, in_w, down_w), (wq, wo, wi, wd)
    own_weights = [
        pltpu.make_async_copy(source, target, w_sem.at[i])
        for i, (source, target) in enumerate(zip(given, held))
    ]
    pieces = weight_pieces(*held)

    def swap(k):
        index, where = pieces[k]
        return remote(
            where(given[index], at.chip),
            where(held[index], at.chip),
            y_send.at[k],
            y_got.at[k],
            at.swap,
        )

    def relay(k):
        index, where = pieces[k]
        part = where(held[index], at.chip)
        return remote(part, part, x_send.at[k], x_got.at[k], at.beside)

    size = wd.shape[0] // 8
    rounds = round_up.shape[0]

    def round_rows(ref, n):
        return ref.at[pl.ds((n % 2) * 4 * size + (4 - rounds // 2 + n // 2) * size, size)]

    def go_up(n):
        return remote(
            round_rows(down_w, n),
            round_up.at[n],
            round_send.at[0, n],
            round_got.at[0, n],
            {"section": section + 1},
        )

    def go_over(n):
        return remote(
            round_up.at[n], round_down.at[n], round_send.at[1, n], round_got.at[1, n], at.swap
        )

    def go_down(n):
        return remote(
            round_down.at[n],
            round_rows(wd, n),
            round_send.at[2, n],
            round_got.at[2, n],
            {"section": section - 1},
        )

    def tokens_over():
        return remote(
            tokens_in.at[1 - at.group],
            round_tokens,
            round_send.at[3, 0],
            round_got.at[3, 0],
            at.across,
        )

    def tokens_down():
        tile = tokens_in.shape[1]
        rows = pl.ds(pl.multiple_of((1 - at.group) * tile, tile), tile)
        return remote(
            round_tokens,
            hbuf.at[core, rows],
            round_send.at[3, 1],
            round_got.at[3, 1],
            {"section": section - 1},
        )

    def pieces_of(*indices):
        return [k for k, (index, _) in enumerate(pieces) if index in indices]

    def pass_on(group):
        for k in group:
            swap(k).wait_recv()
            relay(k).start()

    def begin(group):
        for k in group:
            swap(k).start()

    direct = pieces_of(0, 1, 2, 3)[: -(rounds // 2)]
    detour = pieces_of(3)[-(rounds // 2) :]

    def ready(index):
        @pl.when(at.home)
        def _():
            own_weights[index].wait()

        @pl.when(at.away)
        def _():
            for k in pieces_of(index):
                if k in direct:
                    relay(k).wait_recv()
            if index == 3:

                @pl.when(section > 0)
                def _():
                    for k in detour:
                        relay(k).wait_recv()

                @pl.when(section == 0)
                def _():
                    for n in range(rounds):
                        go_down(n).wait_recv()

    def swap_bias():
        return remote(bias_own, bias, bias_sem.at[0], bias_sem.at[1], at.swap)

    tokens = RowPieces(at, tokens_in, hbuf, token_local, token_send, token_got)
    cotangents = RowPieces(at, cotangent_in, back_out, cot_local, cot_send, cot_got)
    placed = OutPieces(at, result, placed_out, out_local, out_send, out_got)

    @pl.when(at.home)
    def _():
        for copy in own_weights:
            copy.start()

    gains[...] = gains_in[...].astype(jnp.float32)
    biases[...] = biases_in[...].astype(jnp.float32)
    qv = qv_in[...].astype(jnp.float32)
    bias_own[:, :columns] = qv[0:1]
    bias_own[:, columns : 2 * columns] = jnp.zeros_like(qv[0:1])
    bias_own[:, 2 * columns : 3 * columns] = qv[1:2]
    bias_own[:, 3 * columns :] = hidden_bias_in[...].astype(jnp.float32)

    @pl.when(at.home)
    def _():
        bias[...] = bias_own[...]

    greet(section, sections, (at.peer, at.across, at.swap, at.beside))

    @pl.when(section == 0)
    def _():
        tokens.own.start()
        tokens.to_peer.start()

    guide = jnp.logical_and(section == 1, core == 0)
    pl.when(guide)(lambda: tokens_over().start())

    @pl.when(at.away)
    def _():
        swap_bias().start()

        @pl.when(section == 0)
        def _():
            begin(direct)
            for n in range(rounds):
                go_up(n).start()

        @pl.when(section > 1)
        def _():
            begin(direct + detour)

        @pl.when(section == 1)
        def _():
            for n in range(rounds + 1):
                if n < rounds:
                    go_up(n).wait_recv()
                    go_over(n).start()
                if n > 0:
                    go_over(n - 1).wait_recv()
                    go_down(n - 1).start()
                if n == 1:

                    @pl.when(guide)
                    def _():
                        tokens_over().wait_recv()
                        tokens_down().start()

            begin(direct + detour)

        swap_bias().wait()
        pass_on(direct[:4])

        @pl.when(section > 0)
        def _():
            pass_on(direct[4:] + detour)

    @pl.when(jnp.logical_and(guide, at.home))
    def _():
        tokens_over().wait_recv()
        tokens_down().start()

    @pl.when(section == last)
    def _():
        cotangents.own.start()
        cotangents.to_peer.start()
        cotangents.to_across.start()
        cotangents.to_across.wait()
        cotangents.forward.start()
        cotangents.own.wait()
        cotangents.to_peer.wait()
        cotangents.forward.wait()

    def hop(m, j):
        rows = pl.ds(pl.multiple_of(core * half, half), half)
        target = pl.ds(pl.multiple_of(j * chunk + core * half, half), half)
        return pltpu.make_async_remote_copy(
            src_ref=result.at[j, rows],
            dst_ref=hbuf.at[m, target],
            send_sem=hop_send.at[j],
            recv_sem=hop_got.at[m, j],
            device_id={"section": section + 1},
            device_id_type=MESH,
        )

    def hand_over(m, j):
        rows = pl.ds(pl.multiple_of(j * chunk + core * half, half), half)
        return pltpu.make_async_remote_copy(
            src_ref=hbuf.at[m, rows],
            dst_ref=hbuf.at[m, rows],
            send_sem=pass_send.at[m, j],
            recv_sem=pass_got.at[m, j],
            device_id=peer,
            device_id_type=MESH,
        )

    def exchange_a(m, j):
        slot = j
        return pltpu.make_async_remote_copy(
            src_ref=send_a.at[slot],
            dst_ref=got_a.at[j],
            send_sem=a_send.at[slot],
            recv_sem=a_got.at[m, j],
            device_id=peer,
            device_id_type=MESH,
        )

    def exchange_b(m, j):
        slot = lax.rem(j, 2)
        return pltpu.make_async_remote_copy(
            src_ref=send_b.at[slot],
            dst_ref=got_b.at[j],
            send_sem=b_send.at[slot],
            recv_sem=b_got.at[m, j],
            device_id=peer,
            device_id_type=MESH,
        )

    def keep(m, j):
        rows = rows_of(j, chunk)
        return pltpu.make_async_copy(
            hbuf.at[m, rows], inputs_out.at[m, rows], keep_sem.at[m, j]
        )

    def keep_qkv(m, j):
        rows = rows_of(j, chunk)
        return pltpu.make_async_copy(qkv.at[rows], qkv_out.at[m, rows], qkv_sem.at[j])

    def keep_first(m, j):
        rows = rows_of(j, chunk)
        return [
            pltpu.make_async_copy(mixed.at[j], mixed_out.at[m, rows], first_sem.at[0]),
            pltpu.make_async_copy(stat, stat_out.at[m, rows], first_sem.at[1]),
        ]

    def keep_second(m, j):
        rows = rows_of(j, chunk)
        return [
            pltpu.make_async_copy(low_mid, middle_out.at[m, rows], second_sem.at[0]),
            pltpu.make_async_copy(hidden, hidden_out.at[m, rows], second_sem.at[1]),
            pltpu.make_async_copy(slope, slope_out.at[m, rows], second_sem.at[2]),
            pltpu.make_async_copy(scale_a, scale_out.at[m, 0, rows], second_sem.at[3]),
        ]

    def keep_third(m, j):
        rows = rows_of(j, chunk)
        return [
            pltpu.make_async_copy(result.at[j], result_out.at[m, rows], third_sem.at[j]),
            pltpu.make_async_copy(scale_z.at[j], scale_out.at[m, 1, rows], scale_sem.at[j]),
        ]

    def arrive(m, j):
        hop(m, j).wait_recv()
        hand_over(m, j).start()

    def project(m, j):
        rows = rows_of(j, chunk)

        starts, moment = row_facts(at, own_ref, other_ref, m)

        @pl.when(section == 0)
        def _():
            fraction = jnp.full((1, width), moment.astype(jnp.float32)) / 5000.0
            times = time_in[...].astype(jnp.float32)
            hbuf[m, rows] = (
                hbuf[m, rows].astype(jnp.float32) + fraction * times[0:1] + times[1:2]
            ).astype(low_type)

        @pl.when(section > 0)
        def _():
            @pl.when(j + 1 < chunks)
            def _():
                arrive(m, j + 1)

            hand_over(m, j).wait_recv()

        keep(m, j).start()

        @pl.when(m > 0)
        def _():
            keep_qkv(m - 1, j).wait()

        for third in range(3):
            part = slice(third * columns, (third + 1) * columns)
            qkv[rows, part] = (dot_plain(hbuf[m, rows], wq[third]) + bias[:, part]).astype(low_type)
        keep_qkv(m, j).start()
        first, rel, own = doc_lanes(starts, j * chunk, shape)
        extra = jnp.where(own, 1.0, 0.0).astype(low_type)
        ones = jnp.ones(shape, low_type)
        for p in range(pairs):
            k = qkv[rows, columns + p * LANES : columns + (p + 1) * LANES]
            v = qkv[rows, 2 * columns + p * LANES : 2 * columns + (p + 1) * LANES]
            keys[2 * p, rows] = jnp.where(first, k, extra)
            keys[2 * p + 1, rows] = jnp.where(first, extra, k)
            values[2 * p, rows] = jnp.where(first, v, ones)
            values[2 * p + 1, rows] = jnp.where(first, ones, v)

    def mix(m, j):
        rows = rows_of(j, chunk)
        starts, _ = row_facts(at, own_ref, other_ref, m)
        first, rel, own = doc_lanes(starts, j * chunk, shape)
        extra = jnp.where(
            jnp.logical_and(rel < count, jnp.logical_not(own)), MASKED, 0.0
        ).astype(low_type)

        def scores(index):
            p = index // 2
            q = qkv[rows, p * LANES : (p + 1) * LANES] * low_type(HEAD**-0.5)
            q = jnp.where(first, q, extra) if index % 2 == 0 else jnp.where(first, extra, q)
            return dot_rows(q, keys[index])

        current = scores(0)
        peaks, sums = [], []
        for index in range(2 * pairs):
            later = scores(index + 1) if index + 1 < 2 * pairs else None
            peak = jnp.max(current, axis=-1, keepdims=True)
            powers = jnp.exp(current - peak).astype(low_type)
            peaks.append(peak)
            sums.append(dot_plain(powers, values[index]))
            current = later
            if index % 2 == 1:
                lane = slice((index // 2) * LANES, (index // 2 + 1) * LANES)
                total = jnp.where(first, sums[index], sums[index - 1])
                log_sum = jnp.where(first, peaks[index], peaks[index - 1]) + jnp.log(total)
                stat[:, lane] = lanes(rel, count, -log_sum, extra)
                mixed[j, :, lane] = (
                    jnp.where(first, sums[index - 1], sums[index]) / pltpu.roll(total, HEAD, 1)
                ).astype(low_type)
        for copy in keep_first(m, j):
            copy.start()

    def branch(m, j):
        send_a[j] = dot_plain(mixed[j], wo[...]).astype(low_type)
        exchange_a(m, j).start()

    def feed(m, j):
        rows = rows_of(j, chunk)
        slot = lax.rem(j, 2)
        exchange_a(m, j).wait()
        total = (
            send_a[j].astype(jnp.float32)
            + got_a[j].astype(jnp.float32)
            + biases[0:1]
            + hbuf[m, rows].astype(jnp.float32)
        )
        unit, inv_scale = norm_rows(total)
        scale_a[...] = jnp.broadcast_to(inv_scale, shape)
        middle = unit * gains[0:1] + biases[1:2]
        high_mid[slot] = middle
        low_mid[...] = middle.astype(low_type)
        hidden_size = wi.shape[1]
        step = min(1024, hidden_size)

        def before(start):
            part = slice(start, start + step)
            return dot_plain(low_mid[...], wi[:, part]) + bias[:, 3 * columns + start : 3 * columns + start + step]

        pre = before(0)
        branch = jnp.zeros((chunk, width), jnp.float32)
        for start in range(0, hidden_size, step):
            part = slice(start, start + step)
            later = before(start + step) if start + step < hidden_size else None
            normal, density = erf_pair(pre)
            hidden[:, part] = (pre * normal).astype(low_type)
            slope[:, part] = (normal + pre * density).astype(low_type)
            branch = branch + dot_plain(hidden[:, part], wd[part])
            pre = later
        send_b[slot] = branch.astype(low_type)
        exchange_b(m, j).start()
        for copy in keep_second(m, j):
            copy.start()

    def finish(m, j):
        slot = lax.rem(j, 2)
        exchange_b(m, j).wait()
        total = (
            send_b[slot].astype(jnp.float32)
            + got_b[j].astype(jnp.float32)
            + biases[2:3]
            + high_mid[slot]
        )
        unit, inv_scale = norm_rows(total)
        @pl.when(m > 0)
        def _():
            finish_wait(m - 1, j)

        scale_z[j] = jnp.broadcast_to(inv_scale, shape)
        result[j] = (unit * gains[1:2] + biases[3:4]).astype(low_type)

        @pl.when(section < sections - 1)
        def _():
            hop(m, j).start()

        placed.start(m, j)
        for copy in keep_third(m, j):
            copy.start()

    def finish_wait(m, j):
        for copy in keep_third(m, j):
            copy.wait()

        placed.wait(m, j)

        @pl.when(section < sections - 1)
        def _():
            hop(m, j).wait_send()

    def one_row(m, carry):
        @pl.when(jnp.logical_and(section == 0, core == m))
        def _():
            tokens.own.wait()

            @pl.when(core == 0)
            def _():
                tokens_down().wait_recv()

            @pl.when(core > 0)
            def _():
                tokens.to_across.wait_recv()

            tokens.forward.start()

        @pl.when(jnp.logical_and(section == 0, core != m))
        def _():
            tokens.to_peer.wait_recv()
            tokens.forward.wait_recv()

        @pl.when(m == 0)
        def _():
            ready(0)

        @pl.when(jnp.logical_and(section == 0, core == m))
        def _():
            tokens.forward.wait_send()

        @pl.when(section > 0)
        def _():
            arrive(m, 0)

        opening = jnp.logical_and(m == 0, jnp.logical_and(section == 0, at.away))

        @pl.when(opening)
        def _():
            pass_on(direct[4:5])

        def first_step(j, carry):
            project(m, j)

            @pl.when(jnp.logical_and(opening, j == 0))
            def _():
                pass_on(direct[5:6])

            return carry

        lax.fori_loop(0, chunks, first_step, 0)

        @pl.when(jnp.logical_and(m == 0, section > 0))
        def _():
            ready(1)

        @pl.when(opening)
        def _():
            pass_on(direct[6:7])

        lag = jnp.where(jnp.logical_and(section == 0, m == 0), chunks, 1)

        def step(i, carry):
            j = i - lag

            @pl.when(jnp.logical_and(i >= 1, i <= chunks))
            def _():
                for copy in keep_first(m, i - 1):
                    copy.wait()

            @pl.when(i < chunks)
            def _():
                mix(m, i)

                @pl.when(lag == 1)
                def _():
                    branch(m, i)

            for turn, k in enumerate(direct[7:]):

                @pl.when(jnp.logical_and(opening, i == turn))
                def _(k=k):
                    pass_on([k])

            @pl.when(
                jnp.logical_and(
                    jnp.logical_and(section == 0, core > 0),
                    jnp.logical_and(m == 0, i == chunks - 1),
                )
            )
            def _():
                tokens.to_across.start()

            @pl.when(jnp.logical_and(lag > 1, j == 0))
            def _():
                ready(1)
                for turn in range(chunks):
                    branch(m, turn)

            @pl.when(jnp.logical_and(m == 0, j == 0))
            def _():
                ready(2)
                ready(3)

            @pl.when(jnp.logical_and(j >= 1, j <= chunks))
            def _():
                for copy in keep_second(m, j - 1):
                    copy.wait()

            @pl.when(j >= 1)
            def _():
                finish(m, j - 1)

            @pl.when(jnp.logical_and(j >= 0, j < chunks))
            def _():
                feed(m, j)

            return carry

        lax.fori_loop(0, chunks + lag + 1, step, 0)

        @pl.when(m == 0)
        def _():
            for copy in keep_weights:
                copy.start()

        return carry

    keep_weights = [
        pltpu.make_async_copy(source, target, w_sem.at[i])
        for i, (source, target) in enumerate(zip(held, (wq_out, wo_out, wi_out, wd_out)))
    ]
    lax.fori_loop(0, micro, one_row, 0)
    for copy in keep_weights:
        copy.wait()
    for j in range(chunks):
        finish_wait(micro - 1, j)
        keep_qkv(micro - 1, j).wait()
    for m in range(micro):
        for j in range(chunks):
            keep(m, j).wait()
    placed.wait_got()

    @pl.when(at.away)
    def _():
        for k in direct:
            swap(k).wait_send()
            relay(k).wait_send()

        @pl.when(section > 0)
        def _():
            for k in detour:
                swap(k).wait_send()
                relay(k).wait_send()

        for n in range(rounds):

            @pl.when(section == 0)
            def _(n=n):
                go_up(n).wait_send()

            @pl.when(section == 1)
            def _(n=n):
                go_over(n).wait_send()
                go_down(n).wait_send()

    @pl.when(guide)
    def _():
        tokens_over().wait_send()
        tokens_down().wait_send()

    @pl.when(section == 0)
    def _():
        tokens.to_peer.wait_send()

        @pl.when(core > 0)
        def _():
            tokens.to_across.wait_send()

    @pl.when(section > 0)
    def _():
        for m in range(micro):
            for j in range(chunks):
                hand_over(m, j).wait_send()


def forward_pass(sections, facts, vectors, tokens, cotangent, weights):
    wq, wo, wi, wd = weights
    micro, tile, width = tokens.shape
    length = 2 * tile
    columns, hidden = wo.shape[0], wi.shape[1]
    chunk = min(256, length // 4)
    chunks = length // chunk
    low, high = low_type, jnp.float32

    def out(*shape, dtype=low):
        return jax.ShapeDtypeStruct(shape, dtype)

    outs = dict(
        qkv=out(micro, length, 3 * columns),
        log_sums=out(micro, length, columns),
        mixed=out(micro, length, columns),
        middle=out(micro, length, width),
        hidden=out(micro, length, hidden),
        slope=out(micro, length, hidden),
        inputs=out(micro, length, width),
        result=out(micro, length, width),
        scales=out(micro, 2, length, LANES, dtype=high),
        placed=out(*tokens.shape),
        rows_back=out(micro, length, width),
        wq=out(*wq.shape),
        wo=out(*wo.shape),
        wi=out(*wi.shape),
        wd=out(*wd.shape),
    )
    vmem = pl.BlockSpec(memory_space=pltpu.VMEM)
    anywhere = pl.BlockSpec(memory_space=pl.ANY)
    dma = pltpu.SemaphoreType.DMA
    pieces = len(weight_pieces(*weights))
    rounds = 4
    results = pl.pallas_call(
        functools.partial(forward_kernel, sections, chunk),
        in_specs=[pl.BlockSpec(memory_space=pltpu.SMEM)] * 2 + [vmem] * 5 + [anywhere] * 6,
        out_specs=[anywhere] * len(outs),
        out_shape=list(outs.values()),
        scratch_shapes=[
            pltpu.VMEM(wq.shape, low),
            pltpu.VMEM(wo.shape, low),
            pltpu.VMEM(wi.shape, low),
            pltpu.VMEM(wd.shape, low),
            pltpu.VMEM((1, 3 * columns + hidden), high),
            pltpu.VMEM((1, 3 * columns + hidden), high),
            pltpu.VMEM(vectors[2].shape, high),
            pltpu.VMEM(vectors[3].shape, high),
            pltpu.VMEM((micro, length, width), low),
            pltpu.VMEM((length, 3 * columns), low),
            pltpu.VMEM((columns // HEAD, length, LANES), low),
            pltpu.VMEM((columns // HEAD, length, LANES), low),
            pltpu.VMEM((chunks, chunk, columns), low),
            pltpu.VMEM((chunk, columns), low),
            pltpu.VMEM((chunks, chunk, width), low),
            pltpu.VMEM((2, chunk, width), low),
            pltpu.VMEM((chunks, chunk, width), low),
            pltpu.VMEM((chunks, chunk, width), low),
            pltpu.VMEM((2, chunk, width), high),
            pltpu.VMEM((chunk, width), low),
            pltpu.VMEM((chunk, hidden), low),
            pltpu.VMEM((chunk, hidden), low),
            pltpu.VMEM((chunks, chunk, width), low),
            pltpu.VMEM((chunk, LANES), high),
            pltpu.VMEM((chunks, chunk, LANES), high),
            dma((4,)),
            dma((pieces,)),
            dma((pieces,)),
            dma((pieces,)),
            dma((pieces,)),
            pltpu.VMEM((rounds, hidden // 8, width), low),
            pltpu.VMEM((rounds, hidden // 8, width), low),
            pltpu.VMEM((tile, width), low),
            dma((4, rounds)),
            dma((4, rounds)),
            dma((2,)),
            dma,
            dma((3,)),
            dma((3,)),
            dma,
            dma((3,)),
            dma((3,)),
            dma((chunks,)),
            dma((micro, chunks)),
            dma((micro, chunks)),
            dma((micro, chunks)),
            dma((micro, chunks)),
            dma((chunks,)),
            dma((chunks,)),
            dma((micro, chunks)),
            dma((2,)),
            dma((micro, chunks)),
            dma((2,)),
            dma((4,)),
            dma((chunks,)),
            dma((chunks,)),
            dma((chunks,)),
            dma((chunks,)),
            dma((chunks // 2,)),
        ],
        compiler_params=pltpu.CompilerParams(
            collective_id=0, has_side_effects=True, vmem_limit_bytes=62 * 1024 * 1024
        ),
        name="forward_pass",
    )(*facts, *vectors, tokens, cotangent, *weights)
    return dict(zip(outs, results))


def greet(section, sections, partners):
    barrier = pltpu.get_barrier_semaphore()
    for partner in partners:
        pl.semaphore_signal(barrier, inc=1, device_id=partner, device_id_type=MESH)

    @pl.when(section > 0)
    def _():
        pl.semaphore_signal(
            barrier, inc=1, device_id={"section": section - 1}, device_id_type=MESH
        )

    @pl.when(section < sections - 1)
    def _():
        pl.semaphore_signal(
            barrier, inc=1, device_id={"section": section + 1}, device_id_type=MESH
        )

    inner = jnp.logical_and(section > 0, section < sections - 1)

    @pl.when(inner)
    def _():
        pl.semaphore_wait(barrier, len(partners) + 2)

    @pl.when(jnp.logical_not(inner))
    def _():
        pl.semaphore_wait(barrier, len(partners) + 1)


class Seat:
    def __init__(self):
        self.section = lax.axis_index("section")
        self.group = lax.axis_index("tensor")
        dp = lax.axis_index("dp")
        self.core = lax.rem(dp, 2)
        self.chip = dp // 2
        other = dp + 1 - 2 * self.core
        self.peer = {"dp": other}
        self.across = {"tensor": 1 - self.group}
        self.swap = {"tensor": 1 - self.group, "dp": other}
        self.beside = {"dp": dp + 2 - 4 * self.chip}
        self.home = self.group == self.core
        self.away = self.group != self.core


def row_facts(at, own_ref, other_ref, m):
    facts = [
        jnp.where(at.core == m, own_ref[at.group, j], other_ref[at.group, j])
        for j in range(own_ref.shape[1])
    ]
    return facts[:-1], facts[-1]


def remote(source, target, send_sem, recv_sem, device):
    return pltpu.make_async_remote_copy(
        src_ref=source,
        dst_ref=target,
        send_sem=send_sem,
        recv_sem=recv_sem,
        device_id=device,
        device_id_type=MESH,
    )


class RowPieces:
    def __init__(self, at, source, target, local, send, got):
        tile = source.shape[1]

        def half(group):
            return pl.ds(pl.multiple_of(group * tile, tile), tile)

        own = target.at[at.core, half(at.group)]
        other = target.at[at.core, half(1 - at.group)]
        mine = source.at[at.group]
        self.own = pltpu.make_async_copy(mine, own, local)
        self.to_peer = remote(mine, own, send.at[0], got.at[0], at.peer)
        self.to_across = remote(source.at[1 - at.group], own, send.at[1], got.at[1], at.across)
        self.forward = remote(other, other, send.at[2], got.at[2], at.peer)


class OutPieces:
    def __init__(self, at, rows, target, local, send, got):
        self.at, self.rows, self.target = at, rows, target
        self.local, self.send, self.got = local, send, got
        self.chunks, self.chunk = rows.shape[0], rows.shape[1]
        self.per = self.chunks // 2

    def copies(self, m, j):
        place = rows_of(lax.rem(j, self.per), self.chunk)
        spot = self.target.at[self.at.group, place]
        near = pltpu.make_async_copy(self.rows.at[j], spot, self.local.at[j])
        far = remote(
            self.rows.at[j],
            spot,
            self.send.at[j],
            self.got.at[lax.rem(j, self.per)],
            self.at.across,
        )
        mine = self.at.core == m
        stays = j // self.per == self.at.group
        return (
            (jnp.logical_and(mine, stays), near, near.wait),
            (jnp.logical_and(mine, jnp.logical_not(stays)), far, far.wait_send),
        )

    def start(self, m, j):
        for condition, copy, _ in self.copies(m, j):
            pl.when(condition)(copy.start)

    def wait(self, m, j):
        for condition, _, wait in self.copies(m, j):
            pl.when(condition)(wait)

    def wait_got(self):
        for j in range(self.per):
            remote(
                self.rows.at[j],
                self.target.at[1 - self.at.group, pl.ds(j * self.chunk, self.chunk)],
                self.send.at[j],
                self.got.at[j],
                self.at.across,
            ).wait_recv()


def weight_pieces(wq, wo, wi, wd):
    pieces = []

    def split(index, rows, count, lead=()):
        size = rows // 2 // count
        for i in range(count):

            def where(ref, chip, i=i):
                start = pl.multiple_of(chip * (rows // 2) + i * size, size)
                return ref.at[lead + (pl.ds(start, size),)]

            pieces.append((index, where))

    for k in range(wq.shape[0]):
        split(0, wq.shape[1], 1, (k,))
    split(1, wo.shape[0], 1)
    split(2, wi.shape[0], 4)
    split(3, wd.shape[0], 4)
    return pieces


def backward_kernel(
    sections,
    chunk,
    own_ref,
    other_ref,
    gains_in,
    biases_in,
    rows_back,
    qkv_w,
    out_w,
    in_w,
    down_w,
    qkv_in,
    stat_in,
    mixed_in,
    middle_in,
    hidden_in,
    slope_in,
    result_in,
    scale_in,
    row_sums,
    in_sums,
    qkv_sums,
    time_sums,
    gz_out,
    pre_out,
    ga_out,
    gqkv_out,
    grads_out,
    own_in,
    own_down,
    in_first_b,
    in_first_a,
    down_first_b,
    down_first_a,
    wq,
    wo,
    wi,
    wd,
    gains,
    biases,
    gbuf,
    high_ga,
    qkv,
    keys,
    values,
    grad_k,
    grad_v,
    grad_qkv,
    send_a,
    send_b,
    got_a,
    got_b,
    low_gz,
    low_pre,
    low_ga,
    grad_mixed,
    grads,
    result,
    slope,
    scale_z,
    middle,
    scale_a,
    mixed,
    stat,
    w_sem,
    load_sem,
    hop_send,
    hop_got,
    pass_send,
    pass_got,
    a_send,
    a_got,
    b_send,
    b_got,
    qkv_sem,
    first_sem,
    second_sem,
    keep_sem,
    keep_ga_sem,
    keep_qkv_sem,
    grads_sem,
    out_send,
    out_got,
    stage,
    right_sem,
    left_sem,
    store_sem,
    part_send,
    part_got,
):
    at = Seat()
    section, core, peer = at.section, at.core, at.peer
    micro, length, width = gbuf.shape
    count = own_ref.shape[1] - 1
    columns = grad_mixed.shape[1]
    pairs = columns // LANES
    chunks = length // chunk
    half = chunk // 2
    last = sections - 1
    shape = (chunk, LANES)

    weights = [
        pltpu.make_async_copy(source, target, w_sem.at[i])
        for i, (source, target) in enumerate(
            ((down_w, wd), (in_w, wi), (out_w, wo), (qkv_w, wq))
        )
    ]
    for copy in weights:
        copy.start()

    def load(m, j):
        rows = rows_of(j, chunk)
        return pltpu.make_async_copy(
            rows_back.at[m, rows], gbuf.at[m, rows], load_sem.at[m, j]
        )

    def hop(m, j):
        target = pl.ds(pl.multiple_of(j * chunk + core * half, half), half)
        return pltpu.make_async_remote_copy(
            src_ref=grads.at[j, pl.ds(pl.multiple_of(core * half, half), half)],
            dst_ref=gbuf.at[m, target],
            send_sem=hop_send.at[j],
            recv_sem=hop_got.at[m, j],
            device_id={"section": section - 1},
            device_id_type=MESH,
        )

    def hand_over(m, j):
        rows = pl.ds(pl.multiple_of(j * chunk + core * half, half), half)
        return pltpu.make_async_remote_copy(
            src_ref=gbuf.at[m, rows],
            dst_ref=gbuf.at[m, rows],
            send_sem=pass_send.at[m, j],
            recv_sem=pass_got.at[m, j],
            device_id=peer,
            device_id_type=MESH,
        )

    def exchange(send, got, send_sem, got_sem, m, j):
        slot = lax.rem(j, send.shape[0])
        return pltpu.make_async_remote_copy(
            src_ref=send.at[slot],
            dst_ref=got.at[j],
            send_sem=send_sem.at[slot],
            recv_sem=got_sem.at[m, j],
            device_id=peer,
            device_id_type=MESH,
        )

    def exchange_a(m, j):
        return exchange(send_a, got_a, a_send, a_got, m, j)

    def exchange_b(m, j):
        return exchange(send_b, got_b, b_send, b_got, m, j)

    def load_qkv(m):
        return pltpu.make_async_copy(qkv_in.at[m], qkv, qkv_sem)

    def load_first(m, j):
        rows = rows_of(j, chunk)
        slot = lax.rem(j, 2)
        return [
            pltpu.make_async_copy(result_in.at[m, rows], result.at[slot], first_sem.at[slot, 0]),
            pltpu.make_async_copy(slope_in.at[m, rows], slope.at[slot], first_sem.at[slot, 1]),
            pltpu.make_async_copy(scale_in.at[m, 1, rows], scale_z.at[slot], first_sem.at[slot, 2]),
        ]

    def load_second(m, j):
        rows = rows_of(j, chunk)
        return [
            pltpu.make_async_copy(middle_in.at[m, rows], middle, second_sem.at[0]),
            pltpu.make_async_copy(scale_in.at[m, 0, rows], scale_a, second_sem.at[1]),
            pltpu.make_async_copy(mixed_in.at[m, rows], mixed, second_sem.at[2]),
            pltpu.make_async_copy(stat_in.at[m, rows], stat, second_sem.at[3]),
        ]

    def keep_first(m, j):
        rows = rows_of(j, chunk)
        slot = lax.rem(j, 2)
        return [
            pltpu.make_async_copy(low_gz.at[j], gz_out.at[m, rows], keep_sem.at[slot, 0]),
            pltpu.make_async_copy(low_pre.at[slot], pre_out.at[m, rows], keep_sem.at[slot, 1]),
        ]

    def keep_second(m, j):
        rows = rows_of(j, chunk)
        return pltpu.make_async_copy(low_ga, ga_out.at[m, rows], keep_ga_sem)

    def keep_qkv(m):
        return pltpu.make_async_copy(grad_qkv, gqkv_out.at[m], keep_qkv_sem)

    placed = OutPieces(at, grads, grads_out, grads_sem, out_send, out_got)

    load_qkv(0).start()
    for copy in load_first(0, 0) + load_first(0, 1) + load_second(0, 0):
        copy.start()

    @pl.when(section == last)
    def _():
        for m in range(micro):
            for j in range(chunks):
                load(m, j).start()

    gains[...] = gains_in[...].astype(jnp.float32)
    biases[...] = biases_in[...].astype(jnp.float32)
    row_sums[...] = jnp.zeros_like(row_sums)
    in_sums[...] = jnp.zeros_like(in_sums)
    qkv_sums[...] = jnp.zeros_like(qkv_sums)
    time_sums[...] = jnp.zeros_like(time_sums)
    greet(section, sections, (at.peer, at.across, at.beside))

    def add_row(index, value):
        row_sums[index : index + 1] += jnp.sum(value, axis=0, keepdims=True)

    def receive(m, j):
        @pl.when(section < last)
        def _():
            hop(m, j).wait_recv()
            hand_over(m, j).start()

    def norm_back_rows(gradient, unit, inv_scale, gain):
        weighted = gradient * gain
        return inv_scale * (
            weighted
            - jnp.mean(weighted, axis=-1, keepdims=True)
            - unit * jnp.mean(weighted * unit, axis=-1, keepdims=True)
        )

    def feed_back(m, j):
        rows = rows_of(j, chunk)
        slot = lax.rem(j, 2)

        @pl.when(section == last)
        def _():
            load(m, j).wait()

        @pl.when(section < last)
        def _():
            hand_over(m, j).wait_recv()

        for copy in load_first(m, j):
            copy.wait()
        gradient = gbuf[m, rows].astype(jnp.float32)
        unit = (result[slot].astype(jnp.float32) - biases[3:4]) / gains[1:2]
        grad_z = norm_back_rows(gradient, unit, scale_z[slot, :, :1], gains[1:2])
        add_row(1, gradient * unit)
        add_row(5, gradient)
        add_row(4, grad_z)
        low_gz[j] = grad_z.astype(low_type)
        hidden_size = wi.shape[1]
        step = min(1024, hidden_size)

        def before(start):
            return dot_rows(low_gz[j], wd[start : start + step])

        current = before(0)
        branch = jnp.zeros((chunk, width), jnp.float32)
        for start in range(0, hidden_size, step):
            part = slice(start, start + step)
            later = before(start + step) if start + step < hidden_size else None
            low = (current * slope[slot, :, part].astype(jnp.float32)).astype(low_type)
            low_pre[slot, :, part] = low
            in_sums[:, part] += jnp.sum(low.astype(jnp.float32), axis=0, keepdims=True)
            branch = branch + dot_rows(low, wi[:, part])
            current = later
        send_a[j] = branch.astype(low_type)
        exchange_a(m, j).start()
        for copy in keep_first(m, j):
            copy.start()

    def norm_step(m, j):
        rows = rows_of(j, chunk)
        exchange_a(m, j).wait()
        for copy in load_second(m, j):
            copy.wait()
        gradient = (
            send_a[j].astype(jnp.float32)
            + got_a[j].astype(jnp.float32)
            + low_gz[j].astype(jnp.float32)
        )
        unit = (middle[...].astype(jnp.float32) - biases[1:2]) / gains[0:1]
        grad_a = norm_back_rows(gradient, unit, scale_a[:, :1], gains[0:1])
        add_row(0, gradient * unit)
        add_row(3, gradient)
        add_row(2, grad_a)
        high_ga[rows] = grad_a.astype(low_type)
        low_ga[...] = grad_a.astype(low_type)
        keep_second(m, j).start()
        grad_mixed[...] = dot_rows(low_ga[...], wo[...]).astype(low_type)

    def build(m):
        load_qkv(m).wait()

        starts, _ = row_facts(at, own_ref, other_ref, m)

        def step(j, carry):
            rows = rows_of(j, chunk)
            first, rel, own = doc_lanes(starts, j * chunk, shape)
            fixed = jnp.logical_and(rel >= count, rel < count + 3)
            extra_k = jnp.where(jnp.logical_or(own, fixed), 1.0, 0.0).astype(low_type)
            extra_v = jnp.where(fixed, 1.0, 0.0).astype(low_type)
            for p in range(pairs):
                lane = slice(p * LANES, (p + 1) * LANES)
                k = qkv[rows, columns + p * LANES : columns + (p + 1) * LANES]
                v = qkv[rows, 2 * columns + p * LANES : 2 * columns + (p + 1) * LANES]
                keys[2 * p, rows] = jnp.where(first, k, extra_k)
                keys[2 * p + 1, rows] = jnp.where(first, extra_k, k)
                values[2 * p, rows] = jnp.where(first, v, extra_v)
                values[2 * p + 1, rows] = jnp.where(first, extra_v, v)
                grad_k[rows, lane] = jnp.zeros(shape, jnp.float32)
                grad_v[rows, lane] = jnp.zeros(shape, jnp.float32)
            return carry

        lax.fori_loop(0, chunks, step, 0)

    def mix_back(m, j):
        rows = rows_of(j, chunk)
        lane_index = lax.broadcasted_iota(jnp.int32, shape, 1)
        first = lane_index < HEAD
        rel = lane_index % HEAD
        all_first = lax.broadcasted_iota(jnp.int32, (length, LANES), 1) < HEAD
        for p in range(pairs):
            lane = slice(p * LANES, (p + 1) * LANES)
            q = qkv[rows, lane] * low_type(HEAD**-0.5)
            k = qkv[:, columns + p * LANES : columns + (p + 1) * LANES]
            g = grad_mixed[:, lane]
            extra_q = stat[:, lane]
            product = g.astype(jnp.float32) * mixed[:, lane].astype(jnp.float32)
            dots = [
                jnp.sum(jnp.where(first, product, 0.0), axis=-1, keepdims=True),
                jnp.sum(jnp.where(first, 0.0, product), axis=-1, keepdims=True),
            ]
            extra_g = lanes(
                rel, count, -jnp.where(first, dots[1], dots[0]), jnp.zeros_like(extra_q)
            )
            parts = []
            for i in range(2):
                q_head = jnp.where(first, q, extra_q) if i == 0 else jnp.where(first, extra_q, q)
                g_head = jnp.where(first, g, extra_g) if i == 0 else jnp.where(first, extra_g, g)
                probs = jnp.exp(dot_rows(keys[2 * p + i], q_head))
                slopes = (probs * dot_rows(values[2 * p + i], g_head)).astype(low_type)
                parts.append(
                    (
                        dot_plain(probs.astype(low_type), g),
                        dot_plain(slopes, q),
                        dot_first(slopes, k),
                    )
                )
            grad_v[:, lane] += jnp.where(all_first, parts[0][0], parts[1][0])
            grad_k[:, lane] += jnp.where(all_first, parts[0][1], parts[1][1])
            grad_qkv[rows, lane] = (
                jnp.where(first, parts[0][2], parts[1][2]) * (HEAD**-0.5)
            ).astype(low_type)

    def project_back(m, j):
        rows = rows_of(j, chunk)
        low = grad_qkv[rows]
        qkv_sums[...] += jnp.sum(low.astype(jnp.float32), axis=0, keepdims=True)
        total = dot_rows(low[:, :columns], wq[0])
        for third in range(1, 3):
            total = total + dot_rows(low[:, third * columns : (third + 1) * columns], wq[third])
        send_b[lax.rem(j, 2)] = total.astype(low_type)
        exchange_b(m, j).start()

    def finish(m, j):
        rows = rows_of(j, chunk)
        slot = lax.rem(j, 2)
        exchange_b(m, j).wait()

        @pl.when(m > 0)
        def _():
            placed.wait(m - 1, j)

            @pl.when(section > 0)
            def _():
                hop(m - 1, j).wait_send()

        total = (
            send_b[slot].astype(jnp.float32) + got_b[j].astype(jnp.float32) + high_ga[rows].astype(jnp.float32)
        ).astype(low_type)
        grads[j] = total
        time_sums[m] += jnp.sum(total.astype(jnp.float32), axis=0, keepdims=True)

        @pl.when(section > 0)
        def _():
            hop(m, j).start()

        placed.start(m, j)

    def block(order):
        owner = jnp.where(order < 2, 1 - at.chip, at.chip)
        return 2 * owner + lax.rem(order, 2)

    def feed_products():
        @pl.when(section < last)
        def _():
            for m in range(micro):
                for j in range(chunks):
                    hand_over(m, j).wait_send()

        width_half = width
        block_in, block_down = own_in.shape[1], own_down.shape[1]
        phases = (
            (middle_in, pre_out, width_half, block_in),
            (middle_in, pre_out, 0, block_in),
            (hidden_in, gz_out, 0, block_down),
        )

        def room(phase, m):
            if phase % 2 == 0:
                return gbuf.at[m]
            return wi.at[:, pl.ds(m * width, width)]

        def load_right(phase):
            _, right, first, _ = phases[phase]
            return [
                pltpu.make_async_copy(
                    right.at[m, :, pl.ds(first, width)],
                    room(phase, m),
                    right_sem.at[phase % 2, m],
                )
                for m in range(micro)
            ]

        def spot(t):
            return pl.ds(pl.multiple_of(lax.rem(t, 2) * chunk, chunk), chunk)

        for copy in load_right(0):
            copy.start()
        for phase, (left, right, first, rows) in enumerate(phases):
            subs = rows // chunk
            if phase + 1 < len(phases):
                for copy in load_right(phase + 1):
                    copy.start()

            def load_left(t, left=left, rows=rows, subs=subs):
                start = block(t // subs) * rows + lax.rem(t, subs) * chunk
                return [
                    pltpu.make_async_copy(
                        left.at[m, :, pl.ds(pl.multiple_of(start, chunk), chunk)],
                        wd.at[pl.ds(m * length, length), spot(t)],
                        left_sem.at[lax.rem(t, 2), m],
                    )
                    for m in range(micro)
                ]

            def store(t, phase=phase, first=first, subs=subs):
                order = t // subs
                if phase < 2:
                    target = own_in.at[order, :, pl.ds(first, width)]
                else:
                    target = own_down.at[order, rows_of(lax.rem(t, subs), chunk)]
                slot = lax.rem(t, 2)
                return pltpu.make_async_copy(stage.at[slot], target, store_sem.at[slot])

            def after(t, phase=phase, subs=subs, store=store):
                store(t).wait()
                order = t // subs

                @pl.when(lax.rem(t, subs) == subs - 1)
                def _():
                    if phase != 1:

                        @pl.when(order < 2)
                        def _():
                            (part_in_b if phase == 0 else part_down_b)(order).start()

                    if phase > 0:

                        @pl.when(at.away)
                        def _():
                            (part_in_a if phase == 1 else part_down_a)(order).start()

            for copy in load_left(0):
                copy.start()
            for copy in load_right(phase):
                copy.wait()

            def step(
                t, carry, load_left=load_left, store=store, after=after, subs=subs, phase=phase
            ):
                for copy in load_left(t):
                    copy.wait()

                @pl.when(t + 1 < 4 * subs)
                def _():
                    for copy in load_left(t + 1):
                        copy.start()

                value = dot_first(wd[:length, spot(t)], room(phase, 0)[...])
                for m in range(1, micro):
                    value = value + dot_first(
                        wd[m * length : (m + 1) * length, spot(t)], room(phase, m)[...]
                    )

                @pl.when(t > 0)
                def _():
                    after(t - 1)

                stage[lax.rem(t, 2)] = value.astype(low_type)
                store(t).start()
                return carry

            lax.fori_loop(0, 4 * subs, step, 0)
            after(4 * subs - 1)

    def part_in_b(order):
        return remote(
            own_in.at[order, :, pl.ds(width, width)],
            in_first_b.at[order],
            part_send.at[order],
            part_got.at[order],
            at.beside,
        )

    def part_in_a(order):
        return remote(
            own_in.at[order, :, pl.ds(0, width)],
            in_first_a.at[order],
            part_send.at[2 + order],
            part_got.at[2 + order],
            at.across,
        )

    def part_down_b(order):
        return remote(
            own_down.at[order, :, pl.ds(width // 2, width // 2)],
            down_first_b.at[order],
            part_send.at[6 + order],
            part_got.at[6 + order],
            at.beside,
        )

    def part_down_a(order):
        return remote(
            own_down.at[order, :, pl.ds(0, width // 2)],
            down_first_a.at[order],
            part_send.at[8 + order],
            part_got.at[8 + order],
            at.across,
        )

    def one_row(m, carry):
        early = jnp.logical_and(section == 0, m == micro - 1)

        @pl.when(m == 0)
        def _():
            weights[0].wait()
            weights[1].wait()

        receive(m, 0)

        def first_step(j, carry):
            @pl.when(j >= 2)
            def _():
                for copy in keep_first(m, j - 2):
                    copy.wait()

            feed_back(m, j)

            @pl.when(j + 2 < chunks)
            def _():
                for copy in load_first(m, j + 2):
                    copy.start()

            @pl.when(jnp.logical_and(j + 2 >= chunks, m + 1 < micro))
            def _():
                for copy in load_first(m + 1, j + 2 - chunks):
                    copy.start()

            @pl.when(jnp.logical_and(early, j == 2))
            def _():
                receive(m, 3)

            return carry

        def reached(i):
            late = jnp.minimum(i * (i + 1) // 2, chunks)
            return jnp.where(jnp.logical_and(early, i >= 2), chunks, late)

        def step(i, carry):
            @pl.when(i >= 1)
            def _():
                @pl.when(i >= 2)
                def _():
                    keep_second(m, i - 2).wait()

                norm_step(m, i - 1)

                @pl.when(i == 1)
                def _():
                    receive(m, 1)

                @pl.when(jnp.logical_and(i == 2, jnp.logical_not(early)))
                def _():
                    receive(m, 3)

                mix_back(m, i - 1)

                @pl.when(i < chunks)
                def _():
                    for copy in load_second(m, i):
                        copy.start()

                @pl.when(jnp.logical_and(i == chunks, m + 1 < micro))
                def _():
                    for copy in load_second(m + 1, 0):
                        copy.start()

                @pl.when(i == 1)
                def _():
                    receive(m, 2)

            lax.fori_loop(reached(i), reached(i + 1), first_step, 0)

            @pl.when(i == 0)
            def _():
                @pl.when(m == 0)
                def _():
                    weights[2].wait()
                    weights[3].wait()

                build(m)

            @pl.when(jnp.logical_and(early, i == 1))
            def _():
                for copy in keep_first(m, chunks - 2) + keep_first(m, chunks - 1):
                    copy.wait()
                feed_products()

            return carry

        lax.fori_loop(0, chunks + 1, step, 0)

        @pl.when(jnp.logical_not(early))
        def _():
            for copy in keep_first(m, chunks - 2) + keep_first(m, chunks - 1):
                copy.wait()

        keep_second(m, chunks - 1).wait()

        @pl.when(m + 1 < micro)
        def _():
            load_qkv(m + 1).start()

        grad_qkv[:, columns : 2 * columns] = grad_k[...].astype(low_type)
        grad_qkv[:, 2 * columns :] = grad_v[...].astype(low_type)
        keep_qkv(m).start()

        shift = jnp.where(jnp.logical_and(section == 0, at.group == 0), chunks // 2, 0)

        def last_step(i, carry):
            @pl.when(i < chunks)
            def _():
                project_back(m, lax.rem(i + shift, chunks))

            @pl.when(i >= 1)
            def _():
                finish(m, lax.rem(i - 1 + shift, chunks))

            return carry

        lax.fori_loop(0, chunks + 1, last_step, 0)
        keep_qkv(m).wait()
        return carry

    lax.fori_loop(0, micro, one_row, 0)
    for j in range(chunks):
        placed.wait(micro - 1, j)

    @pl.when(section > 0)
    def _():
        for j in range(chunks):
            hop(micro - 1, j).wait_send()

    pl.when(section > 0)(feed_products)
    for order in range(2):
        part_in_b(order).wait()
        part_down_b(order).wait()
    for order in range(4):

        @pl.when(at.away)
        def _(order=order):
            part_in_a(order).wait_send()
            part_down_a(order).wait_send()

        @pl.when(at.home)
        def _(order=order):
            part_in_a(order).wait_recv()
            part_down_a(order).wait_recv()

    placed.wait_got()


def backward_pass(sections, facts, gains, biases, rows_back, params, stash):
    qkv_w, out_w, in_w, down_w = params
    micro, length, width = rows_back.shape
    columns, hidden = out_w.shape[0], in_w.shape[1]
    chunk = min(256, length // 4)
    chunks = length // chunk
    low, high = low_type, jnp.float32

    def out(*shape, dtype=low):
        return jax.ShapeDtypeStruct(shape, dtype)

    outs = dict(
        row_sums=out(6, width, dtype=high),
        in_sums=out(1, hidden, dtype=high),
        qkv_sums=out(1, 3 * columns, dtype=high),
        time_sums=out(micro, 1, width, dtype=high),
        grad_z=out(micro, length, width),
        grad_pre=out(micro, length, hidden),
        grad_a=out(micro, length, width),
        grad_qkv=out(micro, length, 3 * columns),
        grads=out(micro, length // 2, width),
        own_in=out(4, width // 4, hidden),
        own_down=out(4, hidden // 4, width),
        in_first_b=out(2, width // 4, hidden // 2),
        in_first_a=out(4, width // 4, hidden // 2),
        down_first_b=out(2, hidden // 4, width // 2),
        down_first_a=out(4, hidden // 4, width // 2),
    )
    vmem = pl.BlockSpec(memory_space=pltpu.VMEM)
    anywhere = pl.BlockSpec(memory_space=pl.ANY)
    dma = pltpu.SemaphoreType.DMA
    results = pl.pallas_call(
        functools.partial(backward_kernel, sections, chunk),
        in_specs=[pl.BlockSpec(memory_space=pltpu.SMEM)] * 2 + [vmem] * 2 + [anywhere] * 13,
        out_specs=[vmem] * 4 + [anywhere] * 11,
        out_shape=list(outs.values()),
        scratch_shapes=[
            pltpu.VMEM(qkv_w.shape, low),
            pltpu.VMEM(out_w.shape, low),
            pltpu.VMEM(in_w.shape, low),
            pltpu.VMEM(down_w.shape, low),
            pltpu.VMEM(gains.shape, high),
            pltpu.VMEM(biases.shape, high),
            pltpu.VMEM((micro, length, width), low),
            pltpu.VMEM((length, width), low),
            pltpu.VMEM((length, 3 * columns), low),
            pltpu.VMEM((columns // HEAD, length, LANES), low),
            pltpu.VMEM((columns // HEAD, length, LANES), low),
            pltpu.VMEM((length, columns), high),
            pltpu.VMEM((length, columns), high),
            pltpu.VMEM((length, 3 * columns), low),
            pltpu.VMEM((chunks, chunk, width), low),
            pltpu.VMEM((2, chunk, width), low),
            pltpu.VMEM((chunks, chunk, width), low),
            pltpu.VMEM((chunks, chunk, width), low),
            pltpu.VMEM((chunks, chunk, width), low),
            pltpu.VMEM((2, chunk, hidden), low),
            pltpu.VMEM((chunk, width), low),
            pltpu.VMEM((chunk, columns), low),
            pltpu.VMEM((chunks, chunk, width), low),
            pltpu.VMEM((2, chunk, width), low),
            pltpu.VMEM((2, chunk, hidden), low),
            pltpu.VMEM((2, chunk, LANES), high),
            pltpu.VMEM((chunk, width), low),
            pltpu.VMEM((chunk, LANES), high),
            pltpu.VMEM((chunk, columns), low),
            pltpu.VMEM((chunk, columns), low),
            dma((4,)),
            dma((micro, chunks)),
            dma((chunks,)),
            dma((micro, chunks)),
            dma((micro, chunks)),
            dma((micro, chunks)),
            dma((chunks,)),
            dma((micro, chunks)),
            dma((2,)),
            dma((micro, chunks)),
            dma,
            dma((2, 3)),
            dma((4,)),
            dma((2, 2)),
            dma,
            dma,
            dma((chunks,)),
            dma((chunks,)),
            dma((chunks // 2,)),
            pltpu.VMEM((2, chunk, width), low),
            dma((2, micro)),
            dma((2, micro)),
            dma((2,)),
            dma((12,)),
            dma((12,)),
        ],
        compiler_params=pltpu.CompilerParams(
            collective_id=1, has_side_effects=True, vmem_limit_bytes=63 * 1024 * 1024
        ),
        name="backward_pass",
    )(
        *facts,
        gains,
        biases,
        rows_back,
        qkv_w,
        out_w,
        in_w,
        down_w,
        stash["qkv"],
        stash["log_sums"],
        stash["mixed"],
        stash["middle"],
        stash["hidden"],
        stash["slope"],
        stash["result"],
        stash["scales"],
    )
    return dict(zip(outs, results))


def gradient_kernel(
    sections,
    plan,
    ready,
    own_ref,
    other_ref,
    row_sums,
    in_sums,
    qkv_sums,
    time_sums,
    *refs,
):
    count = len(plan)
    done = len(ready)
    number = 1 + max(part[0] for part in plan)
    made = {w: i for i, w in enumerate(sorted({part[0] for part in plan[done:]}))}
    products, arrived = refs[: 1 + max(ready)], refs[1 + max(ready) : 1 + max(ready) + done]
    refs = refs[1 + max(ready) + done :]
    lefts, rights = refs[: len(made)], refs[len(made) : 2 * len(made)]
    refs = refs[2 * len(made) :]
    outs = refs[:number]
    gains_out, biases_out, qv_out, in_out, time_rows_out = refs[number : number + 5]
    refs = refs[number + 5 :]
    tiles, firsts, seconds, shares, finals = (
        refs[i * count : (i + 1) * count] for i in range(5)
    )
    (
        held,
        right,
        small_in,
        small_group,
        small_beside,
        small_out,
        other_out,
        time_out,
        left_sem,
        right_sem,
        first_send,
        first_got,
        second_send,
        second_got,
        share_send,
        share_got,
        final_sem,
        ready_sem,
        small_send,
        small_got,
    ) = refs[5 * count :]
    at = Seat()
    section, chip, core = at.section, at.chip, at.core

    def block(order):
        owner = 1 - chip if order < 2 else chip
        return 2 * owner + order % 2

    steps = []
    for w, (_, rows, _, _, _) in enumerate(plan):
        if w < done:
            continue
        width = min(256, rows)
        for order in range(4):
            for start in range(0, rows, width):
                steps.append((w, order, start, width))

    def load_left(index):
        w, order, start, width = steps[index]
        number, rows, _, _, _ = plan[w]
        first = pl.multiple_of(block(order) * rows + start, width)
        return pltpu.make_async_copy(
            lefts[made[number]].at[:, pl.ds(first, width)],
            held.at[index % 2, :, pl.ds(0, width)],
            left_sem.at[index % 2],
        )

    def room(w):
        return right.at[w % 2, :, pl.ds(0, plan[w][3])]

    def load_right(w):
        number, _, first, columns, _ = plan[w]
        return pltpu.make_async_copy(
            rights[made[number]].at[:, pl.ds(first, columns)], room(w), right_sem.at[w % 2]
        )

    def send_first(w, order):
        if plan[w][4]:
            return remote(
                tiles[w].at[order],
                firsts[w].at[order],
                first_send.at[w, order],
                first_got.at[w, order],
                at.across,
            )
        return remote(
            tiles[w].at[order],
            firsts[w].at[order],
            first_send.at[w, order],
            first_got.at[w, order],
            at.beside,
        )

    def send_second(w, order):
        if plan[w][4]:
            return remote(
                tiles[w].at[order],
                seconds[w].at[order],
                second_send.at[w, order],
                second_got.at[w, order],
                at.beside,
            )
        return remote(
            tiles[w].at[2 + order],
            seconds[w].at[order],
            second_send.at[w, order],
            second_got.at[w, order],
            at.across,
        )

    def send_share(w):
        return remote(
            tiles[w].at[3 - core], shares[w], share_send.at[w], share_got.at[w], at.peer
        )

    def store_final(w):
        number, _, first, columns, _ = plan[w]
        target = outs[number]
        if len(target.shape) == 2:
            places = [(finals[w], target.at[:, pl.ds(first, columns)])]
        else:
            size = target.shape[2]
            places = [
                (finals[w].at[:, pl.ds(i * size, size)], target.at[first // size + i])
                for i in range(columns // size)
            ]
        return [
            pltpu.make_async_copy(source, place, final_sem.at[w, i])
            for i, (source, place) in enumerate(places)
        ]

    def put_final(w, value):
        finals[w][...] = value.astype(finals[w].dtype)
        for copy in store_final(w):
            copy.start()

    def high(value):
        return value.astype(jnp.float32)

    def load_ready(w):
        number, _, first, columns, _ = plan[w]
        return [
            pltpu.make_async_copy(
                products[number].at[:, :, pl.ds(first, columns)], tiles[w], ready_sem.at[w, 0]
            ),
            pltpu.make_async_copy(arrived[w], firsts[w], ready_sem.at[w, 1]),
        ]

    for w in range(done):
        for copy in load_ready(w):
            copy.start()
    load_right(done).start()
    load_right(done + 1).start()
    load_left(0).start()
    small_in[...] = jnp.zeros_like(small_in)
    small_in[0:6] = row_sums[...]
    weighted = jnp.zeros_like(time_sums[0])
    plain = jnp.zeros_like(time_sums[0])
    for m in range(time_sums.shape[0]):
        _, moment = row_facts(at, own_ref, other_ref, m)
        fraction = jnp.full((1, time_sums.shape[2]), moment.astype(jnp.float32)) / 5000.0
        weighted = weighted + fraction * time_sums[m]
        plain = plain + time_sums[m]
    from_first = jnp.where(section == 0, 1.0, 0.0)
    small_in[8:9] = weighted * from_first
    small_in[9:10] = plain * from_first
    width = small_in.shape[1]
    for i in range(in_sums.shape[1] // width):
        small_in[16 + i : 17 + i] = in_sums[:, i * width : (i + 1) * width]
    third = qkv_sums.shape[1] // 3
    small_in[20:21, :third] = qkv_sums[:, :third]
    small_in[20:21, third : 2 * third] = qkv_sums[:, 2 * third :]
    greet(section, sections, (at.peer, at.across, at.beside))

    small_across = remote(
        small_in, small_group, small_send.at[0], small_got.at[0], at.across
    )
    small_chips = remote(
        small_in, small_beside, small_send.at[1], small_got.at[1], at.beside
    )
    small_cores = remote(small_out, other_out, small_send.at[2], small_got.at[2], at.peer)
    time_hop = remote(
        time_out, time_out, small_send.at[3], small_got.at[3], {"section": section + 1}
    )
    small_across.start()

    def second_stage(w):
        shift, condition = (0, at.home) if plan[w][4] else (2, at.away)

        @pl.when(condition)
        def _():
            for order in range(2):
                if w >= done:
                    send_first(w, order).wait_recv()
                tiles[w][shift + order] = (
                    high(tiles[w][shift + order]) + high(firsts[w][order])
                ).astype(low_type)
                send_second(w, order).start()

    for w in range(done):
        for copy in load_ready(w):
            copy.wait()
        second_stage(w)
    seen = 0
    for w, (_, _, _, columns, across_first) in enumerate(plan):
        if w < done:
            continue
        load_right(w).wait()
        for order in range(4):
            while seen < len(steps) and steps[seen][:2] == (w, order):
                load_left(seen).wait()
                if seen + 1 < len(steps):
                    load_left(seen + 1).start()
                _, _, start, step_width = steps[seen]
                tiles[w][order, start : start + step_width] = dot_first(
                    held[seen % 2, :, :step_width], right[w % 2, :, :columns]
                ).astype(low_type)
                seen += 1
            if across_first:
                pl.when(at.away)(send_first(w, order).start)
            elif order < 2:
                send_first(w, order).start()
        if w + 2 < count:
            load_right(w + 2).start()
        if w == done:
            small_across.wait()
            small_in[...] += small_group[...]
            small_chips.start()
        if w == done + 1:
            small_chips.wait()
            small_out[...] = small_in[...] + small_beside[...]
            small_cores.start()

    @pl.when(section == 0)
    def _():
        time_out[...] = small_out[8:16]

    for w in range(done, count):
        second_stage(w)

    @pl.when(at.home)
    def _():
        for w, (_, _, _, _, across_first) in enumerate(plan):
            for order in range(2):
                if w >= done:
                    send_first(w, order + 2 if across_first else order).wait_recv()
                send_second(w, order).wait_recv()

            def total(side):
                first = firsts[w][2 + side] if across_first else firsts[w][side]
                return high(tiles[w][2 + side]) + high(first) + high(seconds[w][side])

            tiles[w][3 - core] = total(1 - core).astype(low_type)
            send_share(w).start()
            put_final(w, total(core))

    @pl.when(at.away)
    def _():
        for w in range(count):
            send_share(w).wait_recv()
            put_final(w, shares[w][...])

    small_cores.wait()
    device = 4 * at.group + 2 * chip + core
    lane = pl.ds(pl.multiple_of(device * LANES, LANES), LANES)
    gains_out[...] = small_out[0:2, lane]
    biases_out[...] = small_out[2:6, lane]

    def place(source):
        quarter = 2 * chip + core
        size = third // 4
        qv_out[0:1] = source[20:21, pl.ds(pl.multiple_of(quarter * size, size), size)]
        qv_out[1:2] = source[20:21, pl.ds(pl.multiple_of(third + quarter * size, size), size)]
        size = in_out.shape[1]
        per = width // size
        spot = pl.ds(pl.multiple_of(lax.rem(quarter, per) * size, size), size)
        for i in range(4 // per):

            @pl.when(quarter // per == i)
            def _(i=i):
                in_out[...] = source[16 + i : 17 + i, spot]

    pl.when(at.home)(functools.partial(place, small_out))
    pl.when(at.away)(functools.partial(place, other_out))

    @pl.when(section > 0)
    def _():
        time_hop.wait_recv()

    @pl.when(section < sections - 1)
    def _():
        time_hop.start()
        time_hop.wait_send()

    time_rows_out[...] = time_out[0:2]
    for w, (_, _, _, _, across_first) in enumerate(plan):
        for copy in store_final(w):
            copy.wait()
        if across_first:

            @pl.when(at.away)
            def _(w=w):
                for order in range(4):
                    if w >= done:
                        send_first(w, order).wait_send()

            @pl.when(at.home)
            def _(w=w):
                for order in range(2):
                    send_second(w, order).wait_send()

        else:
            for order in range(2):
                if w >= done:
                    send_first(w, order).wait_send()

            @pl.when(at.away)
            def _(w=w):
                for order in range(2):
                    send_second(w, order).wait_send()

        pl.when(at.home)(send_share(w).wait_send)


def gradient_pass(sections, facts, back, products, arrived, lefts, rights, splits, order):
    blocks = [product.shape[1:] for product in products]
    blocks += [(left.shape[1] // 4, right.shape[1]) for left, right in zip(lefts, rights)]
    plan = tuple(
        (number, blocks[number][0], first, columns, across)
        for number, first, columns, across in order
    )
    ready = tuple(part[0] for part in plan[: len(arrived)])
    finals = [
        (rows, columns) if split == 1 else (split, rows, columns // split)
        for (rows, columns), split in zip(blocks, splits)
    ]
    length = lefts[0].shape[0]
    low, high = low_type, jnp.float32
    width = back["row_sums"].shape[1]
    count = len(plan)
    vmem = pl.BlockSpec(memory_space=pltpu.VMEM)
    anywhere = pl.BlockSpec(memory_space=pl.ANY)
    dma = pltpu.SemaphoreType.DMA
    small = (24, width)
    hidden = back["in_sums"].shape[1]
    smalls = [
        (2, width // 8),
        (4, width // 8),
        (2, back["qkv_sums"].shape[1] // 12),
        (1, hidden // 4),
        (2, width),
    ]

    def buffers(size):
        return [pltpu.VMEM((size(part), part[1], part[3]), low) for part in plan]

    return pl.pallas_call(
        functools.partial(gradient_kernel, sections, plan, ready),
        in_specs=[pl.BlockSpec(memory_space=pltpu.SMEM)] * 2
        + [vmem] * 4
        + [anywhere] * (len(products) + len(arrived) + 2 * len(lefts)),
        out_specs=[anywhere] * len(finals) + [vmem] * len(smalls),
        out_shape=[jax.ShapeDtypeStruct(shape, low) for shape in finals]
        + [jax.ShapeDtypeStruct(shape, high) for shape in smalls],
        scratch_shapes=buffers(lambda part: 4)
        + buffers(lambda part: 4 if part[4] else 2)
        + buffers(lambda part: 2)
        + [pltpu.VMEM((part[1], part[3]), low) for part in plan]
        + [pltpu.VMEM((part[1], part[3]), low) for part in plan]
        + [
            pltpu.VMEM((2, length, min(256, max(part[1] for part in plan))), low),
            pltpu.VMEM((2, length, max(part[3] for part in plan[len(ready) :])), low),
        ]
        + [pltpu.VMEM(small, high)] * 5
        + [
            pltpu.VMEM((8, width), high),
            dma((2,)),
            dma((2,)),
            dma((count, 4)),
            dma((count, 4)),
            dma((count, 2)),
            dma((count, 2)),
            dma((count,)),
            dma((count,)),
            dma((count, 2)),
            dma((count, 2)),
            dma((4,)),
            dma((4,)),
        ],
        compiler_params=pltpu.CompilerParams(
            collective_id=2, has_side_effects=True, vmem_limit_bytes=62 * 1024 * 1024
        ),
        name="gradient_pass",
    )(
        *facts,
        back["row_sums"],
        back["in_sums"],
        back["qkv_sums"],
        back["time_sums"],
        *products,
        *arrived,
        *lefts,
        *rights,
    )


def unit_norm(value):
    average = jnp.mean(value, axis=-1, keepdims=True)
    centered = value - average
    inv_scale = lax.rsqrt(jnp.mean(centered * centered, axis=-1, keepdims=True) + eps_norm)
    return centered * inv_scale, inv_scale


def norm_back(gradient, normed, inv_scale, gain_row):
    weighted = gradient * gain_row
    adjusted = (
        weighted
        - jnp.mean(weighted, axis=-1, keepdims=True)
        - normed * jnp.mean(weighted * normed, axis=-1, keepdims=True)
    )
    return inv_scale * adjusted


def gelu_pair(pre):
    normal = 0.5 * (1.0 + lax.erf(pre * 0.7071067811865476))
    density = jnp.exp(-0.5 * pre * pre) * 0.3989422804014327
    return pre * normal, normal + pre * density


def forward_layer(at, inputs, starts, params):
    qkv_w, qkv_b, out_w, in_w, in_b, down_w, gains, biases = params
    qkv = (dot_plain(inputs, qkv_w) + qkv_b).astype(low_type)
    mixed, log_sums = attend(qkv, starts)
    branch = at.group_sum(dot_plain(mixed, out_w).astype(low_type))
    unit_a, scale_a = unit_norm(branch + biases[0] + inputs.astype(jnp.float32))
    middle = unit_a * gains[0] + biases[1]
    low_middle = middle.astype(low_type)
    hidden, slope = gelu_pair(dot_plain(low_middle, in_w) + in_b)
    hidden = hidden.astype(low_type)
    branch_two = at.group_sum(dot_plain(hidden, down_w).astype(low_type))
    unit_z, scale_z = unit_norm(branch_two + biases[2] + middle)
    result = (unit_z * gains[1] + biases[3]).astype(low_type)
    saved = dict(
        inputs=inputs,
        qkv=qkv,
        mixed=mixed,
        log_sums=log_sums,
        scale_a=scale_a[:, 0],
        middle=low_middle,
        hidden=hidden,
        slope=slope.astype(low_type),
        scale_z=scale_z[:, 0],
    )
    return result, saved


def backward_layer(at, saved, incoming, starts, params):
    qkv_w, qkv_b, out_w, in_w, in_b, down_w, gains, biases = params
    gradient = incoming.astype(jnp.float32)
    unit_z = (saved["result"].astype(jnp.float32) - biases[3]) / gains[1]
    grad_z = norm_back(gradient, unit_z, saved["scale_z"][:, None], gains[1])
    low_gz = grad_z.astype(low_type)
    grad_pre = (dot_rows(low_gz, down_w) * saved["slope"].astype(jnp.float32)).astype(low_type)
    grad_mid = at.group_sum(dot_rows(grad_pre, in_w).astype(low_type)) + grad_z
    unit_a = (saved["middle"].astype(jnp.float32) - biases[1]) / gains[0]
    grad_a = norm_back(grad_mid, unit_a, saved["scale_a"][:, None], gains[0])
    low_ga = grad_a.astype(low_type)
    grad_mixed = dot_rows(low_ga, out_w).astype(low_type)
    grad_qkv = jnp.concatenate(
        attend_back(saved["qkv"], starts, saved["mixed"], saved["log_sums"], grad_mixed), 1
    )
    grad_x = at.group_sum(dot_rows(grad_qkv, qkv_w).astype(low_type)) + grad_a
    sums = jnp.stack(
        [
            jnp.sum(grad_mid * unit_a, axis=0),
            jnp.sum(gradient * unit_z, axis=0),
            jnp.sum(grad_a, axis=0),
            jnp.sum(grad_mid, axis=0),
            jnp.sum(grad_z, axis=0),
            jnp.sum(gradient, axis=0),
        ]
    )
    kept = dict(grad_z=low_gz, slope=grad_pre, grad_a=low_ga, qkv=grad_qkv)
    return grad_x.astype(low_type), kept, sums


def store(buffers, values, slot):
    return jax.tree.map(
        lambda buffer, value: lax.dynamic_update_index_in_dim(buffer, value, slot, 0),
        buffers,
        values,
    )


def pick(buffers, slot):
    return jax.tree.map(
        lambda buffer: lax.dynamic_index_in_dim(buffer, slot, 0, keepdims=False), buffers
    )


def group_weight(at, weight):
    parts = weight.reshape((at.chips, -1) + weight.shape[1:])

    def across(s, g, u, x, c):
        return (s, c, u, x, g) if g != c else None

    def along(step):
        return lambda s, g, u, x, c: (s, g, u, (x + step) % at.chips, c) if g != c else None

    piece = at.move(lax.dynamic_index_in_dim(parts, at.chip, 0, keepdims=False), across)
    pieces = [piece]
    for step in range(1, at.chips):
        pieces.append(at.move(piece, along(step)))
    whole = parts
    for step, piece in enumerate(pieces):
        spot = (at.chip - step) % at.chips
        own = lax.dynamic_index_in_dim(parts, spot, 0, keepdims=False)
        whole = lax.dynamic_update_index_in_dim(whole, jnp.where(at.home, own, piece), spot, 0)
    return whole.reshape(weight.shape)


def group_rows(at, tokens, section):
    def across(s, g, u, x, c):
        return (s, 1 - g, u, x, c) if s == section else None

    own = lax.dynamic_index_in_dim(tokens, at.group, 0, keepdims=False)
    other = at.move(lax.dynamic_index_in_dim(tokens, 1 - at.group, 0, keepdims=False), across)
    lower = at.group == 0
    pair = jnp.stack([jnp.where(lower, own, other), jnp.where(lower, other, own)])
    whole = at.group_gather(pair)
    whole = whole.reshape((2, at.halves) + pair.shape)
    whole = jnp.swapaxes(whole, 1, 2)
    return whole.reshape(2, -1, tokens.shape[-1])


def spread_rows(at, rows, length):
    def across(s, g, u, x, c):
        return (s, 1 - g, u, x, c)

    row = lax.dynamic_index_in_dim(rows, at.core, 0, keepdims=False)
    tile = length // at.tensor

    def piece(group):
        return lax.dynamic_slice_in_dim(row, (group * at.halves + at.part) * tile, tile, 0)

    own = piece(at.group)
    other = at.move(piece(1 - at.group), across)
    lower = at.group == 0
    return jnp.stack([jnp.where(lower, own, other), jnp.where(lower, other, own)])


def sum_weight(at, gradient, across_first):
    parts = gradient.reshape((at.chips, -1) + gradient.shape[1:])

    def across(s, g, u, x, c):
        return (s, c, u, x, c) if g != c else None

    def along(step):
        def target(s, g, u, x, c):
            if across_first and g != c:
                return None
            return (s, g, u, (x + step) % at.chips, c)

        return target

    def fold_chips(parts):
        total = lax.dynamic_index_in_dim(parts, at.chip, 0, keepdims=False).astype(jnp.float32)
        for step in range(1, at.chips):
            piece = lax.dynamic_index_in_dim(
                parts, (at.chip + step) % at.chips, 0, keepdims=False
            )
            total = total + at.move(piece, along(step)).astype(jnp.float32)
        return total.astype(low_type)

    if across_first:
        total = fold_chips(
            (parts.astype(jnp.float32) + at.move(parts, across).astype(jnp.float32)).astype(
                low_type
            )
        )
    else:
        part = fold_chips(parts)
        total = (part.astype(jnp.float32) + at.move(part, across).astype(jnp.float32)).astype(
            low_type
        )
    halves = total.reshape((2, -1) + total.shape[1:])

    def over(s, g, u, x, c):
        return (s, g, u, x, 1 - c) if g == c else None

    own = lax.dynamic_index_in_dim(halves, at.core, 0, keepdims=False)
    other = at.move(lax.dynamic_index_in_dim(halves, 1 - at.core, 0, keepdims=False), over)
    return jnp.where(at.home, own, other).astype(jnp.float32)


def layer_ticks(at, starts, rows_in, rows_back, params):
    qkv_w = params[0]
    micro_count, length, width = rows_in.shape
    tick_count = micro_count + at.sections - 1
    slots = micro_count + 1

    def hop(result, distance):
        def target(s, g, u, x, c):
            return (s + distance, g, u, x, c) if 0 <= s + distance < at.sections else None

        tile = length // at.size
        piece = at.move(lax.dynamic_slice_in_dim(result, at.rank * tile, tile, 0), target)
        return at.group_gather(piece).reshape(length, width)

    def place_of(tick_value, stage):
        place = tick_value - stage
        usable = jnp.logical_and(place >= 0, place < micro_count)
        return usable, jnp.clip(place, 0, micro_count - 1), jnp.where(usable, place, micro_count)

    def empty(values):
        return jax.tree.map(
            lambda value: jnp.zeros((slots,) + value.shape, value.dtype), values
        )

    def forward_tick(tick_value, arrived, stash, outputs):
        usable, position, slot = place_of(tick_value, at.section)
        inputs = jnp.where(at.section == 0, rows_in[position], arrived)
        result, saved = forward_layer(at, inputs, starts[position], params)
        if stash is None:
            return result, saved
        return result, store(stash, saved, slot), store(outputs, result, slot)

    blank = jnp.zeros((length, width), low_type)
    shapes = jax.eval_shape(lambda: forward_tick(0, blank, None, None))
    stash, outputs = empty(shapes[1]), empty(shapes[0])

    def forward_loop(tick_value, carry):
        result, stash, outputs = forward_tick(tick_value, *carry)
        return hop(result, 1), stash, outputs

    carry = lax.fori_loop(0, tick_count - 1, forward_loop, (blank, stash, outputs))
    _, stash, outputs = forward_tick(tick_count - 1, *carry)

    def backward_tick(tick_value, arrived, stash, grads, totals):
        usable, position, slot = place_of(tick_value, at.sections - 1 - at.section)
        incoming = jnp.where(at.section == at.sections - 1, rows_back[position], arrived)
        grad_x, kept_now, sums = backward_layer(
            at, pick(dict(stash, result=outputs), slot), incoming, starts[position], params
        )
        totals = totals + jnp.where(usable, sums, 0.0)
        kept = store({name: stash[name] for name in kept_now}, kept_now, slot)
        return grad_x, dict(stash, **kept), store(grads, grad_x, slot), totals

    for name in ("grad_z", "grad_a"):
        stash[name] = empty(blank)
    totals = jnp.zeros((6, width), jnp.float32)

    def backward_loop(tick_value, carry):
        grad_x, stash, grads, totals = backward_tick(tick_value, *carry)
        return hop(grad_x, -1), stash, grads, totals

    carry = lax.fori_loop(
        0, tick_count - 1, backward_loop, (blank, stash, empty(blank), totals)
    )
    _, stash, grads, totals = backward_tick(tick_count - 1, *carry)

    def both(buffer):
        return buffer[:micro_count]

    low_gz, grad_pre, low_ga, grad_qkv = (
        both(stash[name]) for name in ("grad_z", "slope", "grad_a", "qkv")
    )
    stash = {name: both(value) for name, value in stash.items()}
    stash["result"] = both(outputs)
    grads = both(grads)
    back = dict(
        row_sums=totals,
        in_sums=jnp.sum(grad_pre, axis=(0, 1), dtype=jnp.float32)[None],
        qkv_sums=jnp.sum(grad_qkv, axis=(0, 1), dtype=jnp.float32)[None],
        time_sums=jnp.sum(grads, axis=1, keepdims=True, dtype=jnp.float32),
        grad_z=low_gz,
        grad_pre=grad_pre,
        grad_a=low_ga,
        grad_qkv=grad_qkv,
        grads=grads,
    )
    return stash, back


def shards(
    tokens,
    timesteps,
    seg_starts,
    time_params,
    qkv_weight,
    qv_bias,
    out_weight,
    ffn_in,
    ffn_bias,
    ffn_out,
    ln_gains,
    row_biases,
    cotangent,
):
    at = Layout()
    width = tokens.shape[-1]
    length = tokens.shape[1] * at.tensor
    columns = qkv_weight.shape[3]

    def over(s, g, u, x, c):
        return (s, g, u, x, 1 - c)

    own_facts = jnp.concatenate([seg_starts, timesteps[:, None]], 1)
    other_facts = at.move(own_facts, over)
    if at.size == 2 and at.chips == 2 and ffn_in.shape[2] == 2 * width == 2 * length:
        facts = (own_facts, other_facts)
        vectors = (qv_bias[0], ffn_bias, ln_gains[0], row_biases[0], time_params)
        weights = (
            jnp.transpose(qkv_weight[0], (1, 0, 2)),
            out_weight[0],
            ffn_in[0],
            ffn_out[0],
        )
        stash = forward_pass(at.sections, facts, vectors, tokens, cotangent, weights)
        weights = tuple(stash[name] for name in ("wq", "wo", "wi", "wd"))
        back = backward_pass(
            at.sections, facts, ln_gains[0], row_biases[0], stash["rows_back"], weights, stash
        )

        def flat(value):
            return value.reshape(-1, value.shape[-1])

        hidden = ffn_in.shape[2]
        in_g, down_g, qkv_g, out_g, gains_g, biases_g, qv_g, hidden_g, time_g = gradient_pass(
            at.sections,
            facts,
            back,
            (back["own_in"], back["own_down"]),
            [back[name] for name in ("in_first_b", "in_first_a", "down_first_b", "down_first_a")],
            [flat(stash[name]) for name in ("inputs", "mixed")],
            [flat(back[name]) for name in ("grad_qkv", "grad_a")],
            (1, 1, 3, 1),
            (
                (0, hidden // 2, hidden // 2, False),
                (0, 0, hidden // 2, True),
                (1, width // 2, width // 2, False),
                (1, 0, width // 2, True),
                (2, columns, 2 * columns, False),
                (2, 0, columns, True),
                (3, 0, width, True),
            ),
        )
        in_g, down_g, qkv_g, out_g = (
            value.astype(jnp.float32) for value in (in_g, down_g, qkv_g, out_g)
        )
        return (
            stash["placed"][None],
            back["grads"][None],
            jnp.transpose(qkv_g, (1, 0, 2))[None],
            qv_g[None],
            out_g[None],
            in_g[None],
            hidden_g,
            down_g[None],
            gains_g[None],
            biases_g[None],
            time_g,
        )

    first = at.core == 0
    facts = jnp.stack(
        [jnp.where(first, own_facts, other_facts), jnp.where(first, other_facts, own_facts)]
    )
    facts = lax.dynamic_index_in_dim(facts, at.group, 1, keepdims=False)
    starts, fractions = facts[:, :-1], facts[:, -1].astype(jnp.float32) / 5000.0
    own_fractions = timesteps.astype(jnp.float32) / 5000.0
    time_values = time_params.astype(jnp.float32)
    embedded = (
        tokens.astype(jnp.float32) + own_fractions[:, None, None] * time_values[0] + time_values[1]
    ).astype(low_type)
    gains, biases = ln_gains[0].astype(jnp.float32), row_biases[0].astype(jnp.float32)
    tensor = lax.axis_index("tensor")
    dp = lax.axis_index("dp")
    rows_in = group_rows(at, embedded, 0)
    qv_low = group_weight(at, qv_bias[0].T).T.astype(jnp.float32)
    params = (
        group_weight(at, qkv_weight[0].reshape(width, 3 * columns)),
        jnp.concatenate([qv_low[0], jnp.zeros((columns,), jnp.float32), qv_low[1]]),
        group_weight(at, out_weight[0]),
        group_weight(at, ffn_in[0]),
        group_weight(at, ffn_bias[0]).astype(jnp.float32),
        group_weight(at, ffn_out[0]),
        gains,
        biases,
    )
    rows_back = group_rows(at, cotangent, at.sections - 1)
    stash, back = layer_ticks(at, starts, rows_in, rows_back, params)
    layer_outs = spread_rows(at, stash["result"], length)
    input_grads = spread_rows(at, back["grads"], length)

    def product(left, right):
        left, right = (v.reshape(-1, v.shape[-1]) for v in (left, right))
        return dot_first(left, right).astype(low_type)

    down_g = sum_weight(at, product(stash["hidden"], back["grad_z"]), True)
    in_g = sum_weight(at, product(stash["middle"], back["grad_pre"]), False)
    out_g = sum_weight(at, product(stash["mixed"], back["grad_a"]), True)
    qkv_g = sum_weight(at, product(stash["inputs"], back["grad_qkv"]), False)
    qkv_bias_g = back["qkv_sums"].reshape(3, columns)
    sliced = jnp.concatenate([qkv_bias_g[0], qkv_bias_g[2], back["in_sums"][0]])
    every = jnp.zeros((at.size,) + sliced.shape, jnp.float32)
    every = lax.dynamic_update_index_in_dim(every, sliced, at.rank, 0)
    row_terms = jnp.where(at.rank == 0, back["row_sums"], 0.0)
    small = lax.psum(
        jnp.concatenate([row_terms.reshape(-1), every.reshape(-1)]), ("tensor", "dp")
    )
    row_sums = small[: row_terms.size].reshape(row_terms.shape)
    mine = lax.dynamic_index_in_dim(
        small[row_terms.size :].reshape(every.shape), tensor, 0, keepdims=False
    )
    row_grads = back["time_sums"][:, 0]
    time_terms = jnp.stack([jnp.sum(fractions[:, None] * row_grads, 0), jnp.sum(row_grads, 0)])
    time_terms = jnp.where(jnp.logical_and(at.section == 0, at.rank == 0), time_terms, 0.0)
    grad_time = lax.psum(time_terms, AXES)

    def share(value, count, index):
        size = value.shape[-1] // count
        return lax.dynamic_slice_in_dim(value, index * size, size, value.ndim - 1)

    qv_g = share(mine[: 2 * columns].reshape(2, columns), at.dp, dp)
    in_bias_g = share(mine[2 * columns :], at.dp, dp)
    row_share = share(row_sums, at.tensor * at.dp, tensor * at.dp + dp)

    return (
        layer_outs[None],
        input_grads[None],
        qkv_g.reshape(-1, 3, columns)[None],
        qv_g[None],
        out_g[None],
        in_g[None],
        in_bias_g[None],
        down_g[None],
        row_share[None, :2],
        row_share[None, 2:],
        grad_time,
    )


def solution(mesh):
    return jax.shard_map(
        shards,
        mesh=mesh,
        in_specs=(
            P("dp", "tensor", None),
            P("dp"),
            P("dp", None),
            P(),
            P("section", None, None, "tensor"),
            P("section", None, "tensor"),
            P("section", "tensor", None),
            P("section", None, "tensor"),
            P("section", "tensor"),
            P("section", "tensor", None),
            P("section", None, None),
            P("section", None, None),
            P("dp", "tensor", None),
        ),
        out_specs=(
            P("section", "dp", "tensor", None),
            P("section", "dp", "tensor", None),
            P("section", "dp", None, "tensor"),
            P("section", None, ("tensor", "dp")),
            P("section", ("tensor", "dp"), None),
            P("section", "dp", "tensor"),
            P("section", ("tensor", "dp")),
            P("section", ("tensor", "dp"), None),
            P("section", None, ("tensor", "dp")),
            P("section", None, ("tensor", "dp")),
            P(),
        ),
        check_vma=False,
    )
```
